32 devices in a mesh: wide: 8 (over z, x), narrow: 4 (over y, core).
Axes of the slice: x: 2, y: 2, z: 4, core: 2. Of those that a mesh axis runs over, the one named last changes fastest.
Arguments:
- cube: bfloat16 [128, 384, 224], P('narrow', 'wide')
Outputs:
- restored: bfloat16 [128, 384, 224], P('narrow', 'wide')
- projector: float32 [224, 224], replicated
All inputs are finite; a program needn't handle non-finite values.
Results may differ from the reference program's by a relative error of at most 0.0034.
Values may be sent and summed in bfloat16 or wider, within the bound.
No kernel may reach another device: no remote copies, remote signals or barrier semaphores. Data moves between devices by JAX's collectives and lax.ppermute only.
A program may use at most 64 MiB of HBM per device.

```python
import jax
import jax.numpy as jnp
from jax import lax

TILE_ROWS = 32
BANDS = 224
RANK = 16
POWER_ITERS = 4
TV_ITERS = 3
HEIGHT = 128
WIDTH = 384
N_NARROW = 4


def draw_cube(key, part):
    key_abund, key_spec, key_noise, key_phase = jax.random.split(key, 4)
    sources = 3 * RANK
    abund = jax.random.normal(key_abund, (HEIGHT, WIDTH, sources), jnp.float32)
    noise = 0.3 * jax.random.normal(key_noise, (HEIGHT, WIDTH, BANDS), jnp.float32)
    spectra = jax.random.normal(key_spec, (sources, BANDS), jnp.float32)
    order = jnp.arange(sources, dtype=jnp.float32)
    spectra = spectra * jnp.exp(-0.07 * order)[:, None]
    phases = jax.random.uniform(key_phase, (2, sources), jnp.float32, 0.0, 1.0)
    rows = jnp.arange(HEIGHT, dtype=jnp.float32) / HEIGHT
    cols = jnp.arange(WIDTH, dtype=jnp.float32) / WIDTH
    row_mod = jnp.exp(0.5 * jnp.cos(2.0 * jnp.pi * (rows[:, None] + phases[0][None, :])))
    col_mod = jnp.exp(0.5 * jnp.cos(2.0 * jnp.pi * (cols[:, None] + phases[1][None, :])))
    abund = abund * row_mod[:, None, :] * col_mod[None, :, :]
    mixed = jnp.einsum('hwr,rb->hwb', abund, spectra, precision=lax.Precision.HIGHEST)
    spread = jnp.exp(jnp.log(3.0) * (rows[:, None] + cols[None, :]) * 0.5)
    return (0.25 * spread[:, :, None] * (mixed + noise)).astype(jnp.bfloat16)


def setup_inputs(seed: int = 0) -> dict:
    seeds = jax.random.split(jax.random.key(seed), 2)
    return {
        "cube": draw_cube(jax.random.fold_in(seeds[1], 71), 0),
    }


hi_prec = lax.Precision.HIGHEST

def smooth_step(field, fitted, grow, gcol, height, width):
    mask_x = ((grow >= 0) & (grow + 1 < height)).astype(jnp.float32)
    mask_y = ((gcol >= 0) & (gcol + 1 < width)).astype(jnp.float32)
    corner = field[:-1, :-1]
    grad_x = (field[1:, :-1] - corner) * mask_x[:-1, None, None]
    grad_y = (field[:-1, 1:] - corner) * mask_y[None, :-1, None]
    magnitude = jnp.sqrt(grad_x * grad_x + grad_y * grad_y + 0.25)
    flow_x = grad_x / magnitude
    flow_y = grad_y / magnitude
    diverg = flow_x[1:, 1:] - flow_x[:-1, 1:] + flow_y[1:, 1:] - flow_y[1:, :-1]
    centre = field[1:-1, 1:-1]
    return centre - 0.5 * (centre - fitted[1:-1, 1:-1] - 0.5 * diverg)

def subspace(gram):
    bands = lax.broadcasted_iota(jnp.float32, (BANDS, RANK), 0)
    cols = lax.broadcasted_iota(jnp.float32, (BANDS, RANK), 1)
    basis = jnp.cos(jnp.pi * (bands + 0.5) * cols / BANDS)
    for step in range(POWER_ITERS):
        grown = jnp.dot(gram, basis, precision=hi_prec)
        inner = jnp.dot(grown.T, grown, precision=hi_prec)
        lower = jnp.linalg.cholesky(inner)
        basis = jax.scipy.linalg.solve_triangular(lower, grown.T, lower=True).T
    return basis

def reference(cube):
    flat = cube.reshape(HEIGHT * WIDTH, BANDS)
    gram = lax.dot_general(flat.astype(jnp.float32), flat.astype(jnp.float32), (((0,), (0,)), ((), ())), preferred_element_type=jnp.float32)
    gram = gram / (HEIGHT * WIDTH)
    basis = subspace(gram)
    projector = jnp.dot(basis, basis.T, precision=hi_prec)
    basis_low = basis.astype(jnp.bfloat16)
    depth = TV_ITERS
    padded = jnp.pad(cube, ((depth, depth), (depth, depth), (0, 0)))
    gcol = jnp.arange(WIDTH + 2 * depth, dtype=jnp.int32) - depth

    def one_block(index):
        start = (index * TILE_ROWS).astype(jnp.int32)
        block = lax.dynamic_slice_in_dim(padded, start, TILE_ROWS + 2 * depth, 0)
        loading = jnp.einsum('hwb,br->hwr', block.astype(jnp.float32), basis_low.astype(jnp.float32), preferred_element_type=jnp.float32)
        fitted = jnp.einsum('hwr,br->hwb', loading, basis, precision=hi_prec)
        grow = start - depth + jnp.arange(TILE_ROWS + 2 * depth, dtype=jnp.int32)
        field = fitted
        rows, cols = (grow, gcol)
        for step in range(TV_ITERS):
            field = smooth_step(field, fitted, rows, cols, HEIGHT, WIDTH)
            fitted = fitted[1:-1, 1:-1]
            rows, cols = (rows[1:-1], cols[1:-1])
        return field.astype(jnp.bfloat16)
    blocks = lax.map(one_block, jnp.arange(N_NARROW, dtype=jnp.int32))
    restored = blocks.reshape(HEIGHT, WIDTH, BANDS)
    return (restored, projector)
```

```python
import functools

import jax
import jax.numpy as jnp
import numpy as np
from jax import lax
from jax.experimental import pallas as pl
from jax.experimental.pallas import tpu as pltpu
from jax.sharding import PartitionSpec as P

BANDS = 224
RANK = 16
POWER_ITERS = 4
TV_ITERS = 3
LANES = 256
HALF = 128
TAIL = BANDS - HALF
SIDE = 8

f32 = jnp.float32
bf16 = jnp.bfloat16


def iotas(shape):
    return lax.broadcasted_iota(jnp.int32, shape, 0), lax.broadcasted_iota(jnp.int32, shape, 1)


def gram_kernel(cube_ref, packed_ref, full):
    rows, cols, bands = cube_ref.shape
    flat = cube_ref[...].reshape(rows * cols, bands)
    full[...] = jnp.zeros_like(full)
    full[0:bands, 0:bands] = lax.dot_general(
        flat, flat, (((0,), (0,)), ((), ())), preferred_element_type=f32
    )
    i, j = iotas((HALF, HALF))
    first = full[0:HALF, 0:HALF]
    second = pltpu.roll(full[HALF:LANES, HALF:LANES], 1, 1)
    packed_ref[0:HALF, :] = jnp.where(j <= i, first, second)
    packed_ref[HALF:LANES, :] = full[0:HALF, HALF:LANES]


def split3(x):
    high = x.astype(bf16)
    rest = x - high.astype(f32)
    mid = rest.astype(bf16)
    low = (rest - mid.astype(f32)).astype(bf16)
    return high, mid, low


def product(left, right, dims):
    def dot(a, b):
        return lax.dot_general(a, b, (dims, ((), ())), preferred_element_type=f32)

    n = left[0].shape[0]
    top = dot(jnp.concatenate(left, axis=0), right[0])
    middle = dot(jnp.concatenate(left[:2], axis=0), right[1])
    last = dot(left[0], right[2])
    small = top[2 * n : 3 * n] + middle[n : 2 * n] + last
    return top[:n] + ((top[n : 2 * n] + middle[:n]) + small)


def unpack(packed, scale):
    i, j = iotas((HALF, HALF))
    merged = packed[0:HALF, :] * scale
    cross = packed[HALF:LANES, :] * scale
    first = jnp.where(j <= i, merged, 0.0) + jnp.where(j < i, merged, 0.0).T
    moved = pltpu.roll(merged, HALF - 1, 1)
    inside = (i < TAIL) & (j < TAIL)
    second = jnp.where(inside & (j >= i), moved, 0.0) + jnp.where(inside & (j > i), moved, 0.0).T
    return jnp.concatenate(
        [
            jnp.concatenate([first, cross], axis=1),
            jnp.concatenate([cross.T, second], axis=1),
        ],
        axis=0,
    )


def orthonormal(grown, inner):
    row = lax.broadcasted_iota(jnp.int32, (RANK, 1), 0)
    diagonal = jnp.ones((RANK, 1), f32)
    for k in range(RANK):
        pivot = inner[k : k + 1, k : k + 1]
        column = inner[:, k : k + 1]
        diagonal = jnp.where(row == k, pivot, diagonal)
        if k < RANK - 1:
            factor = jnp.where(row > k, column * (1.0 / pivot), 0.0)
            inner = inner - factor * inner[k : k + 1, :]
            grown = grown - factor * grown[k : k + 1, :]
    return grown * lax.rsqrt(diagonal)


def subspace(gram, start):
    parts = split3(gram)
    basis = start
    for _ in range(POWER_ITERS):
        grown = product(split3(basis), parts, ((1,), (0,)))
        pieces = split3(grown)
        inner = product(pieces, pieces, ((1,), (1,)))
        basis = orthonormal(grown, inner)
    return basis


def main_kernel(
    depth, inv_count, edge_ref, packed_ref, start_ref, mid_ref, above_ref, below_ref, side_ref,
    out_ref, proj_ref, fit, field_a, field_b
):
    rows, cols, bands = mid_ref.shape
    span = cols + SIDE
    basis = subspace(unpack(packed_ref[...], inv_count), start_ref[...])
    high, mid, low = split3(basis)
    right = jnp.concatenate([high, high, high, mid, mid, low], axis=0)
    left = jnp.concatenate([high, mid, low, high, mid, high], axis=0)
    tn = (((0,), (0,)), ((), ()))
    proj_ref[...] = lax.dot_general(left, right, tn, preferred_element_type=f32)[:bands, :bands]
    mixed = lax.dot_general(
        jnp.concatenate([high, high, high], axis=0),
        jnp.concatenate([high, mid, low], axis=0),
        tn,
        preferred_element_type=f32,
    )[:bands]
    mixed = mixed * 4.0
    mixed_high = mixed.astype(bf16)
    mixed_low = (mixed - mixed_high.astype(f32)).astype(bf16)

    def fitted(block):
        n, w, b = block.shape
        flat = block.reshape(n * w, b)
        res = jnp.dot(flat, mixed_high, preferred_element_type=f32)
        res = res + jnp.dot(flat, mixed_low, preferred_element_type=f32)
        return res.reshape(n, w, LANES)

    fit[0:depth, 0:cols, :] = fitted(above_ref[...])
    fit[depth : depth + rows, 0:cols, :] = fitted(mid_ref[...])
    fit[depth + rows :, 0:cols, :] = fitted(below_ref[...])
    side = side_ref[...].astype(f32).reshape((rows + 2 * depth) * SIDE, bands).astype(bf16)
    res = jnp.dot(side, mixed_high, preferred_element_type=f32)
    res = res + jnp.dot(side, mixed_low, preferred_element_type=f32)
    fit[:, cols:span, :] = res.reshape(rows + 2 * depth, SIDE, LANES)

    at_top, at_bottom, at_left, at_right = (edge_ref[n] for n in range(4))
    place = lax.broadcasted_iota(jnp.int32, (span, HALF), 0)
    closed = ((place == cols - 1) & (at_right > 0)) | ((place == span - 1) & (at_left > 0))
    keep = jnp.where(closed, 0.0, 1.0).astype(f32)

    def slopes(now, later):
        down = later - now
        across = (pltpu.roll(now, span - 1, 0) - now) * keep
        inverse = lax.rsqrt(down * down + across * across + 4.0)
        return down * inverse, across * inverse

    def step(source, target, first, last, final):
        @pl.when(at_top > 0)
        def _():
            source[depth - 1] = source[depth]

        @pl.when(at_bottom > 0)
        def _():
            source[depth + rows] = source[depth + rows - 1]

        lanes = [slice(0, HALF), slice(HALF, LANES)]
        carry = []
        for lane in lanes:
            before, now = source[first - 1, :, lane], source[first, :, lane]
            carry += [now, slopes(before, now)[0]]

        def body(r, carry):
            out = []
            for n, lane in enumerate(lanes):
                now, before = carry[2 * n], carry[2 * n + 1]
                later = source[r + 1, :, lane]
                down, across = slopes(now, later)
                value = (0.5 * (now + fit[r, :, lane]) + (down - before)) + (
                    across - pltpu.roll(across, 1, 0)
                )
                if final:
                    value = (value[:cols] * 0.25).astype(bf16)
                    if n == 0:
                        out_ref[r - depth, :, 0:HALF] = value
                    else:
                        out_ref[r - depth, :, HALF:bands] = value[:, : bands - HALF]
                else:
                    target[r, :, lane] = value
                out += [later, down]
            return tuple(out)

        lax.fori_loop(first, last, body, tuple(carry), unroll=2)

    sources = [fit, field_a, field_b]
    for s in range(TV_ITERS):
        if s == 0:
            @pl.when(at_top > 0)
            def _():
                fit[depth - 1] = fit[depth]

        final = s == TV_ITERS - 1
        target = None if final else sources[s + 1]
        step(sources[s], target, s + 1, rows + 2 * depth - 1 - s, final)


def start_basis():
    bands = np.arange(BANDS, dtype=np.float32)[None, :]
    cols = np.arange(RANK, dtype=np.float32)[:, None]
    angle = np.float32(np.pi) * (bands + np.float32(0.5)) * cols / np.float32(BANDS)
    return np.pad(np.cos(angle).astype(np.float32), ((0, 0), (0, LANES - BANDS)))


def neighbours(block, axis, dim, width):
    count = lax.axis_size(axis)
    size = block.shape[dim]
    head = lax.slice_in_dim(block, 0, width, axis=dim)
    tail = lax.slice_in_dim(block, size - width, size, axis=dim)
    before = lax.ppermute(tail, axis, [(i, i + 1) for i in range(count - 1)])
    after = lax.ppermute(head, axis, [(i + 1, i) for i in range(count - 1)])
    return before, after


def body(cube):
    n_rows = lax.axis_size("narrow")
    n_cols = lax.axis_size("wide")
    count = n_rows * n_cols
    rows, cols, bands = cube.shape
    depth = TV_ITERS
    axes = ("wide", "narrow")

    left, right = neighbours(cube, "wide", 1, depth)
    packed = pl.pallas_call(
        gram_kernel,
        out_shape=jax.ShapeDtypeStruct((LANES, HALF), f32),
        scratch_shapes=[pltpu.VMEM((LANES, LANES), f32)],
        compiler_params=pltpu.CompilerParams(vmem_limit_bytes=48 * 2**20),
    )(cube)
    shares = lax.all_to_all(
        packed.reshape(count, LANES // count, HALF), axes, split_axis=0, concat_axis=0
    )
    share = jnp.sum(shares, axis=0)
    gathered = lax.all_to_all(
        jnp.broadcast_to(share[None], (count, LANES // count, HALF)), axes, split_axis=0, concat_axis=0
    ).reshape(LANES, HALF)

    gap = jnp.zeros((rows, SIDE - 2 * depth, bands), cube.dtype)
    side = jnp.concatenate([right, gap, left], axis=1)
    above, below = neighbours(jnp.concatenate([cube[:depth], cube[rows - depth :]], axis=0), "narrow", 0, depth)
    side_above, side_below = neighbours(side, "narrow", 0, depth)
    side = jnp.concatenate([side_above, side, side_below], axis=0)

    row, col = lax.axis_index("narrow"), lax.axis_index("wide")
    edges = jnp.stack([row == 0, row == n_rows - 1, col == 0, col == n_cols - 1]).astype(jnp.int32)
    tall, span = rows + 2 * depth, cols + SIDE
    vmem = pl.BlockSpec(memory_space=pltpu.VMEM)
    inv_count = 1.0 / (count * rows * cols)
    restored, projector = pl.pallas_call(
        functools.partial(main_kernel, depth, inv_count),
        in_specs=[pl.BlockSpec(memory_space=pltpu.SMEM)] + [vmem] * 6,
        out_specs=[vmem, vmem],
        out_shape=[
            jax.ShapeDtypeStruct((rows, cols, bands), bf16),
            jax.ShapeDtypeStruct((bands, bands), f32),
        ],
        scratch_shapes=[pltpu.VMEM((tall, span, LANES), f32)] * 3,
        compiler_params=pltpu.CompilerParams(vmem_limit_bytes=48 * 2**20),
    )(edges, gathered, jnp.asarray(start_basis()), cube, above, below, side)
    return restored, projector


def solution(mesh):
    return jax.shard_map(
        body,
        mesh=mesh,
        in_specs=(P("narrow", "wide", None),),
        out_specs=(P("narrow", "wide", None), P()),
        check_vma=False,
    )
```

```python
import functools

import jax
import jax.numpy as jnp
import numpy as np
from jax import lax
from jax.experimental import pallas as pl
from jax.experimental.pallas import tpu as pltpu
from jax.sharding import PartitionSpec as P

BANDS = 224
RANK = 16
POWER_ITERS = 4
TV_ITERS = 3
LANES = 256
HALF = 128
TAIL = BANDS - HALF
SIDE = 8

f32 = jnp.float32
bf16 = jnp.bfloat16


def iotas(shape):
    return lax.broadcasted_iota(jnp.int32, shape, 0), lax.broadcasted_iota(jnp.int32, shape, 1)


def gram_kernel(cube_ref, packed_ref, full):
    rows, cols, bands = cube_ref.shape
    flat = cube_ref[...].reshape(rows * cols, bands)
    full[...] = jnp.zeros_like(full)
    full[0:bands, 0:bands] = lax.dot_general(
        flat, flat, (((0,), (0,)), ((), ())), preferred_element_type=f32
    )
    i, j = iotas((HALF, HALF))
    first = full[0:HALF, 0:HALF]
    second = pltpu.roll(full[HALF:LANES, HALF:LANES], 1, 1)
    packed_ref[0:HALF, :] = jnp.where(j <= i, first, second)
    packed_ref[HALF:LANES, :] = full[0:HALF, HALF:LANES]


def split3(x):
    high = x.astype(bf16)
    rest = x - high.astype(f32)
    mid = rest.astype(bf16)
    low = (rest - mid.astype(f32)).astype(bf16)
    return high, mid, low


def product(left, right, dims):
    def dot(a, b):
        return lax.dot_general(a, b, (dims, ((), ())), preferred_element_type=f32)

    n = left[0].shape[0]
    top = dot(jnp.concatenate(left, axis=0), right[0])
    middle = dot(jnp.concatenate(left[:2], axis=0), right[1])
    last = dot(left[0], right[2])
    small = top[2 * n : 3 * n] + middle[n : 2 * n] + last
    return top[:n] + ((top[n : 2 * n] + middle[:n]) + small)


def unpack(packed, scale):
    i, j = iotas((HALF, HALF))
    merged = packed[0:HALF, :] * scale
    cross = packed[HALF:LANES, :] * scale
    first = jnp.where(j <= i, merged, 0.0) + jnp.where(j < i, merged, 0.0).T
    moved = pltpu.roll(merged, HALF - 1, 1)
    inside = (i < TAIL) & (j < TAIL)
    second = jnp.where(inside & (j >= i), moved, 0.0) + jnp.where(inside & (j > i), moved, 0.0).T
    return jnp.concatenate(
        [
            jnp.concatenate([first, cross], axis=1),
            jnp.concatenate([cross.T, second], axis=1),
        ],
        axis=0,
    )


def orthonormal(grown, inner):
    row = lax.broadcasted_iota(jnp.int32, (RANK, 1), 0)
    diagonal = jnp.ones((RANK, 1), f32)
    for k in range(RANK):
        pivot = inner[k : k + 1, k : k + 1]
        column = inner[:, k : k + 1]
        diagonal = jnp.where(row == k, pivot, diagonal)
        if k < RANK - 1:
            factor = jnp.where(row > k, column * (1.0 / pivot), 0.0)
            inner = inner - factor * inner[k : k + 1, :]
            grown = grown - factor * grown[k : k + 1, :]
    return grown * lax.rsqrt(diagonal)


def subspace(gram, start):
    parts = split3(gram)
    basis = start
    for _ in range(POWER_ITERS):
        grown = product(split3(basis), parts, ((1,), (0,)))
        pieces = split3(grown)
        inner = product(pieces, pieces, ((1,), (1,)))
        basis = orthonormal(grown, inner)
    return basis


def main_kernel(
    depth, inv_count, edge_ref, packed_ref, start_ref, mid_ref, above_ref, below_ref, side_ref,
    out_ref, proj_ref, fit, field_a, field_b
):
    rows, cols, bands = mid_ref.shape
    span = cols + SIDE
    basis = subspace(unpack(packed_ref[...], inv_count), start_ref[...])
    high, mid, low = split3(basis)
    right = jnp.concatenate([high, high, high, mid, mid, low], axis=0)
    left = jnp.concatenate([high, mid, low, high, mid, high], axis=0)
    tn = (((0,), (0,)), ((), ()))
    proj_ref[...] = lax.dot_general(left, right, tn, preferred_element_type=f32)[:bands, :bands]
    mixed = lax.dot_general(
        jnp.concatenate([high, high, high], axis=0),
        jnp.concatenate([high, mid, low], axis=0),
        tn,
        preferred_element_type=f32,
    )[:bands]
    mixed = mixed * 4.0
    mixed_high = mixed.astype(bf16)
    mixed_low = (mixed - mixed_high.astype(f32)).astype(bf16)

    def fitted(block):
        n, w, b = block.shape
        if w % 16:
            flat = block.astype(f32).reshape(n * w, b).astype(bf16)
        else:
            flat = block.reshape(n * w, b)
        res = jnp.dot(flat, mixed_high, preferred_element_type=f32)
        res = res + jnp.dot(flat, mixed_low, preferred_element_type=f32)
        return res.reshape(n, w, LANES)

    fit[0:depth] = fitted(above_ref[...])
    fit[depth : depth + rows, 0:cols, :] = fitted(mid_ref[...])
    fit[depth : depth + rows, cols:span, :] = fitted(side_ref[...])
    fit[depth + rows :] = fitted(below_ref[...])

    at_top, at_bottom, at_left, at_right = (edge_ref[n] for n in range(4))
    place = lax.broadcasted_iota(jnp.int32, (span, HALF), 0)
    closed = ((place == cols - 1) & (at_right > 0)) | ((place == span - 1) & (at_left > 0))
    keep = jnp.where(closed, 0.0, 1.0).astype(f32)

    def slopes(now, later):
        down = later - now
        across = (pltpu.roll(now, span - 1, 0) - now) * keep
        inverse = lax.rsqrt(down * down + across * across + 4.0)
        return down * inverse, across * inverse

    def step(source, target, first, last, final):
        @pl.when(at_top > 0)
        def _():
            source[depth - 1] = source[depth]

        @pl.when(at_bottom > 0)
        def _():
            source[depth + rows] = source[depth + rows - 1]

        lanes = [slice(0, HALF), slice(HALF, LANES)]
        carry = []
        for lane in lanes:
            before, now = source[first - 1, :, lane], source[first, :, lane]
            carry += [now, slopes(before, now)[0]]

        def body(r, carry):
            out = []
            for n, lane in enumerate(lanes):
                now, before = carry[2 * n], carry[2 * n + 1]
                later = source[r + 1, :, lane]
                down, across = slopes(now, later)
                value = (0.5 * (now + fit[r, :, lane]) + (down - before)) + (
                    across - pltpu.roll(across, 1, 0)
                )
                if final:
                    value = (value[:cols] * 0.25).astype(bf16)
                    if n == 0:
                        out_ref[r - depth, :, 0:HALF] = value
                    else:
                        out_ref[r - depth, :, HALF:bands] = value[:, : bands - HALF]
                else:
                    target[r, :, lane] = value
                out += [later, down]
            return tuple(out)

        lax.fori_loop(first, last, body, tuple(carry), unroll=2)

    sources = [fit, field_a, field_b]
    for s in range(TV_ITERS):
        if s == 0:
            @pl.when(at_top > 0)
            def _():
                fit[depth - 1] = fit[depth]

        final = s == TV_ITERS - 1
        target = None if final else sources[s + 1]
        step(sources[s], target, s + 1, rows + 2 * depth - 1 - s, final)


def start_basis():
    bands = np.arange(BANDS, dtype=np.float32)[None, :]
    cols = np.arange(RANK, dtype=np.float32)[:, None]
    angle = np.float32(np.pi) * (bands + np.float32(0.5)) * cols / np.float32(BANDS)
    return np.pad(np.cos(angle).astype(np.float32), ((0, 0), (0, LANES - BANDS)))


def neighbours(block, axis, dim, width):
    count = lax.axis_size(axis)
    size = block.shape[dim]
    head = lax.slice_in_dim(block, 0, width, axis=dim)
    tail = lax.slice_in_dim(block, size - width, size, axis=dim)
    before = lax.ppermute(tail, axis, [(i, i + 1) for i in range(count - 1)])
    after = lax.ppermute(head, axis, [(i + 1, i) for i in range(count - 1)])
    return before, after


def exchange(pieces, axis):
    return lax.all_to_all(pieces, axis, split_axis=0, concat_axis=0)


def spread(piece, count):
    return jnp.broadcast_to(piece[None], (count,) + piece.shape)


def body(cube):
    n_rows = lax.axis_size("narrow")
    n_cols = lax.axis_size("wide")
    count = n_rows * n_cols
    rows, cols, bands = cube.shape
    depth = TV_ITERS

    left, right = neighbours(cube, "wide", 1, depth)
    packed = pl.pallas_call(
        gram_kernel,
        out_shape=jax.ShapeDtypeStruct((LANES, HALF), f32),
        scratch_shapes=[pltpu.VMEM((LANES, LANES), f32)],
        compiler_params=pltpu.CompilerParams(vmem_limit_bytes=48 * 2**20),
    )(cube)
    part = exchange(packed.reshape(n_cols, LANES // n_cols, HALF), "wide")
    part = exchange(spread(jnp.sum(part, axis=0), n_rows), "narrow")
    gathered = exchange(spread(jnp.sum(part, axis=0), n_cols), "wide").reshape(LANES, HALF)

    gap = jnp.zeros((rows, SIDE - 2 * depth, bands), cube.dtype)
    side = jnp.concatenate([right, gap, left], axis=1)
    above, below = neighbours(
        jnp.concatenate(
            [
                jnp.concatenate([cube[:depth], side[:depth]], axis=1),
                jnp.concatenate([cube[rows - depth :], side[rows - depth :]], axis=1),
            ],
            axis=0,
        ),
        "narrow",
        0,
        depth,
    )

    row, col = lax.axis_index("narrow"), lax.axis_index("wide")
    edges = jnp.stack([row == 0, row == n_rows - 1, col == 0, col == n_cols - 1]).astype(jnp.int32)
    tall, span = rows + 2 * depth, cols + SIDE
    vmem = pl.BlockSpec(memory_space=pltpu.VMEM)
    inv_count = 1.0 / (count * rows * cols)
    restored, projector = pl.pallas_call(
        functools.partial(main_kernel, depth, inv_count),
        in_specs=[pl.BlockSpec(memory_space=pltpu.SMEM)] + [vmem] * 6,
        out_specs=[vmem, vmem],
        out_shape=[
            jax.ShapeDtypeStruct((rows, cols, bands), bf16),
            jax.ShapeDtypeStruct((bands, bands), f32),
        ],
        scratch_shapes=[pltpu.VMEM((tall, span, LANES), f32)] * 3,
        compiler_params=pltpu.CompilerParams(vmem_limit_bytes=48 * 2**20),
    )(edges, gathered, jnp.asarray(start_basis()), cube, above, below, side)
    return restored, projector


def solution(mesh):
    return jax.shard_map(
        body,
        mesh=mesh,
        in_specs=(P("narrow", "wide", None),),
        out_specs=(P("narrow", "wide", None), P()),
        check_vma=False,
    )
```

```python
import functools

import jax
import jax.numpy as jnp
import numpy as np
from jax import lax
from jax.experimental import pallas as pl
from jax.experimental.pallas import tpu as pltpu
from jax.sharding import PartitionSpec as P

BANDS = 224
RANK = 16
POWER_ITERS = 4
TV_ITERS = 3
LANES = 256
HALF = 128
TAIL = BANDS - HALF
SIDE = 8

f32 = jnp.float32
bf16 = jnp.bfloat16


def iotas(shape):
    return lax.broadcasted_iota(jnp.int32, shape, 0), lax.broadcasted_iota(jnp.int32, shape, 1)


def gram_kernel(pieces, cube_ref, packed_ref, block, full, sems):
    rows, cols, bands = cube_ref.shape
    high = rows // pieces

    def copy(n):
        part = pl.ds(n * high, high)
        return pltpu.make_async_copy(cube_ref.at[part], block.at[part], sems.at[n])

    for n in range(pieces):
        copy(n).start()
    full[...] = jnp.zeros_like(full)
    total = None
    for n in range(pieces):
        copy(n).wait()
        flat = block[n * high : (n + 1) * high].reshape(high * cols, bands)
        term = lax.dot_general(flat, flat, (((0,), (0,)), ((), ())), preferred_element_type=f32)
        total = term if total is None else total + term
    full[0:bands, 0:bands] = total
    i, j = iotas((HALF, HALF))
    first = full[0:HALF, 0:HALF]
    second = pltpu.roll(full[HALF:LANES, HALF:LANES], 1, 1)
    packed_ref[0:HALF, :] = jnp.where(j <= i, first, second)
    packed_ref[HALF:LANES, :] = full[0:HALF, HALF:LANES]


def split3(x):
    high = x.astype(bf16)
    rest = x - high.astype(f32)
    mid = rest.astype(bf16)
    low = (rest - mid.astype(f32)).astype(bf16)
    return high, mid, low


def product(left, right, dims):
    def dot(a, b):
        return lax.dot_general(a, b, (dims, ((), ())), preferred_element_type=f32)

    n = left[0].shape[0]
    top = dot(jnp.concatenate(left, axis=0), right[0])
    middle = dot(jnp.concatenate(left[:2], axis=0), right[1])
    last = dot(left[0], right[2])
    small = top[2 * n : 3 * n] + middle[n : 2 * n] + last
    return top[:n] + ((top[n : 2 * n] + middle[:n]) + small)


def unpack(packed, scale):
    i, j = iotas((HALF, HALF))
    merged = packed[0:HALF, :] * scale
    cross = packed[HALF:LANES, :] * scale
    first = jnp.where(j <= i, merged, 0.0) + jnp.where(j < i, merged, 0.0).T
    moved = pltpu.roll(merged, HALF - 1, 1)
    inside = (i < TAIL) & (j < TAIL)
    second = jnp.where(inside & (j >= i), moved, 0.0) + jnp.where(inside & (j > i), moved, 0.0).T
    return jnp.concatenate(
        [
            jnp.concatenate([first, cross], axis=1),
            jnp.concatenate([cross.T, second], axis=1),
        ],
        axis=0,
    )


def orthonormal(grown, inner):
    row = lax.broadcasted_iota(jnp.int32, (RANK, 1), 0)
    diagonal = jnp.ones((RANK, 1), f32)
    for k in range(RANK):
        pivot = inner[k : k + 1, k : k + 1]
        column = inner[:, k : k + 1]
        diagonal = jnp.where(row == k, pivot, diagonal)
        if k < RANK - 1:
            factor = jnp.where(row > k, column * (1.0 / pivot), 0.0)
            inner = inner - factor * inner[k : k + 1, :]
            grown = grown - factor * grown[k : k + 1, :]
    return grown * lax.rsqrt(diagonal)


def subspace(gram, start):
    parts = split3(gram)
    basis = start
    for _ in range(POWER_ITERS):
        grown = product(split3(basis), parts, ((1,), (0,)))
        pieces = split3(grown)
        inner = product(pieces, pieces, ((1,), (1,)))
        basis = orthonormal(grown, inner)
    return basis


def main_kernel(
    depth, inv_count, edge_ref, packed_ref, start_ref, mid_ref, above_ref, below_ref, side_ref,
    out_ref, proj_ref, fit, field_a, field_b
):
    rows, cols, bands = mid_ref.shape
    span = cols + SIDE
    basis = subspace(unpack(packed_ref[...], inv_count), start_ref[...])
    high, mid, low = split3(basis)
    right = jnp.concatenate([high, high, high, mid, mid, low], axis=0)
    left = jnp.concatenate([high, mid, low, high, mid, high], axis=0)
    tn = (((0,), (0,)), ((), ()))
    proj_ref[...] = lax.dot_general(left, right, tn, preferred_element_type=f32)[:bands, :bands]
    mixed = lax.dot_general(
        jnp.concatenate([high, high, high], axis=0),
        jnp.concatenate([high, mid, low], axis=0),
        tn,
        preferred_element_type=f32,
    )[:bands]
    mixed = mixed * 4.0
    mixed_high = mixed.astype(bf16)
    mixed_low = (mixed - mixed_high.astype(f32)).astype(bf16)

    def fitted(block):
        n, w, b = block.shape
        if w % 16:
            flat = block.astype(f32).reshape(n * w, b).astype(bf16)
        else:
            flat = block.reshape(n * w, b)
        res = jnp.dot(flat, mixed_high, preferred_element_type=f32)
        res = res + jnp.dot(flat, mixed_low, preferred_element_type=f32)
        return res.reshape(n, w, LANES)

    fit[0:depth] = fitted(above_ref[...])
    fit[depth : depth + rows, 0:cols, :] = fitted(mid_ref[...])
    fit[depth : depth + rows, cols:span, :] = fitted(side_ref[...])
    fit[depth + rows :] = fitted(below_ref[...])

    at_top, at_bottom, at_left, at_right = (edge_ref[n] for n in range(4))
    place = lax.broadcasted_iota(jnp.int32, (span, HALF), 0)
    closed = ((place == cols - 1) & (at_right > 0)) | ((place == span - 1) & (at_left > 0))
    keep = jnp.where(closed, 0.0, 1.0).astype(f32)

    def slopes(now, later):
        down = later - now
        across = (pltpu.roll(now, span - 1, 0) - now) * keep
        inverse = lax.rsqrt(down * down + across * across + 4.0)
        return down * inverse, across * inverse

    def step(source, target, first, last, final):
        @pl.when(at_top > 0)
        def _():
            source[depth - 1] = source[depth]

        @pl.when(at_bottom > 0)
        def _():
            source[depth + rows] = source[depth + rows - 1]

        lanes = [slice(0, HALF), slice(HALF, LANES)]
        carry = []
        for lane in lanes:
            before, now = source[first - 1, :, lane], source[first, :, lane]
            carry += [now, slopes(before, now)[0]]

        def body(r, carry):
            out = []
            for n, lane in enumerate(lanes):
                now, before = carry[2 * n], carry[2 * n + 1]
                later = source[r + 1, :, lane]
                down, across = slopes(now, later)
                value = (0.5 * (now + fit[r, :, lane]) + (down - before)) + (
                    across - pltpu.roll(across, 1, 0)
                )
                if final:
                    value = (value[:cols] * 0.25).astype(bf16)
                    if n == 0:
                        out_ref[r - depth, :, 0:HALF] = value
                    else:
                        out_ref[r - depth, :, HALF:bands] = value[:, : bands - HALF]
                else:
                    target[r, :, lane] = value
                out += [later, down]
            return tuple(out)

        lax.fori_loop(first, last, body, tuple(carry), unroll=2)

    sources = [fit, field_a, field_b]
    for s in range(TV_ITERS):
        if s == 0:
            @pl.when(at_top > 0)
            def _():
                fit[depth - 1] = fit[depth]

        final = s == TV_ITERS - 1
        target = None if final else sources[s + 1]
        step(sources[s], target, s + 1, rows + 2 * depth - 1 - s, final)


def start_basis():
    bands = np.arange(BANDS, dtype=np.float32)[None, :]
    cols = np.arange(RANK, dtype=np.float32)[:, None]
    angle = np.float32(np.pi) * (bands + np.float32(0.5)) * cols / np.float32(BANDS)
    return np.pad(np.cos(angle).astype(np.float32), ((0, 0), (0, LANES - BANDS)))


def neighbours(block, axis, dim, width):
    count = lax.axis_size(axis)
    size = block.shape[dim]
    head = lax.slice_in_dim(block, 0, width, axis=dim)
    tail = lax.slice_in_dim(block, size - width, size, axis=dim)
    before = lax.ppermute(tail, axis, [(i, i + 1) for i in range(count - 1)])
    after = lax.ppermute(head, axis, [(i + 1, i) for i in range(count - 1)])
    return before, after


def exchange(pieces, axis):
    return lax.all_to_all(pieces, axis, split_axis=0, concat_axis=0)


def spread(piece, count):
    return jnp.broadcast_to(piece[None], (count,) + piece.shape)


def body(cube):
    n_rows = lax.axis_size("narrow")
    n_cols = lax.axis_size("wide")
    rows, cols, bands = cube.shape
    depth = TV_ITERS

    left, right = neighbours(cube, "wide", 1, depth)
    pieces = 4 if rows % 4 == 0 else 1
    packed = pl.pallas_call(
        functools.partial(gram_kernel, pieces),
        in_specs=[pl.BlockSpec(memory_space=pl.ANY)],
        out_shape=jax.ShapeDtypeStruct((LANES, HALF), f32),
        scratch_shapes=[
            pltpu.VMEM(cube.shape, cube.dtype),
            pltpu.VMEM((LANES, LANES), f32),
            pltpu.SemaphoreType.DMA((pieces,)),
        ],
        compiler_params=pltpu.CompilerParams(vmem_limit_bytes=48 * 2**20),
    )(cube)
    packed, left, right = lax.optimization_barrier((packed, left, right))
    count = n_rows * n_cols
    axes = ("wide", "narrow")
    part = exchange(packed.reshape(count, LANES // count, HALF), axes)
    gathered = exchange(spread(jnp.sum(part, axis=0), count), axes).reshape(LANES, HALF)

    gap = jnp.zeros((rows, SIDE - 2 * depth, bands), cube.dtype)
    side = jnp.concatenate([right, gap, left], axis=1)
    above, below = neighbours(
        jnp.concatenate(
            [
                jnp.concatenate([cube[:depth], side[:depth]], axis=1),
                jnp.concatenate([cube[rows - depth :], side[rows - depth :]], axis=1),
            ],
            axis=0,
        ),
        "narrow",
        0,
        depth,
    )

    row, col = lax.axis_index("narrow"), lax.axis_index("wide")
    edges = jnp.stack([row == 0, row == n_rows - 1, col == 0, col == n_cols - 1]).astype(jnp.int32)
    tall, span = rows + 2 * depth, cols + SIDE
    vmem = pl.BlockSpec(memory_space=pltpu.VMEM)
    inv_count = 1.0 / (count * rows * cols)
    restored, projector = pl.pallas_call(
        functools.partial(main_kernel, depth, inv_count),
        in_specs=[pl.BlockSpec(memory_space=pltpu.SMEM)] + [vmem] * 6,
        out_specs=[vmem, vmem],
        out_shape=[
            jax.ShapeDtypeStruct((rows, cols, bands), bf16),
            jax.ShapeDtypeStruct((bands, bands), f32),
        ],
        scratch_shapes=[pltpu.VMEM((tall, span, LANES), f32)] * 3,
        compiler_params=pltpu.CompilerParams(vmem_limit_bytes=48 * 2**20),
    )(edges, gathered, jnp.asarray(start_basis()), cube, above, below, side)
    return restored, projector


def solution(mesh):
    return jax.shard_map(
        body,
        mesh=mesh,
        in_specs=(P("narrow", "wide", None),),
        out_specs=(P("narrow", "wide", None), P()),
        check_vma=False,
    )
```

```python
import functools

import jax
import jax.numpy as jnp
import numpy as np
from jax import lax
from jax.experimental import pallas as pl
from jax.experimental.pallas import tpu as pltpu
from jax.sharding import PartitionSpec as P

BANDS = 224
RANK = 16
POWER_ITERS = 4
TV_ITERS = 3
LANES = 256
HALF = 128
TAIL = BANDS - HALF
SIDE = 8
SLICE = 8
SLICES = LANES // SLICE

f32 = jnp.float32
bf16 = jnp.bfloat16


def iotas(shape):
    return lax.broadcasted_iota(jnp.int32, shape, 0), lax.broadcasted_iota(jnp.int32, shape, 1)


def gram_kernel(cube_ref, *refs):
    packed_refs, full = refs[:-1], refs[-1]
    rows, cols, bands = cube_ref.shape
    flat = cube_ref[...].reshape(rows * cols, bands)
    full[...] = jnp.zeros_like(full)
    full[0:bands, 0:bands] = lax.dot_general(
        flat, flat, (((0,), (0,)), ((), ())), preferred_element_type=f32
    )
    i, j = iotas((HALF, HALF))
    first = full[0:HALF, 0:HALF]
    second = pltpu.roll(full[HALF:LANES, HALF:LANES], 1, 1)
    merged = jnp.where(j <= i, first, second)
    cross = full[0:HALF, HALF:LANES]
    for n, ref in enumerate(packed_refs):
        source, start = (merged, n * SLICE) if n * SLICE < HALF else (cross, n * SLICE - HALF)
        ref[...] = source[start : start + SLICE]


def split3(x):
    high = x.astype(bf16)
    rest = x - high.astype(f32)
    mid = rest.astype(bf16)
    low = (rest - mid.astype(f32)).astype(bf16)
    return high, mid, low


def product(left, right, dims):
    def dot(a, b):
        return lax.dot_general(a, b, (dims, ((), ())), preferred_element_type=f32)

    n = left[0].shape[0]
    top = dot(jnp.concatenate(left, axis=0), right[0])
    middle = dot(jnp.concatenate(left[:2], axis=0), right[1])
    last = dot(left[0], right[2])
    small = top[2 * n : 3 * n] + middle[n : 2 * n] + last
    return top[:n] + ((top[n : 2 * n] + middle[:n]) + small)


def unpack(packed, scale):
    i, j = iotas((HALF, HALF))
    merged = jnp.concatenate(packed[: SLICES // 2], axis=0) * scale
    cross = jnp.concatenate(packed[SLICES // 2 :], axis=0) * scale
    first = jnp.where(j <= i, merged, 0.0) + jnp.where(j < i, merged, 0.0).T
    moved = pltpu.roll(merged, HALF - 1, 1)
    inside = (i < TAIL) & (j < TAIL)
    second = jnp.where(inside & (j >= i), moved, 0.0) + jnp.where(inside & (j > i), moved, 0.0).T
    return jnp.concatenate(
        [
            jnp.concatenate([first, cross], axis=1),
            jnp.concatenate([cross.T, second], axis=1),
        ],
        axis=0,
    )


def orthonormal(grown, inner):
    row = lax.broadcasted_iota(jnp.int32, (RANK, 1), 0)
    diagonal = jnp.ones((RANK, 1), f32)
    for k in range(RANK):
        pivot = inner[k : k + 1, k : k + 1]
        column = inner[:, k : k + 1]
        diagonal = jnp.where(row == k, pivot, diagonal)
        if k < RANK - 1:
            factor = jnp.where(row > k, column * (1.0 / pivot), 0.0)
            inner = inner - factor * inner[k : k + 1, :]
            grown = grown - factor * grown[k : k + 1, :]
    return grown * lax.rsqrt(diagonal)


def subspace(gram, start):
    parts = split3(gram)
    basis = start
    for _ in range(POWER_ITERS):
        grown = product(split3(basis), parts, ((1,), (0,)))
        pieces = split3(grown)
        inner = product(pieces, pieces, ((1,), (1,)))
        basis = orthonormal(grown, inner)
    return basis


def main_kernel(
    depth, inv_count, edge_ref, start_ref, mid_ref, above_ref, below_ref, side_ref, *refs
):
    packed_refs = refs[:SLICES]
    out_ref, proj_ref, fit, field_a, field_b = refs[SLICES:]
    rows, cols, bands = mid_ref.shape
    span = cols + SIDE
    basis = subspace(unpack([ref[...] for ref in packed_refs], inv_count), start_ref[...])
    high, mid, low = split3(basis)
    right = jnp.concatenate([high, high, high, mid, mid, low], axis=0)
    left = jnp.concatenate([high, mid, low, high, mid, high], axis=0)
    tn = (((0,), (0,)), ((), ()))
    proj_ref[...] = lax.dot_general(left, right, tn, preferred_element_type=f32)[:bands, :bands]
    mixed = lax.dot_general(
        jnp.concatenate([high, high, high], axis=0),
        jnp.concatenate([high, mid, low], axis=0),
        tn,
        preferred_element_type=f32,
    )[:bands]
    mixed = mixed * 4.0
    mixed_high = mixed.astype(bf16)
    mixed_low = (mixed - mixed_high.astype(f32)).astype(bf16)

    def fitted(block):
        n, w, b = block.shape
        if w % 16:
            flat = block.astype(f32).reshape(n * w, b).astype(bf16)
        else:
            flat = block.reshape(n * w, b)
        res = jnp.dot(flat, mixed_high, preferred_element_type=f32)
        res = res + jnp.dot(flat, mixed_low, preferred_element_type=f32)
        return res.reshape(n, w, LANES)

    fit[0:depth] = fitted(above_ref[...])
    fit[depth : depth + rows, 0:cols, :] = fitted(mid_ref[...])
    fit[depth : depth + rows, cols:span, :] = fitted(side_ref[...])
    fit[depth + rows :] = fitted(below_ref[...])

    at_top, at_bottom, at_left, at_right = (edge_ref[n] for n in range(4))
    place = lax.broadcasted_iota(jnp.int32, (span, HALF), 0)
    closed = ((place == cols - 1) & (at_right > 0)) | ((place == span - 1) & (at_left > 0))
    keep = jnp.where(closed, 0.0, 1.0).astype(f32)

    def slopes(now, later):
        down = later - now
        across = (pltpu.roll(now, span - 1, 0) - now) * keep
        inverse = lax.rsqrt(down * down + across * across + 4.0)
        return down * inverse, across * inverse

    def step(source, target, first, last, final):
        @pl.when(at_top > 0)
        def _():
            source[depth - 1] = source[depth]

        @pl.when(at_bottom > 0)
        def _():
            source[depth + rows] = source[depth + rows - 1]

        lanes = [slice(0, HALF), slice(HALF, LANES)]
        carry = []
        for lane in lanes:
            before, now = source[first - 1, :, lane], source[first, :, lane]
            carry += [now, slopes(before, now)[0]]

        def body(r, carry):
            out = []
            for n, lane in enumerate(lanes):
                now, before = carry[2 * n], carry[2 * n + 1]
                later = source[r + 1, :, lane]
                down, across = slopes(now, later)
                value = (0.5 * (now + fit[r, :, lane]) + (down - before)) + (
                    across - pltpu.roll(across, 1, 0)
                )
                if final:
                    value = (value[:cols] * 0.25).astype(bf16)
                    if n == 0:
                        out_ref[r - depth, :, 0:HALF] = value
                    else:
                        out_ref[r - depth, :, HALF:bands] = value[:, : bands - HALF]
                else:
                    target[r, :, lane] = value
                out += [later, down]
            return tuple(out)

        lax.fori_loop(first, last, body, tuple(carry), unroll=2)

    sources = [fit, field_a, field_b]
    for s in range(TV_ITERS):
        if s == 0:
            @pl.when(at_top > 0)
            def _():
                fit[depth - 1] = fit[depth]

        final = s == TV_ITERS - 1
        target = None if final else sources[s + 1]
        step(sources[s], target, s + 1, rows + 2 * depth - 1 - s, final)


def start_basis():
    bands = np.arange(BANDS, dtype=np.float32)[None, :]
    cols = np.arange(RANK, dtype=np.float32)[:, None]
    angle = np.float32(np.pi) * (bands + np.float32(0.5)) * cols / np.float32(BANDS)
    return np.pad(np.cos(angle).astype(np.float32), ((0, 0), (0, LANES - BANDS)))


def neighbours(block, axis, dim, width):
    count = lax.axis_size(axis)
    size = block.shape[dim]
    head = lax.slice_in_dim(block, 0, width, axis=dim)
    tail = lax.slice_in_dim(block, size - width, size, axis=dim)
    before = lax.ppermute(tail, axis, [(i, i + 1) for i in range(count - 1)])
    after = lax.ppermute(head, axis, [(i + 1, i) for i in range(count - 1)])
    return before, after


def body(cube):
    n_rows = lax.axis_size("narrow")
    n_cols = lax.axis_size("wide")
    rows, cols, bands = cube.shape
    depth = TV_ITERS

    left, right = neighbours(cube, "wide", 1, depth)
    packed = pl.pallas_call(
        gram_kernel,
        out_shape=[jax.ShapeDtypeStruct((SLICE, HALF), f32)] * SLICES,
        scratch_shapes=[pltpu.VMEM((LANES, LANES), f32)],
        compiler_params=pltpu.CompilerParams(vmem_limit_bytes=48 * 2**20),
    )(cube)
    packed = lax.psum(packed, ("wide", "narrow"))

    gap = jnp.zeros((rows, SIDE - 2 * depth, bands), cube.dtype)
    side = jnp.concatenate([right, gap, left], axis=1)
    above, below = neighbours(
        jnp.concatenate(
            [
                jnp.concatenate([cube[:depth], side[:depth]], axis=1),
                jnp.concatenate([cube[rows - depth :], side[rows - depth :]], axis=1),
            ],
            axis=0,
        ),
        "narrow",
        0,
        depth,
    )

    row, col = lax.axis_index("narrow"), lax.axis_index("wide")
    edges = jnp.stack([row == 0, row == n_rows - 1, col == 0, col == n_cols - 1]).astype(jnp.int32)
    tall, span = rows + 2 * depth, cols + SIDE
    vmem = pl.BlockSpec(memory_space=pltpu.VMEM)
    inv_count = 1.0 / (n_rows * n_cols * rows * cols)
    restored, projector = pl.pallas_call(
        functools.partial(main_kernel, depth, inv_count),
        in_specs=[pl.BlockSpec(memory_space=pltpu.SMEM)] + [vmem] * (5 + SLICES),
        out_specs=[vmem, vmem],
        out_shape=[
            jax.ShapeDtypeStruct((rows, cols, bands), bf16),
            jax.ShapeDtypeStruct((bands, bands), f32),
        ],
        scratch_shapes=[pltpu.VMEM((tall, span, LANES), f32)] * 3,
        compiler_params=pltpu.CompilerParams(vmem_limit_bytes=48 * 2**20),
    )(edges, jnp.asarray(start_basis()), cube, above, below, side, *packed)
    return restored, projector


def solution(mesh):
    return jax.shard_map(
        body,
        mesh=mesh,
        in_specs=(P("narrow", "wide", None),),
        out_specs=(P("narrow", "wide", None), P()),
        check_vma=False,
    )
```

```python
import functools

import jax
import jax.numpy as jnp
import numpy as np
from jax import lax
from jax.experimental import pallas as pl
from jax.experimental.pallas import tpu as pltpu
from jax.sharding import PartitionSpec as P

BANDS = 224
RANK = 16
POWER_ITERS = 4
TV_ITERS = 3
LANES = 256
HALF = 128
TAIL = BANDS - HALF
SIDE = 8
BLOCK = 4
UNROLL = 4

f32 = jnp.float32
bf16 = jnp.bfloat16


def iotas(shape):
    return lax.broadcasted_iota(jnp.int32, shape, 0), lax.broadcasted_iota(jnp.int32, shape, 1)


def gram_kernel(cube_ref, packed_ref, block, full, sems):
    rows, cols, bands = cube_ref.shape
    pieces = sems.shape[0]
    high = rows // pieces

    def copy(n):
        part = pl.ds(n * high, high)
        return pltpu.make_async_copy(cube_ref.at[part], block.at[part], sems.at[n])

    for n in range(pieces):
        copy(n).start()
    full[...] = jnp.zeros_like(full)
    total = None
    for start in range(0, pieces, max(pieces // 2, 1)):
        stop = start + max(pieces // 2, 1)
        for n in range(start, stop):
            copy(n).wait()
        flat = block[start * high : stop * high].reshape((stop - start) * high * cols, bands)
        term = lax.dot_general(flat, flat, (((0,), (0,)), ((), ())), preferred_element_type=f32)
        total = term if total is None else total + term
    full[0:bands, 0:bands] = total
    i, j = iotas((HALF, HALF))
    first = full[0:HALF, 0:HALF]
    second = pltpu.roll(full[HALF:LANES, HALF:LANES], 1, 1)
    packed_ref[0:HALF, :] = jnp.where(j <= i, first, second)
    packed_ref[HALF:LANES, :] = full[0:HALF, HALF:LANES]


def split3(x):
    high = x.astype(bf16)
    rest = x - high.astype(f32)
    mid = rest.astype(bf16)
    low = (rest - mid.astype(f32)).astype(bf16)
    return high, mid, low


def product(left, right, dims):
    def dot(a, b):
        return lax.dot_general(a, b, (dims, ((), ())), preferred_element_type=f32)

    n = left[0].shape[0]
    top = dot(jnp.concatenate(left, axis=0), right[0])
    middle = dot(jnp.concatenate(left[:2], axis=0), right[1])
    last = dot(left[0], right[2])
    small = top[2 * n : 3 * n] + middle[n : 2 * n] + last
    return top[:n] + ((top[n : 2 * n] + middle[:n]) + small)


def unpack(packed, scale):
    i, j = iotas((HALF, HALF))
    merged = packed[0:HALF, :] * scale
    cross = packed[HALF:LANES, :] * scale
    first = jnp.where(j <= i, merged, 0.0) + jnp.where(j < i, merged, 0.0).T
    moved = pltpu.roll(merged, HALF - 1, 1)
    inside = (i < TAIL) & (j < TAIL)
    second = jnp.where(inside & (j >= i), moved, 0.0) + jnp.where(inside & (j > i), moved, 0.0).T
    return jnp.concatenate(
        [
            jnp.concatenate([first, cross], axis=1),
            jnp.concatenate([cross.T, second], axis=1),
        ],
        axis=0,
    )


def orthonormal(grown, inner):
    row = lax.broadcasted_iota(jnp.int32, (RANK, HALF), 0)
    work = [
        jnp.concatenate([inner, jnp.zeros((RANK, HALF - RANK), f32)], axis=1),
        grown[:, :HALF],
        grown[:, HALF:],
    ]
    diagonal = jnp.ones((RANK, HALF), f32)
    for k in range(0, RANK, BLOCK):
        columns = [
            jnp.broadcast_to(work[0][:, k + c : k + c + 1], (RANK, HALF)) for c in range(BLOCK)
        ]
        tops = [[part[k + r : k + r + 1, :] for part in work] for r in range(BLOCK)]
        small = [
            [columns[c][k + r : k + r + 1, :] for c in range(r + 1)] for r in range(BLOCK)
        ]
        factors = []
        for j in range(BLOCK):
            pivot = small[j][j]
            inverse = 1.0 / pivot
            diagonal = jnp.where(row == k + j, pivot, diagonal)
            factor = jnp.where(row > k + j, columns[j] * inverse, 0.0)
            factors.append(factor)
            below = [small[i][j] for i in range(BLOCK) if i > j]
            for i in range(j + 1, BLOCK):
                ratio = small[i][j] * inverse
                for c in range(j + 1, i + 1):
                    small[i][c] = small[i][c] - ratio * below[c - j - 1]
                tops[i] = [x - ratio * y for x, y in zip(tops[i], tops[j])]
                columns[i] = columns[i] - factor * below[i - j - 1]
        for n in range(len(work)):
            if n > 0 or k + BLOCK < RANK:
                for j in range(BLOCK):
                    work[n] = work[n] - factors[j] * tops[j][n]
    scale = lax.rsqrt(diagonal)
    return jnp.concatenate([work[1] * scale, work[2] * scale], axis=1)


def subspace(gram, start):
    parts = split3(gram)
    basis = start
    for _ in range(POWER_ITERS):
        grown = product(split3(basis), parts, ((1,), (0,)))
        pieces = split3(grown)
        inner = product(pieces, pieces, ((1,), (1,)))
        basis = orthonormal(grown, inner)
    return basis


def main_kernel(
    depth, inv_count, edge_ref, packed_ref, start_ref, mid_ref, above_ref, below_ref, side_ref,
    out_ref, proj_ref, fit, field_a, field_b, out_stage, proj_stage, out_sems, proj_sem
):
    rows, cols, bands = mid_ref.shape
    span = cols + SIDE
    proj_copy = pltpu.make_async_copy(proj_stage, proj_ref, proj_sem)

    def out_copy(n):
        part = pl.ds(n * UNROLL, UNROLL)
        return pltpu.make_async_copy(out_stage.at[part], out_ref.at[part], out_sems.at[n])

    basis = subspace(unpack(packed_ref[...], inv_count), start_ref[...])
    high, mid, low = split3(basis)
    right = jnp.concatenate([high, high, high, mid, mid, low], axis=0)
    left = jnp.concatenate([high, mid, low, high, mid, high], axis=0)
    tn = (((0,), (0,)), ((), ()))
    proj_stage[...] = lax.dot_general(left, right, tn, preferred_element_type=f32)[:bands, :bands]
    proj_copy.start()
    mixed = lax.dot_general(
        jnp.concatenate([high, high, high], axis=0),
        jnp.concatenate([high, mid, low], axis=0),
        tn,
        preferred_element_type=f32,
    )[:bands]
    mixed = mixed * 4.0
    mixed_high = mixed.astype(bf16)
    mixed_low = (mixed - mixed_high.astype(f32)).astype(bf16)

    def fitted(block):
        n, w, b = block.shape
        if w % 16:
            flat = block.astype(f32).reshape(n * w, b).astype(bf16)
        else:
            flat = block.reshape(n * w, b)
        res = jnp.dot(flat, mixed_high, preferred_element_type=f32)
        res = res + jnp.dot(flat, mixed_low, preferred_element_type=f32)
        return res.reshape(n, w, LANES)

    fit[0:depth] = fitted(above_ref[...])
    fit[depth : depth + rows, 0:cols, :] = fitted(mid_ref[...])
    fit[depth : depth + rows, cols:span, :] = fitted(side_ref[...])
    fit[depth + rows :] = fitted(below_ref[...])

    at_top, at_bottom, at_left, at_right = (edge_ref[n] for n in range(4))
    place = lax.broadcasted_iota(jnp.int32, (span, HALF), 0)
    closed = ((place == cols - 1) & (at_right > 0)) | ((place == span - 1) & (at_left > 0))
    keep = jnp.where(closed, 0.0, 1.0).astype(f32)

    def slopes(now, later):
        down = later - now
        across = (pltpu.roll(now, span - 1, 0) - now) * keep
        inverse = lax.rsqrt(down * down + across * across + 4.0)
        return down * inverse, across * inverse

    def step(source, target, first, last, final):
        @pl.when(at_top > 0)
        def _():
            source[depth - 1] = source[depth]

        @pl.when(at_bottom > 0)
        def _():
            source[depth + rows] = source[depth + rows - 1]

        lanes = [slice(0, HALF), slice(HALF, LANES)]
        carry = []
        for lane in lanes:
            before, now = source[first - 1, :, lane], source[first, :, lane]
            carry += [now, slopes(before, now)[0]]

        def row_step(r, carry):
            out = []
            for n, lane in enumerate(lanes):
                now, before = carry[2 * n], carry[2 * n + 1]
                later = source[r + 1, :, lane]
                down, across = slopes(now, later)
                value = (0.5 * (now + fit[r, :, lane]) + (down - before)) + (
                    across - pltpu.roll(across, 1, 0)
                )
                if final:
                    value = (value[:cols] * 0.25).astype(bf16)
                    if n == 0:
                        out_stage[r - depth, :, 0:HALF] = value
                    else:
                        out_stage[r - depth, :, HALF:bands] = value[:, : bands - HALF]
                else:
                    target[r, :, lane] = value
                out += [later, down]
            return out

        def block_step(n, carry):
            for inner in range(UNROLL):
                carry = row_step(first + n * UNROLL + inner, carry)
            if final:
                out_copy(n).start()
            return tuple(carry)

        lax.fori_loop(0, (last - first) // UNROLL, block_step, tuple(carry))

    step(fit, field_a, depth - 2, rows + depth + 2, False)
    step(field_a, field_b, depth - 2, rows + depth + 2, False)
    step(field_b, None, depth, rows + depth, True)
    proj_copy.wait()
    for n in range(rows // UNROLL):
        out_copy(n).wait()


def start_basis():
    bands = np.arange(BANDS, dtype=np.float32)[None, :]
    cols = np.arange(RANK, dtype=np.float32)[:, None]
    angle = np.float32(np.pi) * (bands + np.float32(0.5)) * cols / np.float32(BANDS)
    return np.pad(np.cos(angle).astype(np.float32), ((0, 0), (0, LANES - BANDS)))


def neighbours(block, axis, dim, width):
    count = lax.axis_size(axis)
    size = block.shape[dim]
    head = lax.slice_in_dim(block, 0, width, axis=dim)
    tail = lax.slice_in_dim(block, size - width, size, axis=dim)
    before = lax.ppermute(tail, axis, [(i, i + 1) for i in range(count - 1)])
    after = lax.ppermute(head, axis, [(i + 1, i) for i in range(count - 1)])
    return before, after


def exchange(pieces, axis):
    return lax.all_to_all(pieces, axis, split_axis=0, concat_axis=0)


def spread(piece, count):
    return jnp.broadcast_to(piece[None], (count,) + piece.shape)


def body(cube):
    n_rows = lax.axis_size("narrow")
    n_cols = lax.axis_size("wide")
    count = n_rows * n_cols
    rows, cols, bands = cube.shape
    depth = TV_ITERS
    axes = ("wide", "narrow")

    left, right = neighbours(cube, "wide", 1, depth)
    pieces = 8 if rows % 8 == 0 else 1
    packed = pl.pallas_call(
        gram_kernel,
        in_specs=[pl.BlockSpec(memory_space=pl.ANY)],
        out_shape=jax.ShapeDtypeStruct((LANES, HALF), f32),
        scratch_shapes=[
            pltpu.VMEM(cube.shape, cube.dtype),
            pltpu.VMEM((LANES, LANES), f32),
            pltpu.SemaphoreType.DMA((pieces,)),
        ],
        compiler_params=pltpu.CompilerParams(vmem_limit_bytes=62 * 2**20),
    )(cube)
    part = exchange(packed.reshape(count, LANES // count, HALF), axes)
    gathered = exchange(spread(jnp.sum(part, axis=0), count), axes).reshape(LANES, HALF)

    gap = jnp.zeros((rows, SIDE - 2 * depth, bands), cube.dtype)
    side = jnp.concatenate([right, gap, left], axis=1)
    above, below = neighbours(
        jnp.concatenate(
            [
                jnp.concatenate([cube[:depth], side[:depth]], axis=1),
                jnp.concatenate([cube[rows - depth :], side[rows - depth :]], axis=1),
            ],
            axis=0,
        ),
        "narrow",
        0,
        depth,
    )

    row, col = lax.axis_index("narrow"), lax.axis_index("wide")
    edges = jnp.stack([row == 0, row == n_rows - 1, col == 0, col == n_cols - 1]).astype(jnp.int32)
    tall, span = rows + 2 * depth, cols + SIDE
    vmem = pl.BlockSpec(memory_space=pltpu.VMEM)
    inv_count = 1.0 / (count * rows * cols)
    restored, projector = pl.pallas_call(
        functools.partial(main_kernel, depth, inv_count),
        in_specs=[pl.BlockSpec(memory_space=pltpu.SMEM)] + [vmem] * 6,
        out_specs=[pl.BlockSpec(memory_space=pl.ANY)] * 2,
        out_shape=[
            jax.ShapeDtypeStruct((rows, cols, bands), bf16),
            jax.ShapeDtypeStruct((bands, bands), f32),
        ],
        scratch_shapes=[pltpu.VMEM((tall, span, LANES), f32)] * 3
        + [
            pltpu.VMEM((rows, cols, bands), bf16),
            pltpu.VMEM((bands, bands), f32),
            pltpu.SemaphoreType.DMA((rows // UNROLL,)),
            pltpu.SemaphoreType.DMA,
        ],
        compiler_params=pltpu.CompilerParams(vmem_limit_bytes=48 * 2**20),
    )(edges, gathered, jnp.asarray(start_basis()), cube, above, below, side)
    return restored, projector


def solution(mesh):
    return jax.shard_map(
        body,
        mesh=mesh,
        in_specs=(P("narrow", "wide", None),),
        out_specs=(P("narrow", "wide", None), P()),
        check_vma=False,
    )
```

```python
import functools

import jax
import jax.numpy as jnp
import numpy as np
from jax import lax
from jax.experimental import pallas as pl
from jax.experimental.pallas import tpu as pltpu
from jax.sharding import PartitionSpec as P

BANDS = 224
RANK = 16
POWER_ITERS = 4
TV_ITERS = 3
LANES = 256
HALF = 128
TAIL = BANDS - HALF
SIDE = 8
BLOCK = 4
UNROLL = 4

f32 = jnp.float32
bf16 = jnp.bfloat16


def iotas(shape):
    return lax.broadcasted_iota(jnp.int32, shape, 0), lax.broadcasted_iota(jnp.int32, shape, 1)


def gram_kernel(cube_ref, packed_ref, block, full, sems):
    rows, cols, bands = cube_ref.shape
    pieces = sems.shape[0]
    high = rows // pieces

    def copy(n):
        part = pl.ds(n * high, high)
        return pltpu.make_async_copy(cube_ref.at[part], block.at[part], sems.at[n])

    for n in range(pieces):
        copy(n).start()
    full[...] = jnp.zeros_like(full)
    total = None
    for start in range(0, pieces, max(pieces // 4, 1)):
        stop = start + max(pieces // 4, 1)
        for n in range(start, stop):
            copy(n).wait()
        flat = block[start * high : stop * high].reshape((stop - start) * high * cols, bands)
        term = lax.dot_general(flat, flat, (((0,), (0,)), ((), ())), preferred_element_type=f32)
        total = term if total is None else total + term
    full[0:bands, 0:bands] = total
    i, j = iotas((HALF, HALF))
    first = full[0:HALF, 0:HALF]
    second = pltpu.roll(full[HALF:LANES, HALF:LANES], 1, 1)
    packed_ref[0:HALF, :] = jnp.where(j <= i, first, second)
    packed_ref[HALF:LANES, :] = full[0:HALF, HALF:LANES]


def split3(x):
    high = x.astype(bf16)
    rest = x - high.astype(f32)
    mid = rest.astype(bf16)
    low = (rest - mid.astype(f32)).astype(bf16)
    return high, mid, low


def product(left, right, dims):
    def dot(a, b):
        return lax.dot_general(a, b, (dims, ((), ())), preferred_element_type=f32)

    n = left[0].shape[0]
    top = dot(jnp.concatenate(left, axis=0), right[0])
    middle = dot(jnp.concatenate(left[:2], axis=0), right[1])
    last = dot(left[0], right[2])
    small = top[2 * n : 3 * n] + middle[n : 2 * n] + last
    return top[:n] + ((top[n : 2 * n] + middle[:n]) + small)


def unpack(packed, scale):
    i, j = iotas((HALF, HALF))
    merged = packed[0:HALF, :] * scale
    cross = packed[HALF:LANES, :] * scale
    first = jnp.where(j <= i, merged, 0.0) + jnp.where(j < i, merged, 0.0).T
    moved = pltpu.roll(merged, HALF - 1, 1)
    inside = (i < TAIL) & (j < TAIL)
    second = jnp.where(inside & (j >= i), moved, 0.0) + jnp.where(inside & (j > i), moved, 0.0).T
    return jnp.concatenate(
        [
            jnp.concatenate([first, cross], axis=1),
            jnp.concatenate([cross.T, second], axis=1),
        ],
        axis=0,
    )


def orthonormal(grown, inner):
    row = lax.broadcasted_iota(jnp.int32, (RANK, HALF), 0)
    work = [
        jnp.concatenate([inner, jnp.zeros((RANK, HALF - RANK), f32)], axis=1),
        grown[:, :HALF],
        grown[:, HALF:],
    ]
    diagonal = jnp.ones((RANK, HALF), f32)
    for k in range(0, RANK, BLOCK):
        columns = [
            jnp.broadcast_to(work[0][:, k + c : k + c + 1], (RANK, HALF)) for c in range(BLOCK)
        ]
        tops = [[part[k + r : k + r + 1, :] for part in work] for r in range(BLOCK)]
        small = [
            [columns[c][k + r : k + r + 1, :] for c in range(r + 1)] for r in range(BLOCK)
        ]
        factors = []
        for j in range(BLOCK):
            pivot = small[j][j]
            inverse = 1.0 / pivot
            diagonal = jnp.where(row == k + j, pivot, diagonal)
            factor = jnp.where(row > k + j, columns[j] * inverse, 0.0)
            factors.append(factor)
            below = [small[i][j] for i in range(BLOCK) if i > j]
            for i in range(j + 1, BLOCK):
                ratio = small[i][j] * inverse
                for c in range(j + 1, i + 1):
                    small[i][c] = small[i][c] - ratio * below[c - j - 1]
                tops[i] = [x - ratio * y for x, y in zip(tops[i], tops[j])]
                columns[i] = columns[i] - factor * below[i - j - 1]
        for n in range(len(work)):
            if n > 0 or k + BLOCK < RANK:
                for j in range(BLOCK):
                    work[n] = work[n] - factors[j] * tops[j][n]
    scale = lax.rsqrt(diagonal)
    return jnp.concatenate([work[1] * scale, work[2] * scale], axis=1)


def subspace(gram, start):
    parts = split3(gram)
    basis = start
    for _ in range(POWER_ITERS):
        grown = product(split3(basis), parts, ((1,), (0,)))
        pieces = split3(grown)
        inner = product(pieces, pieces, ((1,), (1,)))
        basis = orthonormal(grown, inner)
    return basis


def subspace_kernel(inv_count, packed_ref, start_ref, basis_ref):
    basis_ref[...] = subspace(unpack(packed_ref[...], inv_count), start_ref[...])


def main_kernel(
    depth, edge_ref, basis_ref, mid_ref, above_ref, below_ref, side_ref,
    out_ref, proj_ref, fit, field_a, field_b, out_stage, proj_stage, out_sems, proj_sem
):
    rows, cols, bands = mid_ref.shape
    span = cols + SIDE
    proj_copy = pltpu.make_async_copy(proj_stage, proj_ref, proj_sem)

    def out_copy(n):
        part = pl.ds(n * UNROLL, UNROLL)
        return pltpu.make_async_copy(out_stage.at[part], out_ref.at[part], out_sems.at[n])

    high, mid, low = split3(basis_ref[...])
    right = jnp.concatenate([high, high, high, mid, mid, low], axis=0)
    left = jnp.concatenate([high, mid, low, high, mid, high], axis=0)
    tn = (((0,), (0,)), ((), ()))
    proj_stage[...] = lax.dot_general(left, right, tn, preferred_element_type=f32)[:bands, :bands]
    proj_copy.start()
    mixed = lax.dot_general(
        jnp.concatenate([high, high, high], axis=0),
        jnp.concatenate([high, mid, low], axis=0),
        tn,
        preferred_element_type=f32,
    )[:bands]
    mixed = mixed * 4.0
    mixed_high = mixed.astype(bf16)
    mixed_low = (mixed - mixed_high.astype(f32)).astype(bf16)

    def fitted(block):
        n, w, b = block.shape
        if w % 16:
            flat = block.astype(f32).reshape(n * w, b).astype(bf16)
        else:
            flat = block.reshape(n * w, b)
        res = jnp.dot(flat, mixed_high, preferred_element_type=f32)
        res = res + jnp.dot(flat, mixed_low, preferred_element_type=f32)
        return res.reshape(n, w, LANES)

    fit[0:depth] = fitted(above_ref[...])
    fit[depth : depth + rows, 0:cols, :] = fitted(mid_ref[...])
    fit[depth : depth + rows, cols:span, :] = fitted(side_ref[...])
    fit[depth + rows :] = fitted(below_ref[...])

    at_top, at_bottom, at_left, at_right = (edge_ref[n] for n in range(4))
    place = lax.broadcasted_iota(jnp.int32, (span, HALF), 0)
    closed = ((place == cols - 1) & (at_right > 0)) | ((place == span - 1) & (at_left > 0))
    keep = jnp.where(closed, 0.0, 1.0).astype(f32)

    def slopes(now, later):
        down = later - now
        across = (pltpu.roll(now, span - 1, 0) - now) * keep
        inverse = lax.rsqrt(down * down + across * across + 4.0)
        return down * inverse, across * inverse

    def step(source, target, first, last, final):
        @pl.when(at_top > 0)
        def _():
            source[depth - 1] = source[depth]

        @pl.when(at_bottom > 0)
        def _():
            source[depth + rows] = source[depth + rows - 1]

        lanes = [slice(0, HALF), slice(HALF, LANES)]
        carry = []
        for lane in lanes:
            before, now = source[first - 1, :, lane], source[first, :, lane]
            carry += [now, slopes(before, now)[0]]

        def row_step(r, carry):
            out = []
            for n, lane in enumerate(lanes):
                now, before = carry[2 * n], carry[2 * n + 1]
                later = source[r + 1, :, lane]
                down, across = slopes(now, later)
                value = (0.5 * (now + fit[r, :, lane]) + (down - before)) + (
                    across - pltpu.roll(across, 1, 0)
                )
                if final:
                    value = (value[:cols] * 0.25).astype(bf16)
                    if n == 0:
                        out_stage[r - depth, :, 0:HALF] = value
                    else:
                        out_stage[r - depth, :, HALF:bands] = value[:, : bands - HALF]
                else:
                    target[r, :, lane] = value
                out += [later, down]
            return out

        def block_step(n, carry):
            for inner in range(UNROLL):
                carry = row_step(first + n * UNROLL + inner, carry)
            if final:
                out_copy(n).start()
            return tuple(carry)

        lax.fori_loop(0, (last - first) // UNROLL, block_step, tuple(carry))

    step(fit, field_a, depth - 2, rows + depth + 2, False)
    step(field_a, field_b, depth - 2, rows + depth + 2, False)
    step(field_b, None, depth, rows + depth, True)
    proj_copy.wait()
    for n in range(rows // UNROLL):
        out_copy(n).wait()


def start_basis():
    bands = np.arange(BANDS, dtype=np.float32)[None, :]
    cols = np.arange(RANK, dtype=np.float32)[:, None]
    angle = np.float32(np.pi) * (bands + np.float32(0.5)) * cols / np.float32(BANDS)
    return np.pad(np.cos(angle).astype(np.float32), ((0, 0), (0, LANES - BANDS)))


def neighbours(block, axis, dim, width):
    count = lax.axis_size(axis)
    size = block.shape[dim]
    head = lax.slice_in_dim(block, 0, width, axis=dim)
    tail = lax.slice_in_dim(block, size - width, size, axis=dim)
    before = lax.ppermute(tail, axis, [(i, i + 1) for i in range(count - 1)])
    after = lax.ppermute(head, axis, [(i + 1, i) for i in range(count - 1)])
    return before, after


def exchange(pieces, axis):
    return lax.all_to_all(pieces, axis, split_axis=0, concat_axis=0)


def spread(piece, count):
    return jnp.broadcast_to(piece[None], (count,) + piece.shape)


def body(cube):
    n_rows = lax.axis_size("narrow")
    n_cols = lax.axis_size("wide")
    count = n_rows * n_cols
    rows, cols, bands = cube.shape
    depth = TV_ITERS
    axes = ("wide", "narrow")

    left, right = neighbours(cube, "wide", 1, depth)
    pieces = 8 if rows % 8 == 0 else 1
    packed = pl.pallas_call(
        gram_kernel,
        in_specs=[pl.BlockSpec(memory_space=pl.ANY)],
        out_shape=jax.ShapeDtypeStruct((LANES, HALF), f32),
        scratch_shapes=[
            pltpu.VMEM(cube.shape, cube.dtype),
            pltpu.VMEM((LANES, LANES), f32),
            pltpu.SemaphoreType.DMA((pieces,)),
        ],
        compiler_params=pltpu.CompilerParams(vmem_limit_bytes=62 * 2**20),
    )(cube)
    part = exchange(packed.reshape(count, LANES // count, HALF), axes)
    share, top, bottom = lax.optimization_barrier(
        (jnp.sum(part, axis=0), cube[:depth], cube[rows - depth :])
    )
    gathered = exchange(spread(share, count), axes).reshape(LANES, HALF)

    gap = jnp.zeros((rows, SIDE - 2 * depth, bands), cube.dtype)
    side = jnp.concatenate([right, gap, left], axis=1)
    above, below = neighbours(
        jnp.concatenate(
            [
                jnp.concatenate([top, side[:depth]], axis=1),
                jnp.concatenate([bottom, side[rows - depth :]], axis=1),
            ],
            axis=0,
        ),
        "narrow",
        0,
        depth,
    )

    row, col = lax.axis_index("narrow"), lax.axis_index("wide")
    edges = jnp.stack([row == 0, row == n_rows - 1, col == 0, col == n_cols - 1]).astype(jnp.int32)
    tall, span = rows + 2 * depth, cols + SIDE
    vmem = pl.BlockSpec(memory_space=pltpu.VMEM)
    inv_count = 1.0 / (count * rows * cols)
    basis = pl.pallas_call(
        functools.partial(subspace_kernel, inv_count),
        in_specs=[vmem] * 2,
        out_specs=vmem,
        out_shape=jax.ShapeDtypeStruct((RANK, LANES), f32),
        cost_estimate=pl.CostEstimate(flops=2**32, bytes_accessed=2**18, transcendentals=0),
        compiler_params=pltpu.CompilerParams(vmem_limit_bytes=16 * 2**20),
    )(gathered, jnp.asarray(start_basis()))
    restored, projector = pl.pallas_call(
        functools.partial(main_kernel, depth),
        in_specs=[pl.BlockSpec(memory_space=pltpu.SMEM)] + [vmem] * 5,
        out_specs=[pl.BlockSpec(memory_space=pl.ANY)] * 2,
        out_shape=[
            jax.ShapeDtypeStruct((rows, cols, bands), bf16),
            jax.ShapeDtypeStruct((bands, bands), f32),
        ],
        scratch_shapes=[pltpu.VMEM((tall, span, LANES), f32)] * 3
        + [
            pltpu.VMEM((rows, cols, bands), bf16),
            pltpu.VMEM((bands, bands), f32),
            pltpu.SemaphoreType.DMA((rows // UNROLL,)),
            pltpu.SemaphoreType.DMA,
        ],
        compiler_params=pltpu.CompilerParams(vmem_limit_bytes=48 * 2**20),
    )(edges, basis, cube, above, below, side)
    return restored, projector


def solution(mesh):
    return jax.shard_map(
        body,
        mesh=mesh,
        in_specs=(P("narrow", "wide", None),),
        out_specs=(P("narrow", "wide", None), P()),
        check_vma=False,
    )
```

```python
import functools

import jax
import jax.numpy as jnp
import numpy as np
from jax import lax
from jax.experimental import pallas as pl
from jax.experimental.pallas import tpu as pltpu
from jax.sharding import PartitionSpec as P

BANDS = 224
RANK = 16
POWER_ITERS = 4
TV_ITERS = 3
LANES = 256
HALF = 128
TAIL = BANDS - HALF
SIDE = 8
BLOCK = 4
UNROLL = 4

f32 = jnp.float32
bf16 = jnp.bfloat16


def iotas(shape):
    return lax.broadcasted_iota(jnp.int32, shape, 0), lax.broadcasted_iota(jnp.int32, shape, 1)


def gram_kernel(cube_ref, packed_ref, block, full, sems):
    rows, cols, bands = cube_ref.shape
    pieces = sems.shape[0]
    high = rows // pieces

    def copy(n):
        part = pl.ds(n * high, high)
        return pltpu.make_async_copy(cube_ref.at[part], block.at[part], sems.at[n])

    for n in range(pieces):
        copy(n).start()
    full[...] = jnp.zeros_like(full)
    total = None
    for start in range(0, pieces, max(pieces // 4, 1)):
        stop = start + max(pieces // 4, 1)
        for n in range(start, stop):
            copy(n).wait()
        flat = block[start * high : stop * high].reshape((stop - start) * high * cols, bands)
        term = lax.dot_general(flat, flat, (((0,), (0,)), ((), ())), preferred_element_type=f32)
        total = term if total is None else total + term
    full[0:bands, 0:bands] = total
    i, j = iotas((HALF, HALF))
    first = full[0:HALF, 0:HALF]
    second = pltpu.roll(full[HALF:LANES, HALF:LANES], 1, 1)
    packed_ref[0:HALF, :] = jnp.where(j <= i, first, second)
    packed_ref[HALF:LANES, :] = full[0:HALF, HALF:LANES]


def split3(x):
    high = x.astype(bf16)
    rest = x - high.astype(f32)
    mid = rest.astype(bf16)
    low = (rest - mid.astype(f32)).astype(bf16)
    return high, mid, low


def product(left, right, dims):
    def dot(a, b):
        return lax.dot_general(a, b, (dims, ((), ())), preferred_element_type=f32)

    n = left[0].shape[0]
    top = dot(jnp.concatenate(left, axis=0), right[0])
    middle = dot(jnp.concatenate(left[:2], axis=0), right[1])
    last = dot(left[0], right[2])
    small = top[2 * n : 3 * n] + middle[n : 2 * n] + last
    return top[:n] + ((top[n : 2 * n] + middle[:n]) + small)


def unpack(packed, scale):
    i, j = iotas((HALF, HALF))
    merged = packed[0:HALF, :] * scale
    cross = packed[HALF:LANES, :] * scale
    first = jnp.where(j <= i, merged, 0.0) + jnp.where(j < i, merged, 0.0).T
    moved = pltpu.roll(merged, HALF - 1, 1)
    inside = (i < TAIL) & (j < TAIL)
    second = jnp.where(inside & (j >= i), moved, 0.0) + jnp.where(inside & (j > i), moved, 0.0).T
    return jnp.concatenate(
        [
            jnp.concatenate([first, cross], axis=1),
            jnp.concatenate([cross.T, second], axis=1),
        ],
        axis=0,
    )


def orthonormal(grown, inner):
    row = lax.broadcasted_iota(jnp.int32, (RANK, HALF), 0)
    work = [
        jnp.concatenate([inner, jnp.zeros((RANK, HALF - RANK), f32)], axis=1),
        grown[:, :HALF],
        grown[:, HALF:],
    ]
    diagonal = jnp.ones((RANK, HALF), f32)
    for k in range(0, RANK, BLOCK):
        columns = [
            jnp.broadcast_to(work[0][:, k + c : k + c + 1], (RANK, HALF)) for c in range(BLOCK)
        ]
        tops = [[part[k + r : k + r + 1, :] for part in work] for r in range(BLOCK)]
        small = [
            [columns[c][k + r : k + r + 1, :] for c in range(r + 1)] for r in range(BLOCK)
        ]
        factors = []
        for j in range(BLOCK):
            pivot = small[j][j]
            inverse = 1.0 / pivot
            diagonal = jnp.where(row == k + j, pivot, diagonal)
            factor = jnp.where(row > k + j, columns[j] * inverse, 0.0)
            factors.append(factor)
            below = [small[i][j] for i in range(BLOCK) if i > j]
            for i in range(j + 1, BLOCK):
                ratio = small[i][j] * inverse
                for c in range(j + 1, i + 1):
                    small[i][c] = small[i][c] - ratio * below[c - j - 1]
                tops[i] = [x - ratio * y for x, y in zip(tops[i], tops[j])]
                columns[i] = columns[i] - factor * below[i - j - 1]
        for n in range(len(work)):
            if n > 0 or k + BLOCK < RANK:
                for j in range(BLOCK):
                    work[n] = work[n] - factors[j] * tops[j][n]
    scale = lax.rsqrt(diagonal)
    return jnp.concatenate([work[1] * scale, work[2] * scale], axis=1)


def subspace(gram, start):
    parts = split3(gram)
    basis = start
    for _ in range(POWER_ITERS):
        grown = product(split3(basis), parts, ((1,), (0,)))
        pieces = split3(grown)
        inner = product(pieces, pieces, ((1,), (1,)))
        basis = orthonormal(grown, inner)
    return basis


def halo_kernel(depth, left_ref, right_ref, top_ref, bottom_ref, up_ref, down_ref, side_ref, wide):
    rows, cols = side_ref.shape[0], top_ref.shape[1]
    wide[...] = jnp.zeros_like(wide)
    wide[:, 0:depth] = right_ref[...].astype(f32)
    wide[:, SIDE - depth :] = left_ref[...].astype(f32)
    side = wide[...].astype(bf16)
    side_ref[...] = side
    up_ref[:, 0:cols] = top_ref[...]
    up_ref[:, cols:] = side[:depth]
    down_ref[:, 0:cols] = bottom_ref[...]
    down_ref[:, cols:] = side[rows - depth :]


def subspace_kernel(inv_count, packed_ref, start_ref, basis_ref):
    basis_ref[...] = subspace(unpack(packed_ref[...], inv_count), start_ref[...])


def main_kernel(
    depth, edge_ref, basis_ref, mid_ref, above_ref, below_ref, side_ref,
    out_ref, proj_ref, fit, field_a, field_b, out_stage, proj_stage, out_sems, proj_sem
):
    rows, cols, bands = mid_ref.shape
    span = cols + SIDE
    proj_copy = pltpu.make_async_copy(proj_stage, proj_ref, proj_sem)

    def out_copy(n):
        part = pl.ds(n * UNROLL, UNROLL)
        return pltpu.make_async_copy(out_stage.at[part], out_ref.at[part], out_sems.at[n])

    high, mid, low = split3(basis_ref[...])
    right = jnp.concatenate([high, high, high, mid, mid, low], axis=0)
    left = jnp.concatenate([high, mid, low, high, mid, high], axis=0)
    tn = (((0,), (0,)), ((), ()))
    proj_stage[...] = lax.dot_general(left, right, tn, preferred_element_type=f32)[:bands, :bands]
    proj_copy.start()
    mixed = lax.dot_general(
        jnp.concatenate([high, high, high], axis=0),
        jnp.concatenate([high, mid, low], axis=0),
        tn,
        preferred_element_type=f32,
    )[:bands]
    mixed = mixed * 4.0
    mixed_high = mixed.astype(bf16)
    mixed_low = (mixed - mixed_high.astype(f32)).astype(bf16)

    def fitted(block):
        n, w, b = block.shape
        if w % 16:
            flat = block.astype(f32).reshape(n * w, b).astype(bf16)
        else:
            flat = block.reshape(n * w, b)
        res = jnp.dot(flat, mixed_high, preferred_element_type=f32)
        res = res + jnp.dot(flat, mixed_low, preferred_element_type=f32)
        return res.reshape(n, w, LANES)

    fit[0:depth] = fitted(above_ref[...])
    fit[depth : depth + rows, 0:cols, :] = fitted(mid_ref[...])
    fit[depth : depth + rows, cols:span, :] = fitted(side_ref[...])
    fit[depth + rows :] = fitted(below_ref[...])

    at_top, at_bottom, at_left, at_right = (edge_ref[n] for n in range(4))
    place = lax.broadcasted_iota(jnp.int32, (span, HALF), 0)
    closed = ((place == cols - 1) & (at_right > 0)) | ((place == span - 1) & (at_left > 0))
    keep = jnp.where(closed, 0.0, 1.0).astype(f32)

    def slopes(now, later):
        down = later - now
        across = (pltpu.roll(now, span - 1, 0) - now) * keep
        inverse = lax.rsqrt(down * down + across * across + 4.0)
        return down * inverse, across * inverse

    def step(source, target, first, last, final):
        @pl.when(at_top > 0)
        def _():
            source[depth - 1] = source[depth]

        @pl.when(at_bottom > 0)
        def _():
            source[depth + rows] = source[depth + rows - 1]

        lanes = [slice(0, HALF), slice(HALF, LANES)]
        carry = []
        for lane in lanes:
            before, now = source[first - 1, :, lane], source[first, :, lane]
            carry += [now, slopes(before, now)[0]]

        def row_step(r, carry):
            out = []
            for n, lane in enumerate(lanes):
                now, before = carry[2 * n], carry[2 * n + 1]
                later = source[r + 1, :, lane]
                down, across = slopes(now, later)
                value = (0.5 * (now + fit[r, :, lane]) + (down - before)) + (
                    across - pltpu.roll(across, 1, 0)
                )
                if final:
                    value = (value[:cols] * 0.25).astype(bf16)
                    if n == 0:
                        out_stage[r - depth, :, 0:HALF] = value
                    else:
                        out_stage[r - depth, :, HALF:bands] = value[:, : bands - HALF]
                else:
                    target[r, :, lane] = value
                out += [later, down]
            return out

        def block_step(n, carry):
            for inner in range(UNROLL):
                carry = row_step(first + n * UNROLL + inner, carry)
            if final:
                out_copy(n).start()
            return tuple(carry)

        lax.fori_loop(0, (last - first) // UNROLL, block_step, tuple(carry))

    step(fit, field_a, depth - 2, rows + depth + 2, False)
    step(field_a, field_b, depth - 2, rows + depth + 2, False)
    step(field_b, None, depth, rows + depth, True)
    proj_copy.wait()
    for n in range(rows // UNROLL):
        out_copy(n).wait()


def start_basis():
    bands = np.arange(BANDS, dtype=np.float32)[None, :]
    cols = np.arange(RANK, dtype=np.float32)[:, None]
    angle = np.float32(np.pi) * (bands + np.float32(0.5)) * cols / np.float32(BANDS)
    return np.pad(np.cos(angle).astype(np.float32), ((0, 0), (0, LANES - BANDS)))


def neighbours(block, axis, dim, width):
    count = lax.axis_size(axis)
    size = block.shape[dim]
    head = lax.slice_in_dim(block, 0, width, axis=dim)
    tail = lax.slice_in_dim(block, size - width, size, axis=dim)
    before = lax.ppermute(tail, axis, [(i, i + 1) for i in range(count - 1)])
    after = lax.ppermute(head, axis, [(i + 1, i) for i in range(count - 1)])
    return before, after


def exchange(pieces, axis):
    return lax.all_to_all(pieces, axis, split_axis=0, concat_axis=0)


def spread(piece, count):
    return jnp.broadcast_to(piece[None], (count,) + piece.shape)


def body(cube):
    n_rows = lax.axis_size("narrow")
    n_cols = lax.axis_size("wide")
    count = n_rows * n_cols
    rows, cols, bands = cube.shape
    depth = TV_ITERS
    axes = ("narrow", "wide")

    left, right = neighbours(cube, "wide", 1, depth)
    pieces = 8 if rows % 8 == 0 else 1
    packed = pl.pallas_call(
        gram_kernel,
        in_specs=[pl.BlockSpec(memory_space=pl.ANY)],
        out_shape=jax.ShapeDtypeStruct((LANES, HALF), f32),
        scratch_shapes=[
            pltpu.VMEM(cube.shape, cube.dtype),
            pltpu.VMEM((LANES, LANES), f32),
            pltpu.SemaphoreType.DMA((pieces,)),
        ],
        compiler_params=pltpu.CompilerParams(vmem_limit_bytes=62 * 2**20),
    )(cube)
    part = exchange(packed.reshape(count, LANES // count, HALF), axes)
    share = jnp.sum(part, axis=0)
    gathered = exchange(spread(share, count), axes).reshape(LANES, HALF)

    vmem = pl.BlockSpec(memory_space=pltpu.VMEM)
    tall, span = rows + 2 * depth, cols + SIDE
    up, down, side = pl.pallas_call(
        functools.partial(halo_kernel, depth),
        in_specs=[vmem] * 4,
        out_specs=[vmem] * 3,
        out_shape=[
            jax.ShapeDtypeStruct((depth, span, bands), bf16),
            jax.ShapeDtypeStruct((depth, span, bands), bf16),
            jax.ShapeDtypeStruct((rows, SIDE, bands), bf16),
        ],
        scratch_shapes=[pltpu.VMEM((rows, SIDE, bands), f32)],
        cost_estimate=pl.CostEstimate(flops=2**32, bytes_accessed=2**18, transcendentals=0),
        compiler_params=pltpu.CompilerParams(vmem_limit_bytes=16 * 2**20),
    )(left, right, cube[:depth], cube[rows - depth :])
    above = lax.ppermute(down, "narrow", [(i, i + 1) for i in range(n_rows - 1)])
    below = lax.ppermute(up, "narrow", [(i + 1, i) for i in range(n_rows - 1)])

    row, col = lax.axis_index("narrow"), lax.axis_index("wide")
    edges = jnp.stack([row == 0, row == n_rows - 1, col == 0, col == n_cols - 1]).astype(jnp.int32)
    inv_count = 1.0 / (count * rows * cols)
    basis = pl.pallas_call(
        functools.partial(subspace_kernel, inv_count),
        in_specs=[vmem] * 2,
        out_specs=vmem,
        out_shape=jax.ShapeDtypeStruct((RANK, LANES), f32),
        cost_estimate=pl.CostEstimate(flops=2**32, bytes_accessed=2**18, transcendentals=0),
        compiler_params=pltpu.CompilerParams(vmem_limit_bytes=16 * 2**20),
    )(gathered, jnp.asarray(start_basis()))
    restored, projector = pl.pallas_call(
        functools.partial(main_kernel, depth),
        in_specs=[pl.BlockSpec(memory_space=pltpu.SMEM)] + [vmem] * 5,
        out_specs=[pl.BlockSpec(memory_space=pl.ANY)] * 2,
        out_shape=[
            jax.ShapeDtypeStruct((rows, cols, bands), bf16),
            jax.ShapeDtypeStruct((bands, bands), f32),
        ],
        scratch_shapes=[pltpu.VMEM((tall, span, LANES), f32)] * 3
        + [
            pltpu.VMEM((rows, cols, bands), bf16),
            pltpu.VMEM((bands, bands), f32),
            pltpu.SemaphoreType.DMA((rows // UNROLL,)),
            pltpu.SemaphoreType.DMA,
        ],
        compiler_params=pltpu.CompilerParams(vmem_limit_bytes=48 * 2**20),
    )(edges, basis, cube, above, below, side)
    return restored, projector


def solution(mesh):
    return jax.shard_map(
        body,
        mesh=mesh,
        in_specs=(P("narrow", "wide", None),),
        out_specs=(P("narrow", "wide", None), P()),
        check_vma=False,
    )
```

```python
import functools

import jax
import jax.numpy as jnp
import numpy as np
from jax import lax
from jax.experimental import pallas as pl
from jax.experimental.pallas import tpu as pltpu
from jax.sharding import PartitionSpec as P

BANDS = 224
RANK = 16
POWER_ITERS = 4
TV_ITERS = 3
LANES = 256
HALF = 128
TAIL = BANDS - HALF
SIDE = 8
BLOCK = 4
UNROLL = 4
OUT_ROWS = 8

f32 = jnp.float32
bf16 = jnp.bfloat16


def iotas(shape):
    return lax.broadcasted_iota(jnp.int32, shape, 0), lax.broadcasted_iota(jnp.int32, shape, 1)


def gram_kernel(cube_ref, packed_ref, block, full, sems):
    rows, cols, bands = cube_ref.shape
    pieces = sems.shape[0]
    high = rows // pieces

    def copy(n):
        part = pl.ds(n * high, high)
        return pltpu.make_async_copy(cube_ref.at[part], block.at[part], sems.at[n])

    for n in range(pieces):
        copy(n).start()
    full[...] = jnp.zeros_like(full)
    for n in range(pieces):
        copy(n).wait()
    flat = block[...].reshape(rows * cols, bands)
    full[0:bands, 0:bands] = lax.dot_general(
        flat, flat, (((0,), (0,)), ((), ())), preferred_element_type=f32
    )
    i, j = iotas((HALF, HALF))
    first = full[0:HALF, 0:HALF]
    second = pltpu.roll(full[HALF:LANES, HALF:LANES], 1, 1)
    packed_ref[0:HALF, :] = jnp.where(j <= i, first, second)
    packed_ref[HALF:LANES, :] = full[0:HALF, HALF:LANES]


def split3(x):
    high = x.astype(bf16)
    rest = x - high.astype(f32)
    mid = rest.astype(bf16)
    low = (rest - mid.astype(f32)).astype(bf16)
    return high, mid, low


def product(left, right, dims):
    def dot(a, b):
        return lax.dot_general(a, b, (dims, ((), ())), preferred_element_type=f32)

    n = left[0].shape[0]
    top = dot(jnp.concatenate(left, axis=0), right[0])
    middle = dot(jnp.concatenate(left[:2], axis=0), right[1])
    last = dot(left[0], right[2])
    small = top[2 * n : 3 * n] + middle[n : 2 * n] + last
    return top[:n] + ((top[n : 2 * n] + middle[:n]) + small)


def unpack(packed, scale):
    i, j = iotas((HALF, HALF))
    merged = packed[0:HALF, :] * scale
    cross = packed[HALF:LANES, :] * scale
    first = jnp.where(j <= i, merged, 0.0) + jnp.where(j < i, merged, 0.0).T
    moved = pltpu.roll(merged, HALF - 1, 1)
    inside = (i < TAIL) & (j < TAIL)
    second = jnp.where(inside & (j >= i), moved, 0.0) + jnp.where(inside & (j > i), moved, 0.0).T
    return jnp.concatenate(
        [
            jnp.concatenate([first, cross], axis=1),
            jnp.concatenate([cross.T, second], axis=1),
        ],
        axis=0,
    )


def orthonormal(grown, inner):
    row = lax.broadcasted_iota(jnp.int32, (RANK, HALF), 0)
    work = [
        jnp.concatenate([inner, jnp.zeros((RANK, HALF - RANK), f32)], axis=1),
        grown[:, :HALF],
        grown[:, HALF:],
    ]
    diagonal = jnp.ones((RANK, HALF), f32)
    for k in range(0, RANK, BLOCK):
        columns = [
            jnp.broadcast_to(work[0][:, k + c : k + c + 1], (RANK, HALF)) for c in range(BLOCK)
        ]
        tops = [[part[k + r : k + r + 1, :] for part in work] for r in range(BLOCK)]
        small = [
            [columns[c][k + r : k + r + 1, :] for c in range(r + 1)] for r in range(BLOCK)
        ]
        factors = []
        for j in range(BLOCK):
            pivot = small[j][j]
            inverse = 1.0 / pivot
            diagonal = jnp.where(row == k + j, pivot, diagonal)
            factor = jnp.where(row > k + j, columns[j] * inverse, 0.0)
            factors.append(factor)
            below = [small[i][j] for i in range(BLOCK) if i > j]
            for i in range(j + 1, BLOCK):
                ratio = small[i][j] * inverse
                for c in range(j + 1, i + 1):
                    small[i][c] = small[i][c] - ratio * below[c - j - 1]
                tops[i] = [x - ratio * y for x, y in zip(tops[i], tops[j])]
                columns[i] = columns[i] - factor * below[i - j - 1]
        for n in range(len(work)):
            if n > 0 or k + BLOCK < RANK:
                for j in range(BLOCK):
                    work[n] = work[n] - factors[j] * tops[j][n]
    scale = lax.rsqrt(diagonal)
    return jnp.concatenate([work[1] * scale, work[2] * scale], axis=1)


def subspace(gram, start):
    parts = split3(gram)
    grown = product(split3(start), parts, ((1,), (0,)))
    for step in range(POWER_ITERS):
        pieces = split3(grown)
        inner = product(pieces, pieces, ((1,), (1,)))
        later = grown if step == POWER_ITERS - 1 else product(pieces, parts, ((1,), (0,)))
        grown = orthonormal(later, inner)
    return grown


def halo_kernel(depth, left_ref, right_ref, top_ref, bottom_ref, up_ref, down_ref, side_ref, wide):
    rows, cols = side_ref.shape[0], top_ref.shape[1]
    wide[...] = jnp.zeros_like(wide)
    wide[:, 0:depth] = right_ref[...].astype(f32)
    wide[:, SIDE - depth :] = left_ref[...].astype(f32)
    side = wide[...].astype(bf16)
    side_ref[...] = side
    up_ref[:, 0:cols] = top_ref[...]
    up_ref[:, cols:] = side[:depth]
    down_ref[:, 0:cols] = bottom_ref[...]
    down_ref[:, cols:] = side[rows - depth :]


def subspace_kernel(inv_count, packed_ref, start_ref, basis_ref):
    basis_ref[...] = subspace(unpack(packed_ref[...], inv_count), start_ref[...])


def main_kernel(
    depth, edge_ref, basis_ref, mid_ref, above_ref, below_ref, side_ref,
    out_ref, proj_ref, fit, field_a, field_b, out_stage, proj_stage, out_sems, proj_sem
):
    rows, cols, bands = mid_ref.shape
    span = cols + SIDE
    proj_copy = pltpu.make_async_copy(proj_stage, proj_ref, proj_sem)

    def out_copy(n):
        part = pl.ds(n * OUT_ROWS, OUT_ROWS)
        return pltpu.make_async_copy(out_stage.at[part], out_ref.at[part], out_sems.at[n])

    high, mid, low = split3(basis_ref[...])
    right = jnp.concatenate([high, high, high, mid, mid, low], axis=0)
    left = jnp.concatenate([high, mid, low, high, mid, high], axis=0)
    tn = (((0,), (0,)), ((), ()))
    proj_stage[...] = lax.dot_general(left, right, tn, preferred_element_type=f32)[:bands, :bands]
    proj_copy.start()
    mixed = lax.dot_general(
        jnp.concatenate([high, high, high], axis=0),
        jnp.concatenate([high, mid, low], axis=0),
        tn,
        preferred_element_type=f32,
    )[:bands]
    mixed = mixed * 4.0
    mixed_high = mixed.astype(bf16)
    mixed_low = (mixed - mixed_high.astype(f32)).astype(bf16)

    def fitted(block):
        n, w, b = block.shape
        if w % 16:
            flat = block.astype(f32).reshape(n * w, b).astype(bf16)
        else:
            flat = block.reshape(n * w, b)
        res = jnp.dot(flat, mixed_high, preferred_element_type=f32)
        res = res + jnp.dot(flat, mixed_low, preferred_element_type=f32)
        return res.reshape(n, w, LANES)

    at_top, at_bottom, at_left, at_right = (edge_ref[n] for n in range(4))
    edge = cols - SIDE
    place = lax.broadcasted_iota(jnp.int32, (2 * SIDE, HALF), 0)
    closed = ((place == SIDE - 1) & (at_right > 0)) | ((place == 2 * SIDE - 1) & (at_left > 0))
    keep = jnp.where(closed, 0.0, 1.0).astype(f32)
    lanes = [slice(0, HALF), slice(HALF, LANES)]

    def slopes(now, later, open_row=None):
        down = later - now
        if open_row is not None:
            down = down * open_row
        across = pltpu.roll(now, span - 1, 0) - now
        across = jnp.concatenate([across[:edge], across[edge:] * keep], axis=0)
        inverse = lax.rsqrt(down * down + across * across + 4.0)
        return down * inverse, across * inverse

    def advance(base, before, down, across):
        return base + ((down - before) + (across - pltpu.roll(across, 1, 0)))

    def fit_rows(start, stop):
        if start < depth:
            fit[0:depth] = fitted(above_ref[...])
        elif start < depth + rows:
            part = slice(start - depth, stop - depth)
            fit[start:stop, 0:cols, :] = fitted(mid_ref[part])
            fit[start:stop, cols:span, :] = fitted(side_ref[part])
        else:
            fit[depth + rows :] = fitted(below_ref[...])

    groups = [(0, depth)]
    groups += [(depth + n, depth + n + UNROLL) for n in range(0, rows, UNROLL)]
    groups += [(depth + rows, rows + 2 * depth)]
    ready = 0
    befores = [None, None]
    for r in range(rows + 2 * depth - 1):
        while ready < len(groups) and groups[ready][0] <= r + 1 + UNROLL:
            fit_rows(*groups[ready])
            ready += 1
        open_row = None
        if r == depth - 1:
            open_row = jnp.where(at_top > 0, 0.0, 1.0)
        elif r == depth + rows - 1:
            open_row = jnp.where(at_bottom > 0, 0.0, 1.0)
        for n, lane in enumerate(lanes):
            now = fit[r, :, lane]
            down, across = slopes(now, fit[r + 1, :, lane], open_row)
            if r > 0:
                field_a[r, :, lane] = advance(now, befores[n], down, across)
            befores[n] = down

    def step(source, target, first, last, unroll, final):
        @pl.when(at_top > 0)
        def _():
            source[depth - 1] = source[depth]

        @pl.when(at_bottom > 0)
        def _():
            source[depth + rows] = source[depth + rows - 1]

        carry = []
        for lane in lanes:
            before, now = source[first - 1, :, lane], source[first, :, lane]
            carry += [now, slopes(before, now)[0]]

        def row_step(r, carry):
            out = []
            for n, lane in enumerate(lanes):
                now, before = carry[2 * n], carry[2 * n + 1]
                later = source[r + 1, :, lane]
                down, across = slopes(now, later)
                value = advance(0.5 * (now + fit[r, :, lane]), before, down, across)
                if final:
                    value = (value[:cols] * 0.25).astype(bf16)
                    if n == 0:
                        out_stage[r - depth, :, 0:HALF] = value
                    else:
                        out_stage[r - depth, :, HALF:bands] = value[:, : bands - HALF]
                else:
                    target[r, :, lane] = value
                out += [later, down]
            return out

        def block_step(n, carry):
            for inner in range(unroll):
                carry = row_step(first + n * unroll + inner, carry)
            if final:
                out_copy(n).start()
            return tuple(carry)

        lax.fori_loop(0, (last - first) // unroll, block_step, tuple(carry))

    step(field_a, field_b, depth - 2, rows + depth + 2, (rows + 4) // 4, False)
    step(field_b, None, depth, rows + depth, OUT_ROWS, True)
    proj_copy.wait()
    for n in range(rows // OUT_ROWS):
        out_copy(n).wait()


def start_basis():
    bands = np.arange(BANDS, dtype=np.float32)[None, :]
    cols = np.arange(RANK, dtype=np.float32)[:, None]
    angle = np.float32(np.pi) * (bands + np.float32(0.5)) * cols / np.float32(BANDS)
    return np.pad(np.cos(angle).astype(np.float32), ((0, 0), (0, LANES - BANDS)))


def neighbours(block, axis, dim, width):
    count = lax.axis_size(axis)
    size = block.shape[dim]
    head = lax.slice_in_dim(block, 0, width, axis=dim)
    tail = lax.slice_in_dim(block, size - width, size, axis=dim)
    before = lax.ppermute(tail, axis, [(i, i + 1) for i in range(count - 1)])
    after = lax.ppermute(head, axis, [(i + 1, i) for i in range(count - 1)])
    return before, after


def exchange(pieces, axis):
    return lax.all_to_all(pieces, axis, split_axis=0, concat_axis=0)


def spread(piece, count):
    return jnp.broadcast_to(piece[None], (count,) + piece.shape)


def body(cube):
    n_rows = lax.axis_size("narrow")
    n_cols = lax.axis_size("wide")
    count = n_rows * n_cols
    rows, cols, bands = cube.shape
    depth = TV_ITERS
    axes = ("narrow", "wide")

    left, right = neighbours(cube, "wide", 1, depth)
    pieces = 8 if rows % 8 == 0 else 1
    packed = pl.pallas_call(
        gram_kernel,
        in_specs=[pl.BlockSpec(memory_space=pl.ANY)],
        out_shape=jax.ShapeDtypeStruct((LANES, HALF), f32),
        scratch_shapes=[
            pltpu.VMEM(cube.shape, cube.dtype),
            pltpu.VMEM((LANES, LANES), f32),
            pltpu.SemaphoreType.DMA((pieces,)),
        ],
        compiler_params=pltpu.CompilerParams(vmem_limit_bytes=62 * 2**20),
    )(cube)
    part = exchange(packed.reshape(count, LANES // count, HALF), axes)
    share = jnp.sum(part, axis=0)
    gathered = exchange(spread(share, count), axes).reshape(LANES, HALF)

    vmem = pl.BlockSpec(memory_space=pltpu.VMEM)
    tall, span = rows + 2 * depth, cols + SIDE
    up, down, side = pl.pallas_call(
        functools.partial(halo_kernel, depth),
        in_specs=[vmem] * 4,
        out_specs=[vmem] * 3,
        out_shape=[
            jax.ShapeDtypeStruct((depth, span, bands), bf16),
            jax.ShapeDtypeStruct((depth, span, bands), bf16),
            jax.ShapeDtypeStruct((rows, SIDE, bands), bf16),
        ],
        scratch_shapes=[pltpu.VMEM((rows, SIDE, bands), f32)],
        cost_estimate=pl.CostEstimate(flops=2**32, bytes_accessed=2**18, transcendentals=0),
        compiler_params=pltpu.CompilerParams(vmem_limit_bytes=16 * 2**20),
    )(left, right, cube[:depth], cube[rows - depth :])
    above = lax.ppermute(down, "narrow", [(i, i + 1) for i in range(n_rows - 1)])
    below = lax.ppermute(up, "narrow", [(i + 1, i) for i in range(n_rows - 1)])

    row, col = lax.axis_index("narrow"), lax.axis_index("wide")
    edges = jnp.stack([row == 0, row == n_rows - 1, col == 0, col == n_cols - 1]).astype(jnp.int32)
    inv_count = 1.0 / (count * rows * cols)
    basis = pl.pallas_call(
        functools.partial(subspace_kernel, inv_count),
        in_specs=[vmem] * 2,
        out_specs=vmem,
        out_shape=jax.ShapeDtypeStruct((RANK, LANES), f32),
        cost_estimate=pl.CostEstimate(flops=2**32, bytes_accessed=2**18, transcendentals=0),
        compiler_params=pltpu.CompilerParams(vmem_limit_bytes=16 * 2**20),
    )(gathered, jnp.asarray(start_basis()))
    restored, projector = pl.pallas_call(
        functools.partial(main_kernel, depth),
        in_specs=[pl.BlockSpec(memory_space=pltpu.SMEM)] + [vmem] * 5,
        out_specs=[pl.BlockSpec(memory_space=pl.ANY)] * 2,
        out_shape=[
            jax.ShapeDtypeStruct((rows, cols, bands), bf16),
            jax.ShapeDtypeStruct((bands, bands), f32),
        ],
        scratch_shapes=[pltpu.VMEM((tall, span, LANES), f32)] * 3
        + [
            pltpu.VMEM((rows, cols, bands), bf16),
            pltpu.VMEM((bands, bands), f32),
            pltpu.SemaphoreType.DMA((rows // OUT_ROWS,)),
            pltpu.SemaphoreType.DMA,
        ],
        compiler_params=pltpu.CompilerParams(vmem_limit_bytes=48 * 2**20),
    )(edges, basis, cube, above, below, side)
    return restored, projector


def solution(mesh):
    return jax.shard_map(
        body,
        mesh=mesh,
        in_specs=(P("narrow", "wide", None),),
        out_specs=(P("narrow", "wide", None), P()),
        check_vma=False,
    )
```

```python
import functools

import jax
import jax.numpy as jnp
import numpy as np
from jax import lax
from jax.experimental import pallas as pl
from jax.experimental.pallas import tpu as pltpu
from jax.sharding import PartitionSpec as P

BANDS = 224
RANK = 16
POWER_ITERS = 4
TV_ITERS = 3
LANES = 256
HALF = 128
TAIL = BANDS - HALF
SIDE = 8
BLOCK = 4
FIT_ROWS = 8
AHEAD = 4
LAG = 3
OUT_ROWS = 8

f32 = jnp.float32
bf16 = jnp.bfloat16


def iotas(shape):
    return lax.broadcasted_iota(jnp.int32, shape, 0), lax.broadcasted_iota(jnp.int32, shape, 1)


def gram_kernel(cube_ref, packed_ref, block, full, sems):
    rows, cols, bands = cube_ref.shape
    pieces = sems.shape[0]
    high = rows // pieces

    def copy(n):
        part = pl.ds(n * high, high)
        return pltpu.make_async_copy(cube_ref.at[part], block.at[part], sems.at[n])

    for n in range(pieces):
        copy(n).start()
    full[...] = jnp.zeros_like(full)
    total = None
    for n in range(pieces):
        copy(n).wait()
        flat = block[n * high : (n + 1) * high].reshape(high * cols, bands)
        term = lax.dot_general(flat, flat, (((0,), (0,)), ((), ())), preferred_element_type=f32)
        total = term if total is None else total + term
    full[0:bands, 0:bands] = total
    i, j = iotas((HALF, HALF))
    first = full[0:HALF, 0:HALF]
    second = pltpu.roll(full[HALF:LANES, HALF:LANES], 1, 1)
    packed_ref[0:HALF, :] = jnp.where(j <= i, first, second)
    packed_ref[HALF:LANES, :] = full[0:HALF, HALF:LANES]


def split3(x):
    high = x.astype(bf16)
    rest = x - high.astype(f32)
    mid = rest.astype(bf16)
    low = (rest - mid.astype(f32)).astype(bf16)
    return high, mid, low


def product(left, right, dims):
    def dot(a, b):
        return lax.dot_general(a, b, (dims, ((), ())), preferred_element_type=f32)

    n = left[0].shape[0]
    top = dot(jnp.concatenate(left, axis=0), right[0])
    middle = dot(jnp.concatenate(left[:2], axis=0), right[1])
    last = dot(left[0], right[2])
    small = top[2 * n : 3 * n] + middle[n : 2 * n] + last
    return top[:n] + ((top[n : 2 * n] + middle[:n]) + small)


def unpack(packed, scale):
    i, j = iotas((HALF, HALF))
    merged = packed[0:HALF, :] * scale
    cross = packed[HALF:LANES, :] * scale
    first = jnp.where(j <= i, merged, 0.0) + jnp.where(j < i, merged, 0.0).T
    moved = pltpu.roll(merged, HALF - 1, 1)
    inside = (i < TAIL) & (j < TAIL)
    second = jnp.where(inside & (j >= i), moved, 0.0) + jnp.where(inside & (j > i), moved, 0.0).T
    return jnp.concatenate(
        [
            jnp.concatenate([first, cross], axis=1),
            jnp.concatenate([cross.T, second], axis=1),
        ],
        axis=0,
    )


def orthonormal(grown, inner):
    row = lax.broadcasted_iota(jnp.int32, (RANK, HALF), 0)
    work = [
        jnp.concatenate([inner, jnp.zeros((RANK, HALF - RANK), f32)], axis=1),
        grown[:, :HALF],
        grown[:, HALF:],
    ]
    diagonal = jnp.ones((RANK, HALF), f32)
    for k in range(0, RANK, BLOCK):
        columns = [
            jnp.broadcast_to(work[0][:, k + c : k + c + 1], (RANK, HALF)) for c in range(BLOCK)
        ]
        tops = [[part[k + r : k + r + 1, :] for part in work] for r in range(BLOCK)]
        small = [
            [columns[c][k + r : k + r + 1, :] for c in range(r + 1)] for r in range(BLOCK)
        ]
        factors = []
        for j in range(BLOCK):
            pivot = small[j][j]
            inverse = 1.0 / pivot
            diagonal = jnp.where(row == k + j, pivot, diagonal)
            factor = jnp.where(row > k + j, columns[j] * inverse, 0.0)
            factors.append(factor)
            below = [small[i][j] for i in range(BLOCK) if i > j]
            for i in range(j + 1, BLOCK):
                ratio = small[i][j] * inverse
                for c in range(j + 1, i + 1):
                    small[i][c] = small[i][c] - ratio * below[c - j - 1]
                tops[i] = [x - ratio * y for x, y in zip(tops[i], tops[j])]
                columns[i] = columns[i] - factor * below[i - j - 1]
        for n in range(len(work)):
            if n > 0 or k + BLOCK < RANK:
                for j in range(BLOCK):
                    work[n] = work[n] - factors[j] * tops[j][n]
    scale = lax.rsqrt(diagonal)
    return jnp.concatenate([work[1] * scale, work[2] * scale], axis=1)


def subspace(gram, start):
    parts = split3(gram)
    grown = product(split3(start), parts, ((1,), (0,)))
    for step in range(POWER_ITERS):
        pieces = split3(grown)
        inner = product(pieces, pieces, ((1,), (1,)))
        later = grown if step == POWER_ITERS - 1 else product(pieces, parts, ((1,), (0,)))
        grown = orthonormal(later, inner)
    return grown


def halo_kernel(depth, left_ref, right_ref, top_ref, bottom_ref, up_ref, down_ref, side_ref, wide):
    rows, cols = side_ref.shape[0], top_ref.shape[1]
    wide[...] = jnp.zeros_like(wide)
    wide[:, 0:depth] = right_ref[...].astype(f32)
    wide[:, SIDE - depth :] = left_ref[...].astype(f32)
    side = wide[...].astype(bf16)
    side_ref[...] = side
    up_ref[:, 0:cols] = top_ref[...]
    up_ref[:, cols:] = side[:depth]
    down_ref[:, 0:cols] = bottom_ref[...]
    down_ref[:, cols:] = side[rows - depth :]


def subspace_kernel(inv_count, packed_ref, start_ref, basis_ref):
    basis_ref[...] = subspace(unpack(packed_ref[...], inv_count), start_ref[...])


def main_kernel(
    depth, edge_ref, basis_ref, mid_ref, above_ref, below_ref, side_ref,
    out_ref, proj_ref, fit, field_a, field_b, out_stage, proj_stage, out_sems, proj_sem
):
    rows, cols, bands = mid_ref.shape
    span = cols + SIDE
    proj_copy = pltpu.make_async_copy(proj_stage, proj_ref, proj_sem)

    def out_copy(n):
        part = pl.ds(n * OUT_ROWS, OUT_ROWS)
        return pltpu.make_async_copy(out_stage.at[part], out_ref.at[part], out_sems.at[n])

    high, mid, low = split3(basis_ref[...])
    right = jnp.concatenate([high, high, high, mid, mid, low], axis=0)
    left = jnp.concatenate([high, mid, low, high, mid, high], axis=0)
    tn = (((0,), (0,)), ((), ()))
    proj_stage[...] = lax.dot_general(left, right, tn, preferred_element_type=f32)[:bands, :bands]
    proj_copy.start()
    mixed = lax.dot_general(
        jnp.concatenate([high, high, high], axis=0),
        jnp.concatenate([high, mid, low], axis=0),
        tn,
        preferred_element_type=f32,
    )[:bands]
    mixed = mixed * 4.0
    mixed_high = mixed.astype(bf16)
    mixed_low = (mixed - mixed_high.astype(f32)).astype(bf16)

    def fitted(flat):
        res = jnp.dot(flat, mixed_high, preferred_element_type=f32)
        return res + jnp.dot(flat, mixed_low, preferred_element_type=f32)

    def fit_rows(start, stop):
        n = stop - start
        if depth <= start < depth + rows:
            part = slice(start - depth, stop - depth)
            center = mid_ref[part].reshape(n * cols, bands)
            side = side_ref[part].astype(f32).reshape(n * SIDE, bands).astype(bf16)
            res = fitted(jnp.concatenate([center, side], axis=0))
            fit[start:stop, 0:cols, :] = res[: n * cols].reshape(n, cols, LANES)
            fit[start:stop, cols:span, :] = res[n * cols :].reshape(n, SIDE, LANES)
        else:
            block = above_ref[...] if start < depth else below_ref[...]
            flat = block.astype(f32).reshape(n * span, bands).astype(bf16)
            fit[start:stop] = fitted(flat).reshape(n, span, LANES)

    at_top, at_bottom, at_left, at_right = (edge_ref[n] for n in range(4))
    edge = cols - SIDE
    place = lax.broadcasted_iota(jnp.int32, (2 * SIDE, HALF), 0)
    closed = ((place == SIDE - 1) & (at_right > 0)) | ((place == 2 * SIDE - 1) & (at_left > 0))
    keep = jnp.where(closed, 0.0, 1.0).astype(f32)
    open_rows = {
        depth - 1: jnp.where(at_top > 0, 0.0, 1.0),
        depth + rows - 1: jnp.where(at_bottom > 0, 0.0, 1.0),
    }
    lanes = [slice(0, HALF), slice(HALF, LANES)]
    fields = [fit, field_a, field_b]
    befores = [[None, None] for _ in fields]

    def tv_row(s, r):
        source = fields[s]
        for n, lane in enumerate(lanes):
            now = source[r, :, lane]
            down = source[r + 1, :, lane] - now
            if r in open_rows:
                down = down * open_rows[r]
            across = pltpu.roll(now, span - 1, 0) - now
            across = jnp.concatenate([across[:edge], across[edge:] * keep], axis=0)
            inverse = lax.rsqrt(down * down + across * across + 4.0)
            down = down * inverse
            before, befores[s][n] = befores[s][n], down
            if before is None:
                continue
            across = across * inverse
            base = now if s == 0 else 0.5 * (now + fit[r, :, lane])
            value = base + ((down - before) + (across - pltpu.roll(across, 1, 0)))
            if s < TV_ITERS - 1:
                fields[s + 1][r, :, lane] = value
            else:
                value = (value[:cols] * 0.25).astype(bf16)
                width = min(lane.stop, bands) - lane.start
                out_stage[r - depth, :, lane.start : lane.start + width] = value[:, :width]

    tall = rows + 2 * depth
    groups = [(0, depth)]
    groups += [(depth + n, depth + n + FIT_ROWS) for n in range(0, rows, FIT_ROWS)]
    groups += [(depth + rows, tall)]
    ready = 0
    for r in range(tall - 1 + LAG * (TV_ITERS - 1)):
        while ready < len(groups) and groups[ready][0] <= r + 1 + AHEAD:
            fit_rows(*groups[ready])
            ready += 1
        for s in range(TV_ITERS):
            at = r - LAG * s
            if s <= at < tall - 1 - s:
                tv_row(s, at)
                done = at - depth + 1
                if s == TV_ITERS - 1 and done > 0 and done % OUT_ROWS == 0:
                    out_copy(done // OUT_ROWS - 1).start()
    proj_copy.wait()
    for n in range(rows // OUT_ROWS):
        out_copy(n).wait()


def start_basis():
    bands = np.arange(BANDS, dtype=np.float32)[None, :]
    cols = np.arange(RANK, dtype=np.float32)[:, None]
    angle = np.float32(np.pi) * (bands + np.float32(0.5)) * cols / np.float32(BANDS)
    return np.pad(np.cos(angle).astype(np.float32), ((0, 0), (0, LANES - BANDS)))


def neighbours(block, axis, dim, width):
    count = lax.axis_size(axis)
    size = block.shape[dim]
    head = lax.slice_in_dim(block, 0, width, axis=dim)
    tail = lax.slice_in_dim(block, size - width, size, axis=dim)
    before = lax.ppermute(tail, axis, [(i, i + 1) for i in range(count - 1)])
    after = lax.ppermute(head, axis, [(i + 1, i) for i in range(count - 1)])
    return before, after


def exchange(pieces, axes):
    count = pieces.shape[0]
    stride = 13 if count % 13 else 1
    order = [n * stride % count for n in range(count)]
    return lax.all_to_all(pieces, axes, split_axis=0, concat_axis=0, axis_index_groups=[order])


def spread(piece, count):
    return jnp.broadcast_to(piece[None], (count,) + piece.shape)


def body(cube):
    n_rows = lax.axis_size("narrow")
    n_cols = lax.axis_size("wide")
    count = n_rows * n_cols
    rows, cols, bands = cube.shape
    depth = TV_ITERS
    axes = ("narrow", "wide")

    left, right = neighbours(cube, "wide", 1, depth)
    pieces = 2 if rows % 2 == 0 else 1
    packed = pl.pallas_call(
        gram_kernel,
        in_specs=[pl.BlockSpec(memory_space=pl.ANY)],
        out_shape=jax.ShapeDtypeStruct((LANES, HALF), f32),
        scratch_shapes=[
            pltpu.VMEM(cube.shape, cube.dtype),
            pltpu.VMEM((LANES, LANES), f32),
            pltpu.SemaphoreType.DMA((pieces,)),
        ],
        compiler_params=pltpu.CompilerParams(vmem_limit_bytes=62 * 2**20),
    )(cube)
    part = exchange(packed.reshape(count, LANES // count, HALF), axes)
    share = jnp.sum(part, axis=0)
    gathered = exchange(spread(share, count), axes).reshape(LANES, HALF)

    vmem = pl.BlockSpec(memory_space=pltpu.VMEM)
    tall, span = rows + 2 * depth, cols + SIDE
    up, down, side = pl.pallas_call(
        functools.partial(halo_kernel, depth),
        in_specs=[vmem] * 4,
        out_specs=[vmem] * 3,
        out_shape=[
            jax.ShapeDtypeStruct((depth, span, bands), bf16),
            jax.ShapeDtypeStruct((depth, span, bands), bf16),
            jax.ShapeDtypeStruct((rows, SIDE, bands), bf16),
        ],
        scratch_shapes=[pltpu.VMEM((rows, SIDE, bands), f32)],
        cost_estimate=pl.CostEstimate(flops=2**32, bytes_accessed=2**18, transcendentals=0),
        compiler_params=pltpu.CompilerParams(vmem_limit_bytes=16 * 2**20),
    )(left, right, cube[:depth], cube[rows - depth :])
    above = lax.ppermute(down, "narrow", [(i, i + 1) for i in range(n_rows - 1)])
    below = lax.ppermute(up, "narrow", [(i + 1, i) for i in range(n_rows - 1)])

    row, col = lax.axis_index("narrow"), lax.axis_index("wide")
    edges = jnp.stack([row == 0, row == n_rows - 1, col == 0, col == n_cols - 1]).astype(jnp.int32)
    inv_count = 1.0 / (count * rows * cols)
    basis = pl.pallas_call(
        functools.partial(subspace_kernel, inv_count),
        in_specs=[vmem] * 2,
        out_specs=vmem,
        out_shape=jax.ShapeDtypeStruct((RANK, LANES), f32),
        cost_estimate=pl.CostEstimate(flops=2**32, bytes_accessed=2**18, transcendentals=0),
        compiler_params=pltpu.CompilerParams(vmem_limit_bytes=16 * 2**20),
    )(gathered, jnp.asarray(start_basis()))
    restored, projector = pl.pallas_call(
        functools.partial(main_kernel, depth),
        in_specs=[pl.BlockSpec(memory_space=pltpu.SMEM)] + [vmem] * 5,
        out_specs=[pl.BlockSpec(memory_space=pl.ANY)] * 2,
        out_shape=[
            jax.ShapeDtypeStruct((rows, cols, bands), bf16),
            jax.ShapeDtypeStruct((bands, bands), f32),
        ],
        scratch_shapes=[pltpu.VMEM((tall, span, LANES), f32)] * 3
        + [
            pltpu.VMEM((rows, cols, bands), bf16),
            pltpu.VMEM((bands, bands), f32),
            pltpu.SemaphoreType.DMA((rows // OUT_ROWS,)),
            pltpu.SemaphoreType.DMA,
        ],
        compiler_params=pltpu.CompilerParams(vmem_limit_bytes=48 * 2**20),
    )(edges, basis, cube, above, below, side)
    return restored, projector


def solution(mesh):
    return jax.shard_map(
        body,
        mesh=mesh,
        in_specs=(P("narrow", "wide", None),),
        out_specs=(P("narrow", "wide", None), P()),
        check_vma=False,
    )
```

```python
import functools

import jax
import jax.numpy as jnp
import numpy as np
from jax import lax
from jax.experimental import pallas as pl
from jax.experimental.pallas import tpu as pltpu
from jax.sharding import PartitionSpec as P

BANDS = 224
RANK = 16
POWER_ITERS = 4
TV_ITERS = 3
LANES = 256
HALF = 128
TAIL = BANDS - HALF
SIDE = 8
BLOCK = 8
FIT_ROWS = (2, 6, 8, 8, 8)
AHEAD = 4
LAG = 3
OUT_ROWS = (8, 8, 8, 4, 2, 2)

f32 = jnp.float32
bf16 = jnp.bfloat16


def iotas(shape):
    return lax.broadcasted_iota(jnp.int32, shape, 0), lax.broadcasted_iota(jnp.int32, shape, 1)


def gram_kernel(cube_ref, packed_ref, block, full, sems):
    rows, cols, bands = cube_ref.shape
    pieces = sems.shape[0]
    high = rows // pieces

    def copy(n):
        part = pl.ds(n * high, high)
        return pltpu.make_async_copy(cube_ref.at[part], block.at[part], sems.at[n])

    for n in range(pieces):
        copy(n).start()
    full[HALF:, HALF:] = jnp.zeros((LANES - HALF, LANES - HALF), f32)
    total = None
    for n in range(pieces):
        copy(n).wait()
        flat = block[n * high : (n + 1) * high].reshape(high * cols, bands)
        term = lax.dot_general(flat, flat, (((0,), (0,)), ((), ())), preferred_element_type=f32)
        total = term if total is None else total + term
    full[0:bands, 0:bands] = total
    i, j = iotas((HALF, HALF))
    first = full[0:HALF, 0:HALF]
    second = pltpu.roll(full[HALF:LANES, HALF:LANES], 1, 1)
    packed_ref[0:HALF, :] = jnp.where(j <= i, first, second)
    packed_ref[HALF:bands, :] = full[HALF:bands, 0:HALF]
    if packed_ref.shape[0] > bands:
        packed_ref[bands:, :] = jnp.zeros((packed_ref.shape[0] - bands, HALF), f32)


def sum_kernel(count, pieces_ref, spread_ref):
    high = pieces_ref.shape[0] // count
    parts = [pieces_ref[n * high : (n + 1) * high, :] for n in range(count)]
    total = functools.reduce(jnp.add, parts)
    for n in range(count):
        spread_ref[n * high : (n + 1) * high, :] = total


def split3(x):
    high = x.astype(bf16)
    rest = x - high.astype(f32)
    mid = rest.astype(bf16)
    low = (rest - mid.astype(f32)).astype(bf16)
    return high, mid, low


def product(left, right, dims):
    def dot(a, b):
        return lax.dot_general(a, b, (dims, ((), ())), preferred_element_type=f32)

    n = left[0].shape[0]
    top = dot(jnp.concatenate(left, axis=0), right[0])
    middle = dot(jnp.concatenate(left[:2], axis=0), right[1])
    last = dot(left[0], right[2])
    small = top[2 * n : 3 * n] + middle[n : 2 * n] + last
    return top[:n] + ((top[n : 2 * n] + middle[:n]) + small)


def unpack(packed, scale):
    i, j = iotas((HALF, HALF))
    merged = packed[0:HALF, :] * scale
    below = packed[HALF:BANDS, :] * scale
    below = jnp.concatenate([below, jnp.zeros((LANES - BANDS, HALF), f32)], axis=0)
    first = jnp.where(j <= i, merged, 0.0) + jnp.where(j < i, merged, 0.0).T
    moved = pltpu.roll(merged, HALF - 1, 1)
    inside = (i < TAIL) & (j < TAIL)
    second = jnp.where(inside & (j >= i), moved, 0.0) + jnp.where(inside & (j > i), moved, 0.0).T
    return jnp.concatenate(
        [
            jnp.concatenate([first, below.T], axis=1),
            jnp.concatenate([below, second], axis=1),
        ],
        axis=0,
    )


def orthonormal(grown, inner):
    row = lax.broadcasted_iota(jnp.int32, (RANK, HALF), 0)
    work = [
        jnp.concatenate([inner, jnp.zeros((RANK, HALF - RANK), f32)], axis=1),
        grown[:, :HALF],
        grown[:, HALF:],
    ]
    diagonal = jnp.ones((RANK, HALF), f32)
    for k in range(0, RANK, BLOCK):
        columns = [
            jnp.broadcast_to(work[0][:, k + c : k + c + 1], (RANK, HALF)) for c in range(BLOCK)
        ]
        tops = [[part[k + r : k + r + 1, :] for part in work] for r in range(BLOCK)]
        small = [
            [columns[c][k + r : k + r + 1, :] for c in range(r + 1)] for r in range(BLOCK)
        ]
        factors = []
        for j in range(BLOCK):
            pivot = small[j][j]
            inverse = 1.0 / pivot
            diagonal = jnp.where(row == k + j, pivot, diagonal)
            factor = jnp.where(row > k + j, columns[j] * inverse, 0.0)
            factors.append(factor)
            below = [small[i][j] for i in range(BLOCK) if i > j]
            for i in range(j + 1, BLOCK):
                ratio = small[i][j] * inverse
                for c in range(j + 1, i + 1):
                    small[i][c] = small[i][c] - ratio * below[c - j - 1]
                tops[i] = [x - ratio * y for x, y in zip(tops[i], tops[j])]
                columns[i] = columns[i] - factor * below[i - j - 1]
        for n in range(len(work)):
            if n > 0 or k + BLOCK < RANK:
                for j in range(BLOCK):
                    work[n] = work[n] - factors[j] * tops[j][n]
    scale = lax.rsqrt(diagonal)
    return jnp.concatenate([work[1] * scale, work[2] * scale], axis=1)


def subspace(gram, start):
    parts = split3(gram)
    grown = product(split3(start), parts, ((1,), (0,)))
    for step in range(POWER_ITERS):
        pieces = split3(grown)
        inner = product(pieces, pieces, ((1,), (1,)))
        later = grown if step == POWER_ITERS - 1 else product(pieces, parts, ((1,), (0,)))
        grown = orthonormal(later, inner)
    return grown


def halo_kernel(depth, left_ref, right_ref, top_ref, bottom_ref, up_ref, down_ref, side_ref, wide):
    rows, cols = side_ref.shape[0], top_ref.shape[1]
    wide[...] = jnp.zeros_like(wide)
    wide[:, 0:depth] = right_ref[...].astype(f32)
    wide[:, SIDE - depth :] = left_ref[...].astype(f32)
    side = wide[...].astype(bf16)
    side_ref[...] = side
    up_ref[:, 0:cols] = top_ref[...]
    up_ref[:, cols:] = side[:depth]
    down_ref[:, 0:cols] = bottom_ref[...]
    down_ref[:, cols:] = side[rows - depth :]


def subspace_kernel(inv_count, packed_ref, start_ref, basis_ref):
    basis_ref[...] = subspace(unpack(packed_ref[...], inv_count), start_ref[...])


def main_kernel(
    depth, edge_ref, basis_ref, mid_ref, above_ref, below_ref, side_ref,
    out_ref, proj_ref, fit, field_a, field_b, out_stage, proj_stage, out_sems, proj_sem
):
    rows, cols, bands = mid_ref.shape
    span = cols + SIDE
    proj_copy = pltpu.make_async_copy(proj_stage, proj_ref, proj_sem)

    def out_copy(n):
        part = pl.ds(sum(OUT_ROWS[:n]), OUT_ROWS[n])
        return pltpu.make_async_copy(out_stage.at[part], out_ref.at[part], out_sems.at[n])

    high, mid, low = split3(basis_ref[...])
    right = jnp.concatenate([high, high, high, mid, mid, low], axis=0)
    left = jnp.concatenate([high, mid, low, high, mid, high], axis=0)
    tn = (((0,), (0,)), ((), ()))
    proj_stage[...] = lax.dot_general(left, right, tn, preferred_element_type=f32)[:bands, :bands]
    proj_copy.start()
    mixed = lax.dot_general(
        jnp.concatenate([high, high, high], axis=0),
        jnp.concatenate([high, mid, low], axis=0),
        tn,
        preferred_element_type=f32,
    )[:bands]
    mixed = mixed * 4.0
    mixed_high = mixed.astype(bf16)
    mixed_low = (mixed - mixed_high.astype(f32)).astype(bf16)

    def fitted(flat):
        res = jnp.dot(flat, mixed_high, preferred_element_type=f32)
        return res + jnp.dot(flat, mixed_low, preferred_element_type=f32)

    def fit_rows(start, stop):
        n = stop - start
        if depth <= start < depth + rows:
            part = slice(start - depth, stop - depth)
            center = mid_ref[part].reshape(n * cols, bands)
            side = side_ref[part].astype(f32).reshape(n * SIDE, bands).astype(bf16)
            res = fitted(jnp.concatenate([center, side], axis=0))
            fit[start:stop, 0:cols, :] = res[: n * cols].reshape(n, cols, LANES)
            fit[start:stop, cols:span, :] = res[n * cols :].reshape(n, SIDE, LANES)
        else:
            block = above_ref[...] if start < depth else below_ref[...]
            flat = block.astype(f32).reshape(n * span, bands).astype(bf16)
            fit[start:stop] = fitted(flat).reshape(n, span, LANES)

    at_top, at_bottom, at_left, at_right = (edge_ref[n] for n in range(4))
    edge = cols - SIDE
    place = lax.broadcasted_iota(jnp.int32, (2 * SIDE, HALF), 0)
    closed = ((place == SIDE - 1) & (at_right > 0)) | ((place == 2 * SIDE - 1) & (at_left > 0))
    keep = jnp.where(closed, 0.0, 1.0).astype(f32)
    open_rows = {
        depth - 1: jnp.where(at_top > 0, 0.0, 1.0),
        depth + rows - 1: jnp.where(at_bottom > 0, 0.0, 1.0),
    }
    lanes = [slice(0, HALF), slice(HALF, LANES)]
    fields = [fit, field_a, field_b]
    befores = [[None, None] for _ in fields]

    def tv_row(s, r):
        source = fields[s]
        for n, lane in enumerate(lanes):
            now = source[r, :, lane]
            down = source[r + 1, :, lane] - now
            if r in open_rows:
                down = down * open_rows[r]
            across = pltpu.roll(now, span - 1, 0) - now
            across = jnp.concatenate([across[:edge], across[edge:] * keep], axis=0)
            inverse = lax.rsqrt(down * down + across * across + 4.0)
            down = down * inverse
            before, befores[s][n] = befores[s][n], down
            if before is None:
                continue
            across = across * inverse
            base = now if s == 0 else 0.5 * (now + fit[r, :, lane])
            value = base + ((down - before) + (across - pltpu.roll(across, 1, 0)))
            if s < TV_ITERS - 1:
                fields[s + 1][r, :, lane] = value
            else:
                value = (value[:cols] * 0.25).astype(bf16)
                width = min(lane.stop, bands) - lane.start
                out_stage[r - depth, :, lane.start : lane.start + width] = value[:, :width]

    tall = rows + 2 * depth
    groups = [(0, depth)]
    for n in FIT_ROWS:
        groups.append((groups[-1][1], groups[-1][1] + n))
    groups += [(depth + rows, tall)]
    ready = sent = 0
    for r in range(tall - 1 + LAG * (TV_ITERS - 1)):
        while ready < len(groups) and groups[ready][0] <= r + 1 + AHEAD:
            fit_rows(*groups[ready])
            ready += 1
        for s in range(TV_ITERS):
            at = r - LAG * s
            if s <= at < tall - 1 - s:
                tv_row(s, at)
                if s == TV_ITERS - 1 and at - depth + 1 == sum(OUT_ROWS[: sent + 1]):
                    out_copy(sent).start()
                    sent += 1
    proj_copy.wait()
    for n in range(len(OUT_ROWS)):
        out_copy(n).wait()


def start_basis():
    bands = np.arange(BANDS, dtype=np.float32)[None, :]
    cols = np.arange(RANK, dtype=np.float32)[:, None]
    angle = np.float32(np.pi) * (bands + np.float32(0.5)) * cols / np.float32(BANDS)
    return np.pad(np.cos(angle).astype(np.float32), ((0, 0), (0, LANES - BANDS)))


def neighbours(block, axis, dim, width):
    count = lax.axis_size(axis)
    size = block.shape[dim]
    head = lax.slice_in_dim(block, 0, width, axis=dim)
    tail = lax.slice_in_dim(block, size - width, size, axis=dim)
    before = lax.ppermute(tail, axis, [(i, i + 1) for i in range(count - 1)])
    after = lax.ppermute(head, axis, [(i + 1, i) for i in range(count - 1)])
    return before, after


def exchange(pieces, axes):
    return lax.all_to_all(pieces, axes, split_axis=0, concat_axis=0)


def body(cube):
    n_rows = lax.axis_size("narrow")
    n_cols = lax.axis_size("wide")
    count = n_rows * n_cols
    rows, cols, bands = cube.shape
    depth = TV_ITERS
    axes = ("narrow", "wide")

    tall_packed = -(-bands // count) * count
    left, right = neighbours(cube, "wide", 1, depth)
    pieces = 2 if rows % 2 == 0 else 1
    packed = pl.pallas_call(
        gram_kernel,
        in_specs=[pl.BlockSpec(memory_space=pl.ANY)],
        out_shape=jax.ShapeDtypeStruct((tall_packed, HALF), f32),
        scratch_shapes=[
            pltpu.VMEM(cube.shape, cube.dtype),
            pltpu.VMEM((LANES, LANES), f32),
            pltpu.SemaphoreType.DMA((pieces,)),
        ],
        compiler_params=pltpu.CompilerParams(vmem_limit_bytes=62 * 2**20),
    )(cube)
    vmem = pl.BlockSpec(memory_space=pltpu.VMEM)
    pieces_shape = (count, 1, tall_packed // count * HALF)
    part = exchange(packed.reshape(pieces_shape), axes).reshape(tall_packed, HALF)
    share = pl.pallas_call(
        functools.partial(sum_kernel, count),
        in_specs=[vmem],
        out_specs=vmem,
        out_shape=jax.ShapeDtypeStruct((tall_packed, HALF), f32),
        compiler_params=pltpu.CompilerParams(vmem_limit_bytes=16 * 2**20),
    )(part)
    gathered = exchange(share.reshape(pieces_shape), axes).reshape(tall_packed, HALF)

    tall, span = rows + 2 * depth, cols + SIDE
    up, down, side = pl.pallas_call(
        functools.partial(halo_kernel, depth),
        in_specs=[vmem] * 4,
        out_specs=[vmem] * 3,
        out_shape=[
            jax.ShapeDtypeStruct((depth, span, bands), bf16),
            jax.ShapeDtypeStruct((depth, span, bands), bf16),
            jax.ShapeDtypeStruct((rows, SIDE, bands), bf16),
        ],
        scratch_shapes=[pltpu.VMEM((rows, SIDE, bands), f32)],
        cost_estimate=pl.CostEstimate(flops=2**32, bytes_accessed=2**18, transcendentals=0),
        compiler_params=pltpu.CompilerParams(vmem_limit_bytes=16 * 2**20),
    )(left, right, cube[:depth], cube[rows - depth :])
    above = lax.ppermute(down, "narrow", [(i, i + 1) for i in range(n_rows - 1)])
    below = lax.ppermute(up, "narrow", [(i + 1, i) for i in range(n_rows - 1)])

    row, col = lax.axis_index("narrow"), lax.axis_index("wide")
    edges = jnp.stack([row == 0, row == n_rows - 1, col == 0, col == n_cols - 1]).astype(jnp.int32)
    inv_count = 1.0 / (count * rows * cols)
    basis = pl.pallas_call(
        functools.partial(subspace_kernel, inv_count),
        in_specs=[vmem] * 2,
        out_specs=vmem,
        out_shape=jax.ShapeDtypeStruct((RANK, LANES), f32),
        cost_estimate=pl.CostEstimate(flops=2**32, bytes_accessed=2**18, transcendentals=0),
        compiler_params=pltpu.CompilerParams(vmem_limit_bytes=16 * 2**20),
    )(gathered, jnp.asarray(start_basis()))
    restored, projector = pl.pallas_call(
        functools.partial(main_kernel, depth),
        in_specs=[pl.BlockSpec(memory_space=pltpu.SMEM)] + [vmem] * 5,
        out_specs=[pl.BlockSpec(memory_space=pl.ANY)] * 2,
        out_shape=[
            jax.ShapeDtypeStruct((rows, cols, bands), bf16),
            jax.ShapeDtypeStruct((bands, bands), f32),
        ],
        scratch_shapes=[pltpu.VMEM((tall, span, LANES), f32)] * 3
        + [
            pltpu.VMEM((rows, cols, bands), bf16),
            pltpu.VMEM((bands, bands), f32),
            pltpu.SemaphoreType.DMA((len(OUT_ROWS),)),
            pltpu.SemaphoreType.DMA,
        ],
        compiler_params=pltpu.CompilerParams(vmem_limit_bytes=48 * 2**20),
    )(edges, basis, cube, above, below, side)
    return restored, projector


def solution(mesh):
    return jax.shard_map(
        body,
        mesh=mesh,
        in_specs=(P("narrow", "wide", None),),
        out_specs=(P("narrow", "wide", None), P()),
        check_vma=False,
    )
```

```python
import functools

import jax
import jax.numpy as jnp
import numpy as np
from jax import lax
from jax.experimental import pallas as pl
from jax.experimental.pallas import tpu as pltpu
from jax.sharding import PartitionSpec as P

BANDS = 224
RANK = 16
POWER_ITERS = 4
TV_ITERS = 3
LANES = 256
HALF = 128
TAIL = BANDS - HALF
SIDE = 8
BLOCK = 8
FIT_ROWS = (2, 6, 8, 8, 8)
AHEAD = 4
LAG = 3
OUT_ROWS = (8, 8, 8, 4, 2, 2)

f32 = jnp.float32
bf16 = jnp.bfloat16


def iotas(shape):
    return lax.broadcasted_iota(jnp.int32, shape, 0), lax.broadcasted_iota(jnp.int32, shape, 1)


def gram_kernel(cube_ref, packed_ref, block, full, sems):
    rows, cols, bands = cube_ref.shape
    pieces = sems.shape[0]
    high = rows // pieces

    def copy(n):
        part = pl.ds(n * high, high)
        return pltpu.make_async_copy(cube_ref.at[part], block.at[part], sems.at[n])

    for n in range(pieces):
        copy(n).start()
    full[HALF:, HALF:] = jnp.zeros((LANES - HALF, LANES - HALF), f32)
    total = None
    for n in range(pieces):
        copy(n).wait()
        flat = block[n * high : (n + 1) * high].reshape(high * cols, bands)
        term = lax.dot_general(flat, flat, (((0,), (0,)), ((), ())), preferred_element_type=f32)
        total = term if total is None else total + term
    full[0:bands, 0:bands] = total
    i, j = iotas((HALF, HALF))
    first = full[0:HALF, 0:HALF]
    second = pltpu.roll(full[HALF:LANES, HALF:LANES], 1, 1)
    packed_ref[0:HALF, :] = jnp.where(j <= i, first, second)
    packed_ref[HALF:bands, :] = full[HALF:bands, 0:HALF]
    if packed_ref.shape[0] > bands:
        packed_ref[bands:, :] = jnp.zeros((packed_ref.shape[0] - bands, HALF), f32)


def sum_kernel(count, pieces_ref, spread_ref):
    high = pieces_ref.shape[0] // count
    parts = [pieces_ref[n * high : (n + 1) * high, :] for n in range(count)]
    total = functools.reduce(jnp.add, parts)
    for n in range(count):
        spread_ref[n * high : (n + 1) * high, :] = total


def split3(x):
    high = x.astype(bf16)
    rest = x - high.astype(f32)
    mid = rest.astype(bf16)
    low = (rest - mid.astype(f32)).astype(bf16)
    return high, mid, low


def product(left, right, dims):
    def dot(a, b):
        return lax.dot_general(a, b, (dims, ((), ())), preferred_element_type=f32)

    n = left[0].shape[0]
    top = dot(jnp.concatenate(left, axis=0), right[0])
    middle = dot(jnp.concatenate(left[:2], axis=0), right[1])
    last = dot(left[0], right[2])
    small = top[2 * n : 3 * n] + middle[n : 2 * n] + last
    return top[:n] + ((top[n : 2 * n] + middle[:n]) + small)


def unpack(packed, scale):
    i, j = iotas((HALF, HALF))
    merged = packed[0:HALF, :] * scale
    below = packed[HALF:BANDS, :] * scale
    below = jnp.concatenate([below, jnp.zeros((LANES - BANDS, HALF), f32)], axis=0)
    first = jnp.where(j <= i, merged, 0.0) + jnp.where(j < i, merged, 0.0).T
    moved = pltpu.roll(merged, HALF - 1, 1)
    inside = (i < TAIL) & (j < TAIL)
    second = jnp.where(inside & (j >= i), moved, 0.0) + jnp.where(inside & (j > i), moved, 0.0).T
    return jnp.concatenate(
        [
            jnp.concatenate([first, below.T], axis=1),
            jnp.concatenate([below, second], axis=1),
        ],
        axis=0,
    )


def full_tile(x):
    return jnp.broadcast_to(x, (BLOCK, HALF))


def orthonormal(grown, inner):
    inner = jnp.concatenate([inner, jnp.zeros((RANK, HALF - RANK), f32)], axis=1)
    parts = [inner, grown[:, :HALF], grown[:, HALF:]]
    row = lax.broadcasted_iota(jnp.int32, (BLOCK, HALF), 0)
    scale0 = None
    tiles = []
    for k in range(0, RANK, BLOCK):
        above = [part[0:BLOCK] for part in parts]
        below = [part[BLOCK:] for part in parts] if parts[0].shape[0] > BLOCK else None
        columns = [full_tile(above[0][:, k + c : k + c + 1]) for c in range(BLOCK)]
        small = [[full_tile(columns[c][r : r + 1, :]) for c in range(r + 1)] for r in range(BLOCK)]
        tops = [[full_tile(part[r : r + 1, :]) for part in above] for r in range(BLOCK)]
        low = factors = None
        if below is not None:
            low = [full_tile(below[0][:, k + c : k + c + 1]) for c in range(BLOCK)]
            factors = []
        pivots = []
        for j in range(0, BLOCK, 2):
            a, b, c = small[j][j], small[j + 1][j], small[j + 1][j + 1]
            inverse = 1.0 / a
            if scale0 is None:
                scale0 = inverse
            a0, b0, c0 = a * scale0, b * scale0, c * scale0
            inverse2 = (a0 * scale0) * (1.0 / (a0 * c0 - b0 * b0))
            ratio = b * inverse
            pivots += [a, c - ratio * b]
            tops[j + 1] = [x - ratio * y for x, y in zip(tops[j + 1], tops[j])]
            first = [small[i][j] for i in range(j + 2, BLOCK)]
            ratio1 = [x * inverse for x in first]
            second = [small[i][j + 1] - x * b for i, x in zip(range(j + 2, BLOCK), ratio1)]
            ratio2 = [x * inverse2 for x in second]
            for m, i in enumerate(range(j + 2, BLOCK)):
                for n in range(m + 1):
                    small[i][j + 2 + n] = (small[i][j + 2 + n] - ratio1[m] * first[n]) - (
                        ratio2[m] * second[n]
                    )
                tops[i] = [
                    (x - ratio1[m] * y) - ratio2[m] * z
                    for x, y, z in zip(tops[i], tops[j], tops[j + 1])
                ]
            if low is not None:
                factor1 = low[j] * inverse
                factor2 = (low[j + 1] - factor1 * b) * inverse2
                factors += [factor1, factor2]
                for n in range(BLOCK - 2 - j):
                    low[j + 2 + n] = (low[j + 2 + n] - factor1 * first[n]) - factor2 * second[n]
        halves = []
        for n in (1, 2):
            tile = tops[0][n] * lax.rsqrt(pivots[0])
            for r in range(1, BLOCK):
                tile = jnp.where(row == r, tops[r][n] * lax.rsqrt(pivots[r]), tile)
            halves.append(tile)
        tiles.append(jnp.concatenate(halves, axis=1))
        if below is not None:
            parts = []
            for n, part in enumerate(below):
                for factor, top in zip(factors, tops):
                    part = part - factor * top[n]
                parts.append(part)
    return jnp.concatenate(tiles, axis=0)


def subspace(gram, start):
    parts = split3(gram)
    grown = product(split3(start), parts, ((1,), (0,)))
    for step in range(POWER_ITERS):
        pieces = split3(grown)
        inner = product(pieces, pieces, ((1,), (1,)))
        later = grown if step == POWER_ITERS - 1 else product(pieces, parts, ((1,), (0,)))
        grown = orthonormal(later, inner)
    return grown


def halo_kernel(depth, left_ref, right_ref, top_ref, bottom_ref, up_ref, down_ref, side_ref, wide):
    rows, cols = side_ref.shape[0], top_ref.shape[1]
    wide[...] = jnp.zeros_like(wide)
    wide[:, 0:depth] = right_ref[...].astype(f32)
    wide[:, SIDE - depth :] = left_ref[...].astype(f32)
    side = wide[...].astype(bf16)
    side_ref[...] = side
    up_ref[:, 0:cols] = top_ref[...]
    up_ref[:, cols:] = side[:depth]
    down_ref[:, 0:cols] = bottom_ref[...]
    down_ref[:, cols:] = side[rows - depth :]


def subspace_kernel(inv_count, packed_ref, start_ref, basis_ref):
    basis_ref[...] = subspace(unpack(packed_ref[...], inv_count), start_ref[...])


def main_kernel(
    depth, edge_ref, basis_ref, mid_ref, above_ref, below_ref, side_ref,
    out_ref, proj_ref, fit, field_a, field_b, out_stage, proj_stage, out_sems, proj_sem
):
    rows, cols, bands = mid_ref.shape
    span = cols + SIDE
    proj_copy = pltpu.make_async_copy(proj_stage, proj_ref, proj_sem)

    def out_copy(n):
        part = pl.ds(sum(OUT_ROWS[:n]), OUT_ROWS[n])
        return pltpu.make_async_copy(out_stage.at[part], out_ref.at[part], out_sems.at[n])

    high, mid, low = split3(basis_ref[...])
    right = jnp.concatenate([high, high, high, mid, mid, low], axis=0)
    left = jnp.concatenate([high, mid, low, high, mid, high], axis=0)
    tn = (((0,), (0,)), ((), ()))
    proj_stage[...] = lax.dot_general(left, right, tn, preferred_element_type=f32)[:bands, :bands]
    proj_copy.start()
    mixed = lax.dot_general(
        jnp.concatenate([high, high, high], axis=0),
        jnp.concatenate([high, mid, low], axis=0),
        tn,
        preferred_element_type=f32,
    )[:bands]
    mixed = mixed * 4.0
    mixed_high = mixed.astype(bf16)
    mixed_low = (mixed - mixed_high.astype(f32)).astype(bf16)

    def fitted(flat):
        res = jnp.dot(flat, mixed_high, preferred_element_type=f32)
        return res + jnp.dot(flat, mixed_low, preferred_element_type=f32)

    def fit_rows(start, stop):
        n = stop - start
        if depth <= start < depth + rows:
            part = slice(start - depth, stop - depth)
            center = mid_ref[part].reshape(n * cols, bands)
            side = side_ref[part].astype(f32).reshape(n * SIDE, bands).astype(bf16)
            res = fitted(jnp.concatenate([center, side], axis=0))
            fit[start:stop, 0:cols, :] = res[: n * cols].reshape(n, cols, LANES)
            fit[start:stop, cols:span, :] = res[n * cols :].reshape(n, SIDE, LANES)
        else:
            block = above_ref[...] if start < depth else below_ref[...]
            flat = block.astype(f32).reshape(n * span, bands).astype(bf16)
            fit[start:stop] = fitted(flat).reshape(n, span, LANES)

    at_top, at_bottom, at_left, at_right = (edge_ref[n] for n in range(4))
    edge = cols - SIDE
    place = lax.broadcasted_iota(jnp.int32, (2 * SIDE, HALF), 0)
    closed = ((place == SIDE - 1) & (at_right > 0)) | ((place == 2 * SIDE - 1) & (at_left > 0))
    keep = jnp.where(closed, 0.0, 1.0).astype(f32)
    open_rows = {
        depth - 1: jnp.where(at_top > 0, 0.0, 1.0),
        depth + rows - 1: jnp.where(at_bottom > 0, 0.0, 1.0),
    }
    lanes = [slice(0, HALF), slice(HALF, LANES)]
    fields = [fit, field_a, field_b]
    befores = [[None, None] for _ in fields]

    def tv_row(s, r, n):
        source, lane = fields[s], lanes[n]
        now = source[r, :, lane]
        down = source[r + 1, :, lane] - now
        if r in open_rows:
            down = down * open_rows[r]
        across = pltpu.roll(now, span - 1, 0) - now
        across = jnp.concatenate([across[:edge], across[edge:] * keep], axis=0)
        inverse = lax.rsqrt(down * down + across * across + 4.0)
        down = down * inverse
        before, befores[s][n] = befores[s][n], down
        if before is None:
            return
        across = across * inverse
        base = now if s == 0 else 0.5 * (now + fit[r, :, lane])
        value = base + ((down - before) + (across - pltpu.roll(across, 1, 0)))
        if s < TV_ITERS - 1:
            fields[s + 1][r, :, lane] = value
        else:
            value = (value[:cols] * 0.25).astype(bf16)
            width = min(lane.stop, bands) - lane.start
            out_stage[r - depth, :, lane.start : lane.start + width] = value[:, :width]

    tall = rows + 2 * depth
    groups = [(0, depth)]
    for n in FIT_ROWS:
        groups.append((groups[-1][1], groups[-1][1] + n))
    groups += [(depth + rows, tall)]
    ready = sent = 0
    for n in range(len(lanes)):
        for r in range(tall - 1 + LAG * (TV_ITERS - 1)):
            while ready < len(groups) and groups[ready][0] <= r + 1 + AHEAD:
                fit_rows(*groups[ready])
                ready += 1
            for s in range(TV_ITERS):
                at = r - LAG * s
                if s <= at < tall - 1 - s:
                    tv_row(s, at, n)
                    last = n == len(lanes) - 1 and s == TV_ITERS - 1
                    if last and at - depth + 1 == sum(OUT_ROWS[: sent + 1]):
                        out_copy(sent).start()
                        sent += 1
    proj_copy.wait()
    for n in range(len(OUT_ROWS)):
        out_copy(n).wait()


def start_basis():
    bands = np.arange(BANDS, dtype=np.float32)[None, :]
    cols = np.arange(RANK, dtype=np.float32)[:, None]
    angle = np.float32(np.pi) * (bands + np.float32(0.5)) * cols / np.float32(BANDS)
    return np.pad(np.cos(angle).astype(np.float32), ((0, 0), (0, LANES - BANDS)))


def neighbours(block, axis, dim, width):
    count = lax.axis_size(axis)
    size = block.shape[dim]
    head = lax.slice_in_dim(block, 0, width, axis=dim)
    tail = lax.slice_in_dim(block, size - width, size, axis=dim)
    before = lax.ppermute(tail, axis, [(i, i + 1) for i in range(count - 1)])
    after = lax.ppermute(head, axis, [(i + 1, i) for i in range(count - 1)])
    return before, after


def exchange(pieces, axes):
    return lax.all_to_all(pieces, axes, split_axis=0, concat_axis=0)


def body(cube):
    n_rows = lax.axis_size("narrow")
    n_cols = lax.axis_size("wide")
    count = n_rows * n_cols
    rows, cols, bands = cube.shape
    depth = TV_ITERS
    axes = ("narrow", "wide")

    tall_packed = -(-bands // count) * count
    left, right = neighbours(cube, "wide", 1, depth)
    pieces = 2 if rows % 2 == 0 else 1
    packed = pl.pallas_call(
        gram_kernel,
        in_specs=[pl.BlockSpec(memory_space=pl.ANY)],
        out_shape=jax.ShapeDtypeStruct((tall_packed, HALF), f32),
        scratch_shapes=[
            pltpu.VMEM(cube.shape, cube.dtype),
            pltpu.VMEM((LANES, LANES), f32),
            pltpu.SemaphoreType.DMA((pieces,)),
        ],
        compiler_params=pltpu.CompilerParams(vmem_limit_bytes=62 * 2**20),
    )(cube)
    vmem = pl.BlockSpec(memory_space=pltpu.VMEM)
    pieces_shape = (count, 1, tall_packed // count * HALF)
    part = exchange(packed.reshape(pieces_shape), axes).reshape(tall_packed, HALF)
    share = pl.pallas_call(
        functools.partial(sum_kernel, count),
        in_specs=[vmem],
        out_specs=vmem,
        out_shape=jax.ShapeDtypeStruct((tall_packed, HALF), f32),
        compiler_params=pltpu.CompilerParams(vmem_limit_bytes=16 * 2**20),
    )(part)
    gathered = exchange(share.reshape(pieces_shape), axes).reshape(tall_packed, HALF)

    tall, span = rows + 2 * depth, cols + SIDE
    up, down, side = pl.pallas_call(
        functools.partial(halo_kernel, depth),
        in_specs=[vmem] * 4,
        out_specs=[vmem] * 3,
        out_shape=[
            jax.ShapeDtypeStruct((depth, span, bands), bf16),
            jax.ShapeDtypeStruct((depth, span, bands), bf16),
            jax.ShapeDtypeStruct((rows, SIDE, bands), bf16),
        ],
        scratch_shapes=[pltpu.VMEM((rows, SIDE, bands), f32)],
        cost_estimate=pl.CostEstimate(flops=2**32, bytes_accessed=2**18, transcendentals=0),
        compiler_params=pltpu.CompilerParams(vmem_limit_bytes=16 * 2**20),
    )(left, right, cube[:depth], cube[rows - depth :])
    above = lax.ppermute(down, "narrow", [(i, i + 1) for i in range(n_rows - 1)])
    below = lax.ppermute(up, "narrow", [(i + 1, i) for i in range(n_rows - 1)])

    row, col = lax.axis_index("narrow"), lax.axis_index("wide")
    edges = jnp.stack([row == 0, row == n_rows - 1, col == 0, col == n_cols - 1]).astype(jnp.int32)
    inv_count = 1.0 / (count * rows * cols)
    basis = pl.pallas_call(
        functools.partial(subspace_kernel, inv_count),
        in_specs=[vmem] * 2,
        out_specs=vmem,
        out_shape=jax.ShapeDtypeStruct((RANK, LANES), f32),
        cost_estimate=pl.CostEstimate(flops=2**32, bytes_accessed=2**18, transcendentals=0),
        compiler_params=pltpu.CompilerParams(vmem_limit_bytes=16 * 2**20),
    )(gathered, jnp.asarray(start_basis()))
    restored, projector = pl.pallas_call(
        functools.partial(main_kernel, depth),
        in_specs=[pl.BlockSpec(memory_space=pltpu.SMEM)] + [vmem] * 5,
        out_specs=[pl.BlockSpec(memory_space=pl.ANY)] * 2,
        out_shape=[
            jax.ShapeDtypeStruct((rows, cols, bands), bf16),
            jax.ShapeDtypeStruct((bands, bands), f32),
        ],
        scratch_shapes=[pltpu.VMEM((tall, span, LANES), f32)] * 3
        + [
            pltpu.VMEM((rows, cols, bands), bf16),
            pltpu.VMEM((bands, bands), f32),
            pltpu.SemaphoreType.DMA((len(OUT_ROWS),)),
            pltpu.SemaphoreType.DMA,
        ],
        compiler_params=pltpu.CompilerParams(vmem_limit_bytes=48 * 2**20),
    )(edges, basis, cube, above, below, side)
    return restored, projector


def solution(mesh):
    return jax.shard_map(
        body,
        mesh=mesh,
        in_specs=(P("narrow", "wide", None),),
        out_specs=(P("narrow", "wide", None), P()),
        check_vma=False,
    )
```

```python
import functools

import jax
import jax.numpy as jnp
import numpy as np
from jax import lax
from jax.experimental import pallas as pl
from jax.experimental.pallas import tpu as pltpu
from jax.sharding import PartitionSpec as P

BANDS = 224
RANK = 16
POWER_ITERS = 4
TV_ITERS = 3
LANES = 256
HALF = 128
TAIL = BANDS - HALF
SIDE = 8
BLOCK = 8
FIT_ROWS = (2, 6, 8, 8, 8)
AHEAD = 4
TV_ROWS = (12, 16)

f32 = jnp.float32
bf16 = jnp.bfloat16


def iotas(shape):
    return lax.broadcasted_iota(jnp.int32, shape, 0), lax.broadcasted_iota(jnp.int32, shape, 1)


def gram_kernel(cube_ref, packed_ref, block, full, sems):
    rows, cols, bands = cube_ref.shape
    pieces = sems.shape[0]
    high = rows // pieces

    def copy(n):
        part = pl.ds(n * high, high)
        return pltpu.make_async_copy(cube_ref.at[part], block.at[part], sems.at[n])

    for n in range(pieces):
        copy(n).start()
    full[HALF:, HALF:] = jnp.zeros((LANES - HALF, LANES - HALF), f32)
    total = None
    for n in range(pieces):
        copy(n).wait()
        flat = block[n * high : (n + 1) * high].reshape(high * cols, bands)
        term = lax.dot_general(flat, flat, (((0,), (0,)), ((), ())), preferred_element_type=f32)
        total = term if total is None else total + term
    full[0:bands, 0:bands] = total
    i, j = iotas((HALF, HALF))
    first = full[0:HALF, 0:HALF]
    second = pltpu.roll(full[HALF:LANES, HALF:LANES], 1, 1)
    packed_ref[0:HALF, :] = jnp.where(j <= i, first, second)
    packed_ref[HALF:bands, :] = full[HALF:bands, 0:HALF]
    if packed_ref.shape[0] > bands:
        packed_ref[bands:, :] = jnp.zeros((packed_ref.shape[0] - bands, HALF), f32)


def sum_kernel(count, pieces_ref, spread_ref):
    high = pieces_ref.shape[0] // count
    parts = [pieces_ref[n * high : (n + 1) * high, :] for n in range(count)]
    total = functools.reduce(jnp.add, parts)
    for n in range(count):
        spread_ref[n * high : (n + 1) * high, :] = total


def split3(x):
    high = x.astype(bf16)
    rest = x - high.astype(f32)
    mid = rest.astype(bf16)
    low = (rest - mid.astype(f32)).astype(bf16)
    return high, mid, low


def product(left, right, dims):
    def dot(a, b):
        return lax.dot_general(a, b, (dims, ((), ())), preferred_element_type=f32)

    n = left[0].shape[0]
    top = dot(jnp.concatenate(left, axis=0), right[0])
    middle = dot(jnp.concatenate(left[:2], axis=0), right[1])
    last = dot(left[0], right[2])
    small = top[2 * n : 3 * n] + middle[n : 2 * n] + last
    return top[:n] + ((top[n : 2 * n] + middle[:n]) + small)


def unpack(packed, scale):
    i, j = iotas((HALF, HALF))
    merged = packed[0:HALF, :] * scale
    below = packed[HALF:BANDS, :] * scale
    below = jnp.concatenate([below, jnp.zeros((LANES - BANDS, HALF), f32)], axis=0)
    first = jnp.where(j <= i, merged, 0.0) + jnp.where(j < i, merged, 0.0).T
    moved = pltpu.roll(merged, HALF - 1, 1)
    inside = (i < TAIL) & (j < TAIL)
    second = jnp.where(inside & (j >= i), moved, 0.0) + jnp.where(inside & (j > i), moved, 0.0).T
    return jnp.concatenate(
        [
            jnp.concatenate([first, below.T], axis=1),
            jnp.concatenate([below, second], axis=1),
        ],
        axis=0,
    )


def orthonormal(grown, inner):
    row = lax.broadcasted_iota(jnp.int32, (RANK, HALF), 0)
    work = [
        jnp.concatenate([inner, jnp.zeros((RANK, HALF - RANK), f32)], axis=1),
        grown[:, :HALF],
        grown[:, HALF:],
    ]
    diagonal = jnp.ones((RANK, HALF), f32)
    for k in range(0, RANK, BLOCK):
        columns = [
            jnp.broadcast_to(work[0][:, k + c : k + c + 1], (RANK, HALF)) for c in range(BLOCK)
        ]
        tops = [[part[k + r : k + r + 1, :] for part in work] for r in range(BLOCK)]
        small = [
            [columns[c][k + r : k + r + 1, :] for c in range(r + 1)] for r in range(BLOCK)
        ]
        factors = []
        for j in range(BLOCK):
            pivot = small[j][j]
            inverse = 1.0 / pivot
            diagonal = jnp.where(row == k + j, pivot, diagonal)
            factor = jnp.where(row > k + j, columns[j] * inverse, 0.0)
            factors.append(factor)
            below = [small[i][j] for i in range(BLOCK) if i > j]
            for i in range(j + 1, BLOCK):
                ratio = small[i][j] * inverse
                for c in range(j + 1, i + 1):
                    small[i][c] = small[i][c] - ratio * below[c - j - 1]
                tops[i] = [x - ratio * y for x, y in zip(tops[i], tops[j])]
                columns[i] = columns[i] - factor * below[i - j - 1]
        for n in range(len(work)):
            if n > 0 or k + BLOCK < RANK:
                for j in range(BLOCK):
                    work[n] = work[n] - factors[j] * tops[j][n]
    scale = lax.rsqrt(diagonal)
    return jnp.concatenate([work[1] * scale, work[2] * scale], axis=1)


def subspace(gram, start, held):
    for n, part in enumerate(split3(gram)):
        held[n] = part

    def times_gram(pieces):
        return product(pieces, [held[n] for n in range(3)], ((1,), (0,)))

    def iterate(_, grown):
        pieces = split3(grown)
        inner = product(pieces, pieces, ((1,), (1,)))
        return orthonormal(times_gram(pieces), inner)

    grown = lax.fori_loop(0, POWER_ITERS - 1, iterate, times_gram(split3(start)))
    pieces = split3(grown)
    return orthonormal(grown, product(pieces, pieces, ((1,), (1,))))


def halo_kernel(depth, left_ref, right_ref, top_ref, bottom_ref, up_ref, down_ref, side_ref, wide):
    rows, cols = side_ref.shape[0], top_ref.shape[1]
    wide[...] = jnp.zeros_like(wide)
    wide[:, 0:depth] = right_ref[...].astype(f32)
    wide[:, SIDE - depth :] = left_ref[...].astype(f32)
    side = wide[...].astype(bf16)
    side_ref[...] = side
    up_ref[:, 0:cols] = top_ref[...]
    up_ref[:, cols:] = side[:depth]
    down_ref[:, 0:cols] = bottom_ref[...]
    down_ref[:, cols:] = side[rows - depth :]


def subspace_kernel(inv_count, packed_ref, start_ref, basis_ref, held):
    basis_ref[...] = subspace(unpack(packed_ref[...], inv_count), start_ref[...], held)


def main_kernel(
    depth, edge_ref, basis_ref, mid_ref, above_ref, below_ref, side_ref,
    out_ref, proj_ref, fit, field_a, field_b, out_stage, proj_stage, out_sems, proj_sem
):
    rows, cols, bands = mid_ref.shape
    span = cols + SIDE
    proj_copy = pltpu.make_async_copy(proj_stage, proj_ref, proj_sem)

    def out_copy(n):
        part = pl.ds(n * TV_ROWS[1], TV_ROWS[1])
        return pltpu.make_async_copy(out_stage.at[part], out_ref.at[part], out_sems.at[n])

    high, mid, low = split3(basis_ref[...])
    right = jnp.concatenate([high, high, high, mid, mid, low], axis=0)
    left = jnp.concatenate([high, mid, low, high, mid, high], axis=0)
    tn = (((0,), (0,)), ((), ()))
    proj_stage[...] = lax.dot_general(left, right, tn, preferred_element_type=f32)[:bands, :bands]
    proj_copy.start()
    mixed = lax.dot_general(
        jnp.concatenate([high, high, high], axis=0),
        jnp.concatenate([high, mid, low], axis=0),
        tn,
        preferred_element_type=f32,
    )[:bands]
    mixed = mixed * 4.0
    mixed_high = mixed.astype(bf16)
    mixed_low = (mixed - mixed_high.astype(f32)).astype(bf16)

    def fitted(flat):
        res = jnp.dot(flat, mixed_high, preferred_element_type=f32)
        return res + jnp.dot(flat, mixed_low, preferred_element_type=f32)

    def fit_rows(start, stop):
        n = stop - start
        if depth <= start < depth + rows:
            part = slice(start - depth, stop - depth)
            center = mid_ref[part].reshape(n * cols, bands)
            side = side_ref[part].astype(f32).reshape(n * SIDE, bands).astype(bf16)
            res = fitted(jnp.concatenate([center, side], axis=0))
            fit[start:stop, 0:cols, :] = res[: n * cols].reshape(n, cols, LANES)
            fit[start:stop, cols:span, :] = res[n * cols :].reshape(n, SIDE, LANES)
        else:
            block = above_ref[...] if start < depth else below_ref[...]
            flat = block.astype(f32).reshape(n * span, bands).astype(bf16)
            fit[start:stop] = fitted(flat).reshape(n, span, LANES)

    at_top, at_bottom, at_left, at_right = (edge_ref[n] for n in range(4))
    edge = cols - SIDE
    place = lax.broadcasted_iota(jnp.int32, (2 * SIDE, HALF), 0)
    closed = ((place == SIDE - 1) & (at_right > 0)) | ((place == 2 * SIDE - 1) & (at_left > 0))
    keep = jnp.where(closed, 0.0, 1.0).astype(f32)
    open_rows = {
        depth - 1: jnp.where(at_top > 0, 0.0, 1.0),
        depth + rows - 1: jnp.where(at_bottom > 0, 0.0, 1.0),
    }
    lanes = [slice(0, HALF), slice(HALF, LANES)]
    fields = [fit, field_a, field_b]

    def slopes(now, later, open_row=None):
        down = later - now
        if open_row is not None:
            down = down * open_row
        across = pltpu.roll(now, span - 1, 0) - now
        across = jnp.concatenate([across[:edge], across[edge:] * keep], axis=0)
        inverse = lax.rsqrt(down * down + across * across + 4.0)
        return down * inverse, across * inverse

    def advance(base, before, down, across):
        return base + ((down - before) + (across - pltpu.roll(across, 1, 0)))

    tall = rows + 2 * depth
    groups = [(0, depth)]
    for n in FIT_ROWS:
        groups.append((groups[-1][1], groups[-1][1] + n))
    groups += [(depth + rows, tall)]
    ready = 0
    befores = [None] * len(lanes)
    for r in range(tall - 1):
        while ready < len(groups) and groups[ready][0] <= r + 1 + AHEAD:
            fit_rows(*groups[ready])
            ready += 1
        for n, lane in enumerate(lanes):
            now = fit[r, :, lane]
            down, across = slopes(now, fit[r + 1, :, lane], open_rows.get(r))
            if r > 0:
                field_a[r, :, lane] = advance(now, befores[n], down, across)
            befores[n] = down

    def step(s, first, trips, unroll):
        source, final = fields[s], s == TV_ITERS - 1

        @pl.when(at_top > 0)
        def _():
            source[depth - 1] = source[depth]

        @pl.when(at_bottom > 0)
        def _():
            source[depth + rows] = source[depth + rows - 1]

        def block_step(n, carry):
            carry = list(carry)
            for inner in range(unroll):
                r = first + n * unroll + inner
                for m, lane in enumerate(lanes):
                    now, before = carry[2 * m], carry[2 * m + 1]
                    later = source[r + 1, :, lane]
                    down, across = slopes(now, later)
                    value = advance(0.5 * (now + fit[r, :, lane]), before, down, across)
                    if final:
                        value = (value[:cols] * 0.25).astype(bf16)
                        width = min(lane.stop, bands) - lane.start
                        out_stage[r - depth, :, lane.start : lane.start + width] = value[:, :width]
                    else:
                        fields[s + 1][r, :, lane] = value
                    carry[2 * m], carry[2 * m + 1] = later, down
            if final:
                out_copy(n).start()
            return tuple(carry)

        carry = []
        for lane in lanes:
            before, now = source[first - 1, :, lane], source[first, :, lane]
            carry += [now, slopes(before, now)[0]]
        lax.fori_loop(0, trips, block_step, tuple(carry))

    step(1, 1, (rows + 4) // TV_ROWS[0], TV_ROWS[0])
    step(2, depth, rows // TV_ROWS[1], TV_ROWS[1])
    proj_copy.wait()
    for n in range(rows // TV_ROWS[1]):
        out_copy(n).wait()


def start_basis():
    bands = np.arange(BANDS, dtype=np.float32)[None, :]
    cols = np.arange(RANK, dtype=np.float32)[:, None]
    angle = np.float32(np.pi) * (bands + np.float32(0.5)) * cols / np.float32(BANDS)
    return np.pad(np.cos(angle).astype(np.float32), ((0, 0), (0, LANES - BANDS)))


def neighbours(block, axis, dim, width):
    count = lax.axis_size(axis)
    size = block.shape[dim]
    head = lax.slice_in_dim(block, 0, width, axis=dim)
    tail = lax.slice_in_dim(block, size - width, size, axis=dim)
    before = lax.ppermute(tail, axis, [(i, i + 1) for i in range(count - 1)])
    after = lax.ppermute(head, axis, [(i + 1, i) for i in range(count - 1)])
    return before, after


def exchange(pieces, axes):
    return lax.all_to_all(pieces, axes, split_axis=0, concat_axis=0)


def body(cube):
    n_rows = lax.axis_size("narrow")
    n_cols = lax.axis_size("wide")
    count = n_rows * n_cols
    rows, cols, bands = cube.shape
    depth = TV_ITERS
    axes = ("narrow", "wide")

    tall_packed = -(-bands // count) * count
    left, right = neighbours(cube, "wide", 1, depth)
    pieces = 2 if rows % 2 == 0 else 1
    packed = pl.pallas_call(
        gram_kernel,
        in_specs=[pl.BlockSpec(memory_space=pl.ANY)],
        out_shape=jax.ShapeDtypeStruct((tall_packed, HALF), f32),
        scratch_shapes=[
            pltpu.VMEM(cube.shape, cube.dtype),
            pltpu.VMEM((LANES, LANES), f32),
            pltpu.SemaphoreType.DMA((pieces,)),
        ],
        compiler_params=pltpu.CompilerParams(vmem_limit_bytes=62 * 2**20),
    )(cube)
    vmem = pl.BlockSpec(memory_space=pltpu.VMEM)
    pieces_shape = (count, 1, tall_packed // count * HALF)
    part = exchange(packed.reshape(pieces_shape), axes).reshape(tall_packed, HALF)
    share = pl.pallas_call(
        functools.partial(sum_kernel, count),
        in_specs=[vmem],
        out_specs=vmem,
        out_shape=jax.ShapeDtypeStruct((tall_packed, HALF), f32),
        compiler_params=pltpu.CompilerParams(vmem_limit_bytes=16 * 2**20),
    )(part)
    gathered = exchange(share.reshape(pieces_shape), axes).reshape(tall_packed, HALF)

    tall, span = rows + 2 * depth, cols + SIDE
    up, down, side = pl.pallas_call(
        functools.partial(halo_kernel, depth),
        in_specs=[vmem] * 4,
        out_specs=[vmem] * 3,
        out_shape=[
            jax.ShapeDtypeStruct((depth, span, bands), bf16),
            jax.ShapeDtypeStruct((depth, span, bands), bf16),
            jax.ShapeDtypeStruct((rows, SIDE, bands), bf16),
        ],
        scratch_shapes=[pltpu.VMEM((rows, SIDE, bands), f32)],
        cost_estimate=pl.CostEstimate(flops=2**32, bytes_accessed=2**18, transcendentals=0),
        compiler_params=pltpu.CompilerParams(vmem_limit_bytes=16 * 2**20),
    )(left, right, cube[:depth], cube[rows - depth :])
    above = lax.ppermute(down, "narrow", [(i, i + 1) for i in range(n_rows - 1)])
    below = lax.ppermute(up, "narrow", [(i + 1, i) for i in range(n_rows - 1)])

    row, col = lax.axis_index("narrow"), lax.axis_index("wide")
    edges = jnp.stack([row == 0, row == n_rows - 1, col == 0, col == n_cols - 1]).astype(jnp.int32)
    inv_count = 1.0 / (count * rows * cols)
    basis = pl.pallas_call(
        functools.partial(subspace_kernel, inv_count),
        in_specs=[vmem] * 2,
        out_specs=vmem,
        out_shape=jax.ShapeDtypeStruct((RANK, LANES), f32),
        scratch_shapes=[pltpu.VMEM((3, LANES, LANES), bf16)],
        cost_estimate=pl.CostEstimate(flops=2**32, bytes_accessed=2**18, transcendentals=0),
        compiler_params=pltpu.CompilerParams(vmem_limit_bytes=16 * 2**20),
    )(gathered, jnp.asarray(start_basis()))
    restored, projector = pl.pallas_call(
        functools.partial(main_kernel, depth),
        in_specs=[pl.BlockSpec(memory_space=pltpu.SMEM)] + [vmem] * 5,
        out_specs=[pl.BlockSpec(memory_space=pl.ANY)] * 2,
        out_shape=[
            jax.ShapeDtypeStruct((rows, cols, bands), bf16),
            jax.ShapeDtypeStruct((bands, bands), f32),
        ],
        scratch_shapes=[pltpu.VMEM((tall, span, LANES), f32)] * 3
        + [
            pltpu.VMEM((rows, cols, bands), bf16),
            pltpu.VMEM((bands, bands), f32),
            pltpu.SemaphoreType.DMA((rows // TV_ROWS[1],)),
            pltpu.SemaphoreType.DMA,
        ],
        compiler_params=pltpu.CompilerParams(vmem_limit_bytes=48 * 2**20),
    )(edges, basis, cube, above, below, side)
    return restored, projector


def solution(mesh):
    return jax.shard_map(
        body,
        mesh=mesh,
        in_specs=(P("narrow", "wide", None),),
        out_specs=(P("narrow", "wide", None), P()),
        check_vma=False,
    )
```

```python
import functools

import jax
import jax.numpy as jnp
import numpy as np
from jax import lax
from jax.experimental import pallas as pl
from jax.experimental.pallas import tpu as pltpu
from jax.sharding import PartitionSpec as P

BANDS = 224
RANK = 16
POWER_ITERS = 4
TV_ITERS = 3
LANES = 256
HALF = 128
TAIL = BANDS - HALF
SIDE = 8
SUB = 8
BLOCK = 8
FIT_ROWS = (2, 6, 8, 8, 8)
AHEAD = 4
TV_ROWS = (12, 16)

f32 = jnp.float32
bf16 = jnp.bfloat16


def iotas(shape):
    return lax.broadcasted_iota(jnp.int32, shape, 0), lax.broadcasted_iota(jnp.int32, shape, 1)


def gram_kernel(cube_ref, packed_ref, block, full, sems):
    rows, cols, bands = cube_ref.shape
    pieces = sems.shape[0]
    high = rows // pieces

    def copy(n):
        part = pl.ds(n * high, high)
        return pltpu.make_async_copy(cube_ref.at[part], block.at[part], sems.at[n])

    for n in range(pieces):
        copy(n).start()
    full[HALF:, HALF:] = jnp.zeros((LANES - HALF, LANES - HALF), f32)
    total = None
    for n in range(pieces):
        copy(n).wait()
        flat = block[n * high : (n + 1) * high].reshape(high * cols, bands)
        term = lax.dot_general(flat, flat, (((0,), (0,)), ((), ())), preferred_element_type=f32)
        total = term if total is None else total + term
    full[0:bands, 0:bands] = total
    i, j = iotas((HALF, HALF))
    first = full[0:HALF, 0:HALF]
    second = pltpu.roll(full[HALF:LANES, HALF:LANES], 1, 1)
    packed_ref[0:HALF, :] = jnp.where(j <= i, first, second)
    packed_ref[HALF:bands, :] = full[HALF:bands, 0:HALF]
    if packed_ref.shape[0] > bands:
        packed_ref[bands:, :] = jnp.zeros((packed_ref.shape[0] - bands, HALF), f32)


def sum_kernel(count, pieces_ref, spread_ref):
    high = pieces_ref.shape[0] // count
    parts = [pieces_ref[n * high : (n + 1) * high, :] for n in range(count)]
    total = functools.reduce(jnp.add, parts)
    for n in range(count):
        spread_ref[n * high : (n + 1) * high, :] = total


def split3(x):
    high = x.astype(bf16)
    rest = x - high.astype(f32)
    mid = rest.astype(bf16)
    low = (rest - mid.astype(f32)).astype(bf16)
    return high, mid, low


def product(left, right, dims):
    def dot(a, b):
        return lax.dot_general(a, b, (dims, ((), ())), preferred_element_type=f32)

    n = left[0].shape[0]
    top = dot(jnp.concatenate(left, axis=0), right[0])
    middle = dot(jnp.concatenate(left[:2], axis=0), right[1])
    small = top[2 * n : 3 * n] + middle[n : 2 * n]
    if len(right) > 2:
        small = small + dot(left[0], right[2])
    return top[:n] + ((top[n : 2 * n] + middle[:n]) + small)


def unpack(packed, scale):
    i, j = iotas((HALF, HALF))
    merged = packed[0:HALF, :] * scale
    below = packed[HALF:BANDS, :] * scale
    below = jnp.concatenate([below, jnp.zeros((LANES - BANDS, HALF), f32)], axis=0)
    first = jnp.where(j <= i, merged, 0.0) + jnp.where(j < i, merged, 0.0).T
    moved = pltpu.roll(merged, HALF - 1, 1)
    inside = (i < TAIL) & (j < TAIL)
    second = jnp.where(inside & (j >= i), moved, 0.0) + jnp.where(inside & (j > i), moved, 0.0).T
    return jnp.concatenate(
        [
            jnp.concatenate([first, below.T], axis=1),
            jnp.concatenate([below, second], axis=1),
        ],
        axis=0,
    )


def orthonormal(grown, inner):
    row = lax.broadcasted_iota(jnp.int32, (RANK, HALF), 0)
    work = [
        jnp.concatenate([inner, jnp.zeros((RANK, HALF - RANK), f32)], axis=1),
        grown[:, :HALF],
        grown[:, HALF:],
    ]
    diagonal = jnp.ones((RANK, HALF), f32)
    for k in range(0, RANK, BLOCK):
        columns = [
            jnp.broadcast_to(work[0][:, k + c : k + c + 1], (RANK, HALF)) for c in range(BLOCK)
        ]
        tops = [[part[k + r : k + r + 1, :] for part in work] for r in range(BLOCK)]
        small = [
            [columns[c][k + r : k + r + 1, :] for c in range(r + 1)] for r in range(BLOCK)
        ]
        factors = []
        for j in range(BLOCK):
            pivot = small[j][j]
            inverse = 1.0 / pivot
            diagonal = jnp.where(row == k + j, pivot, diagonal)
            factor = jnp.where(row > k + j, columns[j] * inverse, 0.0)
            factors.append(factor)
            below = [small[i][j] for i in range(BLOCK) if i > j]
            for i in range(j + 1, BLOCK):
                ratio = small[i][j] * inverse
                for c in range(j + 1, i + 1):
                    small[i][c] = small[i][c] - ratio * below[c - j - 1]
                tops[i] = [x - ratio * y for x, y in zip(tops[i], tops[j])]
                columns[i] = columns[i] - factor * below[i - j - 1]
        for n in range(len(work)):
            if n > 0 or k + BLOCK < RANK:
                for j in range(BLOCK):
                    work[n] = work[n] - factors[j] * tops[j][n]
    scale = lax.rsqrt(diagonal)
    return jnp.concatenate([work[1] * scale, work[2] * scale], axis=1)


def subspace(gram, start, held):
    for n, part in enumerate(split3(gram)[:2]):
        held[n] = part

    def times_gram(pieces):
        return product(pieces, [held[0], held[1]], ((1,), (0,)))

    def iterate(_, grown):
        pieces = split3(grown)
        inner = product(pieces, pieces, ((1,), (1,)))
        return orthonormal(times_gram(pieces), inner)

    grown = lax.fori_loop(0, POWER_ITERS - 1, iterate, times_gram(split3(start)))
    pieces = split3(grown)
    return orthonormal(grown, product(pieces, pieces, ((1,), (1,))))


def halo_kernel(depth, left_ref, right_ref, top_ref, bottom_ref, up_ref, down_ref, side_ref, wide):
    rows, cols = side_ref.shape[0], top_ref.shape[1]
    wide[...] = jnp.zeros_like(wide)
    wide[:, 0:depth] = right_ref[...].astype(f32)
    wide[:, SIDE - depth :] = left_ref[...].astype(f32)
    side = wide[...].astype(bf16)
    side_ref[...] = side
    up_ref[:, 0:cols] = top_ref[...]
    up_ref[:, cols:] = side[:depth]
    down_ref[:, 0:cols] = bottom_ref[...]
    down_ref[:, cols:] = side[rows - depth :]


def subspace_kernel(inv_count, packed_ref, start_ref, basis_ref, held):
    basis_ref[...] = subspace(unpack(packed_ref[...], inv_count), start_ref[...], held)


def main_kernel(
    depth, edge_ref, basis_ref, mid_ref, above_ref, below_ref, side_ref,
    out_ref, proj_ref, fit, field_a, field_b, out_stage, proj_stage, out_sems, proj_sem
):
    rows, cols, bands = mid_ref.shape
    span = cols + SIDE
    proj_copy = pltpu.make_async_copy(proj_stage, proj_ref, proj_sem)

    def out_copy(n):
        part = pl.ds(n * TV_ROWS[1], TV_ROWS[1])
        return pltpu.make_async_copy(out_stage.at[part], out_ref.at[part], out_sems.at[n])

    high, mid, low = split3(basis_ref[...])
    right = jnp.concatenate([high, high, high, mid, mid, low], axis=0)
    left = jnp.concatenate([high, mid, low, high, mid, high], axis=0)
    tn = (((0,), (0,)), ((), ()))
    proj_stage[...] = lax.dot_general(left, right, tn, preferred_element_type=f32)[:bands, :bands]
    proj_copy.start()
    mixed = lax.dot_general(
        jnp.concatenate([high, high, high], axis=0),
        jnp.concatenate([high, mid, low], axis=0),
        tn,
        preferred_element_type=f32,
    )[:bands]
    mixed = mixed * 4.0
    mixed_high = mixed.astype(bf16)
    mixed_low = (mixed - mixed_high.astype(f32)).astype(bf16)

    def fitted(flat):
        res = jnp.dot(flat, mixed_high, preferred_element_type=f32)
        return res + jnp.dot(flat, mixed_low, preferred_element_type=f32)

    def fit_rows(start, stop):
        n = stop - start
        if depth <= start < depth + rows:
            part = slice(start - depth, stop - depth)
            center = mid_ref[part].reshape(n * cols, bands)
            side = side_ref[part].astype(f32).reshape(n * SIDE, bands).astype(bf16)
            res = fitted(jnp.concatenate([center, side], axis=0))
            for h, lane in enumerate(lanes):
                fit[h, start:stop, 0:cols] = res[: n * cols, lane].reshape(n, cols, HALF)
                fit[h, start:stop, cols:span] = res[n * cols :, lane].reshape(n, SIDE, HALF)
        else:
            block = above_ref[...] if start < depth else below_ref[...]
            flat = block.astype(f32).reshape(n * span, bands).astype(bf16)
            res = fitted(flat)
            for h, lane in enumerate(lanes):
                fit[h, start:stop] = res[:, lane].reshape(n, span, HALF)

    at_top, at_bottom, at_left, at_right = (edge_ref[n] for n in range(4))
    per = span // SUB
    place = lax.broadcasted_iota(jnp.int32, (SUB, HALF), 0)
    keeps = {}
    for column, shut in ((cols - 1, at_right), (span - 1, at_left)):
        keep = jnp.where((place == column // per) & (shut > 0), 0.0, 1.0).astype(f32)
        keeps[column % per] = keeps[column % per] * keep if column % per in keeps else keep
    open_rows = {
        depth - 1: jnp.where(at_top > 0, 0.0, 1.0),
        depth + rows - 1: jnp.where(at_bottom > 0, 0.0, 1.0),
    }
    lanes = [slice(0, HALF), slice(HALF, LANES)]
    fields = [fit, field_a, field_b]

    def natural(ref, h, r):
        return [ref[h, r, pl.ds(w, SUB, stride=per), :] for w in range(per)]

    def spread(ref, h, r):
        return [ref[h, r, w * SUB : (w + 1) * SUB, :] for w in range(per)]

    def slopes(now, later, open_row=None):
        follow = now[1:] + [pltpu.roll(now[0], SUB - 1, 0)]
        downs, acrosses = [], []
        for w in range(per):
            down = later[w] - now[w]
            if open_row is not None:
                down = down * open_row
            across = follow[w] - now[w]
            if w in keeps:
                across = across * keeps[w]
            inverse = lax.rsqrt(down * down + (across * across + 4.0))
            downs.append(down * inverse)
            acrosses.append(across * inverse)
        return downs, acrosses

    def advance(base, before, down, across):
        behind = [pltpu.roll(across[-1], 1, 0)] + across[:-1]
        return [
            base[w] + ((down[w] - before[w]) + (across[w] - behind[w])) for w in range(per)
        ]

    def put(ref, h, r, value):
        for w in range(per):
            ref[h, r, w * SUB : (w + 1) * SUB, :] = value[w]

    tall = rows + 2 * depth
    groups = [(0, depth)]
    for n in FIT_ROWS:
        groups.append((groups[-1][1], groups[-1][1] + n))
    groups += [(depth + rows, tall)]
    ready = 0
    befores = [None] * len(lanes)
    for r in range(tall - 1):
        while ready < len(groups) and groups[ready][0] <= r + 1 + AHEAD:
            fit_rows(*groups[ready])
            ready += 1
        for h in range(len(lanes)):
            now = natural(fit, h, r)
            down, across = slopes(now, natural(fit, h, r + 1), open_rows.get(r))
            if r > 0:
                put(field_a, h, r, advance(now, befores[h], down, across))
            befores[h] = down

    def step(s, first, trips, unroll):
        source, final = fields[s], s == TV_ITERS - 1

        @pl.when(at_top > 0)
        def _():
            source[:, depth - 1] = source[:, depth]

        @pl.when(at_bottom > 0)
        def _():
            source[:, depth + rows] = source[:, depth + rows - 1]

        def block_step(n, carry):
            carry = list(carry)
            for inner in range(unroll):
                r = first + n * unroll + inner
                for h, lane in enumerate(lanes):
                    now, before = carry[2 * h], carry[2 * h + 1]
                    later = spread(source, h, r + 1)
                    down, across = slopes(now, later)
                    base = [0.5 * (x + y) for x, y in zip(now, natural(fit, h, r))]
                    value = advance(base, before, down, across)
                    if final:
                        for w in range(per):
                            field_a[h, r, pl.ds(w, SUB, stride=per), :] = value[w]
                        result = (field_a[h, r, 0:cols, :] * 0.25).astype(bf16)
                        width = min(lane.stop, bands) - lane.start
                        out_stage[r - depth, :, lane.start : lane.start + width] = result[:, :width]
                    else:
                        put(fields[s + 1], h, r, value)
                    carry[2 * h], carry[2 * h + 1] = later, down
            if final:
                out_copy(n).start()
            return tuple(carry)

        carry = []
        for h in range(len(lanes)):
            before, now = spread(source, h, first - 1), spread(source, h, first)
            carry += [now, slopes(before, now)[0]]
        lax.fori_loop(0, trips, block_step, tuple(carry))

    step(1, 1, (rows + 4) // TV_ROWS[0], TV_ROWS[0])
    step(2, depth, rows // TV_ROWS[1], TV_ROWS[1])
    proj_copy.wait()
    for n in range(rows // TV_ROWS[1]):
        out_copy(n).wait()


def start_basis():
    bands = np.arange(BANDS, dtype=np.float32)[None, :]
    cols = np.arange(RANK, dtype=np.float32)[:, None]
    angle = np.float32(np.pi) * (bands + np.float32(0.5)) * cols / np.float32(BANDS)
    return np.pad(np.cos(angle).astype(np.float32), ((0, 0), (0, LANES - BANDS)))


def neighbours(block, axis, dim, width):
    count = lax.axis_size(axis)
    size = block.shape[dim]
    head = lax.slice_in_dim(block, 0, width, axis=dim)
    tail = lax.slice_in_dim(block, size - width, size, axis=dim)
    before = lax.ppermute(tail, axis, [(i, i + 1) for i in range(count - 1)])
    after = lax.ppermute(head, axis, [(i + 1, i) for i in range(count - 1)])
    return before, after


def exchange(pieces, axes):
    return lax.all_to_all(pieces, axes, split_axis=0, concat_axis=0)


def body(cube):
    n_rows = lax.axis_size("narrow")
    n_cols = lax.axis_size("wide")
    count = n_rows * n_cols
    rows, cols, bands = cube.shape
    depth = TV_ITERS
    axes = ("narrow", "wide")

    tall_packed = -(-bands // count) * count
    left, right = neighbours(cube, "wide", 1, depth)
    pieces = 2 if rows % 2 == 0 else 1
    packed = pl.pallas_call(
        gram_kernel,
        in_specs=[pl.BlockSpec(memory_space=pl.ANY)],
        out_shape=jax.ShapeDtypeStruct((tall_packed, HALF), f32),
        scratch_shapes=[
            pltpu.VMEM(cube.shape, cube.dtype),
            pltpu.VMEM((LANES, LANES), f32),
            pltpu.SemaphoreType.DMA((pieces,)),
        ],
        compiler_params=pltpu.CompilerParams(vmem_limit_bytes=62 * 2**20),
    )(cube)
    vmem = pl.BlockSpec(memory_space=pltpu.VMEM)
    pieces_shape = (count, 1, tall_packed // count * HALF)
    part = exchange(packed.reshape(pieces_shape), axes).reshape(tall_packed, HALF)
    share = pl.pallas_call(
        functools.partial(sum_kernel, count),
        in_specs=[vmem],
        out_specs=vmem,
        out_shape=jax.ShapeDtypeStruct((tall_packed, HALF), f32),
        compiler_params=pltpu.CompilerParams(vmem_limit_bytes=16 * 2**20),
    )(part)
    gathered = exchange(share.reshape(pieces_shape), axes).reshape(tall_packed, HALF)

    tall, span = rows + 2 * depth, cols + SIDE
    up, down, side = pl.pallas_call(
        functools.partial(halo_kernel, depth),
        in_specs=[vmem] * 4,
        out_specs=[vmem] * 3,
        out_shape=[
            jax.ShapeDtypeStruct((depth, span, bands), bf16),
            jax.ShapeDtypeStruct((depth, span, bands), bf16),
            jax.ShapeDtypeStruct((rows, SIDE, bands), bf16),
        ],
        scratch_shapes=[pltpu.VMEM((rows, SIDE, bands), f32)],
        cost_estimate=pl.CostEstimate(flops=2**32, bytes_accessed=2**18, transcendentals=0),
        compiler_params=pltpu.CompilerParams(vmem_limit_bytes=16 * 2**20),
    )(left, right, cube[:depth], cube[rows - depth :])
    above = lax.ppermute(down, "narrow", [(i, i + 1) for i in range(n_rows - 1)])
    below = lax.ppermute(up, "narrow", [(i + 1, i) for i in range(n_rows - 1)])

    row, col = lax.axis_index("narrow"), lax.axis_index("wide")
    edges = jnp.stack([row == 0, row == n_rows - 1, col == 0, col == n_cols - 1]).astype(jnp.int32)
    inv_count = 1.0 / (count * rows * cols)
    basis = pl.pallas_call(
        functools.partial(subspace_kernel, inv_count),
        in_specs=[vmem] * 2,
        out_specs=vmem,
        out_shape=jax.ShapeDtypeStruct((RANK, LANES), f32),
        scratch_shapes=[pltpu.VMEM((2, LANES, LANES), bf16)],
        cost_estimate=pl.CostEstimate(flops=2**32, bytes_accessed=2**18, transcendentals=0),
        compiler_params=pltpu.CompilerParams(vmem_limit_bytes=16 * 2**20),
    )(gathered, jnp.asarray(start_basis()))
    restored, projector = pl.pallas_call(
        functools.partial(main_kernel, depth),
        in_specs=[pl.BlockSpec(memory_space=pltpu.SMEM)] + [vmem] * 5,
        out_specs=[pl.BlockSpec(memory_space=pl.ANY)] * 2,
        out_shape=[
            jax.ShapeDtypeStruct((rows, cols, bands), bf16),
            jax.ShapeDtypeStruct((bands, bands), f32),
        ],
        scratch_shapes=[pltpu.VMEM((2, tall, span, HALF), f32)] * 3
        + [
            pltpu.VMEM((rows, cols, bands), bf16),
            pltpu.VMEM((bands, bands), f32),
            pltpu.SemaphoreType.DMA((rows // TV_ROWS[1],)),
            pltpu.SemaphoreType.DMA,
        ],
        compiler_params=pltpu.CompilerParams(vmem_limit_bytes=48 * 2**20),
    )(edges, basis, cube, above, below, side)
    return restored, projector


def solution(mesh):
    return jax.shard_map(
        body,
        mesh=mesh,
        in_specs=(P("narrow", "wide", None),),
        out_specs=(P("narrow", "wide", None), P()),
        check_vma=False,
    )
```

```python
import functools

import jax
import jax.numpy as jnp
import numpy as np
from jax import lax
from jax.experimental import pallas as pl
from jax.experimental.pallas import tpu as pltpu
from jax.sharding import PartitionSpec as P

BANDS = 224
RANK = 16
POWER_ITERS = 4
TV_ITERS = 3
LANES = 256
HALF = 128
TAIL = BANDS - HALF
SIDE = 8
SUB = 8
BLOCK = 8
FIT_ROWS = (2, 6, 8, 8, 8)
AHEAD = 4
TV_ROWS = (12, 16)
OUT_ROWS = 4

f32 = jnp.float32
bf16 = jnp.bfloat16


def iotas(shape):
    return lax.broadcasted_iota(jnp.int32, shape, 0), lax.broadcasted_iota(jnp.int32, shape, 1)


def gram_kernel(cube_ref, packed_ref, block, full, sems):
    rows, cols, bands = cube_ref.shape
    pieces = sems.shape[0]
    high = rows // pieces

    def copy(n):
        part = pl.ds(n * high, high)
        return pltpu.make_async_copy(cube_ref.at[part], block.at[part], sems.at[n])

    for n in range(pieces):
        copy(n).start()
    full[HALF:, HALF:] = jnp.zeros((LANES - HALF, LANES - HALF), f32)
    total = None
    for n in range(pieces):
        copy(n).wait()
        flat = block[n * high : (n + 1) * high].reshape(high * cols, bands)
        term = lax.dot_general(flat, flat, (((0,), (0,)), ((), ())), preferred_element_type=f32)
        total = term if total is None else total + term
    full[0:bands, 0:bands] = total
    i, j = iotas((HALF, HALF))
    first = full[0:HALF, 0:HALF]
    second = pltpu.roll(full[HALF:LANES, HALF:LANES], 1, 1)
    packed_ref[0:HALF, :] = jnp.where(j <= i, first, second)
    packed_ref[HALF:bands, :] = full[HALF:bands, 0:HALF]
    if packed_ref.shape[0] > bands:
        packed_ref[bands:, :] = jnp.zeros((packed_ref.shape[0] - bands, HALF), f32)


def sum_kernel(count, pieces_ref, spread_ref):
    high = pieces_ref.shape[0] // count
    parts = [pieces_ref[n * high : (n + 1) * high, :] for n in range(count)]
    total = functools.reduce(jnp.add, parts)
    for n in range(count):
        spread_ref[n * high : (n + 1) * high, :] = total


def split3(x):
    high = x.astype(bf16)
    rest = x - high.astype(f32)
    mid = rest.astype(bf16)
    low = (rest - mid.astype(f32)).astype(bf16)
    return high, mid, low


def product(left, right, dims):
    def dot(a, b):
        return lax.dot_general(a, b, (dims, ((), ())), preferred_element_type=f32)

    n = left[0].shape[0]
    top = dot(jnp.concatenate(left, axis=0), right[0])
    middle = dot(jnp.concatenate(left[:2], axis=0), right[1])
    small = top[2 * n : 3 * n] + middle[n : 2 * n]
    if len(right) > 2:
        small = small + dot(left[0], right[2])
    return top[:n] + ((top[n : 2 * n] + middle[:n]) + small)


def unpack(packed, scale):
    i, j = iotas((HALF, HALF))
    merged = packed[0:HALF, :] * scale
    below = packed[HALF:BANDS, :] * scale
    below = jnp.concatenate([below, jnp.zeros((LANES - BANDS, HALF), f32)], axis=0)
    first = jnp.where(j <= i, merged, 0.0) + jnp.where(j < i, merged, 0.0).T
    moved = pltpu.roll(merged, HALF - 1, 1)
    inside = (i < TAIL) & (j < TAIL)
    second = jnp.where(inside & (j >= i), moved, 0.0) + jnp.where(inside & (j > i), moved, 0.0).T
    return jnp.concatenate(
        [
            jnp.concatenate([first, below.T], axis=1),
            jnp.concatenate([below, second], axis=1),
        ],
        axis=0,
    )


def orthonormal(grown, inner):
    row = lax.broadcasted_iota(jnp.int32, (RANK, HALF), 0)
    work = [
        jnp.concatenate([inner, jnp.zeros((RANK, HALF - RANK), f32)], axis=1),
        grown[:, :HALF],
        grown[:, HALF:],
    ]
    diagonal = jnp.ones((RANK, HALF), f32)
    for k in range(0, RANK, BLOCK):
        columns = [
            jnp.broadcast_to(work[0][:, k + c : k + c + 1], (RANK, HALF)) for c in range(BLOCK)
        ]
        tops = [[part[k + r : k + r + 1, :] for part in work] for r in range(BLOCK)]
        small = [
            [columns[c][k + r : k + r + 1, :] for c in range(r + 1)] for r in range(BLOCK)
        ]
        factors = []
        for j in range(BLOCK):
            pivot = small[j][j]
            inverse = 1.0 / pivot
            diagonal = jnp.where(row == k + j, pivot, diagonal)
            factor = jnp.where(row > k + j, columns[j] * inverse, 0.0)
            factors.append(factor)
            below = [small[i][j] for i in range(BLOCK) if i > j]
            for i in range(j + 1, BLOCK):
                ratio = small[i][j] * inverse
                for c in range(j + 1, i + 1):
                    small[i][c] = small[i][c] - ratio * below[c - j - 1]
                tops[i] = [x - ratio * y for x, y in zip(tops[i], tops[j])]
                columns[i] = columns[i] - factor * below[i - j - 1]
        for n in range(len(work)):
            if n > 0 or k + BLOCK < RANK:
                for j in range(BLOCK):
                    work[n] = work[n] - factors[j] * tops[j][n]
    scale = lax.rsqrt(diagonal)
    return jnp.concatenate([work[1] * scale, work[2] * scale], axis=1)


def subspace(gram, start, held):
    for n, part in enumerate(split3(gram)[:2]):
        held[n] = part

    def times_gram(pieces):
        return product(pieces, [held[0], held[1]], ((1,), (0,)))

    def iterate(_, grown):
        pieces = split3(grown)
        inner = product(pieces, pieces, ((1,), (1,)))
        return orthonormal(times_gram(pieces), inner)

    grown = lax.fori_loop(0, POWER_ITERS - 1, iterate, times_gram(split3(start)))
    pieces = split3(grown)
    return orthonormal(grown, product(pieces, pieces, ((1,), (1,))))


def halo_kernel(depth, left_ref, right_ref, top_ref, bottom_ref, up_ref, down_ref, side_ref, wide):
    rows, cols = side_ref.shape[0], top_ref.shape[1]
    wide[...] = jnp.zeros_like(wide)
    wide[:, 0:depth] = right_ref[...].astype(f32)
    wide[:, SIDE - depth :] = left_ref[...].astype(f32)
    side = wide[...].astype(bf16)
    side_ref[...] = side
    up_ref[:, 0:cols] = top_ref[...]
    up_ref[:, cols:] = side[:depth]
    down_ref[:, 0:cols] = bottom_ref[...]
    down_ref[:, cols:] = side[rows - depth :]


def subspace_kernel(inv_count, packed_ref, start_ref, basis_ref, held):
    basis_ref[...] = subspace(unpack(packed_ref[...], inv_count), start_ref[...], held)


def main_kernel(
    depth, edge_ref, basis_ref, mid_ref, above_ref, below_ref, side_ref,
    out_ref, proj_ref, fit, field_a, field_b, out_stage, proj_stage, out_sems, proj_sem
):
    rows, cols, bands = mid_ref.shape
    span = cols + SIDE
    proj_copy = pltpu.make_async_copy(proj_stage, proj_ref, proj_sem)

    def out_copy(n):
        part = pl.ds(n * OUT_ROWS, OUT_ROWS)
        return pltpu.make_async_copy(out_stage.at[part], out_ref.at[part], out_sems.at[n])

    high, mid, low = split3(basis_ref[...])
    tn = (((0,), (0,)), ((), ()))
    mixed = lax.dot_general(
        jnp.concatenate([high, high, high], axis=0),
        jnp.concatenate([high, mid, low], axis=0),
        tn,
        preferred_element_type=f32,
    )
    mixed = mixed * 4.0
    mixed_high = mixed.astype(bf16)
    mixed_low = (mixed - mixed_high.astype(f32)).astype(bf16)
    mixed_both = jnp.concatenate([mixed_high, mixed_low], axis=0)

    def fitted(flat):
        padded = jnp.concatenate([flat, jnp.zeros((flat.shape[0], LANES - bands), bf16)], axis=1)
        both = jnp.concatenate([padded, padded], axis=1)
        return jnp.dot(both, mixed_both, preferred_element_type=f32)

    def project():
        right = jnp.concatenate([high, high, high, mid, mid, low], axis=0)
        left = jnp.concatenate([high, mid, low, high, mid, high], axis=0)
        full = lax.dot_general(left, right, tn, preferred_element_type=f32)
        proj_stage[...] = full[:bands, :bands]
        proj_copy.start()

    def fit_rows(start, stop):
        n = stop - start
        if depth <= start < depth + rows:
            part = slice(start - depth, stop - depth)
            center = mid_ref[part].reshape(n * cols, bands)
            side = side_ref[part].astype(f32).reshape(n * SIDE, bands).astype(bf16)
            res = fitted(jnp.concatenate([center, side], axis=0))
            for h, lane in enumerate(lanes):
                fit[h, start:stop, 0:cols] = res[: n * cols, lane].reshape(n, cols, HALF)
                fit[h, start:stop, cols:span] = res[n * cols :, lane].reshape(n, SIDE, HALF)
        else:
            block = above_ref[...] if start < depth else below_ref[...]
            flat = block.astype(f32).reshape(n * span, bands).astype(bf16)
            res = fitted(flat)
            for h, lane in enumerate(lanes):
                fit[h, start:stop] = res[:, lane].reshape(n, span, HALF)

    at_top, at_bottom, at_left, at_right = (edge_ref[n] for n in range(4))
    per = span // SUB
    place = lax.broadcasted_iota(jnp.int32, (SUB, HALF), 0)
    keeps = {}
    for column, shut in ((cols - 1, at_right), (span - 1, at_left)):
        keep = jnp.where((place == column // per) & (shut > 0), 0.0, 1.0).astype(f32)
        keeps[column % per] = keeps[column % per] * keep if column % per in keeps else keep
    open_rows = {
        depth - 1: jnp.where(at_top > 0, 0.0, 1.0),
        depth + rows - 1: jnp.where(at_bottom > 0, 0.0, 1.0),
    }
    lanes = [slice(0, HALF), slice(HALF, LANES)]
    fields = [fit, field_a, field_b]

    def natural(ref, h, r):
        return [ref[h, r, pl.ds(w, SUB, stride=per), :] for w in range(per)]

    def spread(ref, h, r):
        return [ref[h, r, w * SUB : (w + 1) * SUB, :] for w in range(per)]

    def slopes(now, later, open_row=None):
        follow = now[1:] + [pltpu.roll(now[0], SUB - 1, 0)]
        downs, acrosses = [], []
        for w in range(per):
            down = later[w] - now[w]
            if open_row is not None:
                down = down * open_row
            across = follow[w] - now[w]
            if w in keeps:
                across = across * keeps[w]
            inverse = lax.rsqrt(down * down + (across * across + 4.0))
            downs.append(down * inverse)
            acrosses.append(across * inverse)
        return downs, acrosses

    def advance(base, before, down, across):
        behind = [pltpu.roll(across[-1], 1, 0)] + across[:-1]
        return [
            base[w] + ((down[w] - before[w]) + (across[w] - behind[w])) for w in range(per)
        ]

    def put(ref, h, r, value):
        for w in range(per):
            ref[h, r, w * SUB : (w + 1) * SUB, :] = value[w]

    tall = rows + 2 * depth
    groups = [(0, depth)]
    for n in FIT_ROWS:
        groups.append((groups[-1][1], groups[-1][1] + n))
    groups += [(depth + rows, tall)]
    ready = 0
    befores = [None] * len(lanes)
    for r in range(tall - 1):
        while ready < len(groups) and groups[ready][0] <= r + 1 + AHEAD:
            fit_rows(*groups[ready])
            ready += 1
            if ready == 4:
                project()
        for h in range(len(lanes)):
            now = natural(fit, h, r)
            down, across = slopes(now, natural(fit, h, r + 1), open_rows.get(r))
            if r > 0:
                put(field_a, h, r, advance(now, befores[h], down, across))
            befores[h] = down

    def step(s, first, trips, unroll):
        source, final = fields[s], s == TV_ITERS - 1

        @pl.when(at_top > 0)
        def _():
            source[:, depth - 1] = source[:, depth]

        @pl.when(at_bottom > 0)
        def _():
            source[:, depth + rows] = source[:, depth + rows - 1]

        def block_step(n, carry):
            carry = list(carry)
            for inner in range(unroll):
                r = first + n * unroll + inner
                for h, lane in enumerate(lanes):
                    now, before = carry[2 * h], carry[2 * h + 1]
                    later = spread(source, h, r + 1)
                    down, across = slopes(now, later)
                    base = [0.5 * (x + y) for x, y in zip(now, natural(fit, h, r))]
                    value = advance(base, before, down, across)
                    if final:
                        for w in range(per):
                            field_a[h, r, pl.ds(w, SUB, stride=per), :] = value[w]
                        result = (field_a[h, r, 0:cols, :] * 0.25).astype(bf16)
                        width = min(lane.stop, bands) - lane.start
                        out_stage[r - depth, :, lane.start : lane.start + width] = result[:, :width]
                    else:
                        put(fields[s + 1], h, r, value)
                    carry[2 * h], carry[2 * h + 1] = later, down
                if final and inner % OUT_ROWS == OUT_ROWS - 1:
                    out_copy(n * (unroll // OUT_ROWS) + inner // OUT_ROWS).start()
            return tuple(carry)

        carry = []
        for h in range(len(lanes)):
            before, now = spread(source, h, first - 1), spread(source, h, first)
            carry += [now, slopes(before, now)[0]]
        lax.fori_loop(0, trips, block_step, tuple(carry))

    step(1, 1, (rows + 4) // TV_ROWS[0], TV_ROWS[0])
    step(2, depth, rows // TV_ROWS[1], TV_ROWS[1])
    proj_copy.wait()
    for n in range(rows // OUT_ROWS):
        out_copy(n).wait()


def start_basis():
    bands = np.arange(BANDS, dtype=np.float32)[None, :]
    cols = np.arange(RANK, dtype=np.float32)[:, None]
    angle = np.float32(np.pi) * (bands + np.float32(0.5)) * cols / np.float32(BANDS)
    return np.pad(np.cos(angle).astype(np.float32), ((0, 0), (0, LANES - BANDS)))


def neighbours(block, axis, dim, width):
    count = lax.axis_size(axis)
    size = block.shape[dim]
    head = lax.slice_in_dim(block, 0, width, axis=dim)
    tail = lax.slice_in_dim(block, size - width, size, axis=dim)
    before = lax.ppermute(tail, axis, [(i, i + 1) for i in range(count - 1)])
    after = lax.ppermute(head, axis, [(i + 1, i) for i in range(count - 1)])
    return before, after


def exchange(pieces, axes):
    return lax.all_to_all(pieces, axes, split_axis=0, concat_axis=0)


def body(cube):
    n_rows = lax.axis_size("narrow")
    n_cols = lax.axis_size("wide")
    count = n_rows * n_cols
    rows, cols, bands = cube.shape
    depth = TV_ITERS
    axes = ("narrow", "wide")

    tall_packed = -(-bands // count) * count
    left, right = neighbours(cube, "wide", 1, depth)
    pieces = 2 if rows % 2 == 0 else 1
    packed = pl.pallas_call(
        gram_kernel,
        in_specs=[pl.BlockSpec(memory_space=pl.ANY)],
        out_shape=jax.ShapeDtypeStruct((tall_packed, HALF), f32),
        scratch_shapes=[
            pltpu.VMEM(cube.shape, cube.dtype),
            pltpu.VMEM((LANES, LANES), f32),
            pltpu.SemaphoreType.DMA((pieces,)),
        ],
        compiler_params=pltpu.CompilerParams(vmem_limit_bytes=62 * 2**20),
    )(cube)
    vmem = pl.BlockSpec(memory_space=pltpu.VMEM)
    pieces_shape = (count, 1, tall_packed // count * HALF)
    part = exchange(packed.reshape(pieces_shape), axes).reshape(tall_packed, HALF)
    share = pl.pallas_call(
        functools.partial(sum_kernel, count),
        in_specs=[vmem],
        out_specs=vmem,
        out_shape=jax.ShapeDtypeStruct((tall_packed, HALF), f32),
        compiler_params=pltpu.CompilerParams(vmem_limit_bytes=16 * 2**20),
    )(part)
    gathered = exchange(share.reshape(pieces_shape), axes).reshape(tall_packed, HALF)

    tall, span = rows + 2 * depth, cols + SIDE
    up, down, side = pl.pallas_call(
        functools.partial(halo_kernel, depth),
        in_specs=[vmem] * 4,
        out_specs=[vmem] * 3,
        out_shape=[
            jax.ShapeDtypeStruct((depth, span, bands), bf16),
            jax.ShapeDtypeStruct((depth, span, bands), bf16),
            jax.ShapeDtypeStruct((rows, SIDE, bands), bf16),
        ],
        scratch_shapes=[pltpu.VMEM((rows, SIDE, bands), f32)],
        cost_estimate=pl.CostEstimate(flops=2**32, bytes_accessed=2**18, transcendentals=0),
        compiler_params=pltpu.CompilerParams(vmem_limit_bytes=16 * 2**20),
    )(left, right, cube[:depth], cube[rows - depth :])
    above = lax.ppermute(down, "narrow", [(i, i + 1) for i in range(n_rows - 1)])
    below = lax.ppermute(up, "narrow", [(i + 1, i) for i in range(n_rows - 1)])

    row, col = lax.axis_index("narrow"), lax.axis_index("wide")
    edges = jnp.stack([row == 0, row == n_rows - 1, col == 0, col == n_cols - 1]).astype(jnp.int32)
    inv_count = 1.0 / (count * rows * cols)
    basis = pl.pallas_call(
        functools.partial(subspace_kernel, inv_count),
        in_specs=[vmem] * 2,
        out_specs=vmem,
        out_shape=jax.ShapeDtypeStruct((RANK, LANES), f32),
        scratch_shapes=[pltpu.VMEM((2, LANES, LANES), bf16)],
        cost_estimate=pl.CostEstimate(flops=2**32, bytes_accessed=2**18, transcendentals=0),
        compiler_params=pltpu.CompilerParams(vmem_limit_bytes=16 * 2**20),
    )(gathered, jnp.asarray(start_basis()))
    restored, projector = pl.pallas_call(
        functools.partial(main_kernel, depth),
        in_specs=[pl.BlockSpec(memory_space=pltpu.SMEM)] + [vmem] * 5,
        out_specs=[pl.BlockSpec(memory_space=pl.ANY)] * 2,
        out_shape=[
            jax.ShapeDtypeStruct((rows, cols, bands), bf16),
            jax.ShapeDtypeStruct((bands, bands), f32),
        ],
        scratch_shapes=[pltpu.VMEM((2, tall, span, HALF), f32)] * 3
        + [
            pltpu.VMEM((rows, cols, bands), bf16),
            pltpu.VMEM((bands, bands), f32),
            pltpu.SemaphoreType.DMA((rows // OUT_ROWS,)),
            pltpu.SemaphoreType.DMA,
        ],
        compiler_params=pltpu.CompilerParams(vmem_limit_bytes=48 * 2**20),
    )(edges, basis, cube, above, below, side)
    return restored, projector


def solution(mesh):
    return jax.shard_map(
        body,
        mesh=mesh,
        in_specs=(P("narrow", "wide", None),),
        out_specs=(P("narrow", "wide", None), P()),
        check_vma=False,
    )
```

```python
import functools

import jax
import jax.numpy as jnp
import numpy as np
from jax import lax
from jax.experimental import pallas as pl
from jax.experimental.pallas import tpu as pltpu
from jax.sharding import PartitionSpec as P

BANDS = 224
RANK = 16
POWER_ITERS = 4
TV_ITERS = 3
LANES = 256
HALF = 128
TAIL = BANDS - HALF
SIDE = 8
SUB = 8
BLOCK = 8
FIT_ROWS = (2, 6, 8, 8, 8)
AHEAD = 4
TV_ROWS = (12, 16)
OUT_ROWS = 4

f32 = jnp.float32
bf16 = jnp.bfloat16


def iotas(shape):
    return lax.broadcasted_iota(jnp.int32, shape, 0), lax.broadcasted_iota(jnp.int32, shape, 1)


def gram_kernel(cube_ref, packed_ref, block, full, sems):
    rows, cols, bands = cube_ref.shape
    pieces = sems.shape[0]
    high = rows // pieces

    def copy(n):
        part = pl.ds(n * high, high)
        return pltpu.make_async_copy(cube_ref.at[part], block.at[part], sems.at[n])

    for n in range(pieces):
        copy(n).start()
    full[HALF:, HALF:] = jnp.zeros((LANES - HALF, LANES - HALF), f32)
    total = None
    for n in range(pieces):
        copy(n).wait()
        flat = block[n * high : (n + 1) * high].reshape(high * cols, bands)
        term = lax.dot_general(flat, flat, (((0,), (0,)), ((), ())), preferred_element_type=f32)
        total = term if total is None else total + term
    full[0:bands, 0:bands] = total
    i, j = iotas((HALF, HALF))
    first = full[0:HALF, 0:HALF]
    second = pltpu.roll(full[HALF:LANES, HALF:LANES], 1, 1)
    packed_ref[0:HALF, :] = jnp.where(j <= i, first, second)
    packed_ref[HALF:bands, :] = full[HALF:bands, 0:HALF]
    if packed_ref.shape[0] > bands:
        packed_ref[bands:, :] = jnp.zeros((packed_ref.shape[0] - bands, HALF), f32)


def sum_kernel(count, pieces_ref, spread_ref):
    high = pieces_ref.shape[0] // count
    parts = [pieces_ref[n * high : (n + 1) * high, :] for n in range(count)]
    total = functools.reduce(jnp.add, parts)
    for n in range(count):
        spread_ref[n * high : (n + 1) * high, :] = total


def split3(x):
    high = x.astype(bf16)
    rest = x - high.astype(f32)
    mid = rest.astype(bf16)
    low = (rest - mid.astype(f32)).astype(bf16)
    return high, mid, low


def product(left, right, dims):
    def dot(a, b):
        return lax.dot_general(a, b, (dims, ((), ())), preferred_element_type=f32)

    n = left[0].shape[0]
    top = dot(jnp.concatenate(left, axis=0), right[0])
    middle = dot(jnp.concatenate(left[:2], axis=0), right[1])
    small = top[2 * n : 3 * n] + middle[n : 2 * n]
    if len(right) > 2:
        small = small + dot(left[0], right[2])
    return top[:n] + ((top[n : 2 * n] + middle[:n]) + small)


def unpack(packed, scale):
    i, j = iotas((HALF, HALF))
    merged = packed[0:HALF, :] * scale
    below = packed[HALF:BANDS, :] * scale
    below = jnp.concatenate([below, jnp.zeros((LANES - BANDS, HALF), f32)], axis=0)
    first = jnp.where(j <= i, merged, 0.0) + jnp.where(j < i, merged, 0.0).T
    moved = pltpu.roll(merged, HALF - 1, 1)
    inside = (i < TAIL) & (j < TAIL)
    second = jnp.where(inside & (j >= i), moved, 0.0) + jnp.where(inside & (j > i), moved, 0.0).T
    return jnp.concatenate(
        [
            jnp.concatenate([first, below.T], axis=1),
            jnp.concatenate([below, second], axis=1),
        ],
        axis=0,
    )


def orthonormal(grown, inner):
    row = lax.broadcasted_iota(jnp.int32, (RANK, HALF), 0)
    work = [
        jnp.concatenate([inner, jnp.zeros((RANK, HALF - RANK), f32)], axis=1),
        grown[:, :HALF],
        grown[:, HALF:],
    ]
    diagonal = jnp.ones((RANK, HALF), f32)
    for k in range(0, RANK, BLOCK):
        columns = [
            jnp.broadcast_to(work[0][:, k + c : k + c + 1], (RANK, HALF)) for c in range(BLOCK)
        ]
        tops = [[part[k + r : k + r + 1, :] for part in work] for r in range(BLOCK)]
        small = [
            [columns[c][k + r : k + r + 1, :] for c in range(r + 1)] for r in range(BLOCK)
        ]
        factors = []
        for j in range(BLOCK):
            pivot = small[j][j]
            inverse = 1.0 / pivot
            diagonal = jnp.where(row == k + j, pivot, diagonal)
            factor = jnp.where(row > k + j, columns[j] * inverse, 0.0)
            factors.append(factor)
            below = [small[i][j] for i in range(BLOCK) if i > j]
            for i in range(j + 1, BLOCK):
                ratio = small[i][j] * inverse
                for c in range(j + 1, i + 1):
                    small[i][c] = small[i][c] - ratio * below[c - j - 1]
                tops[i] = [x - ratio * y for x, y in zip(tops[i], tops[j])]
                columns[i] = columns[i] - factor * below[i - j - 1]
        for n in range(len(work)):
            if n > 0 or k + BLOCK < RANK:
                for j in range(BLOCK):
                    work[n] = work[n] - factors[j] * tops[j][n]
    scale = lax.rsqrt(diagonal)
    return jnp.concatenate([work[1] * scale, work[2] * scale], axis=1)


def subspace(gram, start, held):
    for n, part in enumerate(split3(gram)[:2]):
        held[n] = part

    def times_gram(pieces):
        return product(pieces, [held[0], held[1]], ((1,), (0,)))

    def iterate(_, grown):
        pieces = split3(grown)
        inner = product(pieces, pieces, ((1,), (1,)))
        return orthonormal(times_gram(pieces), inner)

    grown = lax.fori_loop(0, POWER_ITERS - 1, iterate, times_gram(split3(start)))
    pieces = split3(grown)
    return orthonormal(grown, product(pieces, pieces, ((1,), (1,))))


def halo_kernel(depth, left_ref, right_ref, top_ref, bottom_ref, up_ref, down_ref, side_ref, wide):
    rows, cols = side_ref.shape[0], top_ref.shape[1]
    wide[...] = jnp.zeros_like(wide)
    wide[:, 0:depth] = right_ref[...].astype(f32)
    wide[:, SIDE - depth :] = left_ref[...].astype(f32)
    side = wide[...].astype(bf16)
    side_ref[...] = side
    up_ref[:, 0:cols] = top_ref[...]
    up_ref[:, cols:] = side[:depth]
    down_ref[:, 0:cols] = bottom_ref[...]
    down_ref[:, cols:] = side[rows - depth :]


def subspace_kernel(inv_count, packed_ref, start_ref, basis_ref, held):
    basis_ref[...] = subspace(unpack(packed_ref[...], inv_count), start_ref[...], held)


def main_kernel(
    depth, n_rows, n_cols, basis_ref, mid_ref, above_ref, below_ref, side_ref,
    out_ref, proj_ref, fit, field_a, field_b, out_stage, proj_stage, out_sems, proj_sem
):
    rows, cols, bands = mid_ref.shape
    span = cols + SIDE
    proj_copy = pltpu.make_async_copy(proj_stage, proj_ref, proj_sem)

    def out_copy(n):
        part = pl.ds(n * OUT_ROWS, OUT_ROWS)
        return pltpu.make_async_copy(out_stage.at[part], out_ref.at[part], out_sems.at[n])

    high, mid, low = split3(basis_ref[...])
    tn = (((0,), (0,)), ((), ()))
    mixed = lax.dot_general(
        jnp.concatenate([high, high, high], axis=0),
        jnp.concatenate([high, mid, low], axis=0),
        tn,
        preferred_element_type=f32,
    )
    mixed = mixed * 4.0
    mixed_high = mixed.astype(bf16)
    mixed_low = (mixed - mixed_high.astype(f32)).astype(bf16)
    mixed_both = jnp.concatenate([mixed_high, mixed_low], axis=0)

    def fitted(flat):
        padded = jnp.concatenate([flat, jnp.zeros((flat.shape[0], LANES - bands), bf16)], axis=1)
        both = jnp.concatenate([padded, padded], axis=1)
        return jnp.dot(both, mixed_both, preferred_element_type=f32)

    def project():
        right = jnp.concatenate([high, high, high, mid, mid, low], axis=0)
        left = jnp.concatenate([high, mid, low, high, mid, high], axis=0)
        full = lax.dot_general(left, right, tn, preferred_element_type=f32)
        proj_stage[...] = full[:bands, :bands]
        proj_copy.start()

    def fit_rows(start, stop):
        n = stop - start
        if depth <= start < depth + rows:
            part = slice(start - depth, stop - depth)
            center = mid_ref[part].reshape(n * cols, bands)
            side = side_ref[part].astype(f32).reshape(n * SIDE, bands).astype(bf16)
            res = fitted(jnp.concatenate([center, side], axis=0))
            for h, lane in enumerate(lanes):
                fit[h, start:stop, 0:cols] = res[: n * cols, lane].reshape(n, cols, HALF)
                fit[h, start:stop, cols:span] = res[n * cols :, lane].reshape(n, SIDE, HALF)
        else:
            block = above_ref[...] if start < depth else below_ref[...]
            flat = block.astype(f32).reshape(n * span, bands).astype(bf16)
            res = fitted(flat)
            for h, lane in enumerate(lanes):
                fit[h, start:stop] = res[:, lane].reshape(n, span, HALF)

    row, col = lax.axis_index("narrow"), lax.axis_index("wide")
    at_top, at_bottom = row == 0, row == n_rows - 1
    at_left, at_right = col == 0, col == n_cols - 1
    per = span // SUB
    place = lax.broadcasted_iota(jnp.int32, (SUB, HALF), 0)
    keeps = {}
    for column, shut in ((cols - 1, at_right), (span - 1, at_left)):
        keep = jnp.where((place == column // per) & shut, 0.0, 1.0).astype(f32)
        keeps[column % per] = keeps[column % per] * keep if column % per in keeps else keep
    open_rows = {
        depth - 1: jnp.where(at_top, 0.0, 1.0),
        depth + rows - 1: jnp.where(at_bottom, 0.0, 1.0),
    }
    lanes = [slice(0, HALF), slice(HALF, LANES)]
    fields = [fit, field_a, field_b]

    def natural(ref, h, r):
        return [ref[h, r, pl.ds(w, SUB, stride=per), :] for w in range(per)]

    def spread(ref, h, r):
        return [ref[h, r, w * SUB : (w + 1) * SUB, :] for w in range(per)]

    def slopes(now, later, open_row=None):
        follow = now[1:] + [pltpu.roll(now[0], SUB - 1, 0)]
        downs, acrosses = [], []
        for w in range(per):
            down = later[w] - now[w]
            if open_row is not None:
                down = down * open_row
            across = follow[w] - now[w]
            if w in keeps:
                across = across * keeps[w]
            inverse = lax.rsqrt(down * down + (across * across + 4.0))
            downs.append(down * inverse)
            acrosses.append(across * inverse)
        return downs, acrosses

    def advance(base, before, down, across):
        behind = [pltpu.roll(across[-1], 1, 0)] + across[:-1]
        return [
            base[w] + ((down[w] - before[w]) + (across[w] - behind[w])) for w in range(per)
        ]

    def put(ref, h, r, value):
        for w in range(per):
            ref[h, r, w * SUB : (w + 1) * SUB, :] = value[w]

    tall = rows + 2 * depth
    groups = [(0, depth)]
    for n in FIT_ROWS:
        groups.append((groups[-1][1], groups[-1][1] + n))
    groups += [(depth + rows, tall)]
    ready = 0
    befores = [None] * len(lanes)
    for r in range(tall - 1):
        while ready < len(groups) and groups[ready][0] <= r + 1 + AHEAD:
            fit_rows(*groups[ready])
            ready += 1
            if ready == 4:
                project()
        for h in range(len(lanes)):
            now = natural(fit, h, r)
            down, across = slopes(now, natural(fit, h, r + 1), open_rows.get(r))
            if r > 0:
                put(field_a, h, r, advance(now, befores[h], down, across))
            befores[h] = down

    def step(s, first, trips, unroll):
        source, final = fields[s], s == TV_ITERS - 1

        @pl.when(at_top)
        def _():
            source[:, depth - 1] = source[:, depth]

        @pl.when(at_bottom)
        def _():
            source[:, depth + rows] = source[:, depth + rows - 1]

        def block_step(n, carry):
            carry = list(carry)
            for inner in range(unroll):
                r = first + n * unroll + inner
                for h, lane in enumerate(lanes):
                    now, before = carry[2 * h], carry[2 * h + 1]
                    later = spread(source, h, r + 1)
                    down, across = slopes(now, later)
                    base = [0.5 * (x + y) for x, y in zip(now, natural(fit, h, r))]
                    value = advance(base, before, down, across)
                    if final:
                        for w in range(per):
                            field_a[h, r, pl.ds(w, SUB, stride=per), :] = value[w]
                        result = (field_a[h, r, 0:cols, :] * 0.25).astype(bf16)
                        width = min(lane.stop, bands) - lane.start
                        out_stage[r - depth, :, lane.start : lane.start + width] = result[:, :width]
                    else:
                        put(fields[s + 1], h, r, value)
                    carry[2 * h], carry[2 * h + 1] = later, down
                if final and inner % OUT_ROWS == OUT_ROWS - 1:
                    out_copy(n * (unroll // OUT_ROWS) + inner // OUT_ROWS).start()
            return tuple(carry)

        carry = []
        for h in range(len(lanes)):
            before, now = spread(source, h, first - 1), spread(source, h, first)
            carry += [now, slopes(before, now)[0]]
        lax.fori_loop(0, trips, block_step, tuple(carry))

    step(1, 1, (rows + 4) // TV_ROWS[0], TV_ROWS[0])
    step(2, depth, rows // TV_ROWS[1], TV_ROWS[1])
    proj_copy.wait()
    for n in range(rows // OUT_ROWS):
        out_copy(n).wait()


def start_basis():
    bands = np.arange(BANDS, dtype=np.float32)[None, :]
    cols = np.arange(RANK, dtype=np.float32)[:, None]
    angle = np.float32(np.pi) * (bands + np.float32(0.5)) * cols / np.float32(BANDS)
    return np.pad(np.cos(angle).astype(np.float32), ((0, 0), (0, LANES - BANDS)))


def neighbours(block, axis, dim, width):
    count = lax.axis_size(axis)
    size = block.shape[dim]
    head = lax.slice_in_dim(block, 0, width, axis=dim)
    tail = lax.slice_in_dim(block, size - width, size, axis=dim)
    before = lax.ppermute(tail, axis, [(i, i + 1) for i in range(count - 1)])
    after = lax.ppermute(head, axis, [(i + 1, i) for i in range(count - 1)])
    return before, after


def exchange(pieces, axes):
    return lax.all_to_all(pieces, axes, split_axis=0, concat_axis=0)


def body(cube):
    n_rows = lax.axis_size("narrow")
    n_cols = lax.axis_size("wide")
    count = n_rows * n_cols
    rows, cols, bands = cube.shape
    depth = TV_ITERS
    axes = ("narrow", "wide")

    tall_packed = -(-bands // count) * count
    left, right = neighbours(cube, "wide", 1, depth)
    pieces = 2 if rows % 2 == 0 else 1
    packed = pl.pallas_call(
        gram_kernel,
        in_specs=[pl.BlockSpec(memory_space=pl.ANY)],
        out_shape=jax.ShapeDtypeStruct((tall_packed, HALF), f32),
        scratch_shapes=[
            pltpu.VMEM(cube.shape, cube.dtype),
            pltpu.VMEM((LANES, LANES), f32),
            pltpu.SemaphoreType.DMA((pieces,)),
        ],
        compiler_params=pltpu.CompilerParams(vmem_limit_bytes=62 * 2**20),
    )(cube)
    vmem = pl.BlockSpec(memory_space=pltpu.VMEM)
    pieces_shape = (count, 1, tall_packed // count * HALF)
    part = exchange(packed.reshape(pieces_shape), axes).reshape(tall_packed, HALF)
    share = pl.pallas_call(
        functools.partial(sum_kernel, count),
        in_specs=[vmem],
        out_specs=vmem,
        out_shape=jax.ShapeDtypeStruct((tall_packed, HALF), f32),
        compiler_params=pltpu.CompilerParams(vmem_limit_bytes=16 * 2**20),
    )(part)
    gathered = exchange(share.reshape(pieces_shape), axes).reshape(tall_packed, HALF)

    tall, span = rows + 2 * depth, cols + SIDE
    up, down, side = pl.pallas_call(
        functools.partial(halo_kernel, depth),
        in_specs=[vmem] * 4,
        out_specs=[vmem] * 3,
        out_shape=[
            jax.ShapeDtypeStruct((depth, span, bands), bf16),
            jax.ShapeDtypeStruct((depth, span, bands), bf16),
            jax.ShapeDtypeStruct((rows, SIDE, bands), bf16),
        ],
        scratch_shapes=[pltpu.VMEM((rows, SIDE, bands), f32)],
        cost_estimate=pl.CostEstimate(flops=2**32, bytes_accessed=2**18, transcendentals=0),
        compiler_params=pltpu.CompilerParams(vmem_limit_bytes=16 * 2**20),
    )(left, right, cube[:depth], cube[rows - depth :])
    above = lax.ppermute(down, "narrow", [(i, i + 1) for i in range(n_rows - 1)])
    below = lax.ppermute(up, "narrow", [(i + 1, i) for i in range(n_rows - 1)])

    inv_count = 1.0 / (count * rows * cols)
    basis = pl.pallas_call(
        functools.partial(subspace_kernel, inv_count),
        in_specs=[vmem] * 2,
        out_specs=vmem,
        out_shape=jax.ShapeDtypeStruct((RANK, LANES), f32),
        scratch_shapes=[pltpu.VMEM((2, LANES, LANES), bf16)],
        cost_estimate=pl.CostEstimate(flops=2**32, bytes_accessed=2**18, transcendentals=0),
        compiler_params=pltpu.CompilerParams(vmem_limit_bytes=16 * 2**20),
    )(gathered, jnp.asarray(start_basis()))
    restored, projector = pl.pallas_call(
        functools.partial(main_kernel, depth, n_rows, n_cols),
        in_specs=[vmem] * 5,
        out_specs=[pl.BlockSpec(memory_space=pl.ANY)] * 2,
        out_shape=[
            jax.ShapeDtypeStruct((rows, cols, bands), bf16),
            jax.ShapeDtypeStruct((bands, bands), f32),
        ],
        scratch_shapes=[pltpu.VMEM((2, tall, span, HALF), f32)] * 3
        + [
            pltpu.VMEM((rows, cols, bands), bf16),
            pltpu.VMEM((bands, bands), f32),
            pltpu.SemaphoreType.DMA((rows // OUT_ROWS,)),
            pltpu.SemaphoreType.DMA,
        ],
        compiler_params=pltpu.CompilerParams(vmem_limit_bytes=48 * 2**20),
    )(basis, cube, above, below, side)
    return restored, projector


def solution(mesh):
    return jax.shard_map(
        body,
        mesh=mesh,
        in_specs=(P("narrow", "wide", None),),
        out_specs=(P("narrow", "wide", None), P()),
        check_vma=False,
    )
```

```python
import functools

import jax
import jax.numpy as jnp
import numpy as np
from jax import lax
from jax.experimental import pallas as pl
from jax.experimental.pallas import tpu as pltpu
from jax.sharding import PartitionSpec as P

BANDS = 224
RANK = 16
POWER_ITERS = 4
TV_ITERS = 3
LANES = 256
HALF = 128
TAIL = BANDS - HALF
SIDE = 8
SUB = 8
BLOCK = 8
FIT_ROWS = (2, 6, 8, 8, 8)
AHEAD = 4
TV_ROWS = (17, 16)
OUT_ROWS = 4

f32 = jnp.float32
bf16 = jnp.bfloat16


def iotas(shape):
    return lax.broadcasted_iota(jnp.int32, shape, 0), lax.broadcasted_iota(jnp.int32, shape, 1)


def gram_kernel(cube_ref, packed_ref, block, full, sems):
    rows, cols, bands = cube_ref.shape
    pieces = sems.shape[0]
    high = rows // pieces

    def copy(n):
        part = pl.ds(n * high, high)
        return pltpu.make_async_copy(cube_ref.at[part], block.at[part], sems.at[n])

    for n in range(pieces):
        copy(n).start()
    full[HALF:, HALF:] = jnp.zeros((LANES - HALF, LANES - HALF), f32)
    total = None
    for n in range(pieces):
        copy(n).wait()
        flat = block[n * high : (n + 1) * high].reshape(high * cols, bands)
        term = lax.dot_general(flat, flat, (((0,), (0,)), ((), ())), preferred_element_type=f32)
        total = term if total is None else total + term
    full[0:bands, 0:bands] = total
    i, j = iotas((HALF, HALF))
    first = full[0:HALF, 0:HALF]
    second = pltpu.roll(full[HALF:LANES, HALF:LANES], 1, 1)
    packed_ref[0:HALF, :] = jnp.where(j <= i, first, second)
    packed_ref[HALF:bands, :] = full[HALF:bands, 0:HALF]
    if packed_ref.shape[0] > bands:
        packed_ref[bands:, :] = jnp.zeros((packed_ref.shape[0] - bands, HALF), f32)


def sum_kernel(count, pieces_ref, spread_ref):
    high = pieces_ref.shape[0] // count
    parts = [pieces_ref[n * high : (n + 1) * high, :] for n in range(count)]
    total = functools.reduce(jnp.add, parts)
    for n in range(count):
        spread_ref[n * high : (n + 1) * high, :] = total


def split3(x):
    high = x.astype(bf16)
    rest = x - high.astype(f32)
    mid = rest.astype(bf16)
    low = (rest - mid.astype(f32)).astype(bf16)
    return high, mid, low


def product(left, right, dims):
    def dot(a, b):
        return lax.dot_general(a, b, (dims, ((), ())), preferred_element_type=f32)

    n = left[0].shape[0]
    top = dot(jnp.concatenate(left, axis=0), right[0])
    middle = dot(jnp.concatenate(left[:2], axis=0), right[1])
    small = top[2 * n : 3 * n] + middle[n : 2 * n]
    if len(right) > 2:
        small = small + dot(left[0], right[2])
    return top[:n] + ((top[n : 2 * n] + middle[:n]) + small)


def unpack(packed, scale):
    i, j = iotas((HALF, HALF))
    merged = packed[0:HALF, :] * scale
    below = packed[HALF:BANDS, :] * scale
    below = jnp.concatenate([below, jnp.zeros((LANES - BANDS, HALF), f32)], axis=0)
    first = jnp.where(j <= i, merged, 0.0) + jnp.where(j < i, merged, 0.0).T
    moved = pltpu.roll(merged, HALF - 1, 1)
    inside = (i < TAIL) & (j < TAIL)
    second = jnp.where(inside & (j >= i), moved, 0.0) + jnp.where(inside & (j > i), moved, 0.0).T
    return jnp.concatenate(
        [
            jnp.concatenate([first, below.T], axis=1),
            jnp.concatenate([below, second], axis=1),
        ],
        axis=0,
    )


def orthonormal(grown, inner):
    row = lax.broadcasted_iota(jnp.int32, (RANK, HALF), 0)
    work = [
        jnp.concatenate([inner, jnp.zeros((RANK, HALF - RANK), f32)], axis=1),
        grown[:, :HALF],
        grown[:, HALF:],
    ]
    diagonal = jnp.ones((RANK, HALF), f32)
    for k in range(0, RANK, BLOCK):
        columns = [
            jnp.broadcast_to(work[0][:, k + c : k + c + 1], (RANK, HALF)) for c in range(BLOCK)
        ]
        tops = [[part[k + r : k + r + 1, :] for part in work] for r in range(BLOCK)]
        small = [
            [columns[c][k + r : k + r + 1, :] for c in range(r + 1)] for r in range(BLOCK)
        ]
        factors = []
        for j in range(BLOCK):
            pivot = small[j][j]
            inverse = pl.reciprocal(pivot, full_range=False)
            diagonal = jnp.where(row == k + j, pivot, diagonal)
            factor = jnp.where(row > k + j, columns[j] * inverse, 0.0)
            factors.append(factor)
            below = [small[i][j] for i in range(BLOCK) if i > j]
            for i in range(j + 1, BLOCK):
                ratio = small[i][j] * inverse
                for c in range(j + 1, i + 1):
                    small[i][c] = small[i][c] - ratio * below[c - j - 1]
                tops[i] = [x - ratio * y for x, y in zip(tops[i], tops[j])]
                columns[i] = columns[i] - factor * below[i - j - 1]
        for n in range(len(work)):
            if n > 0 or k + BLOCK < RANK:
                for j in range(BLOCK):
                    work[n] = work[n] - factors[j] * tops[j][n]
    scale = lax.rsqrt(diagonal)
    return jnp.concatenate([work[1] * scale, work[2] * scale], axis=1)


def subspace(gram, start, held):
    for n, part in enumerate(split3(gram)[:2]):
        held[n] = part

    def times_gram(pieces):
        return product(pieces, [held[0], held[1]], ((1,), (0,)))

    def iterate(_, grown):
        pieces = split3(grown)
        inner = product(pieces, pieces, ((1,), (1,)))
        return orthonormal(times_gram(pieces), inner)

    grown = lax.fori_loop(0, POWER_ITERS - 1, iterate, times_gram(split3(start)))
    pieces = split3(grown)
    return orthonormal(grown, product(pieces, pieces, ((1,), (1,))))


def halo_kernel(depth, left_ref, right_ref, top_ref, bottom_ref, up_ref, down_ref, side_ref, wide):
    rows, cols = side_ref.shape[0], top_ref.shape[1]
    wide[...] = jnp.zeros_like(wide)
    wide[:, 0:depth] = right_ref[...].astype(f32)
    wide[:, SIDE - depth :] = left_ref[...].astype(f32)
    side = wide[...].astype(bf16)
    side_ref[...] = side
    up_ref[:, 0:cols] = top_ref[...]
    up_ref[:, cols:] = side[:depth]
    down_ref[:, 0:cols] = bottom_ref[...]
    down_ref[:, cols:] = side[rows - depth :]


def subspace_kernel(inv_count, packed_ref, start_ref, basis_ref, held):
    basis_ref[...] = subspace(unpack(packed_ref[...], inv_count), start_ref[...], held)


def main_kernel(
    depth, n_rows, n_cols, basis_ref, mid_ref, above_ref, below_ref, side_ref,
    out_ref, proj_ref, fit, field_a, field_b, out_stage, proj_stage, out_sems, proj_sem
):
    rows, cols, bands = mid_ref.shape
    span = cols + SIDE
    proj_copy = pltpu.make_async_copy(proj_stage, proj_ref, proj_sem)

    def out_copy(n):
        part = pl.ds(n * OUT_ROWS, OUT_ROWS)
        return pltpu.make_async_copy(out_stage.at[part], out_ref.at[part], out_sems.at[n])

    high, mid, low = split3(basis_ref[...])
    tn = (((0,), (0,)), ((), ()))
    mixed = lax.dot_general(
        jnp.concatenate([high, high, high], axis=0),
        jnp.concatenate([high, mid, low], axis=0),
        tn,
        preferred_element_type=f32,
    )
    mixed = mixed * 4.0
    mixed_high = mixed.astype(bf16)
    mixed_low = (mixed - mixed_high.astype(f32)).astype(bf16)
    mixed_both = jnp.concatenate([mixed_high, mixed_low], axis=0)

    def fitted(flat):
        padded = jnp.concatenate([flat, jnp.zeros((flat.shape[0], LANES - bands), bf16)], axis=1)
        both = jnp.concatenate([padded, padded], axis=1)
        return jnp.dot(both, mixed_both, preferred_element_type=f32)

    def project():
        right = jnp.concatenate([high, high, high, mid, mid, low], axis=0)
        left = jnp.concatenate([high, mid, low, high, mid, high], axis=0)
        full = lax.dot_general(left, right, tn, preferred_element_type=f32)
        proj_stage[...] = full[:bands, :bands]
        proj_copy.start()

    def fit_rows(start, stop):
        n = stop - start
        if depth <= start < depth + rows:
            part = slice(start - depth, stop - depth)
            center = mid_ref[part].reshape(n * cols, bands)
            side = side_ref[part].astype(f32).reshape(n * SIDE, bands).astype(bf16)
            res = fitted(jnp.concatenate([center, side], axis=0))
            for h, lane in enumerate(lanes):
                fit[h, start:stop, 0:cols] = res[: n * cols, lane].reshape(n, cols, HALF)
                fit[h, start:stop, cols:span] = res[n * cols :, lane].reshape(n, SIDE, HALF)
        else:
            block = above_ref[...] if start < depth else below_ref[...]
            flat = block.astype(f32).reshape(n * span, bands).astype(bf16)
            res = fitted(flat)
            for h, lane in enumerate(lanes):
                fit[h, start:stop] = res[:, lane].reshape(n, span, HALF)

    row, col = lax.axis_index("narrow"), lax.axis_index("wide")
    at_top, at_bottom = row == 0, row == n_rows - 1
    at_left, at_right = col == 0, col == n_cols - 1
    per = span // SUB
    place = lax.broadcasted_iota(jnp.int32, (SUB, HALF), 0)
    keeps = {}
    for column, shut in ((cols - 1, at_right), (span - 1, at_left)):
        keep = jnp.where((place == column // per) & shut, 0.0, 1.0).astype(f32)
        keeps[column % per] = keeps[column % per] * keep if column % per in keeps else keep
    open_rows = {
        depth - 1: jnp.where(at_top, 0.0, 1.0),
        depth + rows - 1: jnp.where(at_bottom, 0.0, 1.0),
    }
    lanes = [slice(0, HALF), slice(HALF, LANES)]
    fields = [fit, field_a, field_b]

    def natural(ref, h, r):
        return [ref[h, r, pl.ds(w, SUB, stride=per), :] for w in range(per)]

    def spread(ref, h, r):
        return [ref[h, r, w * SUB : (w + 1) * SUB, :] for w in range(per)]

    def slopes(now, later, open_row=None):
        follow = now[1:] + [pltpu.roll(now[0], SUB - 1, 0)]
        downs, acrosses = [], []
        for w in range(per):
            down = later[w] - now[w]
            if open_row is not None:
                down = down * open_row
            across = follow[w] - now[w]
            if w in keeps:
                across = across * keeps[w]
            inverse = lax.rsqrt(down * down + (across * across + 4.0))
            downs.append(down * inverse)
            acrosses.append(across * inverse)
        return downs, acrosses

    def advance(base, before, down, across):
        behind = [pltpu.roll(across[-1], 1, 0)] + across[:-1]
        return [
            base[w] + ((down[w] - before[w]) + (across[w] - behind[w])) for w in range(per)
        ]

    def put(ref, h, r, value):
        for w in range(per):
            ref[h, r, w * SUB : (w + 1) * SUB, :] = value[w]

    tall = rows + 2 * depth
    groups = [(0, depth)]
    for n in FIT_ROWS:
        groups.append((groups[-1][1], groups[-1][1] + n))
    groups += [(depth + rows, tall)]
    ready = 0
    befores = [None] * len(lanes)
    for r in range(tall - 1):
        while ready < len(groups) and groups[ready][0] <= r + 1 + AHEAD:
            fit_rows(*groups[ready])
            ready += 1
            if ready == 4:
                project()
        for h in range(len(lanes)):
            now = natural(fit, h, r)
            down, across = slopes(now, natural(fit, h, r + 1), open_rows.get(r))
            if r > 0:
                put(field_a, h, r, advance(now, befores[h], down, across))
            befores[h] = down

    def step(s, first, trips, unroll):
        source, final = fields[s], s == TV_ITERS - 1

        @pl.when(at_top)
        def _():
            source[:, depth - 1] = source[:, depth]

        @pl.when(at_bottom)
        def _():
            source[:, depth + rows] = source[:, depth + rows - 1]

        def block_step(n, carry):
            carry = list(carry)
            for inner in range(unroll):
                r = first + n * unroll + inner
                for h, lane in enumerate(lanes):
                    now, before = carry[2 * h], carry[2 * h + 1]
                    later = spread(source, h, r + 1)
                    down, across = slopes(now, later)
                    base = [0.5 * (x + y) for x, y in zip(now, natural(fit, h, r))]
                    value = advance(base, before, down, across)
                    if final:
                        for w in range(per):
                            field_a[h, r, pl.ds(w, SUB, stride=per), :] = value[w]
                        result = (field_a[h, r, 0:cols, :] * 0.25).astype(bf16)
                        width = min(lane.stop, bands) - lane.start
                        out_stage[r - depth, :, lane.start : lane.start + width] = result[:, :width]
                    else:
                        put(fields[s + 1], h, r, value)
                    carry[2 * h], carry[2 * h + 1] = later, down
                if final and inner % OUT_ROWS == OUT_ROWS - 1:
                    out_copy(n * (unroll // OUT_ROWS) + inner // OUT_ROWS).start()
            return tuple(carry)

        carry = []
        for h in range(len(lanes)):
            before, now = spread(source, h, first - 1), spread(source, h, first)
            carry += [now, slopes(before, now)[0]]
        lax.fori_loop(0, trips, block_step, tuple(carry))

    step(1, 2, (rows + 2) // TV_ROWS[0], TV_ROWS[0])
    step(2, depth, rows // TV_ROWS[1], TV_ROWS[1])
    proj_copy.wait()
    for n in range(rows // OUT_ROWS):
        out_copy(n).wait()


def start_basis():
    bands = np.arange(BANDS, dtype=np.float32)[None, :]
    cols = np.arange(RANK, dtype=np.float32)[:, None]
    angle = np.float32(np.pi) * (bands + np.float32(0.5)) * cols / np.float32(BANDS)
    return np.pad(np.cos(angle).astype(np.float32), ((0, 0), (0, LANES - BANDS)))


def neighbours(block, axis, dim, width):
    count = lax.axis_size(axis)
    size = block.shape[dim]
    head = lax.slice_in_dim(block, 0, width, axis=dim)
    tail = lax.slice_in_dim(block, size - width, size, axis=dim)
    before = lax.ppermute(tail, axis, [(i, i + 1) for i in range(count - 1)])
    after = lax.ppermute(head, axis, [(i + 1, i) for i in range(count - 1)])
    return before, after


def exchange(pieces, axes):
    return lax.all_to_all(pieces, axes, split_axis=0, concat_axis=0)


def body(cube):
    n_rows = lax.axis_size("narrow")
    n_cols = lax.axis_size("wide")
    count = n_rows * n_cols
    rows, cols, bands = cube.shape
    depth = TV_ITERS
    axes = ("narrow", "wide")

    tall_packed = -(-bands // count) * count
    pieces = 2 if rows % 2 == 0 else 1
    packed = pl.pallas_call(
        gram_kernel,
        in_specs=[pl.BlockSpec(memory_space=pl.ANY)],
        out_shape=jax.ShapeDtypeStruct((tall_packed, HALF), f32),
        scratch_shapes=[
            pltpu.VMEM(cube.shape, cube.dtype),
            pltpu.VMEM((LANES, LANES), f32),
            pltpu.SemaphoreType.DMA((pieces,)),
        ],
        compiler_params=pltpu.CompilerParams(vmem_limit_bytes=62 * 2**20),
    )(cube)
    packed, cube = lax.optimization_barrier((packed, cube))
    left, right = neighbours(cube, "wide", 1, depth)
    vmem = pl.BlockSpec(memory_space=pltpu.VMEM)
    pieces_shape = (count, 1, tall_packed // count * HALF)
    part = exchange(packed.reshape(pieces_shape), axes).reshape(tall_packed, HALF)
    share = pl.pallas_call(
        functools.partial(sum_kernel, count),
        in_specs=[vmem],
        out_specs=vmem,
        out_shape=jax.ShapeDtypeStruct((tall_packed, HALF), f32),
        compiler_params=pltpu.CompilerParams(vmem_limit_bytes=16 * 2**20),
    )(part)
    gathered = exchange(share.reshape(pieces_shape), axes).reshape(tall_packed, HALF)

    tall, span = rows + 2 * depth, cols + SIDE
    up, down, side = pl.pallas_call(
        functools.partial(halo_kernel, depth),
        in_specs=[vmem] * 4,
        out_specs=[vmem] * 3,
        out_shape=[
            jax.ShapeDtypeStruct((depth, span, bands), bf16),
            jax.ShapeDtypeStruct((depth, span, bands), bf16),
            jax.ShapeDtypeStruct((rows, SIDE, bands), bf16),
        ],
        scratch_shapes=[pltpu.VMEM((rows, SIDE, bands), f32)],
        cost_estimate=pl.CostEstimate(flops=2**32, bytes_accessed=2**18, transcendentals=0),
        compiler_params=pltpu.CompilerParams(vmem_limit_bytes=16 * 2**20),
    )(left, right, cube[:depth], cube[rows - depth :])
    above = lax.ppermute(down, "narrow", [(i, i + 1) for i in range(n_rows - 1)])
    below = lax.ppermute(up, "narrow", [(i + 1, i) for i in range(n_rows - 1)])

    inv_count = 1.0 / (count * rows * cols)
    basis = pl.pallas_call(
        functools.partial(subspace_kernel, inv_count),
        in_specs=[vmem] * 2,
        out_specs=vmem,
        out_shape=jax.ShapeDtypeStruct((RANK, LANES), f32),
        scratch_shapes=[pltpu.VMEM((2, LANES, LANES), bf16)],
        cost_estimate=pl.CostEstimate(flops=2**32, bytes_accessed=2**18, transcendentals=0),
        compiler_params=pltpu.CompilerParams(vmem_limit_bytes=16 * 2**20),
    )(gathered, jnp.asarray(start_basis()))
    restored, projector = pl.pallas_call(
        functools.partial(main_kernel, depth, n_rows, n_cols),
        in_specs=[vmem] * 5,
        out_specs=[pl.BlockSpec(memory_space=pl.ANY)] * 2,
        out_shape=[
            jax.ShapeDtypeStruct((rows, cols, bands), bf16),
            jax.ShapeDtypeStruct((bands, bands), f32),
        ],
        scratch_shapes=[pltpu.VMEM((2, tall, span, HALF), f32)] * 3
        + [
            pltpu.VMEM((rows, cols, bands), bf16),
            pltpu.VMEM((bands, bands), f32),
            pltpu.SemaphoreType.DMA((rows // OUT_ROWS,)),
            pltpu.SemaphoreType.DMA,
        ],
        compiler_params=pltpu.CompilerParams(vmem_limit_bytes=48 * 2**20),
    )(basis, cube, above, below, side)
    return restored, projector


def solution(mesh):
    return jax.shard_map(
        body,
        mesh=mesh,
        in_specs=(P("narrow", "wide", None),),
        out_specs=(P("narrow", "wide", None), P()),
        check_vma=False,
    )
```

```python
import functools

import jax
import jax.numpy as jnp
import numpy as np
from jax import lax
from jax.experimental import pallas as pl
from jax.experimental.pallas import tpu as pltpu
from jax.sharding import PartitionSpec as P

BANDS = 224
RANK = 16
POWER_ITERS = 4
TV_ITERS = 3
LANES = 256
HALF = 128
TAIL = BANDS - HALF
SIDE = 8
SUB = 8
BLOCK = 8
FIT_ROWS = (2, 6, 8, 8, 8)
AHEAD = 4
OUT_ROWS = (8, 8, 8, 4, 2, 2)

f32 = jnp.float32
bf16 = jnp.bfloat16


def iotas(shape):
    return lax.broadcasted_iota(jnp.int32, shape, 0), lax.broadcasted_iota(jnp.int32, shape, 1)


def gram_kernel(cube_ref, packed_ref, block, full, sems):
    rows, cols, bands = cube_ref.shape
    pieces = sems.shape[0]
    high = rows // pieces

    def copy(n):
        part = pl.ds(n * high, high)
        return pltpu.make_async_copy(cube_ref.at[part], block.at[part], sems.at[n])

    for n in range(pieces):
        copy(n).start()
    full[HALF:, HALF:] = jnp.zeros((LANES - HALF, LANES - HALF), f32)
    total = None
    for n in range(pieces):
        copy(n).wait()
        flat = block[n * high : (n + 1) * high].reshape(high * cols, bands)
        term = lax.dot_general(flat, flat, (((0,), (0,)), ((), ())), preferred_element_type=f32)
        total = term if total is None else total + term
    full[0:bands, 0:bands] = total
    i, j = iotas((HALF, HALF))
    first = full[0:HALF, 0:HALF]
    second = pltpu.roll(full[HALF:LANES, HALF:LANES], 1, 1)
    packed_ref[0:HALF, :] = jnp.where(j <= i, first, second)
    packed_ref[HALF:bands, :] = full[HALF:bands, 0:HALF]
    if packed_ref.shape[0] > bands:
        packed_ref[bands:, :] = jnp.zeros((packed_ref.shape[0] - bands, HALF), f32)


def sum_kernel(count, pieces_ref, spread_ref):
    high = pieces_ref.shape[0] // count
    parts = [pieces_ref[n * high : (n + 1) * high, :] for n in range(count)]
    total = functools.reduce(jnp.add, parts)
    for n in range(count):
        spread_ref[n * high : (n + 1) * high, :] = total


def split3(x):
    high = x.astype(bf16)
    rest = x - high.astype(f32)
    mid = rest.astype(bf16)
    low = (rest - mid.astype(f32)).astype(bf16)
    return high, mid, low


def product(left, right, dims):
    def dot(a, b):
        return lax.dot_general(a, b, (dims, ((), ())), preferred_element_type=f32)

    n = left[0].shape[0]
    top = dot(jnp.concatenate(left, axis=0), right[0])
    middle = dot(jnp.concatenate(left[:2], axis=0), right[1])
    small = top[2 * n : 3 * n] + middle[n : 2 * n]
    if len(right) > 2:
        small = small + dot(left[0], right[2])
    return top[:n] + ((top[n : 2 * n] + middle[:n]) + small)


def unpack(packed, scale):
    i, j = iotas((HALF, HALF))
    merged = packed[0:HALF, :] * scale
    below = packed[HALF:BANDS, :] * scale
    below = jnp.concatenate([below, jnp.zeros((LANES - BANDS, HALF), f32)], axis=0)
    first = jnp.where(j <= i, merged, 0.0) + jnp.where(j < i, merged, 0.0).T
    moved = pltpu.roll(merged, HALF - 1, 1)
    inside = (i < TAIL) & (j < TAIL)
    second = jnp.where(inside & (j >= i), moved, 0.0) + jnp.where(inside & (j > i), moved, 0.0).T
    return jnp.concatenate(
        [
            jnp.concatenate([first, below.T], axis=1),
            jnp.concatenate([below, second], axis=1),
        ],
        axis=0,
    )


def orthonormal(grown, inner):
    row = lax.broadcasted_iota(jnp.int32, (RANK, HALF), 0)
    work = [
        jnp.concatenate([inner, jnp.zeros((RANK, HALF - RANK), f32)], axis=1),
        grown[:, :HALF],
        grown[:, HALF:],
    ]
    diagonal = jnp.ones((RANK, HALF), f32)
    for k in range(0, RANK, BLOCK):
        columns = [
            jnp.broadcast_to(work[0][:, k + c : k + c + 1], (RANK, HALF)) for c in range(BLOCK)
        ]
        tops = [[part[k + r : k + r + 1, :] for part in work] for r in range(BLOCK)]
        small = [
            [columns[c][k + r : k + r + 1, :] for c in range(r + 1)] for r in range(BLOCK)
        ]
        factors = []
        for j in range(BLOCK):
            pivot = small[j][j]
            inverse = pl.reciprocal(pivot, full_range=False)
            diagonal = jnp.where(row == k + j, pivot, diagonal)
            factor = jnp.where(row > k + j, columns[j] * inverse, 0.0)
            factors.append(factor)
            below = [small[i][j] for i in range(BLOCK) if i > j]
            for i in range(j + 1, BLOCK):
                ratio = small[i][j] * inverse
                for c in range(j + 1, i + 1):
                    small[i][c] = small[i][c] - ratio * below[c - j - 1]
                tops[i] = [x - ratio * y for x, y in zip(tops[i], tops[j])]
                columns[i] = columns[i] - factor * below[i - j - 1]
        for n in range(len(work)):
            if n > 0 or k + BLOCK < RANK:
                for j in range(BLOCK):
                    work[n] = work[n] - factors[j] * tops[j][n]
    scale = lax.rsqrt(diagonal)
    return jnp.concatenate([work[1] * scale, work[2] * scale], axis=1)


def subspace(gram, start, held):
    for n, part in enumerate(split3(gram)[:2]):
        held[n] = part

    def times_gram(pieces):
        return product(pieces, [held[0], held[1]], ((1,), (0,)))

    def iterate(_, grown):
        pieces = split3(grown)
        inner = product(pieces, pieces, ((1,), (1,)))
        return orthonormal(times_gram(pieces), inner)

    grown = lax.fori_loop(0, POWER_ITERS - 1, iterate, times_gram(split3(start)))
    pieces = split3(grown)
    return orthonormal(grown, product(pieces, pieces, ((1,), (1,))))


def halo_kernel(depth, left_ref, right_ref, top_ref, bottom_ref, up_ref, down_ref, side_ref, wide):
    rows, cols = side_ref.shape[0], top_ref.shape[1]
    wide[...] = jnp.zeros_like(wide)
    wide[:, 0:depth] = right_ref[...].astype(f32)
    wide[:, SIDE - depth :] = left_ref[...].astype(f32)
    side = wide[...].astype(bf16)
    side_ref[...] = side
    up_ref[:, 0:cols] = top_ref[...]
    up_ref[:, cols:] = side[:depth]
    down_ref[:, 0:cols] = bottom_ref[...]
    down_ref[:, cols:] = side[rows - depth :]


def subspace_kernel(inv_count, packed_ref, start_ref, basis_ref, held):
    basis_ref[...] = subspace(unpack(packed_ref[...], inv_count), start_ref[...], held)


def main_kernel(
    depth, n_rows, n_cols, basis_ref, mid_ref, above_ref, below_ref, side_ref,
    out_ref, proj_ref, fit, field_a, field_b, out_stage, proj_stage, out_sems, proj_sem
):
    rows, cols, bands = mid_ref.shape
    span = cols + SIDE
    proj_copy = pltpu.make_async_copy(proj_stage, proj_ref, proj_sem)

    def out_copy(n):
        part = pl.ds(sum(OUT_ROWS[:n]), OUT_ROWS[n])
        return pltpu.make_async_copy(out_stage.at[part], out_ref.at[part], out_sems.at[n])

    high, mid, low = split3(basis_ref[...])
    tn = (((0,), (0,)), ((), ()))
    mixed = lax.dot_general(
        jnp.concatenate([high, high, high], axis=0),
        jnp.concatenate([high, mid, low], axis=0),
        tn,
        preferred_element_type=f32,
    )
    mixed = mixed * 4.0
    mixed_high = mixed.astype(bf16)
    mixed_low = (mixed - mixed_high.astype(f32)).astype(bf16)
    mixed_both = jnp.concatenate([mixed_high, mixed_low], axis=0)

    def fitted(flat):
        padded = jnp.concatenate([flat, jnp.zeros((flat.shape[0], LANES - bands), bf16)], axis=1)
        both = jnp.concatenate([padded, padded], axis=1)
        return jnp.dot(both, mixed_both, preferred_element_type=f32)

    def project():
        right = jnp.concatenate([high, high, high, mid, mid, low], axis=0)
        left = jnp.concatenate([high, mid, low, high, mid, high], axis=0)
        full = lax.dot_general(left, right, tn, preferred_element_type=f32)
        proj_stage[...] = full[:bands, :bands]
        proj_copy.start()

    def fit_rows(start, stop):
        n = stop - start
        if depth <= start < depth + rows:
            part = slice(start - depth, stop - depth)
            center = mid_ref[part].reshape(n * cols, bands)
            side = side_ref[part].astype(f32).reshape(n * SIDE, bands).astype(bf16)
            res = fitted(jnp.concatenate([center, side], axis=0))
            for h, lane in enumerate(lanes):
                fit[h, start:stop, 0:cols] = res[: n * cols, lane].reshape(n, cols, HALF)
                fit[h, start:stop, cols:span] = res[n * cols :, lane].reshape(n, SIDE, HALF)
        else:
            block = above_ref[...] if start < depth else below_ref[...]
            flat = block.astype(f32).reshape(n * span, bands).astype(bf16)
            res = fitted(flat)
            for h, lane in enumerate(lanes):
                fit[h, start:stop] = res[:, lane].reshape(n, span, HALF)

    row, col = lax.axis_index("narrow"), lax.axis_index("wide")
    at_top, at_bottom = row == 0, row == n_rows - 1
    at_left, at_right = col == 0, col == n_cols - 1
    per = span // SUB
    place = lax.broadcasted_iota(jnp.int32, (SUB, HALF), 0)
    keeps = {}
    for column, shut in ((cols - 1, at_right), (span - 1, at_left)):
        keep = jnp.where((place == column // per) & shut, 0.0, 1.0).astype(f32)
        keeps[column % per] = keeps[column % per] * keep if column % per in keeps else keep
    open_rows = {
        depth - 1: jnp.where(at_top, 0.0, 1.0),
        depth + rows - 1: jnp.where(at_bottom, 0.0, 1.0),
    }
    lanes = [slice(0, HALF), slice(HALF, LANES)]
    fields = [fit, field_a, field_b]

    def natural(ref, h, r):
        return [ref[h, r, pl.ds(w, SUB, stride=per), :] for w in range(per)]

    def spread(ref, h, r):
        return [ref[h, r, w * SUB : (w + 1) * SUB, :] for w in range(per)]

    def slopes(now, later, open_row=None):
        follow = now[1:] + [pltpu.roll(now[0], SUB - 1, 0)]
        downs, acrosses = [], []
        for w in range(per):
            down = later[w] - now[w]
            if open_row is not None:
                down = down * open_row
            across = follow[w] - now[w]
            if w in keeps:
                across = across * keeps[w]
            inverse = lax.rsqrt(down * down + (across * across + 4.0))
            downs.append(down * inverse)
            acrosses.append(across * inverse)
        return downs, acrosses

    def advance(base, before, down, across):
        behind = [pltpu.roll(across[-1], 1, 0)] + across[:-1]
        return [
            base[w] + ((down[w] - before[w]) + (across[w] - behind[w])) for w in range(per)
        ]

    def put(ref, h, r, value):
        for w in range(per):
            ref[h, r, w * SUB : (w + 1) * SUB, :] = value[w]

    tall = rows + 2 * depth
    groups = [(0, depth)]
    for n in FIT_ROWS:
        groups.append((groups[-1][1], groups[-1][1] + n))
    groups += [(depth + rows, tall)]
    ready = 0
    befores = [None] * len(lanes)
    for r in range(tall - 1):
        while ready < len(groups) and groups[ready][0] <= r + 1 + AHEAD:
            fit_rows(*groups[ready])
            ready += 1
            if ready == 4:
                project()
        for h in range(len(lanes)):
            now = natural(fit, h, r)
            down, across = slopes(now, natural(fit, h, r + 1), open_rows.get(r))
            if r > 0:
                put(field_a, h, r, advance(now, befores[h], down, across))
            befores[h] = down

    sent = 0
    for s in range(1, TV_ITERS):
        source = fields[s]
        nows = [spread(source, h, s) for h in range(len(lanes))]
        befores = [None] * len(lanes)
        for r in range(s, tall - 1 - s):
            for h, lane in enumerate(lanes):
                now, later = nows[h], spread(source, h, r + 1)
                down, across = slopes(now, later, open_rows.get(r))
                if r > s:
                    base = [0.5 * (x + y) for x, y in zip(now, natural(fit, h, r))]
                    value = advance(base, befores[h], down, across)
                    if s < TV_ITERS - 1:
                        put(fields[s + 1], h, r, value)
                    else:
                        for w in range(per):
                            field_a[h, r, pl.ds(w, SUB, stride=per), :] = value[w]
                        result = (field_a[h, r, 0:cols, :] * 0.25).astype(bf16)
                        width = min(lane.stop, bands) - lane.start
                        out_stage[r - depth, :, lane.start : lane.start + width] = result[:, :width]
                nows[h], befores[h] = later, down
            if s == TV_ITERS - 1 and r - depth + 1 == sum(OUT_ROWS[: sent + 1]):
                out_copy(sent).start()
                sent += 1
    proj_copy.wait()
    for n in range(len(OUT_ROWS)):
        out_copy(n).wait()


def start_basis():
    bands = np.arange(BANDS, dtype=np.float32)[None, :]
    cols = np.arange(RANK, dtype=np.float32)[:, None]
    angle = np.float32(np.pi) * (bands + np.float32(0.5)) * cols / np.float32(BANDS)
    return np.pad(np.cos(angle).astype(np.float32), ((0, 0), (0, LANES - BANDS)))


def neighbours(block, axis, dim, width):
    count = lax.axis_size(axis)
    size = block.shape[dim]
    head = lax.slice_in_dim(block, 0, width, axis=dim)
    tail = lax.slice_in_dim(block, size - width, size, axis=dim)
    before = lax.ppermute(tail, axis, [(i, i + 1) for i in range(count - 1)])
    after = lax.ppermute(head, axis, [(i + 1, i) for i in range(count - 1)])
    return before, after


def exchange(pieces, axes):
    return lax.all_to_all(pieces, axes, split_axis=0, concat_axis=0)


def body(cube):
    n_rows = lax.axis_size("narrow")
    n_cols = lax.axis_size("wide")
    count = n_rows * n_cols
    rows, cols, bands = cube.shape
    depth = TV_ITERS
    axes = ("narrow", "wide")

    tall_packed = -(-bands // count) * count
    pieces = 2 if rows % 2 == 0 else 1
    packed = pl.pallas_call(
        gram_kernel,
        in_specs=[pl.BlockSpec(memory_space=pl.ANY)],
        out_shape=jax.ShapeDtypeStruct((tall_packed, HALF), f32),
        scratch_shapes=[
            pltpu.VMEM(cube.shape, cube.dtype),
            pltpu.VMEM((LANES, LANES), f32),
            pltpu.SemaphoreType.DMA((pieces,)),
        ],
        compiler_params=pltpu.CompilerParams(vmem_limit_bytes=62 * 2**20),
    )(cube)
    packed, cube = lax.optimization_barrier((packed, cube))
    left, right = neighbours(cube, "wide", 1, depth)
    vmem = pl.BlockSpec(memory_space=pltpu.VMEM)
    pieces_shape = (count, 1, tall_packed // count * HALF)
    part = exchange(packed.reshape(pieces_shape), axes).reshape(tall_packed, HALF)
    share = pl.pallas_call(
        functools.partial(sum_kernel, count),
        in_specs=[vmem],
        out_specs=vmem,
        out_shape=jax.ShapeDtypeStruct((tall_packed, HALF), f32),
        compiler_params=pltpu.CompilerParams(vmem_limit_bytes=16 * 2**20),
    )(part)
    gathered = exchange(share.reshape(pieces_shape), axes).reshape(tall_packed, HALF)

    tall, span = rows + 2 * depth, cols + SIDE
    up, down, side = pl.pallas_call(
        functools.partial(halo_kernel, depth),
        in_specs=[vmem] * 4,
        out_specs=[vmem] * 3,
        out_shape=[
            jax.ShapeDtypeStruct((depth, span, bands), bf16),
            jax.ShapeDtypeStruct((depth, span, bands), bf16),
            jax.ShapeDtypeStruct((rows, SIDE, bands), bf16),
        ],
        scratch_shapes=[pltpu.VMEM((rows, SIDE, bands), f32)],
        cost_estimate=pl.CostEstimate(flops=2**32, bytes_accessed=2**18, transcendentals=0),
        compiler_params=pltpu.CompilerParams(vmem_limit_bytes=16 * 2**20),
    )(left, right, cube[:depth], cube[rows - depth :])
    above = lax.ppermute(down, "narrow", [(i, i + 1) for i in range(n_rows - 1)])
    below = lax.ppermute(up, "narrow", [(i + 1, i) for i in range(n_rows - 1)])

    inv_count = 1.0 / (count * rows * cols)
    basis = pl.pallas_call(
        functools.partial(subspace_kernel, inv_count),
        in_specs=[vmem] * 2,
        out_specs=vmem,
        out_shape=jax.ShapeDtypeStruct((RANK, LANES), f32),
        scratch_shapes=[pltpu.VMEM((2, LANES, LANES), bf16)],
        cost_estimate=pl.CostEstimate(flops=2**32, bytes_accessed=2**18, transcendentals=0),
        compiler_params=pltpu.CompilerParams(vmem_limit_bytes=16 * 2**20),
    )(gathered, jnp.asarray(start_basis()))
    restored, projector = pl.pallas_call(
        functools.partial(main_kernel, depth, n_rows, n_cols),
        in_specs=[vmem] * 5,
        out_specs=[pl.BlockSpec(memory_space=pl.ANY)] * 2,
        out_shape=[
            jax.ShapeDtypeStruct((rows, cols, bands), bf16),
            jax.ShapeDtypeStruct((bands, bands), f32),
        ],
        scratch_shapes=[pltpu.VMEM((2, tall, span, HALF), f32)] * 3
        + [
            pltpu.VMEM((rows, cols, bands), bf16),
            pltpu.VMEM((bands, bands), f32),
            pltpu.SemaphoreType.DMA((len(OUT_ROWS),)),
            pltpu.SemaphoreType.DMA,
        ],
        compiler_params=pltpu.CompilerParams(vmem_limit_bytes=48 * 2**20),
    )(basis, cube, above, below, side)
    return restored, projector


def solution(mesh):
    return jax.shard_map(
        body,
        mesh=mesh,
        in_specs=(P("narrow", "wide", None),),
        out_specs=(P("narrow", "wide", None), P()),
        check_vma=False,
    )
```

```python
import functools

import jax
import jax.numpy as jnp
import numpy as np
from jax import lax
from jax.experimental import pallas as pl
from jax.experimental.pallas import tpu as pltpu
from jax.sharding import PartitionSpec as P

BANDS = 224
RANK = 16
POWER_ITERS = 4
TV_ITERS = 3
LANES = 256
HALF = 128
TAIL = BANDS - HALF
SIDE = 8
SUB = 8
BLOCK = 8
FIT_ROWS = (2, 6, 8, 8, 8)
AHEAD = 4
TV_ROWS = (17, 16)
OUT_ROWS = 4

f32 = jnp.float32
bf16 = jnp.bfloat16


def iotas(shape):
    return lax.broadcasted_iota(jnp.int32, shape, 0), lax.broadcasted_iota(jnp.int32, shape, 1)


def gram_kernel(cube_ref, packed_ref, block, full, sems):
    rows, cols, bands = cube_ref.shape
    pieces = sems.shape[0]
    high = rows // pieces

    def copy(n):
        part = pl.ds(n * high, high)
        return pltpu.make_async_copy(cube_ref.at[part], block.at[part], sems.at[n])

    for n in range(pieces):
        copy(n).start()
    full[HALF:, HALF:] = jnp.zeros((LANES - HALF, LANES - HALF), f32)
    total = None
    for n in range(pieces):
        copy(n).wait()
        flat = block[n * high : (n + 1) * high].reshape(high * cols, bands)
        term = lax.dot_general(flat, flat, (((0,), (0,)), ((), ())), preferred_element_type=f32)
        total = term if total is None else total + term
    full[0:bands, 0:bands] = total
    i, j = iotas((HALF, HALF))
    first = full[0:HALF, 0:HALF]
    second = pltpu.roll(full[HALF:LANES, HALF:LANES], 1, 1)
    packed_ref[0:HALF, :] = jnp.where(j <= i, first, second)
    packed_ref[HALF:bands, :] = full[HALF:bands, 0:HALF]
    if packed_ref.shape[0] > bands:
        packed_ref[bands:, :] = jnp.zeros((packed_ref.shape[0] - bands, HALF), f32)


def sum_kernel(count, pieces_ref, spread_ref):
    high = pieces_ref.shape[0] // count
    parts = [pieces_ref[n * high : (n + 1) * high, :] for n in range(count)]
    total = functools.reduce(jnp.add, parts)
    for n in range(count):
        spread_ref[n * high : (n + 1) * high, :] = total


def split3(x):
    high = x.astype(bf16)
    rest = x - high.astype(f32)
    mid = rest.astype(bf16)
    low = (rest - mid.astype(f32)).astype(bf16)
    return high, mid, low


def product(left, right, dims):
    def dot(a, b):
        return lax.dot_general(a, b, (dims, ((), ())), preferred_element_type=f32)

    n = left[0].shape[0]
    top = dot(jnp.concatenate(left, axis=0), right[0])
    middle = dot(jnp.concatenate(left[:2], axis=0), right[1])
    small = top[2 * n : 3 * n] + middle[n : 2 * n]
    if len(right) > 2:
        small = small + dot(left[0], right[2])
    return top[:n] + ((top[n : 2 * n] + middle[:n]) + small)


def unpack(packed, scale):
    i, j = iotas((HALF, HALF))
    merged = packed[0:HALF, :] * scale
    below = packed[HALF:BANDS, :] * scale
    below = jnp.concatenate([below, jnp.zeros((LANES - BANDS, HALF), f32)], axis=0)
    first = jnp.where(j <= i, merged, 0.0) + jnp.where(j < i, merged, 0.0).T
    moved = pltpu.roll(merged, HALF - 1, 1)
    inside = (i < TAIL) & (j < TAIL)
    second = jnp.where(inside & (j >= i), moved, 0.0) + jnp.where(inside & (j > i), moved, 0.0).T
    return jnp.concatenate(
        [
            jnp.concatenate([first, below.T], axis=1),
            jnp.concatenate([below, second], axis=1),
        ],
        axis=0,
    )


def orthonormal(grown, inner):
    row = lax.broadcasted_iota(jnp.int32, (RANK, HALF), 0)
    work = [
        jnp.concatenate([inner, jnp.zeros((RANK, HALF - RANK), f32)], axis=1),
        grown[:, :HALF],
        grown[:, HALF:],
    ]
    diagonal = jnp.ones((RANK, HALF), f32)
    for k in range(0, RANK, BLOCK):
        columns = [
            jnp.broadcast_to(work[0][:, k + c : k + c + 1], (RANK, HALF)) for c in range(BLOCK)
        ]
        tops = [[part[k + r : k + r + 1, :] for part in work] for r in range(BLOCK)]
        small = [
            [columns[c][k + r : k + r + 1, :] for c in range(r + 1)] for r in range(BLOCK)
        ]
        factors = []
        for j in range(BLOCK):
            pivot = small[j][j]
            inverse = pl.reciprocal(pivot, full_range=False)
            diagonal = jnp.where(row == k + j, pivot, diagonal)
            factor = jnp.where(row > k + j, columns[j] * inverse, 0.0)
            factors.append(factor)
            below = [small[i][j] for i in range(BLOCK) if i > j]
            for i in range(j + 1, BLOCK):
                ratio = small[i][j] * inverse
                for c in range(j + 1, i + 1):
                    small[i][c] = small[i][c] - ratio * below[c - j - 1]
                tops[i] = [x - ratio * y for x, y in zip(tops[i], tops[j])]
                columns[i] = columns[i] - factor * below[i - j - 1]
        for n in range(len(work)):
            if n > 0 or k + BLOCK < RANK:
                for j in range(BLOCK):
                    work[n] = work[n] - factors[j] * tops[j][n]
    scale = lax.rsqrt(diagonal)
    return jnp.concatenate([work[1] * scale, work[2] * scale], axis=1)


def subspace(gram, start, held):
    for n, part in enumerate(split3(gram)[:2]):
        held[n] = part

    def times_gram(pieces):
        return product(pieces, [held[0], held[1]], ((1,), (0,)))

    def iterate(_, grown):
        pieces = split3(grown)
        inner = product(pieces, pieces, ((1,), (1,)))
        return orthonormal(times_gram(pieces), inner)

    grown = lax.fori_loop(0, POWER_ITERS - 1, iterate, times_gram(split3(start)))
    pieces = split3(grown)
    return orthonormal(grown, product(pieces, pieces, ((1,), (1,))))


def halo_kernel(depth, left_ref, right_ref, top_ref, bottom_ref, up_ref, down_ref, side_ref, wide):
    rows, cols = side_ref.shape[0], top_ref.shape[1]
    wide[...] = jnp.zeros_like(wide)
    wide[:, 0:depth] = right_ref[...].astype(f32)
    wide[:, SIDE - depth :] = left_ref[...].astype(f32)
    side = wide[...].astype(bf16)
    side_ref[...] = side
    up_ref[:, 0:cols] = top_ref[...]
    up_ref[:, cols:] = side[:depth]
    down_ref[:, 0:cols] = bottom_ref[...]
    down_ref[:, cols:] = side[rows - depth :]


def subspace_kernel(inv_count, packed_ref, start_ref, basis_ref, held):
    basis_ref[...] = subspace(unpack(packed_ref[...], inv_count), start_ref[...], held)


def main_kernel(
    depth, n_rows, n_cols, basis_ref, mid_ref, above_ref, below_ref, side_ref,
    out_ref, proj_ref, fit, field_a, field_b, out_stage, proj_stage, out_sems, proj_sem
):
    rows, cols, bands = mid_ref.shape
    span = cols + SIDE
    proj_copy = pltpu.make_async_copy(proj_stage, proj_ref, proj_sem)

    def out_copy(n):
        part = pl.ds(n * OUT_ROWS, OUT_ROWS)
        return pltpu.make_async_copy(out_stage.at[part], out_ref.at[part], out_sems.at[n])

    high, mid, low = split3(basis_ref[...])
    tn = (((0,), (0,)), ((), ()))
    mixed = lax.dot_general(
        jnp.concatenate([high, high, high], axis=0),
        jnp.concatenate([high, mid, low], axis=0),
        tn,
        preferred_element_type=f32,
    )
    mixed = mixed * 4.0
    mixed_high = mixed.astype(bf16)
    mixed_low = (mixed - mixed_high.astype(f32)).astype(bf16)
    mixed_both = jnp.concatenate([mixed_high, mixed_low], axis=0)

    def fitted(flat):
        padded = jnp.concatenate([flat, jnp.zeros((flat.shape[0], LANES - bands), bf16)], axis=1)
        both = jnp.concatenate([padded, padded], axis=1)
        return jnp.dot(both, mixed_both, preferred_element_type=f32)

    def project():
        right = jnp.concatenate([high, high, high, mid, mid, low], axis=0)
        left = jnp.concatenate([high, mid, low, high, mid, high], axis=0)
        full = lax.dot_general(left, right, tn, preferred_element_type=f32)
        proj_stage[...] = full[:bands, :bands]
        proj_copy.start()

    def fit_rows(start, stop):
        n = stop - start
        if depth <= start < depth + rows:
            part = slice(start - depth, stop - depth)
            center = mid_ref[part].reshape(n * cols, bands)
            side = side_ref[part].astype(f32).reshape(n * SIDE, bands).astype(bf16)
            res = fitted(jnp.concatenate([center, side], axis=0))
            for h, lane in enumerate(lanes):
                fit[h, start:stop, 0:cols] = res[: n * cols, lane].reshape(n, cols, HALF)
                fit[h, start:stop, cols:span] = res[n * cols :, lane].reshape(n, SIDE, HALF)
        else:
            block = above_ref[...] if start < depth else below_ref[...]
            flat = block.astype(f32).reshape(n * span, bands).astype(bf16)
            res = fitted(flat)
            for h, lane in enumerate(lanes):
                fit[h, start:stop] = res[:, lane].reshape(n, span, HALF)

    row, col = lax.axis_index("narrow"), lax.axis_index("wide")
    at_top, at_bottom = row == 0, row == n_rows - 1
    at_left, at_right = col == 0, col == n_cols - 1
    per = span // SUB
    place = lax.broadcasted_iota(jnp.int32, (SUB, HALF), 0)
    keeps = {}
    for column, shut in ((cols - 1, at_right), (span - 1, at_left)):
        keep = jnp.where((place == column // per) & shut, 0.0, 1.0).astype(f32)
        keeps[column % per] = keeps[column % per] * keep if column % per in keeps else keep
    open_rows = {
        depth - 1: jnp.where(at_top, 0.0, 1.0),
        depth + rows - 1: jnp.where(at_bottom, 0.0, 1.0),
    }
    lanes = [slice(0, HALF), slice(HALF, LANES)]
    fields = [fit, field_a, field_b]

    def natural(ref, h, r):
        return [ref[h, r, pl.ds(w, SUB, stride=per), :] for w in range(per)]

    def spread(ref, h, r):
        return [ref[h, r, w * SUB : (w + 1) * SUB, :] for w in range(per)]

    def slopes(now, later, open_row=None):
        follow = now[1:] + [pltpu.roll(now[0], SUB - 1, 0)]
        downs, acrosses = [], []
        for w in range(per):
            down = later[w] - now[w]
            if open_row is not None:
                down = down * open_row
            across = follow[w] - now[w]
            if w in keeps:
                across = across * keeps[w]
            inverse = lax.rsqrt(down * down + (across * across + 4.0))
            downs.append(down * inverse)
            acrosses.append(across * inverse)
        return downs, acrosses

    def advance(base, before, down, across):
        behind = [pltpu.roll(across[-1], 1, 0)] + across[:-1]
        return [
            base[w] + ((down[w] - before[w]) + (across[w] - behind[w])) for w in range(per)
        ]

    def put(ref, h, r, value):
        for w in range(per):
            ref[h, r, w * SUB : (w + 1) * SUB, :] = value[w]

    tall = rows + 2 * depth
    groups = [(0, depth)]
    for n in FIT_ROWS:
        groups.append((groups[-1][1], groups[-1][1] + n))
    groups += [(depth + rows, tall)]
    ready = 0
    befores = [None] * len(lanes)
    for r in range(tall - 1):
        while ready < len(groups) and groups[ready][0] <= r + 1 + AHEAD:
            fit_rows(*groups[ready])
            ready += 1
            if ready == 4:
                project()
        for h in range(len(lanes)):
            now = natural(fit, h, r)
            down, across = slopes(now, natural(fit, h, r + 1), open_rows.get(r))
            if r > 0:
                put(field_a, h, r, advance(now, befores[h], down, across))
            befores[h] = down

    def step(s, first, trips, unroll):
        source, final = fields[s], s == TV_ITERS - 1

        @pl.when(at_top)
        def _():
            source[:, depth - 1] = source[:, depth]

        @pl.when(at_bottom)
        def _():
            source[:, depth + rows] = source[:, depth + rows - 1]

        def block_step(n, carry):
            carry = list(carry)
            for inner in range(unroll):
                r = first + n * unroll + inner
                for h, lane in enumerate(lanes):
                    now, before = carry[2 * h], carry[2 * h + 1]
                    later = spread(source, h, r + 1)
                    down, across = slopes(now, later)
                    base = [0.5 * (x + y) for x, y in zip(now, natural(fit, h, r))]
                    value = advance(base, before, down, across)
                    if final:
                        for w in range(per):
                            field_a[h, r, pl.ds(w, SUB, stride=per), :] = value[w]
                        result = (field_a[h, r, 0:cols, :] * 0.25).astype(bf16)
                        width = min(lane.stop, bands) - lane.start
                        out_stage[r - depth, :, lane.start : lane.start + width] = result[:, :width]
                    else:
                        put(fields[s + 1], h, r, value)
                    carry[2 * h], carry[2 * h + 1] = later, down
                if final and inner % OUT_ROWS == OUT_ROWS - 1:
                    out_copy(n * (unroll // OUT_ROWS) + inner // OUT_ROWS).start()
            return tuple(carry)

        carry = []
        for h in range(len(lanes)):
            before, now = spread(source, h, first - 1), spread(source, h, first)
            carry += [now, slopes(before, now)[0]]
        lax.fori_loop(0, trips, block_step, tuple(carry))

    step(1, 2, (rows + 2) // TV_ROWS[0], TV_ROWS[0])
    step(2, depth, rows // TV_ROWS[1], TV_ROWS[1])
    proj_copy.wait()
    for n in range(rows // OUT_ROWS):
        out_copy(n).wait()


def start_basis():
    bands = np.arange(BANDS, dtype=np.float32)[None, :]
    cols = np.arange(RANK, dtype=np.float32)[:, None]
    angle = np.float32(np.pi) * (bands + np.float32(0.5)) * cols / np.float32(BANDS)
    return np.pad(np.cos(angle).astype(np.float32), ((0, 0), (0, LANES - BANDS)))


def neighbours(block, axis, dim, width):
    count = lax.axis_size(axis)
    size = block.shape[dim]
    head = lax.slice_in_dim(block, 0, width, axis=dim)
    tail = lax.slice_in_dim(block, size - width, size, axis=dim)
    before = lax.ppermute(tail, axis, [(i, i + 1) for i in range(count - 1)])
    after = lax.ppermute(head, axis, [(i + 1, i) for i in range(count - 1)])
    return before, after


def exchange(pieces, axes):
    count = pieces.shape[0]
    first = lax.axis_size(axes[1]) // 2
    order = [(n + first) % count for n in range(count)]
    return lax.all_to_all(pieces, axes, split_axis=0, concat_axis=0, axis_index_groups=[order])


def body(cube):
    n_rows = lax.axis_size("narrow")
    n_cols = lax.axis_size("wide")
    count = n_rows * n_cols
    rows, cols, bands = cube.shape
    depth = TV_ITERS
    axes = ("narrow", "wide")

    tall_packed = -(-bands // count) * count
    pieces = 2 if rows % 2 == 0 else 1
    packed = pl.pallas_call(
        gram_kernel,
        in_specs=[pl.BlockSpec(memory_space=pl.ANY)],
        out_shape=jax.ShapeDtypeStruct((tall_packed, HALF), f32),
        scratch_shapes=[
            pltpu.VMEM(cube.shape, cube.dtype),
            pltpu.VMEM((LANES, LANES), f32),
            pltpu.SemaphoreType.DMA((pieces,)),
        ],
        compiler_params=pltpu.CompilerParams(vmem_limit_bytes=62 * 2**20),
    )(cube)
    packed, cube = lax.optimization_barrier((packed, cube))
    left, right = neighbours(cube, "wide", 1, depth)
    vmem = pl.BlockSpec(memory_space=pltpu.VMEM)
    pieces_shape = (count, 1, tall_packed // count * HALF)
    part = exchange(packed.reshape(pieces_shape), axes).reshape(tall_packed, HALF)
    share = pl.pallas_call(
        functools.partial(sum_kernel, count),
        in_specs=[vmem],
        out_specs=vmem,
        out_shape=jax.ShapeDtypeStruct((tall_packed, HALF), f32),
        compiler_params=pltpu.CompilerParams(vmem_limit_bytes=16 * 2**20),
    )(part)
    gathered = exchange(share.reshape(pieces_shape), axes).reshape(tall_packed, HALF)

    tall, span = rows + 2 * depth, cols + SIDE
    up, down, side = pl.pallas_call(
        functools.partial(halo_kernel, depth),
        in_specs=[vmem] * 4,
        out_specs=[vmem] * 3,
        out_shape=[
            jax.ShapeDtypeStruct((depth, span, bands), bf16),
            jax.ShapeDtypeStruct((depth, span, bands), bf16),
            jax.ShapeDtypeStruct((rows, SIDE, bands), bf16),
        ],
        scratch_shapes=[pltpu.VMEM((rows, SIDE, bands), f32)],
        cost_estimate=pl.CostEstimate(flops=2**32, bytes_accessed=2**18, transcendentals=0),
        compiler_params=pltpu.CompilerParams(vmem_limit_bytes=16 * 2**20),
    )(left, right, cube[:depth], cube[rows - depth :])
    above = lax.ppermute(down, "narrow", [(i, i + 1) for i in range(n_rows - 1)])
    below = lax.ppermute(up, "narrow", [(i + 1, i) for i in range(n_rows - 1)])

    inv_count = 1.0 / (count * rows * cols)
    basis = pl.pallas_call(
        functools.partial(subspace_kernel, inv_count),
        in_specs=[vmem] * 2,
        out_specs=vmem,
        out_shape=jax.ShapeDtypeStruct((RANK, LANES), f32),
        scratch_shapes=[pltpu.VMEM((2, LANES, LANES), bf16)],
        cost_estimate=pl.CostEstimate(flops=2**32, bytes_accessed=2**18, transcendentals=0),
        compiler_params=pltpu.CompilerParams(vmem_limit_bytes=16 * 2**20),
    )(gathered, jnp.asarray(start_basis()))
    restored, projector = pl.pallas_call(
        functools.partial(main_kernel, depth, n_rows, n_cols),
        in_specs=[vmem] * 5,
        out_specs=[pl.BlockSpec(memory_space=pl.ANY)] * 2,
        out_shape=[
            jax.ShapeDtypeStruct((rows, cols, bands), bf16),
            jax.ShapeDtypeStruct((bands, bands), f32),
        ],
        scratch_shapes=[pltpu.VMEM((2, tall, span, HALF), f32)] * 3
        + [
            pltpu.VMEM((rows, cols, bands), bf16),
            pltpu.VMEM((bands, bands), f32),
            pltpu.SemaphoreType.DMA((rows // OUT_ROWS,)),
            pltpu.SemaphoreType.DMA,
        ],
        compiler_params=pltpu.CompilerParams(vmem_limit_bytes=48 * 2**20),
    )(basis, cube, above, below, side)
    return restored, projector


def solution(mesh):
    return jax.shard_map(
        body,
        mesh=mesh,
        in_specs=(P("narrow", "wide", None),),
        out_specs=(P("narrow", "wide", None), P()),
        check_vma=False,
    )
```

```python
import functools

import jax
import jax.numpy as jnp
import numpy as np
from jax import lax
from jax.experimental import pallas as pl
from jax.experimental.pallas import tpu as pltpu
from jax.sharding import PartitionSpec as P

BANDS = 224
RANK = 16
POWER_ITERS = 4
TV_ITERS = 3
LANES = 256
HALF = 128
TAIL = BANDS - HALF
SIDE = 8
SUB = 8
BLOCK = 8
FIT_ROWS = (2, 6, 8, 8, 8)
AHEAD = 4
TV_ROWS = (17, 16)
OUT_ROWS = 4

f32 = jnp.float32
bf16 = jnp.bfloat16


def iotas(shape):
    return lax.broadcasted_iota(jnp.int32, shape, 0), lax.broadcasted_iota(jnp.int32, shape, 1)


def gram_kernel(cube_ref, packed_ref, block, full, sems):
    rows, cols, bands = cube_ref.shape
    pieces = sems.shape[0]
    high = rows // pieces

    def copy(n):
        part = pl.ds(n * high, high)
        return pltpu.make_async_copy(cube_ref.at[part], block.at[part], sems.at[n])

    for n in range(pieces):
        copy(n).start()
    full[HALF:, HALF:] = jnp.zeros((LANES - HALF, LANES - HALF), f32)
    total = None
    for n in range(pieces):
        copy(n).wait()
        flat = block[n * high : (n + 1) * high].reshape(high * cols, bands)
        term = lax.dot_general(flat, flat, (((0,), (0,)), ((), ())), preferred_element_type=f32)
        total = term if total is None else total + term
    full[0:bands, 0:bands] = total
    i, j = iotas((HALF, HALF))
    first = full[0:HALF, 0:HALF]
    second = pltpu.roll(full[HALF:LANES, HALF:LANES], 1, 1)
    packed_ref[0:HALF, :] = jnp.where(j <= i, first, second)
    packed_ref[HALF:bands, :] = full[HALF:bands, 0:HALF]
    if packed_ref.shape[0] > bands:
        packed_ref[bands:, :] = jnp.zeros((packed_ref.shape[0] - bands, HALF), f32)


def sum_kernel(count, pieces_ref, spread_ref):
    high = pieces_ref.shape[0] // count
    parts = [pieces_ref[n * high : (n + 1) * high, :] for n in range(count)]
    total = functools.reduce(jnp.add, parts)
    for n in range(count):
        spread_ref[n * high : (n + 1) * high, :] = total


def split3(x):
    high = x.astype(bf16)
    rest = x - high.astype(f32)
    mid = rest.astype(bf16)
    low = (rest - mid.astype(f32)).astype(bf16)
    return high, mid, low


def product(left, right, dims):
    def dot(a, b):
        return lax.dot_general(a, b, (dims, ((), ())), preferred_element_type=f32)

    n = left[0].shape[0]
    top = dot(jnp.concatenate(left, axis=0), right[0])
    middle = dot(jnp.concatenate(left[:2], axis=0), right[1])
    small = top[2 * n : 3 * n] + middle[n : 2 * n]
    if len(right) > 2:
        small = small + dot(left[0], right[2])
    return top[:n] + ((top[n : 2 * n] + middle[:n]) + small)


def unpack(packed, scale):
    i, j = iotas((HALF, HALF))
    merged = packed[0:HALF, :] * scale
    below = packed[HALF:BANDS, :] * scale
    below = jnp.concatenate([below, jnp.zeros((LANES - BANDS, HALF), f32)], axis=0)
    first = jnp.where(j <= i, merged, 0.0) + jnp.where(j < i, merged, 0.0).T
    moved = pltpu.roll(merged, HALF - 1, 1)
    inside = (i < TAIL) & (j < TAIL)
    second = jnp.where(inside & (j >= i), moved, 0.0) + jnp.where(inside & (j > i), moved, 0.0).T
    return jnp.concatenate(
        [
            jnp.concatenate([first, below.T], axis=1),
            jnp.concatenate([below, second], axis=1),
        ],
        axis=0,
    )


def orthonormal(grown, inner):
    row = lax.broadcasted_iota(jnp.int32, (RANK, HALF), 0)
    work = [
        jnp.concatenate([inner, jnp.zeros((RANK, HALF - RANK), f32)], axis=1),
        grown[:, :HALF],
        grown[:, HALF:],
    ]
    diagonal = jnp.ones((RANK, HALF), f32)
    for k in range(0, RANK, BLOCK):
        columns = [
            jnp.broadcast_to(work[0][:, k + c : k + c + 1], (RANK, HALF)) for c in range(BLOCK)
        ]
        tops = [[part[k + r : k + r + 1, :] for part in work] for r in range(BLOCK)]
        small = [
            [columns[c][k + r : k + r + 1, :] for c in range(r + 1)] for r in range(BLOCK)
        ]
        factors = []
        for j in range(BLOCK):
            pivot = small[j][j]
            inverse = pl.reciprocal(pivot, full_range=False)
            diagonal = jnp.where(row == k + j, pivot, diagonal)
            factor = jnp.where(row > k + j, columns[j] * inverse, 0.0)
            factors.append(factor)
            below = [small[i][j] for i in range(BLOCK) if i > j]
            for i in range(j + 1, BLOCK):
                ratio = small[i][j] * inverse
                for c in range(j + 1, i + 1):
                    small[i][c] = small[i][c] - ratio * below[c - j - 1]
                tops[i] = [x - ratio * y for x, y in zip(tops[i], tops[j])]
                columns[i] = columns[i] - factor * below[i - j - 1]
        for n in range(len(work)):
            if n > 0 or k + BLOCK < RANK:
                for j in range(BLOCK):
                    work[n] = work[n] - factors[j] * tops[j][n]
    scale = lax.rsqrt(diagonal)
    return jnp.concatenate([work[1] * scale, work[2] * scale], axis=1)


def subspace(gram, start, held):
    for n, part in enumerate(split3(gram)[:2]):
        held[n] = part

    def times_gram(pieces):
        return product(pieces, [held[0], held[1]], ((1,), (0,)))

    def iterate(_, grown):
        pieces = split3(grown)
        inner = product(pieces, pieces, ((1,), (1,)))
        return orthonormal(times_gram(pieces), inner)

    grown = lax.fori_loop(0, POWER_ITERS - 1, iterate, times_gram(split3(start)))
    pieces = split3(grown)
    return orthonormal(grown, product(pieces, pieces, ((1,), (1,))))


def halo_kernel(depth, left_ref, right_ref, top_ref, bottom_ref, up_ref, down_ref, side_ref, wide):
    rows, cols = side_ref.shape[0], top_ref.shape[1]
    wide[...] = jnp.zeros_like(wide)
    wide[:, 0:depth] = right_ref[...].astype(f32)
    wide[:, SIDE - depth :] = left_ref[...].astype(f32)
    side = wide[...].astype(bf16)
    side_ref[...] = side
    up_ref[:, 0:cols] = top_ref[...]
    up_ref[:, cols:] = side[:depth]
    down_ref[:, 0:cols] = bottom_ref[...]
    down_ref[:, cols:] = side[rows - depth :]


def subspace_kernel(inv_count, packed_ref, start_ref, basis_ref, held):
    basis_ref[...] = subspace(unpack(packed_ref[...], inv_count), start_ref[...], held)


def main_kernel(
    depth, n_rows, n_cols, basis_ref, mid_ref, above_ref, below_ref, side_ref,
    out_ref, proj_ref, fit, half_fit, field_a, field_b, out_stage, proj_stage, out_sems, proj_sem
):
    rows, cols, bands = mid_ref.shape
    span = cols + SIDE
    proj_copy = pltpu.make_async_copy(proj_stage, proj_ref, proj_sem)

    def out_copy(n):
        part = pl.ds(n * OUT_ROWS, OUT_ROWS)
        return pltpu.make_async_copy(out_stage.at[part], out_ref.at[part], out_sems.at[n])

    high, mid, low = split3(basis_ref[...])
    tn = (((0,), (0,)), ((), ()))
    mixed = lax.dot_general(
        jnp.concatenate([high, high, high], axis=0),
        jnp.concatenate([high, mid, low], axis=0),
        tn,
        preferred_element_type=f32,
    )
    mixed = mixed * 4.0
    mixed_high = mixed.astype(bf16)
    mixed_low = (mixed - mixed_high.astype(f32)).astype(bf16)
    mixed_both = jnp.concatenate([mixed_high, mixed_low], axis=0)

    def fitted(flat):
        padded = jnp.concatenate([flat, jnp.zeros((flat.shape[0], LANES - bands), bf16)], axis=1)
        both = jnp.concatenate([padded, padded], axis=1)
        return jnp.dot(both, mixed_both, preferred_element_type=f32)

    def project():
        right = jnp.concatenate([high, high, high, mid, mid, low], axis=0)
        left = jnp.concatenate([high, mid, low, high, mid, high], axis=0)
        full = lax.dot_general(left, right, tn, preferred_element_type=f32)
        proj_stage[...] = full[:bands, :bands]
        proj_copy.start()

    def fit_rows(start, stop):
        n = stop - start
        if depth <= start < depth + rows:
            part = slice(start - depth, stop - depth)
            center = mid_ref[part].reshape(n * cols, bands)
            side = side_ref[part].astype(f32).reshape(n * SIDE, bands).astype(bf16)
            res = fitted(jnp.concatenate([center, side], axis=0))
            for h, lane in enumerate(lanes):
                fit[h, start:stop, 0:cols] = res[: n * cols, lane].reshape(n, cols, HALF)
                fit[h, start:stop, cols:span] = res[n * cols :, lane].reshape(n, SIDE, HALF)
        else:
            block = above_ref[...] if start < depth else below_ref[...]
            flat = block.astype(f32).reshape(n * span, bands).astype(bf16)
            res = fitted(flat)
            for h, lane in enumerate(lanes):
                fit[h, start:stop] = res[:, lane].reshape(n, span, HALF)

    row, col = lax.axis_index("narrow"), lax.axis_index("wide")
    at_top, at_bottom = row == 0, row == n_rows - 1
    at_left, at_right = col == 0, col == n_cols - 1
    per = span // SUB
    place = lax.broadcasted_iota(jnp.int32, (SUB, HALF), 0)
    keeps = {}
    for column, shut in ((cols - 1, at_right), (span - 1, at_left)):
        keep = jnp.where((place == column // per) & shut, 0.0, 1.0).astype(f32)
        keeps[column % per] = keeps[column % per] * keep if column % per in keeps else keep
    open_rows = {
        depth - 1: jnp.where(at_top, 0.0, 1.0),
        depth + rows - 1: jnp.where(at_bottom, 0.0, 1.0),
    }
    lanes = [slice(0, HALF), slice(HALF, LANES)]
    fields = [fit, field_a, field_b]

    def natural(ref, h, r):
        return [ref[h, r, pl.ds(w, SUB, stride=per), :] for w in range(per)]

    def spread(ref, h, r):
        return [ref[h, r, w * SUB : (w + 1) * SUB, :] for w in range(per)]

    def slopes(now, later, open_row=None):
        follow = now[1:] + [pltpu.roll(now[0], SUB - 1, 0)]
        downs, acrosses = [], []
        for w in range(per):
            down = later[w] - now[w]
            if open_row is not None:
                down = down * open_row
            across = follow[w] - now[w]
            if w in keeps:
                across = across * keeps[w]
            inverse = lax.rsqrt(down * down + (across * across + 4.0))
            downs.append(down * inverse)
            acrosses.append(across * inverse)
        return downs, acrosses

    def advance(base, before, down, across):
        behind = [pltpu.roll(across[-1], 1, 0)] + across[:-1]
        return [
            base[w] + ((down[w] - before[w]) + (across[w] - behind[w])) for w in range(per)
        ]

    def put(ref, h, r, value):
        for w in range(per):
            ref[h, r, w * SUB : (w + 1) * SUB, :] = value[w]

    tall = rows + 2 * depth
    groups = [(0, depth)]
    for n in FIT_ROWS:
        groups.append((groups[-1][1], groups[-1][1] + n))
    groups += [(depth + rows, tall)]
    ready = 0
    befores, nows = [None] * len(lanes), [None] * len(lanes)
    for r in range(tall - 1):
        while ready < len(groups) and groups[ready][0] <= r + 1 + AHEAD:
            fit_rows(*groups[ready])
            ready += 1
            if ready == 4:
                project()
        for h in range(len(lanes)):
            now = nows[h] if r > 0 else natural(fit, h, r)
            later = natural(fit, h, r + 1)
            down, across = slopes(now, later, open_rows.get(r))
            if r > 0:
                put(field_a, h, r, advance(now, befores[h], down, across))
                put(half_fit, h, r, [0.5 * x for x in now])
            nows[h], befores[h] = later, down

    def step(s, first, trips, unroll):
        source, final = fields[s], s == TV_ITERS - 1

        @pl.when(at_top)
        def _():
            source[:, depth - 1] = source[:, depth]

        @pl.when(at_bottom)
        def _():
            source[:, depth + rows] = source[:, depth + rows - 1]

        def block_step(n, carry):
            carry = list(carry)
            for inner in range(unroll):
                r = first + n * unroll + inner
                for h, lane in enumerate(lanes):
                    now, before = carry[2 * h], carry[2 * h + 1]
                    later = spread(source, h, r + 1)
                    down, across = slopes(now, later)
                    base = [0.5 * x + y for x, y in zip(now, spread(half_fit, h, r))]
                    value = advance(base, before, down, across)
                    if final:
                        for w in range(per):
                            field_a[h, r, pl.ds(w, SUB, stride=per), :] = value[w]
                        result = (field_a[h, r, 0:cols, :] * 0.25).astype(bf16)
                        width = min(lane.stop, bands) - lane.start
                        out_stage[r - depth, :, lane.start : lane.start + width] = result[:, :width]
                    else:
                        put(fields[s + 1], h, r, value)
                    carry[2 * h], carry[2 * h + 1] = later, down
                if final and inner % OUT_ROWS == OUT_ROWS - 1:
                    out_copy(n * (unroll // OUT_ROWS) + inner // OUT_ROWS).start()
            return tuple(carry)

        carry = []
        for h in range(len(lanes)):
            before, now = spread(source, h, first - 1), spread(source, h, first)
            carry += [now, slopes(before, now)[0]]
        lax.fori_loop(0, trips, block_step, tuple(carry))

    step(1, 2, (rows + 2) // TV_ROWS[0], TV_ROWS[0])
    step(2, depth, rows // TV_ROWS[1], TV_ROWS[1])
    proj_copy.wait()
    for n in range(rows // OUT_ROWS):
        out_copy(n).wait()


def start_basis():
    bands = np.arange(BANDS, dtype=np.float32)[None, :]
    cols = np.arange(RANK, dtype=np.float32)[:, None]
    angle = np.float32(np.pi) * (bands + np.float32(0.5)) * cols / np.float32(BANDS)
    return np.pad(np.cos(angle).astype(np.float32), ((0, 0), (0, LANES - BANDS)))


def neighbours(block, axis, dim, width):
    count = lax.axis_size(axis)
    size = block.shape[dim]
    head = lax.slice_in_dim(block, 0, width, axis=dim)
    tail = lax.slice_in_dim(block, size - width, size, axis=dim)
    before = lax.ppermute(tail, axis, [(i, i + 1) for i in range(count - 1)])
    after = lax.ppermute(head, axis, [(i + 1, i) for i in range(count - 1)])
    return before, after


def exchange(pieces, axes):
    return lax.all_to_all(pieces, axes, split_axis=0, concat_axis=0)


def body(cube):
    n_rows = lax.axis_size("narrow")
    n_cols = lax.axis_size("wide")
    count = n_rows * n_cols
    rows, cols, bands = cube.shape
    depth = TV_ITERS
    axes = ("narrow", "wide")

    tall_packed = -(-bands // count) * count
    pieces = 2 if rows % 2 == 0 else 1
    packed = pl.pallas_call(
        gram_kernel,
        in_specs=[pl.BlockSpec(memory_space=pl.ANY)],
        out_shape=jax.ShapeDtypeStruct((tall_packed, HALF), f32),
        scratch_shapes=[
            pltpu.VMEM(cube.shape, cube.dtype),
            pltpu.VMEM((LANES, LANES), f32),
            pltpu.SemaphoreType.DMA((pieces,)),
        ],
        compiler_params=pltpu.CompilerParams(vmem_limit_bytes=62 * 2**20),
    )(cube)
    packed, cube = lax.optimization_barrier((packed, cube))
    left, right = neighbours(cube, "wide", 1, depth)
    vmem = pl.BlockSpec(memory_space=pltpu.VMEM)
    pieces_shape = (count, 1, tall_packed // count * HALF)
    part = exchange(packed.reshape(pieces_shape), axes).reshape(tall_packed, HALF)
    share = pl.pallas_call(
        functools.partial(sum_kernel, count),
        in_specs=[vmem],
        out_specs=vmem,
        out_shape=jax.ShapeDtypeStruct((tall_packed, HALF), f32),
        compiler_params=pltpu.CompilerParams(vmem_limit_bytes=16 * 2**20),
    )(part)
    gathered = exchange(share.reshape(pieces_shape), axes).reshape(tall_packed, HALF)

    tall, span = rows + 2 * depth, cols + SIDE
    up, down, side = pl.pallas_call(
        functools.partial(halo_kernel, depth),
        in_specs=[vmem] * 4,
        out_specs=[vmem] * 3,
        out_shape=[
            jax.ShapeDtypeStruct((depth, span, bands), bf16),
            jax.ShapeDtypeStruct((depth, span, bands), bf16),
            jax.ShapeDtypeStruct((rows, SIDE, bands), bf16),
        ],
        scratch_shapes=[pltpu.VMEM((rows, SIDE, bands), f32)],
        cost_estimate=pl.CostEstimate(flops=2**32, bytes_accessed=2**18, transcendentals=0),
        compiler_params=pltpu.CompilerParams(vmem_limit_bytes=16 * 2**20),
    )(left, right, cube[:depth], cube[rows - depth :])
    above = lax.ppermute(down, "narrow", [(i, i + 1) for i in range(n_rows - 1)])
    below = lax.ppermute(up, "narrow", [(i + 1, i) for i in range(n_rows - 1)])

    inv_count = 1.0 / (count * rows * cols)
    basis = pl.pallas_call(
        functools.partial(subspace_kernel, inv_count),
        in_specs=[vmem] * 2,
        out_specs=vmem,
        out_shape=jax.ShapeDtypeStruct((RANK, LANES), f32),
        scratch_shapes=[pltpu.VMEM((2, LANES, LANES), bf16)],
        cost_estimate=pl.CostEstimate(flops=2**32, bytes_accessed=2**18, transcendentals=0),
        compiler_params=pltpu.CompilerParams(vmem_limit_bytes=16 * 2**20),
    )(gathered, jnp.asarray(start_basis()))
    restored, projector = pl.pallas_call(
        functools.partial(main_kernel, depth, n_rows, n_cols),
        in_specs=[vmem] * 5,
        out_specs=[pl.BlockSpec(memory_space=pl.ANY)] * 2,
        out_shape=[
            jax.ShapeDtypeStruct((rows, cols, bands), bf16),
            jax.ShapeDtypeStruct((bands, bands), f32),
        ],
        scratch_shapes=[pltpu.VMEM((2, tall, span, HALF), f32)] * 4
        + [
            pltpu.VMEM((rows, cols, bands), bf16),
            pltpu.VMEM((bands, bands), f32),
            pltpu.SemaphoreType.DMA((rows // OUT_ROWS,)),
            pltpu.SemaphoreType.DMA,
        ],
        compiler_params=pltpu.CompilerParams(vmem_limit_bytes=48 * 2**20),
    )(basis, cube, above, below, side)
    return restored, projector


def solution(mesh):
    return jax.shard_map(
        body,
        mesh=mesh,
        in_specs=(P("narrow", "wide", None),),
        out_specs=(P("narrow", "wide", None), P()),
        check_vma=False,
    )
```

```python
import functools

import jax
import jax.numpy as jnp
import numpy as np
from jax import lax
from jax.experimental import pallas as pl
from jax.experimental.pallas import tpu as pltpu
from jax.sharding import PartitionSpec as P

BANDS = 224
RANK = 16
POWER_ITERS = 4
TV_ITERS = 3
LANES = 256
HALF = 128
TAIL = BANDS - HALF
SIDE = 8
SUB = 8
BLOCK = 8
FIT_ROWS = (7, 12, 19)
AHEAD = 5
TV_ROWS = (17, 16)
OUT_ROWS = 4

f32 = jnp.float32
bf16 = jnp.bfloat16


def iotas(shape):
    return lax.broadcasted_iota(jnp.int32, shape, 0), lax.broadcasted_iota(jnp.int32, shape, 1)


def gram_kernel(cube_ref, packed_ref, block, full, sems):
    rows, cols, bands = cube_ref.shape
    pieces = sems.shape[0]
    high = rows // pieces

    def copy(n):
        part = pl.ds(n * high, high)
        return pltpu.make_async_copy(cube_ref.at[part], block.at[part], sems.at[n])

    for n in range(pieces):
        copy(n).start()
    full[HALF:, HALF:] = jnp.zeros((LANES - HALF, LANES - HALF), f32)
    total = None
    for n in range(pieces):
        copy(n).wait()
        flat = block[n * high : (n + 1) * high].reshape(high * cols, bands)
        term = lax.dot_general(flat, flat, (((0,), (0,)), ((), ())), preferred_element_type=f32)
        total = term if total is None else total + term
    full[0:bands, 0:bands] = total
    i, j = iotas((HALF, HALF))
    first = full[0:HALF, 0:HALF]
    second = pltpu.roll(full[HALF:LANES, HALF:LANES], 1, 1)
    packed_ref[0:HALF, :] = jnp.where(j <= i, first, second)
    packed_ref[HALF:bands, :] = full[HALF:bands, 0:HALF]
    if packed_ref.shape[0] > bands:
        packed_ref[bands:, :] = jnp.zeros((packed_ref.shape[0] - bands, HALF), f32)


def sum_kernel(count, pieces_ref, spread_ref):
    high = pieces_ref.shape[0] // count
    parts = [pieces_ref[n * high : (n + 1) * high, :] for n in range(count)]
    total = functools.reduce(jnp.add, parts)
    for n in range(count):
        spread_ref[n * high : (n + 1) * high, :] = total


def split3(x):
    high = x.astype(bf16)
    rest = x - high.astype(f32)
    mid = rest.astype(bf16)
    low = (rest - mid.astype(f32)).astype(bf16)
    return high, mid, low


def product(left, right, dims):
    def dot(a, b):
        return lax.dot_general(a, b, (dims, ((), ())), preferred_element_type=f32)

    n = left[0].shape[0]
    top = dot(jnp.concatenate(left, axis=0), right[0])
    middle = dot(jnp.concatenate(left[:2], axis=0), right[1])
    small = top[2 * n : 3 * n] + middle[n : 2 * n]
    if len(right) > 2:
        small = small + dot(left[0], right[2])
    return top[:n] + ((top[n : 2 * n] + middle[:n]) + small)


def unpack(packed, scale):
    i, j = iotas((HALF, HALF))
    merged = packed[0:HALF, :] * scale
    below = packed[HALF:BANDS, :] * scale
    below = jnp.concatenate([below, jnp.zeros((LANES - BANDS, HALF), f32)], axis=0)
    first = jnp.where(j <= i, merged, 0.0) + jnp.where(j < i, merged, 0.0).T
    moved = pltpu.roll(merged, HALF - 1, 1)
    inside = (i < TAIL) & (j < TAIL)
    second = jnp.where(inside & (j >= i), moved, 0.0) + jnp.where(inside & (j > i), moved, 0.0).T
    return jnp.concatenate(
        [
            jnp.concatenate([first, below.T], axis=1),
            jnp.concatenate([below, second], axis=1),
        ],
        axis=0,
    )


def orthonormal(grown, inner):
    row = lax.broadcasted_iota(jnp.int32, (RANK, HALF), 0)
    work = [
        jnp.concatenate([inner, jnp.zeros((RANK, HALF - RANK), f32)], axis=1),
        grown[:, :HALF],
        grown[:, HALF:],
    ]
    diagonal = jnp.ones((RANK, HALF), f32)
    scale0 = None
    for k in range(0, RANK, BLOCK):
        columns = [
            jnp.broadcast_to(work[0][:, k + c : k + c + 1], (RANK, HALF)) for c in range(BLOCK)
        ]
        tops = [[part[k + r : k + r + 1, :] for part in work] for r in range(BLOCK)]
        small = [
            [columns[c][k + r : k + r + 1, :] for c in range(r + 1)] for r in range(BLOCK)
        ]
        factors = []
        for j in range(0, BLOCK, 2):
            a, b, c = small[j][j], small[j + 1][j], small[j + 1][j + 1]
            inverse = pl.reciprocal(a, full_range=False)
            if scale0 is None:
                scale0 = inverse
            a0, b0, c0 = a * scale0, b * scale0, c * scale0
            inverse2 = (a0 * scale0) * pl.reciprocal(a0 * c0 - b0 * b0, full_range=False)
            ratio = b * inverse
            diagonal = jnp.where(row == k + j, a, diagonal)
            diagonal = jnp.where(row == k + j + 1, c - ratio * b, diagonal)
            factor1 = jnp.where(row > k + j, columns[j] * inverse, 0.0)
            follow = columns[j + 1] - factor1 * b
            factor2 = jnp.where(row > k + j + 1, follow * inverse2, 0.0)
            factors += [factor1, factor2]
            tops[j + 1] = [x - ratio * y for x, y in zip(tops[j + 1], tops[j])]
            first = [small[i][j] for i in range(j + 2, BLOCK)]
            ratio1 = [x * inverse for x in first]
            second = [small[i][j + 1] - x * b for i, x in zip(range(j + 2, BLOCK), ratio1)]
            ratio2 = [x * inverse2 for x in second]
            for m, i in enumerate(range(j + 2, BLOCK)):
                for n in range(m + 1):
                    small[i][j + 2 + n] = (small[i][j + 2 + n] - ratio1[m] * first[n]) - (
                        ratio2[m] * second[n]
                    )
                tops[i] = [
                    (x - ratio1[m] * y) - ratio2[m] * z
                    for x, y, z in zip(tops[i], tops[j], tops[j + 1])
                ]
                columns[i] = (columns[i] - factor1 * first[m]) - factor2 * second[m]
        for n in range(len(work)):
            if n > 0 or k + BLOCK < RANK:
                for j in range(BLOCK):
                    work[n] = work[n] - factors[j] * tops[j][n]
    scale = lax.rsqrt(diagonal)
    return jnp.concatenate([work[1] * scale, work[2] * scale], axis=1)


def subspace(gram, start, held):
    for n, part in enumerate(split3(gram)[:2]):
        held[n] = part

    def times_gram(pieces):
        return product(pieces, [held[0], held[1]], ((1,), (0,)))

    def iterate(_, grown):
        pieces = split3(grown)
        inner = product(pieces, pieces, ((1,), (1,)))
        return orthonormal(times_gram(pieces), inner)

    grown = lax.fori_loop(0, POWER_ITERS - 1, iterate, times_gram(split3(start)))
    pieces = split3(grown)
    return orthonormal(grown, product(pieces, pieces, ((1,), (1,))))


def halo_kernel(depth, left_ref, right_ref, top_ref, bottom_ref, up_ref, down_ref, side_ref, wide):
    rows, cols = side_ref.shape[0], top_ref.shape[1]
    wide[...] = jnp.zeros_like(wide)
    wide[:, 0:depth] = right_ref[...].astype(f32)
    wide[:, SIDE - depth :] = left_ref[...].astype(f32)
    side = wide[...].astype(bf16)
    side_ref[...] = side
    up_ref[:, 0:cols] = top_ref[...]
    up_ref[:, cols:] = side[:depth]
    down_ref[:, 0:cols] = bottom_ref[...]
    down_ref[:, cols:] = side[rows - depth :]


def subspace_kernel(inv_count, packed_ref, start_ref, basis_ref, held):
    basis_ref[...] = subspace(unpack(packed_ref[...], inv_count), start_ref[...], held)


def main_kernel(
    depth, n_rows, n_cols, basis_ref, mid_ref, above_ref, below_ref, side_ref,
    out_ref, proj_ref, fit, field_a, field_b, out_stage, proj_stage, out_sems, proj_sem
):
    rows, cols, bands = mid_ref.shape
    span = cols + SIDE
    proj_copy = pltpu.make_async_copy(proj_stage, proj_ref, proj_sem)

    def out_copy(n):
        part = pl.ds(n * OUT_ROWS, OUT_ROWS)
        return pltpu.make_async_copy(out_stage.at[part], out_ref.at[part], out_sems.at[n])

    high, mid, low = split3(basis_ref[...])
    tn = (((0,), (0,)), ((), ()))
    mixed = lax.dot_general(
        jnp.concatenate([high, high, high], axis=0),
        jnp.concatenate([high, mid, low], axis=0),
        tn,
        preferred_element_type=f32,
    )
    mixed = mixed * 4.0
    mixed_high = mixed.astype(bf16)
    mixed_low = (mixed - mixed_high.astype(f32)).astype(bf16)
    mixed_both = jnp.concatenate([mixed_high, mixed_low], axis=0)

    def fitted(flat):
        padded = jnp.concatenate([flat, jnp.zeros((flat.shape[0], LANES - bands), bf16)], axis=1)
        both = jnp.concatenate([padded, padded], axis=1)
        return jnp.dot(both, mixed_both, preferred_element_type=f32)

    def project():
        right = jnp.concatenate([high, high, high, mid, mid, low], axis=0)
        left = jnp.concatenate([high, mid, low, high, mid, high], axis=0)
        full = lax.dot_general(left, right, tn, preferred_element_type=f32)
        proj_stage[...] = full[:bands, :bands]
        proj_copy.start()

    def fit_rows(start, stop):
        low, high_row = max(start, depth), min(stop, depth + rows)
        n = high_row - low
        part = slice(low - depth, high_row - depth)
        blocks = [(mid_ref[part].reshape(n * cols, bands), low, n, slice(0, cols))]
        side = side_ref[part].astype(f32).reshape(n * SIDE, bands).astype(bf16)
        blocks.append((side, low, n, slice(cols, span)))
        for ref, first in ((above_ref, 0), (below_ref, depth + rows)):
            if start <= first and first + depth <= stop:
                flat = ref[...].astype(f32).reshape(depth * span, bands).astype(bf16)
                blocks.append((flat, first, depth, slice(0, span)))
        res = fitted(jnp.concatenate([block[0] for block in blocks], axis=0))
        offset = 0
        for flat, first, n, place in blocks:
            stretch = res[offset : offset + flat.shape[0]]
            offset += flat.shape[0]
            for h, lane in enumerate(lanes):
                fit[h, first : first + n, place] = stretch[:, lane].reshape(n, -1, HALF)

    row, col = lax.axis_index("narrow"), lax.axis_index("wide")
    at_top, at_bottom = row == 0, row == n_rows - 1
    at_left, at_right = col == 0, col == n_cols - 1
    per = span // SUB
    place = lax.broadcasted_iota(jnp.int32, (SUB, HALF), 0)
    keeps = {}
    for column, shut in ((cols - 1, at_right), (span - 1, at_left)):
        keep = jnp.where((place == column // per) & shut, 0.0, 1.0).astype(f32)
        keeps[column % per] = keeps[column % per] * keep if column % per in keeps else keep
    open_rows = {
        depth - 1: jnp.where(at_top, 0.0, 1.0),
        depth + rows - 1: jnp.where(at_bottom, 0.0, 1.0),
    }
    lanes = [slice(0, HALF), slice(HALF, LANES)]
    fields = [fit, field_a, field_b]

    def natural(ref, h, r):
        return [ref[h, r, pl.ds(w, SUB, stride=per), :] for w in range(per)]

    def spread(ref, h, r):
        return [ref[h, r, w * SUB : (w + 1) * SUB, :] for w in range(per)]

    def slopes(now, later, open_row=None):
        follow = now[1:] + [pltpu.roll(now[0], SUB - 1, 0)]
        downs, acrosses = [], []
        for w in range(per):
            down = later[w] - now[w]
            if open_row is not None:
                down = down * open_row
            across = follow[w] - now[w]
            if w in keeps:
                across = across * keeps[w]
            inverse = lax.rsqrt(down * down + (across * across + 4.0))
            downs.append(down * inverse)
            acrosses.append(across * inverse)
        return downs, acrosses

    def advance(base, before, down, across):
        behind = [pltpu.roll(across[-1], 1, 0)] + across[:-1]
        return [
            base[w] + ((down[w] - before[w]) + (across[w] - behind[w])) for w in range(per)
        ]

    def put(ref, h, r, value):
        for w in range(per):
            ref[h, r, w * SUB : (w + 1) * SUB, :] = value[w]

    tall = rows + 2 * depth
    groups = [(0, FIT_ROWS[0])]
    for n in FIT_ROWS[1:]:
        groups.append((groups[-1][1], groups[-1][1] + n))
    ready = 0
    befores = [None] * len(lanes)
    for r in range(tall - 1):
        while ready < len(groups) and groups[ready][0] <= r + 1 + AHEAD:
            fit_rows(*groups[ready])
            ready += 1
            if ready == 2:
                project()
        for h in range(len(lanes)):
            now = natural(fit, h, r)
            down, across = slopes(now, natural(fit, h, r + 1), open_rows.get(r))
            if r > 0:
                put(field_a, h, r, advance(now, befores[h], down, across))
            befores[h] = down

    def step(s, first, trips, unroll):
        source, final = fields[s], s == TV_ITERS - 1

        @pl.when(at_top)
        def _():
            source[:, depth - 1] = source[:, depth]

        @pl.when(at_bottom)
        def _():
            source[:, depth + rows] = source[:, depth + rows - 1]

        def block_step(n, carry):
            carry = list(carry)
            for inner in range(unroll):
                r = first + n * unroll + inner
                for h, lane in enumerate(lanes):
                    now, before = carry[2 * h], carry[2 * h + 1]
                    later = spread(source, h, r + 1)
                    down, across = slopes(now, later)
                    base = [0.5 * (x + y) for x, y in zip(now, natural(fit, h, r))]
                    value = advance(base, before, down, across)
                    if final:
                        for w in range(per):
                            field_a[h, r, pl.ds(w, SUB, stride=per), :] = value[w]
                        result = (field_a[h, r, 0:cols, :] * 0.25).astype(bf16)
                        width = min(lane.stop, bands) - lane.start
                        out_stage[r - depth, :, lane.start : lane.start + width] = result[:, :width]
                    else:
                        put(fields[s + 1], h, r, value)
                    carry[2 * h], carry[2 * h + 1] = later, down
                if final and inner % OUT_ROWS == OUT_ROWS - 1:
                    out_copy(n * (unroll // OUT_ROWS) + inner // OUT_ROWS).start()
            return tuple(carry)

        carry = []
        for h in range(len(lanes)):
            before, now = spread(source, h, first - 1), spread(source, h, first)
            carry += [now, slopes(before, now)[0]]
        lax.fori_loop(0, trips, block_step, tuple(carry))

    step(1, 2, (rows + 2) // TV_ROWS[0], TV_ROWS[0])
    step(2, depth, rows // TV_ROWS[1], TV_ROWS[1])
    proj_copy.wait()
    for n in range(rows // OUT_ROWS):
        out_copy(n).wait()


def start_basis():
    bands = np.arange(BANDS, dtype=np.float32)[None, :]
    cols = np.arange(RANK, dtype=np.float32)[:, None]
    angle = np.float32(np.pi) * (bands + np.float32(0.5)) * cols / np.float32(BANDS)
    return np.pad(np.cos(angle).astype(np.float32), ((0, 0), (0, LANES - BANDS)))


def neighbours(block, axis, dim, width):
    count = lax.axis_size(axis)
    size = block.shape[dim]
    head = lax.slice_in_dim(block, 0, width, axis=dim)
    tail = lax.slice_in_dim(block, size - width, size, axis=dim)
    before = lax.ppermute(tail, axis, [(i, i + 1) for i in range(count - 1)])
    after = lax.ppermute(head, axis, [(i + 1, i) for i in range(count - 1)])
    return before, after


def exchange(pieces, axes):
    return lax.all_to_all(pieces, axes, split_axis=0, concat_axis=0)


def body(cube):
    n_rows = lax.axis_size("narrow")
    n_cols = lax.axis_size("wide")
    count = n_rows * n_cols
    rows, cols, bands = cube.shape
    depth = TV_ITERS
    axes = ("narrow", "wide")

    tall_packed = -(-bands // count) * count
    pieces = 2 if rows % 2 == 0 else 1
    packed = pl.pallas_call(
        gram_kernel,
        in_specs=[pl.BlockSpec(memory_space=pl.ANY)],
        out_shape=jax.ShapeDtypeStruct((tall_packed, HALF), f32),
        scratch_shapes=[
            pltpu.VMEM(cube.shape, cube.dtype),
            pltpu.VMEM((LANES, LANES), f32),
            pltpu.SemaphoreType.DMA((pieces,)),
        ],
        compiler_params=pltpu.CompilerParams(vmem_limit_bytes=62 * 2**20),
    )(cube)
    packed, cube = lax.optimization_barrier((packed, cube))
    left, right = neighbours(cube, "wide", 1, depth)
    vmem = pl.BlockSpec(memory_space=pltpu.VMEM)
    pieces_shape = (count, 1, tall_packed // count * HALF)
    part = exchange(packed.reshape(pieces_shape), axes).reshape(tall_packed, HALF)
    share = pl.pallas_call(
        functools.partial(sum_kernel, count),
        in_specs=[vmem],
        out_specs=vmem,
        out_shape=jax.ShapeDtypeStruct((tall_packed, HALF), f32),
        compiler_params=pltpu.CompilerParams(vmem_limit_bytes=16 * 2**20),
    )(part)
    gathered = exchange(share.reshape(pieces_shape), axes).reshape(tall_packed, HALF)

    tall, span = rows + 2 * depth, cols + SIDE
    up, down, side = pl.pallas_call(
        functools.partial(halo_kernel, depth),
        in_specs=[vmem] * 4,
        out_specs=[vmem] * 3,
        out_shape=[
            jax.ShapeDtypeStruct((depth, span, bands), bf16),
            jax.ShapeDtypeStruct((depth, span, bands), bf16),
            jax.ShapeDtypeStruct((rows, SIDE, bands), bf16),
        ],
        scratch_shapes=[pltpu.VMEM((rows, SIDE, bands), f32)],
        cost_estimate=pl.CostEstimate(flops=2**32, bytes_accessed=2**18, transcendentals=0),
        compiler_params=pltpu.CompilerParams(vmem_limit_bytes=16 * 2**20),
    )(left, right, cube[:depth], cube[rows - depth :])
    above = lax.ppermute(down, "narrow", [(i, i + 1) for i in range(n_rows - 1)])
    below = lax.ppermute(up, "narrow", [(i + 1, i) for i in range(n_rows - 1)])

    inv_count = 1.0 / (count * rows * cols)
    basis = pl.pallas_call(
        functools.partial(subspace_kernel, inv_count),
        in_specs=[vmem] * 2,
        out_specs=vmem,
        out_shape=jax.ShapeDtypeStruct((RANK, LANES), f32),
        scratch_shapes=[pltpu.VMEM((2, LANES, LANES), bf16)],
        cost_estimate=pl.CostEstimate(flops=2**32, bytes_accessed=2**18, transcendentals=0),
        compiler_params=pltpu.CompilerParams(vmem_limit_bytes=16 * 2**20),
    )(gathered, jnp.asarray(start_basis()))
    restored, projector = pl.pallas_call(
        functools.partial(main_kernel, depth, n_rows, n_cols),
        in_specs=[vmem] * 5,
        out_specs=[pl.BlockSpec(memory_space=pl.ANY)] * 2,
        out_shape=[
            jax.ShapeDtypeStruct((rows, cols, bands), bf16),
            jax.ShapeDtypeStruct((bands, bands), f32),
        ],
        scratch_shapes=[pltpu.VMEM((2, tall, span, HALF), f32)] * 3
        + [
            pltpu.VMEM((rows, cols, bands), bf16),
            pltpu.VMEM((bands, bands), f32),
            pltpu.SemaphoreType.DMA((rows // OUT_ROWS,)),
            pltpu.SemaphoreType.DMA,
        ],
        compiler_params=pltpu.CompilerParams(vmem_limit_bytes=48 * 2**20),
    )(basis, cube, above, below, side)
    return restored, projector


def solution(mesh):
    return jax.shard_map(
        body,
        mesh=mesh,
        in_specs=(P("narrow", "wide", None),),
        out_specs=(P("narrow", "wide", None), P()),
        check_vma=False,
    )
```

```python
import functools

import jax
import jax.numpy as jnp
import numpy as np
from jax import lax
from jax.experimental import pallas as pl
from jax.experimental.pallas import tpu as pltpu
from jax.sharding import PartitionSpec as P

BANDS = 224
RANK = 16
POWER_ITERS = 4
TV_ITERS = 3
LANES = 256
HALF = 128
TAIL = BANDS - HALF
SIDE = 8
SUB = 8
BLOCK = 8
FIT_ROWS = (2, 6, 8, 8, 8)
AHEAD = 4
TV_ROWS = (17, 16)
OUT_ROWS = 4

f32 = jnp.float32
bf16 = jnp.bfloat16


def iotas(shape):
    return lax.broadcasted_iota(jnp.int32, shape, 0), lax.broadcasted_iota(jnp.int32, shape, 1)


def gram_kernel(cube_ref, packed_ref, block, full, sems):
    rows, cols, bands = cube_ref.shape
    pieces = sems.shape[0]
    high = rows // pieces

    def copy(n):
        part = pl.ds(n * high, high)
        return pltpu.make_async_copy(cube_ref.at[part], block.at[part], sems.at[n])

    for n in range(pieces):
        copy(n).start()
    full[HALF:, HALF:] = jnp.zeros((LANES - HALF, LANES - HALF), f32)
    total = None
    for n in range(pieces):
        copy(n).wait()
        flat = block[n * high : (n + 1) * high].reshape(high * cols, bands)
        term = lax.dot_general(flat, flat, (((0,), (0,)), ((), ())), preferred_element_type=f32)
        total = term if total is None else total + term
    full[0:bands, 0:bands] = total
    i, j = iotas((HALF, HALF))
    first = full[0:HALF, 0:HALF]
    second = pltpu.roll(full[HALF:LANES, HALF:LANES], 1, 1)
    packed_ref[0:HALF, :] = jnp.where(j <= i, first, second)
    packed_ref[HALF:bands, :] = full[HALF:bands, 0:HALF]
    if packed_ref.shape[0] > bands:
        packed_ref[bands:, :] = jnp.zeros((packed_ref.shape[0] - bands, HALF), f32)


def sum_kernel(count, pieces_ref, spread_ref):
    high = pieces_ref.shape[0] // count
    parts = [pieces_ref[n * high : (n + 1) * high, :] for n in range(count)]
    total = functools.reduce(jnp.add, parts)
    for n in range(count):
        spread_ref[n * high : (n + 1) * high, :] = total


def split3(x):
    high = x.astype(bf16)
    rest = x - high.astype(f32)
    mid = rest.astype(bf16)
    low = (rest - mid.astype(f32)).astype(bf16)
    return high, mid, low


def product(left, right, dims):
    def dot(a, b):
        return lax.dot_general(a, b, (dims, ((), ())), preferred_element_type=f32)

    n = left[0].shape[0]
    top = dot(jnp.concatenate(left, axis=0), right[0])
    middle = dot(jnp.concatenate(left[:2], axis=0), right[1])
    small = top[2 * n : 3 * n] + middle[n : 2 * n]
    if len(right) > 2:
        small = small + dot(left[0], right[2])
    return top[:n] + ((top[n : 2 * n] + middle[:n]) + small)


def unpack(packed, scale):
    i, j = iotas((HALF, HALF))
    merged = packed[0:HALF, :] * scale
    below = packed[HALF:BANDS, :] * scale
    below = jnp.concatenate([below, jnp.zeros((LANES - BANDS, HALF), f32)], axis=0)
    first = jnp.where(j <= i, merged, 0.0) + jnp.where(j < i, merged, 0.0).T
    moved = pltpu.roll(merged, HALF - 1, 1)
    inside = (i < TAIL) & (j < TAIL)
    second = jnp.where(inside & (j >= i), moved, 0.0) + jnp.where(inside & (j > i), moved, 0.0).T
    return jnp.concatenate(
        [
            jnp.concatenate([first, below.T], axis=1),
            jnp.concatenate([below, second], axis=1),
        ],
        axis=0,
    )


def orthonormal(grown, inner):
    row = lax.broadcasted_iota(jnp.int32, (RANK, HALF), 0)
    work = [
        jnp.concatenate([inner, jnp.zeros((RANK, HALF - RANK), f32)], axis=1),
        grown[:, :HALF],
        grown[:, HALF:],
    ]
    diagonal = jnp.ones((RANK, HALF), f32)
    for k in range(0, RANK, BLOCK):
        columns = [
            jnp.broadcast_to(work[0][:, k + c : k + c + 1], (RANK, HALF)) for c in range(BLOCK)
        ]
        tops = [[part[k + r : k + r + 1, :] for part in work] for r in range(BLOCK)]
        small = [
            [columns[c][k + r : k + r + 1, :] for c in range(r + 1)] for r in range(BLOCK)
        ]
        factors = []
        for j in range(BLOCK):
            pivot = small[j][j]
            inverse = pl.reciprocal(pivot, full_range=False)
            diagonal = jnp.where(row == k + j, pivot, diagonal)
            factor = jnp.where(row > k + j, columns[j] * inverse, 0.0)
            factors.append(factor)
            below = [small[i][j] for i in range(BLOCK) if i > j]
            for i in range(j + 1, BLOCK):
                ratio = small[i][j] * inverse
                for c in range(j + 1, i + 1):
                    small[i][c] = small[i][c] - ratio * below[c - j - 1]
                tops[i] = [x - ratio * y for x, y in zip(tops[i], tops[j])]
                columns[i] = columns[i] - factor * below[i - j - 1]
        for n in range(len(work)):
            if n > 0 or k + BLOCK < RANK:
                for j in range(BLOCK):
                    work[n] = work[n] - factors[j] * tops[j][n]
    scale = lax.rsqrt(diagonal)
    return jnp.concatenate([work[1] * scale, work[2] * scale], axis=1)


def subspace(gram, start, held):
    for n, part in enumerate(split3(gram)[:2]):
        held[n] = part

    def times_gram(pieces):
        return product(pieces, [held[0], held[1]], ((1,), (0,)))

    def iterate(_, grown):
        pieces = split3(grown)
        inner = product(pieces, pieces, ((1,), (1,)))
        return orthonormal(times_gram(pieces), inner)

    grown = lax.fori_loop(0, POWER_ITERS - 1, iterate, times_gram(split3(start)))
    pieces = split3(grown)
    return orthonormal(grown, product(pieces, pieces, ((1,), (1,))))


def halo_kernel(depth, left_ref, right_ref, top_ref, bottom_ref, up_ref, down_ref, side_ref, wide):
    rows, cols = side_ref.shape[0], top_ref.shape[1]
    wide[...] = jnp.zeros_like(wide)
    wide[:, 0:depth] = right_ref[...].astype(f32)
    wide[:, SIDE - depth :] = left_ref[...].astype(f32)
    side = wide[...].astype(bf16)
    side_ref[...] = side
    up_ref[:, 0:cols] = top_ref[...]
    up_ref[:, cols:] = side[:depth]
    down_ref[:, 0:cols] = bottom_ref[...]
    down_ref[:, cols:] = side[rows - depth :]


def subspace_kernel(inv_count, packed_ref, start_ref, basis_ref, held):
    basis_ref[...] = subspace(unpack(packed_ref[...], inv_count), start_ref[...], held)


def main_kernel(
    depth, n_rows, n_cols, basis_ref, mid_ref, above_ref, below_ref, side_ref,
    out_ref, proj_ref, fit, field_a, field_b, out_stage, proj_stage, out_sems, proj_sem
):
    rows, cols, bands = mid_ref.shape
    span = cols + SIDE
    proj_copy = pltpu.make_async_copy(proj_stage, proj_ref, proj_sem)

    def out_copy(n):
        part = pl.ds(n * OUT_ROWS, OUT_ROWS)
        return pltpu.make_async_copy(out_stage.at[part], out_ref.at[part], out_sems.at[n])

    high, mid, low = split3(basis_ref[...])
    tn = (((0,), (0,)), ((), ()))
    mixed = lax.dot_general(
        jnp.concatenate([high, high, high], axis=0),
        jnp.concatenate([high, mid, low], axis=0),
        tn,
        preferred_element_type=f32,
    )
    mixed = (mixed[:bands] * 4.0).astype(bf16)

    def fitted(flat):
        return jnp.dot(flat, mixed, preferred_element_type=f32)

    def project():
        right = jnp.concatenate([high, high, high, mid, mid, low], axis=0)
        left = jnp.concatenate([high, mid, low, high, mid, high], axis=0)
        full = lax.dot_general(left, right, tn, preferred_element_type=f32)
        proj_stage[...] = full[:bands, :bands]
        proj_copy.start()

    def fit_rows(start, stop):
        n = stop - start
        if depth <= start < depth + rows:
            part = slice(start - depth, stop - depth)
            center = mid_ref[part].reshape(n * cols, bands)
            side = side_ref[part].astype(f32).reshape(n * SIDE, bands).astype(bf16)
            res = fitted(jnp.concatenate([center, side], axis=0))
            for h, lane in enumerate(lanes):
                fit[h, start:stop, 0:cols] = res[: n * cols, lane].reshape(n, cols, HALF)
                fit[h, start:stop, cols:span] = res[n * cols :, lane].reshape(n, SIDE, HALF)
        else:
            block = above_ref[...] if start < depth else below_ref[...]
            flat = block.astype(f32).reshape(n * span, bands).astype(bf16)
            res = fitted(flat)
            for h, lane in enumerate(lanes):
                fit[h, start:stop] = res[:, lane].reshape(n, span, HALF)

    row, col = lax.axis_index("narrow"), lax.axis_index("wide")
    at_top, at_bottom = row == 0, row == n_rows - 1
    at_left, at_right = col == 0, col == n_cols - 1
    per = span // SUB
    place = lax.broadcasted_iota(jnp.int32, (SUB, HALF), 0)
    keeps = {}
    for column, shut in ((cols - 1, at_right), (span - 1, at_left)):
        keep = jnp.where((place == column // per) & shut, 0.0, 1.0).astype(f32)
        keeps[column % per] = keeps[column % per] * keep if column % per in keeps else keep
    open_rows = {
        depth - 1: jnp.where(at_top, 0.0, 1.0),
        depth + rows - 1: jnp.where(at_bottom, 0.0, 1.0),
    }
    lanes = [slice(0, HALF), slice(HALF, LANES)]
    fields = [fit, field_a, field_b]

    def natural(ref, h, r):
        return [ref[h, r, pl.ds(w, SUB, stride=per), :] for w in range(per)]

    def spread(ref, h, r):
        return [ref[h, r, w * SUB : (w + 1) * SUB, :] for w in range(per)]

    def slopes(now, later, open_row=None):
        follow = now[1:] + [pltpu.roll(now[0], SUB - 1, 0)]
        downs, acrosses = [], []
        for w in range(per):
            down = later[w] - now[w]
            if open_row is not None:
                down = down * open_row
            across = follow[w] - now[w]
            if w in keeps:
                across = across * keeps[w]
            inverse = lax.rsqrt(down * down + (across * across + 4.0))
            downs.append(down * inverse)
            acrosses.append(across * inverse)
        return downs, acrosses

    def advance(base, before, down, across):
        behind = [pltpu.roll(across[-1], 1, 0)] + across[:-1]
        return [
            base[w] + ((down[w] - before[w]) + (across[w] - behind[w])) for w in range(per)
        ]

    def put(ref, h, r, value):
        for w in range(per):
            ref[h, r, w * SUB : (w + 1) * SUB, :] = value[w]

    tall = rows + 2 * depth
    groups = [(0, depth)]
    for n in FIT_ROWS:
        groups.append((groups[-1][1], groups[-1][1] + n))
    groups += [(depth + rows, tall)]
    ready = 0
    befores = [None] * len(lanes)
    for r in range(tall - 1):
        while ready < len(groups) and groups[ready][0] <= r + 1 + AHEAD:
            fit_rows(*groups[ready])
            ready += 1
            if ready == 4:
                project()
        for h in range(len(lanes)):
            now = natural(fit, h, r)
            down, across = slopes(now, natural(fit, h, r + 1), open_rows.get(r))
            if r > 0:
                put(field_a, h, r, advance(now, befores[h], down, across))
            befores[h] = down

    def step(s, first, trips, unroll):
        source, final = fields[s], s == TV_ITERS - 1

        @pl.when(at_top)
        def _():
            source[:, depth - 1] = source[:, depth]

        @pl.when(at_bottom)
        def _():
            source[:, depth + rows] = source[:, depth + rows - 1]

        def block_step(n, carry):
            carry = list(carry)
            for inner in range(unroll):
                r = first + n * unroll + inner
                for h, lane in enumerate(lanes):
                    now, before = carry[2 * h], carry[2 * h + 1]
                    later = spread(source, h, r + 1)
                    down, across = slopes(now, later)
                    base = [0.5 * (x + y) for x, y in zip(now, natural(fit, h, r))]
                    value = advance(base, before, down, across)
                    if final:
                        for w in range(per):
                            field_a[h, r, pl.ds(w, SUB, stride=per), :] = value[w]
                        result = (field_a[h, r, 0:cols, :] * 0.25).astype(bf16)
                        width = min(lane.stop, bands) - lane.start
                        out_stage[r - depth, :, lane.start : lane.start + width] = result[:, :width]
                    else:
                        put(fields[s + 1], h, r, value)
                    carry[2 * h], carry[2 * h + 1] = later, down
                if final and inner % OUT_ROWS == OUT_ROWS - 1:
                    out_copy(n * (unroll // OUT_ROWS) + inner // OUT_ROWS).start()
            return tuple(carry)

        carry = []
        for h in range(len(lanes)):
            before, now = spread(source, h, first - 1), spread(source, h, first)
            carry += [now, slopes(before, now)[0]]
        lax.fori_loop(0, trips, block_step, tuple(carry))

    step(1, 2, (rows + 2) // TV_ROWS[0], TV_ROWS[0])
    step(2, depth, rows // TV_ROWS[1], TV_ROWS[1])
    proj_copy.wait()
    for n in range(rows // OUT_ROWS):
        out_copy(n).wait()


def start_basis():
    bands = np.arange(BANDS, dtype=np.float32)[None, :]
    cols = np.arange(RANK, dtype=np.float32)[:, None]
    angle = np.float32(np.pi) * (bands + np.float32(0.5)) * cols / np.float32(BANDS)
    return np.pad(np.cos(angle).astype(np.float32), ((0, 0), (0, LANES - BANDS)))


def neighbours(block, axis, dim, width):
    count = lax.axis_size(axis)
    size = block.shape[dim]
    head = lax.slice_in_dim(block, 0, width, axis=dim)
    tail = lax.slice_in_dim(block, size - width, size, axis=dim)
    before = lax.ppermute(tail, axis, [(i, i + 1) for i in range(count - 1)])
    after = lax.ppermute(head, axis, [(i + 1, i) for i in range(count - 1)])
    return before, after


def exchange(pieces, axes):
    return lax.all_to_all(pieces, axes, split_axis=0, concat_axis=0)


def body(cube):
    n_rows = lax.axis_size("narrow")
    n_cols = lax.axis_size("wide")
    count = n_rows * n_cols
    rows, cols, bands = cube.shape
    depth = TV_ITERS
    axes = ("narrow", "wide")

    tall_packed = -(-bands // count) * count
    pieces = 2 if rows % 2 == 0 else 1
    packed = pl.pallas_call(
        gram_kernel,
        in_specs=[pl.BlockSpec(memory_space=pl.ANY)],
        out_shape=jax.ShapeDtypeStruct((tall_packed, HALF), f32),
        scratch_shapes=[
            pltpu.VMEM(cube.shape, cube.dtype),
            pltpu.VMEM((LANES, LANES), f32),
            pltpu.SemaphoreType.DMA((pieces,)),
        ],
        compiler_params=pltpu.CompilerParams(vmem_limit_bytes=62 * 2**20),
    )(cube)
    packed, cube = lax.optimization_barrier((packed, cube))
    left, right = neighbours(cube, "wide", 1, depth)
    vmem = pl.BlockSpec(memory_space=pltpu.VMEM)
    pieces_shape = (count, 1, tall_packed // count * HALF)
    part = exchange(packed.reshape(pieces_shape), axes).reshape(tall_packed, HALF)
    share = pl.pallas_call(
        functools.partial(sum_kernel, count),
        in_specs=[vmem],
        out_specs=vmem,
        out_shape=jax.ShapeDtypeStruct((tall_packed, HALF), f32),
        compiler_params=pltpu.CompilerParams(vmem_limit_bytes=16 * 2**20),
    )(part)
    gathered = exchange(share.reshape(pieces_shape), axes).reshape(tall_packed, HALF)

    tall, span = rows + 2 * depth, cols + SIDE
    up, down, side = pl.pallas_call(
        functools.partial(halo_kernel, depth),
        in_specs=[vmem] * 4,
        out_specs=[vmem] * 3,
        out_shape=[
            jax.ShapeDtypeStruct((depth, span, bands), bf16),
            jax.ShapeDtypeStruct((depth, span, bands), bf16),
            jax.ShapeDtypeStruct((rows, SIDE, bands), bf16),
        ],
        scratch_shapes=[pltpu.VMEM((rows, SIDE, bands), f32)],
        cost_estimate=pl.CostEstimate(flops=2**32, bytes_accessed=2**18, transcendentals=0),
        compiler_params=pltpu.CompilerParams(vmem_limit_bytes=16 * 2**20),
    )(left, right, cube[:depth], cube[rows - depth :])
    above = lax.ppermute(down, "narrow", [(i, i + 1) for i in range(n_rows - 1)])
    below = lax.ppermute(up, "narrow", [(i + 1, i) for i in range(n_rows - 1)])

    inv_count = 1.0 / (count * rows * cols)
    basis = pl.pallas_call(
        functools.partial(subspace_kernel, inv_count),
        in_specs=[vmem] * 2,
        out_specs=vmem,
        out_shape=jax.ShapeDtypeStruct((RANK, LANES), f32),
        scratch_shapes=[pltpu.VMEM((2, LANES, LANES), bf16)],
        cost_estimate=pl.CostEstimate(flops=2**32, bytes_accessed=2**18, transcendentals=0),
        compiler_params=pltpu.CompilerParams(vmem_limit_bytes=16 * 2**20),
    )(gathered, jnp.asarray(start_basis()))
    restored, projector = pl.pallas_call(
        functools.partial(main_kernel, depth, n_rows, n_cols),
        in_specs=[vmem] * 5,
        out_specs=[pl.BlockSpec(memory_space=pl.ANY)] * 2,
        out_shape=[
            jax.ShapeDtypeStruct((rows, cols, bands), bf16),
            jax.ShapeDtypeStruct((bands, bands), f32),
        ],
        scratch_shapes=[pltpu.VMEM((2, tall, span, HALF), f32)] * 3
        + [
            pltpu.VMEM((rows, cols, bands), bf16),
            pltpu.VMEM((bands, bands), f32),
            pltpu.SemaphoreType.DMA((rows // OUT_ROWS,)),
            pltpu.SemaphoreType.DMA,
        ],
        compiler_params=pltpu.CompilerParams(vmem_limit_bytes=48 * 2**20),
    )(basis, cube, above, below, side)
    return restored, projector


def solution(mesh):
    return jax.shard_map(
        body,
        mesh=mesh,
        in_specs=(P("narrow", "wide", None),),
        out_specs=(P("narrow", "wide", None), P()),
        check_vma=False,
    )
```

```python
import functools

import jax
import jax.numpy as jnp
import numpy as np
from jax import lax
from jax.experimental import pallas as pl
from jax.experimental.pallas import tpu as pltpu
from jax.sharding import PartitionSpec as P

BANDS = 224
RANK = 16
POWER_ITERS = 4
TV_ITERS = 3
LANES = 256
HALF = 128
TAIL = BANDS - HALF
SIDE = 8
SUB = 8
BLOCK = 8
FIT_ROWS = (2, 6, 8, 8, 8)
AHEAD = 4
TV_ROWS = (17, 16)
OUT_ROWS = 4

f32 = jnp.float32
bf16 = jnp.bfloat16


def iotas(shape):
    return lax.broadcasted_iota(jnp.int32, shape, 0), lax.broadcasted_iota(jnp.int32, shape, 1)


def gram_kernel(cube_ref, packed_ref, full):
    rows, cols, bands = cube_ref.shape
    flat = cube_ref[...].reshape(rows * cols, bands)
    full[HALF:, HALF:] = jnp.zeros((LANES - HALF, LANES - HALF), f32)
    full[0:bands, 0:bands] = lax.dot_general(
        flat, flat, (((0,), (0,)), ((), ())), preferred_element_type=f32
    )
    i, j = iotas((HALF, HALF))
    first = full[0:HALF, 0:HALF]
    second = pltpu.roll(full[HALF:LANES, HALF:LANES], 1, 1)
    packed_ref[0:HALF, :] = jnp.where(j <= i, first, second)
    packed_ref[HALF:bands, :] = full[HALF:bands, 0:HALF]
    if packed_ref.shape[0] > bands:
        packed_ref[bands:, :] = jnp.zeros((packed_ref.shape[0] - bands, HALF), f32)


def sum_kernel(count, pieces_ref, spread_ref):
    high = pieces_ref.shape[0] // count
    parts = [pieces_ref[n * high : (n + 1) * high, :] for n in range(count)]
    total = functools.reduce(jnp.add, parts)
    for n in range(count):
        spread_ref[n * high : (n + 1) * high, :] = total


def split3(x):
    high = x.astype(bf16)
    rest = x - high.astype(f32)
    mid = rest.astype(bf16)
    low = (rest - mid.astype(f32)).astype(bf16)
    return high, mid, low


def product(left, right, dims):
    def dot(a, b):
        return lax.dot_general(a, b, (dims, ((), ())), preferred_element_type=f32)

    n = left[0].shape[0]
    top = dot(jnp.concatenate(left, axis=0), right[0])
    middle = dot(jnp.concatenate(left[:2], axis=0), right[1])
    small = top[2 * n : 3 * n] + middle[n : 2 * n]
    if len(right) > 2:
        small = small + dot(left[0], right[2])
    return top[:n] + ((top[n : 2 * n] + middle[:n]) + small)


def unpack(packed, scale):
    i, j = iotas((HALF, HALF))
    merged = packed[0:HALF, :] * scale
    below = packed[HALF:BANDS, :] * scale
    below = jnp.concatenate([below, jnp.zeros((LANES - BANDS, HALF), f32)], axis=0)
    first = jnp.where(j <= i, merged, 0.0) + jnp.where(j < i, merged, 0.0).T
    moved = pltpu.roll(merged, HALF - 1, 1)
    inside = (i < TAIL) & (j < TAIL)
    second = jnp.where(inside & (j >= i), moved, 0.0) + jnp.where(inside & (j > i), moved, 0.0).T
    return jnp.concatenate(
        [
            jnp.concatenate([first, below.T], axis=1),
            jnp.concatenate([below, second], axis=1),
        ],
        axis=0,
    )


def orthonormal(grown, inner):
    row = lax.broadcasted_iota(jnp.int32, (RANK, HALF), 0)
    work = [
        jnp.concatenate([inner, jnp.zeros((RANK, HALF - RANK), f32)], axis=1),
        grown[:, :HALF],
        grown[:, HALF:],
    ]
    diagonal = jnp.ones((RANK, HALF), f32)
    for k in range(0, RANK, BLOCK):
        columns = [
            jnp.broadcast_to(work[0][:, k + c : k + c + 1], (RANK, HALF)) for c in range(BLOCK)
        ]
        tops = [[part[k + r : k + r + 1, :] for part in work] for r in range(BLOCK)]
        small = [
            [columns[c][k + r : k + r + 1, :] for c in range(r + 1)] for r in range(BLOCK)
        ]
        factors = []
        for j in range(BLOCK):
            pivot = small[j][j]
            inverse = pl.reciprocal(pivot, full_range=False)
            diagonal = jnp.where(row == k + j, pivot, diagonal)
            factor = jnp.where(row > k + j, columns[j] * inverse, 0.0)
            factors.append(factor)
            below = [small[i][j] for i in range(BLOCK) if i > j]
            for i in range(j + 1, BLOCK):
                ratio = small[i][j] * inverse
                for c in range(j + 1, i + 1):
                    small[i][c] = small[i][c] - ratio * below[c - j - 1]
                tops[i] = [x - ratio * y for x, y in zip(tops[i], tops[j])]
                columns[i] = columns[i] - factor * below[i - j - 1]
        for n in range(len(work)):
            if n > 0 or k + BLOCK < RANK:
                for j in range(BLOCK):
                    work[n] = work[n] - factors[j] * tops[j][n]
    scale = lax.rsqrt(diagonal)
    return jnp.concatenate([work[1] * scale, work[2] * scale], axis=1)


def subspace(gram, start, held):
    for n, part in enumerate(split3(gram)[:2]):
        held[n] = part

    def times_gram(pieces):
        return product(pieces, [held[0], held[1]], ((1,), (0,)))

    def iterate(_, grown):
        pieces = split3(grown)
        inner = product(pieces, pieces, ((1,), (1,)))
        return orthonormal(times_gram(pieces), inner)

    grown = lax.fori_loop(0, POWER_ITERS - 1, iterate, times_gram(split3(start)))
    pieces = split3(grown)
    return orthonormal(grown, product(pieces, pieces, ((1,), (1,))))


def halo_kernel(depth, left_ref, right_ref, top_ref, bottom_ref, up_ref, down_ref, side_ref, wide):
    rows, cols = side_ref.shape[0], top_ref.shape[1]
    wide[...] = jnp.zeros_like(wide)
    wide[:, 0:depth] = right_ref[...].astype(f32)
    wide[:, SIDE - depth :] = left_ref[...].astype(f32)
    side = wide[...].astype(bf16)
    side_ref[...] = side
    up_ref[:, 0:cols] = top_ref[...]
    up_ref[:, cols:] = side[:depth]
    down_ref[:, 0:cols] = bottom_ref[...]
    down_ref[:, cols:] = side[rows - depth :]


def subspace_kernel(inv_count, packed_ref, start_ref, basis_ref, held):
    basis_ref[...] = subspace(unpack(packed_ref[...], inv_count), start_ref[...], held)


def main_kernel(
    depth, n_rows, n_cols, basis_ref, mid_ref, above_ref, below_ref, side_ref,
    out_ref, proj_ref, fit, field_a, field_b, out_stage, proj_stage, out_sems, proj_sem
):
    rows, cols, bands = mid_ref.shape
    span = cols + SIDE
    proj_copy = pltpu.make_async_copy(proj_stage, proj_ref, proj_sem)

    def out_copy(n):
        part = pl.ds(n * OUT_ROWS, OUT_ROWS)
        return pltpu.make_async_copy(out_stage.at[part], out_ref.at[part], out_sems.at[n])

    high, mid, low = split3(basis_ref[...])
    tn = (((0,), (0,)), ((), ()))
    mixed = lax.dot_general(
        jnp.concatenate([high, high, high], axis=0),
        jnp.concatenate([high, mid, low], axis=0),
        tn,
        preferred_element_type=f32,
    )
    mixed = mixed * 4.0
    mixed_high = mixed.astype(bf16)
    mixed_low = (mixed - mixed_high.astype(f32)).astype(bf16)
    mixed_both = jnp.concatenate([mixed_high, mixed_low], axis=0)

    def fitted(flat):
        padded = jnp.concatenate([flat, jnp.zeros((flat.shape[0], LANES - bands), bf16)], axis=1)
        both = jnp.concatenate([padded, padded], axis=1)
        return jnp.dot(both, mixed_both, preferred_element_type=f32)

    def project():
        right = jnp.concatenate([high, high, high, mid, mid, low], axis=0)
        left = jnp.concatenate([high, mid, low, high, mid, high], axis=0)
        full = lax.dot_general(left, right, tn, preferred_element_type=f32)
        proj_stage[...] = full[:bands, :bands]
        proj_copy.start()

    def fit_rows(start, stop):
        n = stop - start
        if depth <= start < depth + rows:
            part = slice(start - depth, stop - depth)
            center = mid_ref[part].reshape(n * cols, bands)
            side = side_ref[part].astype(f32).reshape(n * SIDE, bands).astype(bf16)
            res = fitted(jnp.concatenate([center, side], axis=0))
            for h, lane in enumerate(lanes):
                fit[h, start:stop, 0:cols] = res[: n * cols, lane].reshape(n, cols, HALF)
                fit[h, start:stop, cols:span] = res[n * cols :, lane].reshape(n, SIDE, HALF)
        else:
            block = above_ref[...] if start < depth else below_ref[...]
            flat = block.astype(f32).reshape(n * span, bands).astype(bf16)
            res = fitted(flat)
            for h, lane in enumerate(lanes):
                fit[h, start:stop] = res[:, lane].reshape(n, span, HALF)

    row, col = lax.axis_index("narrow"), lax.axis_index("wide")
    at_top, at_bottom = row == 0, row == n_rows - 1
    at_left, at_right = col == 0, col == n_cols - 1
    per = span // SUB
    place = lax.broadcasted_iota(jnp.int32, (SUB, HALF), 0)
    keeps = {}
    for column, shut in ((cols - 1, at_right), (span - 1, at_left)):
        keep = jnp.where((place == column // per) & shut, 0.0, 1.0).astype(f32)
        keeps[column % per] = keeps[column % per] * keep if column % per in keeps else keep
    open_rows = {
        depth - 1: jnp.where(at_top, 0.0, 1.0),
        depth + rows - 1: jnp.where(at_bottom, 0.0, 1.0),
    }
    lanes = [slice(0, HALF), slice(HALF, LANES)]
    fields = [fit, field_a, field_b]

    def natural(ref, h, r):
        return [ref[h, r, pl.ds(w, SUB, stride=per), :] for w in range(per)]

    def spread(ref, h, r):
        return [ref[h, r, w * SUB : (w + 1) * SUB, :] for w in range(per)]

    def slopes(now, later, open_row=None):
        follow = now[1:] + [pltpu.roll(now[0], SUB - 1, 0)]
        downs, acrosses = [], []
        for w in range(per):
            down = later[w] - now[w]
            if open_row is not None:
                down = down * open_row
            across = follow[w] - now[w]
            if w in keeps:
                across = across * keeps[w]
            inverse = lax.rsqrt(down * down + (across * across + 4.0))
            downs.append(down * inverse)
            acrosses.append(across * inverse)
        return downs, acrosses

    def advance(base, before, down, across):
        behind = [pltpu.roll(across[-1], 1, 0)] + across[:-1]
        return [
            base[w] + ((down[w] - before[w]) + (across[w] - behind[w])) for w in range(per)
        ]

    def put(ref, h, r, value):
        for w in range(per):
            ref[h, r, w * SUB : (w + 1) * SUB, :] = value[w]

    tall = rows + 2 * depth
    groups = [(0, depth)]
    for n in FIT_ROWS:
        groups.append((groups[-1][1], groups[-1][1] + n))
    groups += [(depth + rows, tall)]
    ready = 0
    befores = [None] * len(lanes)
    for r in range(tall - 1):
        while ready < len(groups) and groups[ready][0] <= r + 1 + AHEAD:
            fit_rows(*groups[ready])
            ready += 1
            if ready == 4:
                project()
        for h in range(len(lanes)):
            now = natural(fit, h, r)
            down, across = slopes(now, natural(fit, h, r + 1), open_rows.get(r))
            if r > 0:
                put(field_a, h, r, advance(now, befores[h], down, across))
            befores[h] = down

    def step(s, first, trips, unroll):
        source, final = fields[s], s == TV_ITERS - 1

        @pl.when(at_top)
        def _():
            source[:, depth - 1] = source[:, depth]

        @pl.when(at_bottom)
        def _():
            source[:, depth + rows] = source[:, depth + rows - 1]

        def block_step(n, carry):
            carry = list(carry)
            for inner in range(unroll):
                r = first + n * unroll + inner
                for h, lane in enumerate(lanes):
                    now, before = carry[2 * h], carry[2 * h + 1]
                    later = spread(source, h, r + 1)
                    down, across = slopes(now, later)
                    base = [0.5 * (x + y) for x, y in zip(now, natural(fit, h, r))]
                    value = advance(base, before, down, across)
                    if final:
                        for w in range(per):
                            field_a[h, r, pl.ds(w, SUB, stride=per), :] = value[w]
                        result = (field_a[h, r, 0:cols, :] * 0.25).astype(bf16)
                        width = min(lane.stop, bands) - lane.start
                        out_stage[r - depth, :, lane.start : lane.start + width] = result[:, :width]
                    else:
                        put(fields[s + 1], h, r, value)
                    carry[2 * h], carry[2 * h + 1] = later, down
                if final and inner % OUT_ROWS == OUT_ROWS - 1:
                    out_copy(n * (unroll // OUT_ROWS) + inner // OUT_ROWS).start()
            return tuple(carry)

        carry = []
        for h in range(len(lanes)):
            before, now = spread(source, h, first - 1), spread(source, h, first)
            carry += [now, slopes(before, now)[0]]
        lax.fori_loop(0, trips, block_step, tuple(carry))

    step(1, 2, (rows + 2) // TV_ROWS[0], TV_ROWS[0])
    step(2, depth, rows // TV_ROWS[1], TV_ROWS[1])
    proj_copy.wait()
    for n in range(rows // OUT_ROWS):
        out_copy(n).wait()


def start_basis():
    bands = np.arange(BANDS, dtype=np.float32)[None, :]
    cols = np.arange(RANK, dtype=np.float32)[:, None]
    angle = np.float32(np.pi) * (bands + np.float32(0.5)) * cols / np.float32(BANDS)
    return np.pad(np.cos(angle).astype(np.float32), ((0, 0), (0, LANES - BANDS)))


def neighbours(block, axis, dim, width):
    count = lax.axis_size(axis)
    size = block.shape[dim]
    head = lax.slice_in_dim(block, 0, width, axis=dim)
    tail = lax.slice_in_dim(block, size - width, size, axis=dim)
    before = lax.ppermute(tail, axis, [(i, i + 1) for i in range(count - 1)])
    after = lax.ppermute(head, axis, [(i + 1, i) for i in range(count - 1)])
    return before, after


def exchange(pieces, axes):
    return lax.all_to_all(pieces, axes, split_axis=0, concat_axis=0)


def body(cube):
    n_rows = lax.axis_size("narrow")
    n_cols = lax.axis_size("wide")
    count = n_rows * n_cols
    rows, cols, bands = cube.shape
    depth = TV_ITERS
    axes = ("narrow", "wide")

    tall_packed = -(-bands // count) * count
    vmem = pl.BlockSpec(memory_space=pltpu.VMEM)
    packed = pl.pallas_call(
        gram_kernel,
        in_specs=[vmem],
        out_specs=vmem,
        out_shape=jax.ShapeDtypeStruct((tall_packed, HALF), f32),
        scratch_shapes=[pltpu.VMEM((LANES, LANES), f32)],
        compiler_params=pltpu.CompilerParams(vmem_limit_bytes=32 * 2**20),
    )(cube)
    packed, cube = lax.optimization_barrier((packed, cube))
    left, right = neighbours(cube, "wide", 1, depth)
    pieces_shape = (count, 1, tall_packed // count * HALF)
    part = exchange(packed.reshape(pieces_shape), axes).reshape(tall_packed, HALF)
    share = pl.pallas_call(
        functools.partial(sum_kernel, count),
        in_specs=[vmem],
        out_specs=vmem,
        out_shape=jax.ShapeDtypeStruct((tall_packed, HALF), f32),
        compiler_params=pltpu.CompilerParams(vmem_limit_bytes=16 * 2**20),
    )(part)
    gathered = exchange(share.reshape(pieces_shape), axes).reshape(tall_packed, HALF)

    tall, span = rows + 2 * depth, cols + SIDE
    up, down, side = pl.pallas_call(
        functools.partial(halo_kernel, depth),
        in_specs=[vmem] * 4,
        out_specs=[vmem] * 3,
        out_shape=[
            jax.ShapeDtypeStruct((depth, span, bands), bf16),
            jax.ShapeDtypeStruct((depth, span, bands), bf16),
            jax.ShapeDtypeStruct((rows, SIDE, bands), bf16),
        ],
        scratch_shapes=[pltpu.VMEM((rows, SIDE, bands), f32)],
        cost_estimate=pl.CostEstimate(flops=2**32, bytes_accessed=2**18, transcendentals=0),
        compiler_params=pltpu.CompilerParams(vmem_limit_bytes=16 * 2**20),
    )(left, right, cube[:depth], cube[rows - depth :])
    above = lax.ppermute(down, "narrow", [(i, i + 1) for i in range(n_rows - 1)])
    below = lax.ppermute(up, "narrow", [(i + 1, i) for i in range(n_rows - 1)])

    inv_count = 1.0 / (count * rows * cols)
    basis = pl.pallas_call(
        functools.partial(subspace_kernel, inv_count),
        in_specs=[vmem] * 2,
        out_specs=vmem,
        out_shape=jax.ShapeDtypeStruct((RANK, LANES), f32),
        scratch_shapes=[pltpu.VMEM((2, LANES, LANES), bf16)],
        cost_estimate=pl.CostEstimate(flops=2**32, bytes_accessed=2**18, transcendentals=0),
        compiler_params=pltpu.CompilerParams(vmem_limit_bytes=16 * 2**20),
    )(gathered, jnp.asarray(start_basis()))
    restored, projector = pl.pallas_call(
        functools.partial(main_kernel, depth, n_rows, n_cols),
        in_specs=[vmem] * 5,
        out_specs=[pl.BlockSpec(memory_space=pl.ANY)] * 2,
        out_shape=[
            jax.ShapeDtypeStruct((rows, cols, bands), bf16),
            jax.ShapeDtypeStruct((bands, bands), f32),
        ],
        scratch_shapes=[pltpu.VMEM((2, tall, span, HALF), f32)] * 3
        + [
            pltpu.VMEM((rows, cols, bands), bf16),
            pltpu.VMEM((bands, bands), f32),
            pltpu.SemaphoreType.DMA((rows // OUT_ROWS,)),
            pltpu.SemaphoreType.DMA,
        ],
        compiler_params=pltpu.CompilerParams(vmem_limit_bytes=48 * 2**20),
    )(basis, cube, above, below, side)
    return restored, projector


def solution(mesh):
    return jax.shard_map(
        body,
        mesh=mesh,
        in_specs=(P("narrow", "wide", None),),
        out_specs=(P("narrow", "wide", None), P()),
        check_vma=False,
    )
```

```python
import functools

import jax
import jax.numpy as jnp
import numpy as np
from jax import lax
from jax.experimental import pallas as pl
from jax.experimental.pallas import tpu as pltpu
from jax.sharding import PartitionSpec as P

BANDS = 224
RANK = 16
POWER_ITERS = 4
TV_ITERS = 3
LANES = 256
HALF = 128
TAIL = BANDS - HALF
SIDE = 8
SUB = 8
BLOCK = 8
FIT_ROWS = (2, 4, 6, 8, 12)
AHEAD = 3
TV_ROWS = (17, 16)
OUT_ROWS = 4

f32 = jnp.float32
bf16 = jnp.bfloat16


def iotas(shape):
    return lax.broadcasted_iota(jnp.int32, shape, 0), lax.broadcasted_iota(jnp.int32, shape, 1)


def gram_kernel(cube_ref, packed_ref, full):
    rows, cols, bands = cube_ref.shape
    flat = cube_ref[...].reshape(rows * cols, bands)
    full[HALF:, HALF:] = jnp.zeros((LANES - HALF, LANES - HALF), f32)
    full[0:bands, 0:bands] = lax.dot_general(
        flat, flat, (((0,), (0,)), ((), ())), preferred_element_type=f32
    )
    i, j = iotas((HALF, HALF))
    first = full[0:HALF, 0:HALF]
    second = pltpu.roll(full[HALF:LANES, HALF:LANES], 1, 1)
    packed_ref[0:HALF, :] = jnp.where(j <= i, first, second)
    packed_ref[HALF:bands, :] = full[HALF:bands, 0:HALF]
    if packed_ref.shape[0] > bands:
        packed_ref[bands:, :] = jnp.zeros((packed_ref.shape[0] - bands, HALF), f32)


def sum_kernel(count, pieces_ref, spread_ref):
    high = pieces_ref.shape[0] // count
    parts = [pieces_ref[n * high : (n + 1) * high, :] for n in range(count)]
    total = functools.reduce(jnp.add, parts)
    for n in range(count):
        spread_ref[n * high : (n + 1) * high, :] = total


def split3(x):
    high = x.astype(bf16)
    rest = x - high.astype(f32)
    mid = rest.astype(bf16)
    low = (rest - mid.astype(f32)).astype(bf16)
    return high, mid, low


def product(left, right, dims):
    def dot(a, b):
        return lax.dot_general(a, b, (dims, ((), ())), preferred_element_type=f32)

    n = left[0].shape[0]
    top = dot(jnp.concatenate(left, axis=0), right[0])
    middle = dot(jnp.concatenate(left[:2], axis=0), right[1])
    small = top[2 * n : 3 * n] + middle[n : 2 * n]
    if len(right) > 2:
        small = small + dot(left[0], right[2])
    return top[:n] + ((top[n : 2 * n] + middle[:n]) + small)


def unpack(packed, scale):
    i, j = iotas((HALF, HALF))
    merged = packed[0:HALF, :] * scale
    below = packed[HALF:BANDS, :] * scale
    below = jnp.concatenate([below, jnp.zeros((LANES - BANDS, HALF), f32)], axis=0)
    first = jnp.where(j <= i, merged, 0.0) + jnp.where(j < i, merged, 0.0).T
    moved = pltpu.roll(merged, HALF - 1, 1)
    inside = (i < TAIL) & (j < TAIL)
    second = jnp.where(inside & (j >= i), moved, 0.0) + jnp.where(inside & (j > i), moved, 0.0).T
    return jnp.concatenate(
        [
            jnp.concatenate([first, below.T], axis=1),
            jnp.concatenate([below, second], axis=1),
        ],
        axis=0,
    )


def orthonormal(grown, inner):
    row = lax.broadcasted_iota(jnp.int32, (RANK, HALF), 0)
    work = [
        jnp.concatenate([inner, jnp.zeros((RANK, HALF - RANK), f32)], axis=1),
        grown[:, :HALF],
        grown[:, HALF:],
    ]
    diagonal = jnp.ones((RANK, HALF), f32)
    for k in range(0, RANK, BLOCK):
        columns = [
            jnp.broadcast_to(work[0][:, k + c : k + c + 1], (RANK, HALF)) for c in range(BLOCK)
        ]
        tops = [[part[k + r : k + r + 1, :] for part in work] for r in range(BLOCK)]
        small = [
            [columns[c][k + r : k + r + 1, :] for c in range(r + 1)] for r in range(BLOCK)
        ]
        factors = []
        for j in range(BLOCK):
            pivot = small[j][j]
            inverse = pl.reciprocal(pivot, full_range=False)
            diagonal = jnp.where(row == k + j, pivot, diagonal)
            factor = jnp.where(row > k + j, columns[j] * inverse, 0.0)
            factors.append(factor)
            below = [small[i][j] for i in range(BLOCK) if i > j]
            for i in range(j + 1, BLOCK):
                ratio = small[i][j] * inverse
                for c in range(j + 1, i + 1):
                    small[i][c] = small[i][c] - ratio * below[c - j - 1]
                tops[i] = [x - ratio * y for x, y in zip(tops[i], tops[j])]
                columns[i] = columns[i] - factor * below[i - j - 1]
        for n in range(len(work)):
            if n > 0 or k + BLOCK < RANK:
                for j in range(BLOCK):
                    work[n] = work[n] - factors[j] * tops[j][n]
    scale = lax.rsqrt(diagonal)
    return jnp.concatenate([work[1] * scale, work[2] * scale], axis=1)


def subspace(gram, start, held):
    for n, part in enumerate(split3(gram)[:2]):
        held[n] = part

    def times_gram(pieces):
        return product(pieces, [held[0], held[1]], ((1,), (0,)))

    def iterate(_, grown):
        pieces = split3(grown)
        inner = product(pieces, pieces, ((1,), (1,)))
        return orthonormal(times_gram(pieces), inner)

    grown = lax.fori_loop(0, POWER_ITERS - 1, iterate, times_gram(split3(start)))
    pieces = split3(grown)
    return orthonormal(grown, product(pieces, pieces, ((1,), (1,))))


def halo_kernel(depth, left_ref, right_ref, top_ref, bottom_ref, up_ref, down_ref, side_ref, wide):
    rows, cols = side_ref.shape[0], top_ref.shape[1]
    wide[...] = jnp.zeros_like(wide)
    wide[:, 0:depth] = right_ref[...].astype(f32)
    wide[:, SIDE - depth :] = left_ref[...].astype(f32)
    side = wide[...].astype(bf16)
    side_ref[...] = side
    up_ref[:, 0:cols] = top_ref[...]
    up_ref[:, cols:] = side[:depth]
    down_ref[:, 0:cols] = bottom_ref[...]
    down_ref[:, cols:] = side[rows - depth :]


def subspace_kernel(inv_count, packed_ref, start_ref, basis_ref, held):
    basis_ref[...] = subspace(unpack(packed_ref[...], inv_count), start_ref[...], held)


def main_kernel(
    depth, n_rows, n_cols, basis_ref, mid_ref, above_ref, below_ref, side_ref,
    out_ref, proj_ref, fit, field_a, field_b, out_stage, proj_stage, out_sems, proj_sem
):
    rows, cols, bands = mid_ref.shape
    span = cols + SIDE
    proj_copy = pltpu.make_async_copy(proj_stage, proj_ref, proj_sem)

    def out_copy(n):
        part = pl.ds(n * OUT_ROWS, OUT_ROWS)
        return pltpu.make_async_copy(out_stage.at[part], out_ref.at[part], out_sems.at[n])

    high, mid, low = split3(basis_ref[...])
    tn = (((0,), (0,)), ((), ()))
    mixed = lax.dot_general(
        jnp.concatenate([high, high, high], axis=0),
        jnp.concatenate([high, mid, low], axis=0),
        tn,
        preferred_element_type=f32,
    )
    mixed = mixed * 4.0
    mixed_high = mixed.astype(bf16)
    mixed_low = (mixed - mixed_high.astype(f32)).astype(bf16)
    mixed_both = jnp.concatenate([mixed_high, mixed_low], axis=0)

    def fitted(flat):
        padded = jnp.concatenate([flat, jnp.zeros((flat.shape[0], LANES - bands), bf16)], axis=1)
        both = jnp.concatenate([padded, padded], axis=1)
        return jnp.dot(both, mixed_both, preferred_element_type=f32)

    def project():
        right = jnp.concatenate([high, high, high, mid, mid, low], axis=0)
        left = jnp.concatenate([high, mid, low, high, mid, high], axis=0)
        full = lax.dot_general(left, right, tn, preferred_element_type=f32)
        proj_stage[...] = full[:bands, :bands]
        proj_copy.start()

    def fit_rows(start, stop):
        n = stop - start
        if depth <= start < depth + rows:
            part = slice(start - depth, stop - depth)
            center = mid_ref[part].reshape(n * cols, bands)
            side = side_ref[part].astype(f32).reshape(n * SIDE, bands).astype(bf16)
            res = fitted(jnp.concatenate([center, side], axis=0))
            for h, lane in enumerate(lanes):
                fit[h, start:stop, 0:cols] = res[: n * cols, lane].reshape(n, cols, HALF)
                fit[h, start:stop, cols:span] = res[n * cols :, lane].reshape(n, SIDE, HALF)
        else:
            block = above_ref[...] if start < depth else below_ref[...]
            flat = block.astype(f32).reshape(n * span, bands).astype(bf16)
            res = fitted(flat)
            for h, lane in enumerate(lanes):
                fit[h, start:stop] = res[:, lane].reshape(n, span, HALF)

    row, col = lax.axis_index("narrow"), lax.axis_index("wide")
    at_top, at_bottom = row == 0, row == n_rows - 1
    at_left, at_right = col == 0, col == n_cols - 1
    per = span // SUB
    place = lax.broadcasted_iota(jnp.int32, (SUB, HALF), 0)
    keeps = {}
    for column, shut in ((cols - 1, at_right), (span - 1, at_left)):
        keep = jnp.where((place == column // per) & shut, 0.0, 1.0).astype(f32)
        keeps[column % per] = keeps[column % per] * keep if column % per in keeps else keep
    open_rows = {
        depth - 1: jnp.where(at_top, 0.0, 1.0),
        depth + rows - 1: jnp.where(at_bottom, 0.0, 1.0),
    }
    lanes = [slice(0, HALF), slice(HALF, LANES)]
    fields = [fit, field_a, field_b]

    def natural(ref, h, r):
        return [ref[h, r, pl.ds(w, SUB, stride=per), :] for w in range(per)]

    def spread(ref, h, r):
        return [ref[h, r, w * SUB : (w + 1) * SUB, :] for w in range(per)]

    def slopes(now, later, open_row=None):
        follow = now[1:] + [pltpu.roll(now[0], SUB - 1, 0)]
        downs, acrosses = [], []
        for w in range(per):
            down = later[w] - now[w]
            if open_row is not None:
                down = down * open_row
            across = follow[w] - now[w]
            if w in keeps:
                across = across * keeps[w]
            inverse = lax.rsqrt(down * down + (across * across + 4.0))
            downs.append(down * inverse)
            acrosses.append(across * inverse)
        return downs, acrosses

    def advance(base, before, down, across):
        behind = [pltpu.roll(across[-1], 1, 0)] + across[:-1]
        return [
            base[w] + ((down[w] - before[w]) + (across[w] - behind[w])) for w in range(per)
        ]

    def put(ref, h, r, value):
        for w in range(per):
            ref[h, r, w * SUB : (w + 1) * SUB, :] = value[w]

    tall = rows + 2 * depth
    groups = [(0, depth)]
    for n in FIT_ROWS:
        groups.append((groups[-1][1], groups[-1][1] + n))
    groups += [(depth + rows, tall)]
    ready = 0
    befores = [None] * len(lanes)
    for r in range(tall - 1):
        while ready < len(groups) and groups[ready][0] <= r + 1 + AHEAD:
            fit_rows(*groups[ready])
            ready += 1
            if ready == 4:
                project()
        for h in range(len(lanes)):
            now = natural(fit, h, r)
            down, across = slopes(now, natural(fit, h, r + 1), open_rows.get(r))
            if r > 0:
                put(field_a, h, r, advance(now, befores[h], down, across))
            befores[h] = down

    def step(s, first, trips, unroll):
        source, final = fields[s], s == TV_ITERS - 1

        @pl.when(at_top)
        def _():
            source[:, depth - 1] = source[:, depth]

        @pl.when(at_bottom)
        def _():
            source[:, depth + rows] = source[:, depth + rows - 1]

        def block_step(n, carry):
            carry = list(carry)
            for inner in range(unroll):
                r = first + n * unroll + inner
                for h, lane in enumerate(lanes):
                    now, before = carry[2 * h], carry[2 * h + 1]
                    later = spread(source, h, r + 1)
                    down, across = slopes(now, later)
                    base = [0.5 * (x + y) for x, y in zip(now, natural(fit, h, r))]
                    value = advance(base, before, down, across)
                    if final:
                        for w in range(per):
                            field_a[h, r, pl.ds(w, SUB, stride=per), :] = value[w]
                        result = (field_a[h, r, 0:cols, :] * 0.25).astype(bf16)
                        width = min(lane.stop, bands) - lane.start
                        out_stage[r - depth, :, lane.start : lane.start + width] = result[:, :width]
                    else:
                        put(fields[s + 1], h, r, value)
                    carry[2 * h], carry[2 * h + 1] = later, down
                if final and inner % OUT_ROWS == OUT_ROWS - 1:
                    out_copy(n * (unroll // OUT_ROWS) + inner // OUT_ROWS).start()
            return tuple(carry)

        carry = []
        for h in range(len(lanes)):
            before, now = spread(source, h, first - 1), spread(source, h, first)
            carry += [now, slopes(before, now)[0]]
        lax.fori_loop(0, trips, block_step, tuple(carry))

    step(1, 2, (rows + 2) // TV_ROWS[0], TV_ROWS[0])
    step(2, depth, rows // TV_ROWS[1], TV_ROWS[1])
    proj_copy.wait()
    for n in range(rows // OUT_ROWS):
        out_copy(n).wait()


def start_basis():
    bands = np.arange(BANDS, dtype=np.float32)[None, :]
    cols = np.arange(RANK, dtype=np.float32)[:, None]
    angle = np.float32(np.pi) * (bands + np.float32(0.5)) * cols / np.float32(BANDS)
    return np.pad(np.cos(angle).astype(np.float32), ((0, 0), (0, LANES - BANDS)))


def neighbours(block, axis, dim, width):
    count = lax.axis_size(axis)
    size = block.shape[dim]
    head = lax.slice_in_dim(block, 0, width, axis=dim)
    tail = lax.slice_in_dim(block, size - width, size, axis=dim)
    before = lax.ppermute(tail, axis, [(i, i + 1) for i in range(count - 1)])
    after = lax.ppermute(head, axis, [(i + 1, i) for i in range(count - 1)])
    return before, after


def exchange(pieces, axes):
    return lax.all_to_all(pieces, axes, split_axis=0, concat_axis=0)


def body(cube):
    n_rows = lax.axis_size("narrow")
    n_cols = lax.axis_size("wide")
    count = n_rows * n_cols
    rows, cols, bands = cube.shape
    depth = TV_ITERS
    axes = ("narrow", "wide")

    tall_packed = -(-bands // count) * count
    vmem = pl.BlockSpec(memory_space=pltpu.VMEM)
    packed = pl.pallas_call(
        gram_kernel,
        in_specs=[vmem],
        out_specs=vmem,
        out_shape=jax.ShapeDtypeStruct((tall_packed, HALF), f32),
        scratch_shapes=[pltpu.VMEM((LANES, LANES), f32)],
        compiler_params=pltpu.CompilerParams(vmem_limit_bytes=32 * 2**20),
    )(cube)
    packed, cube = lax.optimization_barrier((packed, cube))
    left, right = neighbours(cube, "wide", 1, depth)
    pieces_shape = (count, 1, tall_packed // count * HALF)
    part = exchange(packed.reshape(pieces_shape), axes).reshape(tall_packed, HALF)
    share = pl.pallas_call(
        functools.partial(sum_kernel, count),
        in_specs=[vmem],
        out_specs=vmem,
        out_shape=jax.ShapeDtypeStruct((tall_packed, HALF), f32),
        compiler_params=pltpu.CompilerParams(vmem_limit_bytes=16 * 2**20),
    )(part)
    gathered = exchange(share.reshape(pieces_shape), axes).reshape(tall_packed, HALF)

    tall, span = rows + 2 * depth, cols + SIDE
    up, down, side = pl.pallas_call(
        functools.partial(halo_kernel, depth),
        in_specs=[vmem] * 4,
        out_specs=[vmem] * 3,
        out_shape=[
            jax.ShapeDtypeStruct((depth, span, bands), bf16),
            jax.ShapeDtypeStruct((depth, span, bands), bf16),
            jax.ShapeDtypeStruct((rows, SIDE, bands), bf16),
        ],
        scratch_shapes=[pltpu.VMEM((rows, SIDE, bands), f32)],
        cost_estimate=pl.CostEstimate(flops=2**32, bytes_accessed=2**18, transcendentals=0),
        compiler_params=pltpu.CompilerParams(vmem_limit_bytes=16 * 2**20),
    )(left, right, cube[:depth], cube[rows - depth :])
    above = lax.ppermute(down, "narrow", [(i, i + 1) for i in range(n_rows - 1)])
    below = lax.ppermute(up, "narrow", [(i + 1, i) for i in range(n_rows - 1)])

    inv_count = 1.0 / (count * rows * cols)
    basis = pl.pallas_call(
        functools.partial(subspace_kernel, inv_count),
        in_specs=[vmem] * 2,
        out_specs=vmem,
        out_shape=jax.ShapeDtypeStruct((RANK, LANES), f32),
        scratch_shapes=[pltpu.VMEM((2, LANES, LANES), bf16)],
        cost_estimate=pl.CostEstimate(flops=2**32, bytes_accessed=2**18, transcendentals=0),
        compiler_params=pltpu.CompilerParams(vmem_limit_bytes=16 * 2**20),
    )(gathered, jnp.asarray(start_basis()))
    restored, projector = pl.pallas_call(
        functools.partial(main_kernel, depth, n_rows, n_cols),
        in_specs=[vmem] * 5,
        out_specs=[pl.BlockSpec(memory_space=pl.ANY)] * 2,
        out_shape=[
            jax.ShapeDtypeStruct((rows, cols, bands), bf16),
            jax.ShapeDtypeStruct((bands, bands), f32),
        ],
        scratch_shapes=[pltpu.VMEM((2, tall, span, HALF), f32)] * 3
        + [
            pltpu.VMEM((rows, cols, bands), bf16),
            pltpu.VMEM((bands, bands), f32),
            pltpu.SemaphoreType.DMA((rows // OUT_ROWS,)),
            pltpu.SemaphoreType.DMA,
        ],
        compiler_params=pltpu.CompilerParams(vmem_limit_bytes=48 * 2**20),
    )(basis, cube, above, below, side)
    return restored, projector


def solution(mesh):
    return jax.shard_map(
        body,
        mesh=mesh,
        in_specs=(P("narrow", "wide", None),),
        out_specs=(P("narrow", "wide", None), P()),
        check_vma=False,
    )
```

```python
import functools

import jax
import jax.numpy as jnp
import numpy as np
from jax import lax
from jax.experimental import pallas as pl
from jax.experimental.pallas import tpu as pltpu
from jax.sharding import PartitionSpec as P

BANDS = 224
RANK = 16
POWER_ITERS = 4
TV_ITERS = 3
LANES = 256
HALF = 128
TAIL = BANDS - HALF
SIDE = 8
SUB = 8
BLOCK = 8
FIT_ROWS = (2, 6, 8, 8, 8)
AHEAD = 12
TV_ROWS = (17, 16)
OUT_ROWS = 4

f32 = jnp.float32
bf16 = jnp.bfloat16


def iotas(shape):
    return lax.broadcasted_iota(jnp.int32, shape, 0), lax.broadcasted_iota(jnp.int32, shape, 1)


def gram_kernel(cube_ref, packed_ref, full):
    rows, cols, bands = cube_ref.shape
    flat = cube_ref[...].reshape(rows * cols, bands)
    full[HALF:, HALF:] = jnp.zeros((LANES - HALF, LANES - HALF), f32)
    full[0:bands, 0:bands] = lax.dot_general(
        flat, flat, (((0,), (0,)), ((), ())), preferred_element_type=f32
    )
    i, j = iotas((HALF, HALF))
    first = full[0:HALF, 0:HALF]
    second = pltpu.roll(full[HALF:LANES, HALF:LANES], 1, 1)
    packed_ref[0:HALF, :] = jnp.where(j <= i, first, second)
    packed_ref[HALF:bands, :] = full[HALF:bands, 0:HALF]
    if packed_ref.shape[0] > bands:
        packed_ref[bands:, :] = jnp.zeros((packed_ref.shape[0] - bands, HALF), f32)


def sum_kernel(count, pieces_ref, spread_ref):
    high = pieces_ref.shape[0] // count
    parts = [pieces_ref[n * high : (n + 1) * high, :] for n in range(count)]
    total = functools.reduce(jnp.add, parts)
    for n in range(count):
        spread_ref[n * high : (n + 1) * high, :] = total


def split3(x):
    high = x.astype(bf16)
    rest = x - high.astype(f32)
    mid = rest.astype(bf16)
    low = (rest - mid.astype(f32)).astype(bf16)
    return high, mid, low


def product(left, right, dims):
    def dot(a, b):
        return lax.dot_general(a, b, (dims, ((), ())), preferred_element_type=f32)

    n = left[0].shape[0]
    top = dot(jnp.concatenate(left, axis=0), right[0])
    middle = dot(jnp.concatenate(left[:2], axis=0), right[1])
    small = top[2 * n : 3 * n] + middle[n : 2 * n]
    if len(right) > 2:
        small = small + dot(left[0], right[2])
    return top[:n] + ((top[n : 2 * n] + middle[:n]) + small)


def unpack(packed, scale):
    i, j = iotas((HALF, HALF))
    merged = packed[0:HALF, :] * scale
    below = packed[HALF:BANDS, :] * scale
    below = jnp.concatenate([below, jnp.zeros((LANES - BANDS, HALF), f32)], axis=0)
    first = jnp.where(j <= i, merged, 0.0) + jnp.where(j < i, merged, 0.0).T
    moved = pltpu.roll(merged, HALF - 1, 1)
    inside = (i < TAIL) & (j < TAIL)
    second = jnp.where(inside & (j >= i), moved, 0.0) + jnp.where(inside & (j > i), moved, 0.0).T
    return jnp.concatenate(
        [
            jnp.concatenate([first, below.T], axis=1),
            jnp.concatenate([below, second], axis=1),
        ],
        axis=0,
    )


def orthonormal(grown, inner):
    row = lax.broadcasted_iota(jnp.int32, (RANK, HALF), 0)
    work = [
        jnp.concatenate([inner, jnp.zeros((RANK, HALF - RANK), f32)], axis=1),
        grown[:, :HALF],
        grown[:, HALF:],
    ]
    diagonal = jnp.ones((RANK, HALF), f32)
    for k in range(0, RANK, BLOCK):
        columns = [
            jnp.broadcast_to(work[0][:, k + c : k + c + 1], (RANK, HALF)) for c in range(BLOCK)
        ]
        tops = [[part[k + r : k + r + 1, :] for part in work] for r in range(BLOCK)]
        small = [
            [columns[c][k + r : k + r + 1, :] for c in range(r + 1)] for r in range(BLOCK)
        ]
        factors = []
        for j in range(BLOCK):
            pivot = small[j][j]
            inverse = pl.reciprocal(pivot, full_range=False)
            diagonal = jnp.where(row == k + j, pivot, diagonal)
            factor = jnp.where(row > k + j, columns[j] * inverse, 0.0)
            factors.append(factor)
            below = [small[i][j] for i in range(BLOCK) if i > j]
            for i in range(j + 1, BLOCK):
                ratio = small[i][j] * inverse
                for c in range(j + 1, i + 1):
                    small[i][c] = small[i][c] - ratio * below[c - j - 1]
                tops[i] = [x - ratio * y for x, y in zip(tops[i], tops[j])]
                columns[i] = columns[i] - factor * below[i - j - 1]
        for n in range(len(work)):
            if n > 0 or k + BLOCK < RANK:
                for j in range(BLOCK):
                    work[n] = work[n] - factors[j] * tops[j][n]
    scale = lax.rsqrt(diagonal)
    return jnp.concatenate([work[1] * scale, work[2] * scale], axis=1)


def subspace(gram, start, held):
    for n, part in enumerate(split3(gram)[:2]):
        held[n] = part

    def times_gram(pieces):
        return product(pieces, [held[0], held[1]], ((1,), (0,)))

    def iterate(_, grown):
        pieces = split3(grown)
        inner = product(pieces, pieces, ((1,), (1,)))
        return orthonormal(times_gram(pieces), inner)

    grown = lax.fori_loop(0, POWER_ITERS - 1, iterate, times_gram(split3(start)))
    pieces = split3(grown)
    return orthonormal(grown, product(pieces, pieces, ((1,), (1,))))


def halo_kernel(depth, left_ref, right_ref, top_ref, bottom_ref, up_ref, down_ref, side_ref, wide):
    rows, cols = side_ref.shape[0], top_ref.shape[1]
    wide[...] = jnp.zeros_like(wide)
    wide[:, 0:depth] = right_ref[...].astype(f32)
    wide[:, SIDE - depth :] = left_ref[...].astype(f32)
    side = wide[...].astype(bf16)
    side_ref[...] = side
    up_ref[:, 0:cols] = top_ref[...]
    up_ref[:, cols:] = side[:depth]
    down_ref[:, 0:cols] = bottom_ref[...]
    down_ref[:, cols:] = side[rows - depth :]


def subspace_kernel(inv_count, packed_ref, start_ref, basis_ref, held):
    basis_ref[...] = subspace(unpack(packed_ref[...], inv_count), start_ref[...], held)


def main_kernel(
    depth, n_rows, n_cols, basis_ref, mid_ref, above_ref, below_ref, side_ref,
    out_ref, proj_ref, fit, field_a, field_b, out_stage, proj_stage, out_sems, proj_sem
):
    rows, cols, bands = mid_ref.shape
    span = cols + SIDE
    proj_copy = pltpu.make_async_copy(proj_stage, proj_ref, proj_sem)

    def out_copy(n):
        part = pl.ds(n * OUT_ROWS, OUT_ROWS)
        return pltpu.make_async_copy(out_stage.at[part], out_ref.at[part], out_sems.at[n])

    high, mid, low = split3(basis_ref[...])
    tn = (((0,), (0,)), ((), ()))
    mixed = lax.dot_general(
        jnp.concatenate([high, high, high], axis=0),
        jnp.concatenate([high, mid, low], axis=0),
        tn,
        preferred_element_type=f32,
    )
    mixed = mixed * 4.0
    mixed_high = mixed.astype(bf16)
    mixed_low = (mixed - mixed_high.astype(f32)).astype(bf16)
    mixed_both = jnp.concatenate([mixed_high, mixed_low], axis=0)

    def fitted(flat):
        padded = jnp.concatenate([flat, jnp.zeros((flat.shape[0], LANES - bands), bf16)], axis=1)
        both = jnp.concatenate([padded, padded], axis=1)
        return jnp.dot(both, mixed_both, preferred_element_type=f32)

    def project():
        right = jnp.concatenate([high, high, high, mid, mid, low], axis=0)
        left = jnp.concatenate([high, mid, low, high, mid, high], axis=0)
        full = lax.dot_general(left, right, tn, preferred_element_type=f32)
        proj_stage[...] = full[:bands, :bands]
        proj_copy.start()

    def fit_rows(start, stop):
        n = stop - start
        if depth <= start < depth + rows:
            part = slice(start - depth, stop - depth)
            center = mid_ref[part].reshape(n * cols, bands)
            side = side_ref[part].astype(f32).reshape(n * SIDE, bands).astype(bf16)
            res = fitted(jnp.concatenate([center, side], axis=0))
            for h, lane in enumerate(lanes):
                fit[h, start:stop, 0:cols] = res[: n * cols, lane].reshape(n, cols, HALF)
                fit[h, start:stop, cols:span] = res[n * cols :, lane].reshape(n, SIDE, HALF)
        else:
            block = above_ref[...] if start < depth else below_ref[...]
            flat = block.astype(f32).reshape(n * span, bands).astype(bf16)
            res = fitted(flat)
            for h, lane in enumerate(lanes):
                fit[h, start:stop] = res[:, lane].reshape(n, span, HALF)

    row, col = lax.axis_index("narrow"), lax.axis_index("wide")
    at_top, at_bottom = row == 0, row == n_rows - 1
    at_left, at_right = col == 0, col == n_cols - 1
    per = span // SUB
    place = lax.broadcasted_iota(jnp.int32, (SUB, HALF), 0)
    keeps = {}
    for column, shut in ((cols - 1, at_right), (span - 1, at_left)):
        keep = jnp.where((place == column // per) & shut, 0.0, 1.0).astype(f32)
        keeps[column % per] = keeps[column % per] * keep if column % per in keeps else keep
    open_rows = {
        depth - 1: jnp.where(at_top, 0.0, 1.0),
        depth + rows - 1: jnp.where(at_bottom, 0.0, 1.0),
    }
    lanes = [slice(0, HALF), slice(HALF, LANES)]
    fields = [fit, field_a, field_b]

    def natural(ref, h, r):
        return [ref[h, r, pl.ds(w, SUB, stride=per), :] for w in range(per)]

    def spread(ref, h, r):
        return [ref[h, r, w * SUB : (w + 1) * SUB, :] for w in range(per)]

    def slopes(now, later, open_row=None):
        follow = now[1:] + [pltpu.roll(now[0], SUB - 1, 0)]
        downs, acrosses = [], []
        for w in range(per):
            down = later[w] - now[w]
            if open_row is not None:
                down = down * open_row
            across = follow[w] - now[w]
            if w in keeps:
                across = across * keeps[w]
            inverse = lax.rsqrt(down * down + (across * across + 4.0))
            downs.append(down * inverse)
            acrosses.append(across * inverse)
        return downs, acrosses

    def advance(base, before, down, across):
        behind = [pltpu.roll(across[-1], 1, 0)] + across[:-1]
        return [
            base[w] + ((down[w] - before[w]) + (across[w] - behind[w])) for w in range(per)
        ]

    def put(ref, h, r, value):
        for w in range(per):
            ref[h, r, w * SUB : (w + 1) * SUB, :] = value[w]

    tall = rows + 2 * depth
    groups = [(0, depth)]
    for n in FIT_ROWS:
        groups.append((groups[-1][1], groups[-1][1] + n))
    groups += [(depth + rows, tall)]
    ready = 0
    befores = [None] * len(lanes)
    for r in range(tall - 1):
        while ready < len(groups) and groups[ready][0] <= r + 1 + AHEAD:
            fit_rows(*groups[ready])
            ready += 1
            if ready == 4:
                project()
        for h in range(len(lanes)):
            now = natural(fit, h, r)
            down, across = slopes(now, natural(fit, h, r + 1), open_rows.get(r))
            if r > 0:
                put(field_a, h, r, advance(now, befores[h], down, across))
            befores[h] = down

    def step(s, first, trips, unroll):
        source, final = fields[s], s == TV_ITERS - 1

        @pl.when(at_top)
        def _():
            source[:, depth - 1] = source[:, depth]

        @pl.when(at_bottom)
        def _():
            source[:, depth + rows] = source[:, depth + rows - 1]

        def block_step(n, carry):
            carry = list(carry)
            for inner in range(unroll):
                r = first + n * unroll + inner
                for h, lane in enumerate(lanes):
                    now, before = carry[2 * h], carry[2 * h + 1]
                    later = spread(source, h, r + 1)
                    down, across = slopes(now, later)
                    base = [0.5 * (x + y) for x, y in zip(now, natural(fit, h, r))]
                    value = advance(base, before, down, across)
                    if final:
                        for w in range(per):
                            field_a[h, r, pl.ds(w, SUB, stride=per), :] = value[w]
                        result = (field_a[h, r, 0:cols, :] * 0.25).astype(bf16)
                        width = min(lane.stop, bands) - lane.start
                        out_stage[r - depth, :, lane.start : lane.start + width] = result[:, :width]
                    else:
                        put(fields[s + 1], h, r, value)
                    carry[2 * h], carry[2 * h + 1] = later, down
                if final and inner % OUT_ROWS == OUT_ROWS - 1:
                    out_copy(n * (unroll // OUT_ROWS) + inner // OUT_ROWS).start()
            return tuple(carry)

        carry = []
        for h in range(len(lanes)):
            before, now = spread(source, h, first - 1), spread(source, h, first)
            carry += [now, slopes(before, now)[0]]
        lax.fori_loop(0, trips, block_step, tuple(carry))

    step(1, 2, (rows + 2) // TV_ROWS[0], TV_ROWS[0])
    step(2, depth, rows // TV_ROWS[1], TV_ROWS[1])
    proj_copy.wait()
    for n in range(rows // OUT_ROWS):
        out_copy(n).wait()


def start_basis():
    bands = np.arange(BANDS, dtype=np.float32)[None, :]
    cols = np.arange(RANK, dtype=np.float32)[:, None]
    angle = np.float32(np.pi) * (bands + np.float32(0.5)) * cols / np.float32(BANDS)
    return np.pad(np.cos(angle).astype(np.float32), ((0, 0), (0, LANES - BANDS)))


def neighbours(block, axis, dim, width):
    count = lax.axis_size(axis)
    size = block.shape[dim]
    head = lax.slice_in_dim(block, 0, width, axis=dim)
    tail = lax.slice_in_dim(block, size - width, size, axis=dim)
    before = lax.ppermute(tail, axis, [(i, i + 1) for i in range(count - 1)])
    after = lax.ppermute(head, axis, [(i + 1, i) for i in range(count - 1)])
    return before, after


def exchange(pieces, axes):
    return lax.all_to_all(pieces, axes, split_axis=0, concat_axis=0)


def body(cube):
    n_rows = lax.axis_size("narrow")
    n_cols = lax.axis_size("wide")
    count = n_rows * n_cols
    rows, cols, bands = cube.shape
    depth = TV_ITERS
    axes = ("narrow", "wide")

    tall_packed = -(-bands // count) * count
    vmem = pl.BlockSpec(memory_space=pltpu.VMEM)
    packed = pl.pallas_call(
        gram_kernel,
        in_specs=[vmem],
        out_specs=vmem,
        out_shape=jax.ShapeDtypeStruct((tall_packed, HALF), f32),
        scratch_shapes=[pltpu.VMEM((LANES, LANES), f32)],
        compiler_params=pltpu.CompilerParams(vmem_limit_bytes=32 * 2**20),
    )(cube)
    packed, cube = lax.optimization_barrier((packed, cube))
    left, right = neighbours(cube, "wide", 1, depth)
    pieces_shape = (count, 1, tall_packed // count * HALF)
    part = exchange(packed.reshape(pieces_shape), axes).reshape(tall_packed, HALF)
    share = pl.pallas_call(
        functools.partial(sum_kernel, count),
        in_specs=[vmem],
        out_specs=vmem,
        out_shape=jax.ShapeDtypeStruct((tall_packed, HALF), f32),
        compiler_params=pltpu.CompilerParams(vmem_limit_bytes=16 * 2**20),
    )(part)
    gathered = exchange(share.reshape(pieces_shape), axes).reshape(tall_packed, HALF)

    tall, span = rows + 2 * depth, cols + SIDE
    up, down, side = pl.pallas_call(
        functools.partial(halo_kernel, depth),
        in_specs=[vmem] * 4,
        out_specs=[vmem] * 3,
        out_shape=[
            jax.ShapeDtypeStruct((depth, span, bands), bf16),
            jax.ShapeDtypeStruct((depth, span, bands), bf16),
            jax.ShapeDtypeStruct((rows, SIDE, bands), bf16),
        ],
        scratch_shapes=[pltpu.VMEM((rows, SIDE, bands), f32)],
        cost_estimate=pl.CostEstimate(flops=2**32, bytes_accessed=2**18, transcendentals=0),
        compiler_params=pltpu.CompilerParams(vmem_limit_bytes=16 * 2**20),
    )(left, right, cube[:depth], cube[rows - depth :])
    above = lax.ppermute(down, "narrow", [(i, i + 1) for i in range(n_rows - 1)])
    below = lax.ppermute(up, "narrow", [(i + 1, i) for i in range(n_rows - 1)])

    inv_count = 1.0 / (count * rows * cols)
    basis = pl.pallas_call(
        functools.partial(subspace_kernel, inv_count),
        in_specs=[vmem] * 2,
        out_specs=vmem,
        out_shape=jax.ShapeDtypeStruct((RANK, LANES), f32),
        scratch_shapes=[pltpu.VMEM((2, LANES, LANES), bf16)],
        cost_estimate=pl.CostEstimate(flops=2**32, bytes_accessed=2**18, transcendentals=0),
        compiler_params=pltpu.CompilerParams(vmem_limit_bytes=16 * 2**20),
    )(gathered, jnp.asarray(start_basis()))
    restored, projector = pl.pallas_call(
        functools.partial(main_kernel, depth, n_rows, n_cols),
        in_specs=[vmem] * 5,
        out_specs=[pl.BlockSpec(memory_space=pl.ANY)] * 2,
        out_shape=[
            jax.ShapeDtypeStruct((rows, cols, bands), bf16),
            jax.ShapeDtypeStruct((bands, bands), f32),
        ],
        scratch_shapes=[pltpu.VMEM((2, tall, span, HALF), f32)] * 3
        + [
            pltpu.VMEM((rows, cols, bands), bf16),
            pltpu.VMEM((bands, bands), f32),
            pltpu.SemaphoreType.DMA((rows // OUT_ROWS,)),
            pltpu.SemaphoreType.DMA,
        ],
        compiler_params=pltpu.CompilerParams(vmem_limit_bytes=48 * 2**20),
    )(basis, cube, above, below, side)
    return restored, projector


def solution(mesh):
    return jax.shard_map(
        body,
        mesh=mesh,
        in_specs=(P("narrow", "wide", None),),
        out_specs=(P("narrow", "wide", None), P()),
        check_vma=False,
    )
```

```python
import functools

import jax
import jax.numpy as jnp
import numpy as np
from jax import lax
from jax.experimental import pallas as pl
from jax.experimental.pallas import tpu as pltpu
from jax.sharding import PartitionSpec as P

BANDS = 224
RANK = 16
POWER_ITERS = 4
TV_ITERS = 3
LANES = 256
HALF = 128
TAIL = BANDS - HALF
SIDE = 8
SUB = 8
BLOCK = 8
FIT_ROWS = (2, 6, 8, 8, 8)
AHEAD = 4
TV_ROWS = (17, 16)
OUT_ROWS = 4

f32 = jnp.float32
bf16 = jnp.bfloat16


def iotas(shape):
    return lax.broadcasted_iota(jnp.int32, shape, 0), lax.broadcasted_iota(jnp.int32, shape, 1)


def gram_kernel(cube_ref, packed_ref, full):
    rows, cols, bands = cube_ref.shape
    flat = cube_ref[...].reshape(rows * cols, bands)
    full[HALF:, HALF:] = jnp.zeros((LANES - HALF, LANES - HALF), f32)
    full[0:bands, 0:bands] = lax.dot_general(
        flat, flat, (((0,), (0,)), ((), ())), preferred_element_type=f32
    )
    i, j = iotas((HALF, HALF))
    first = full[0:HALF, 0:HALF]
    second = pltpu.roll(full[HALF:LANES, HALF:LANES], 1, 1)
    packed_ref[0:HALF, :] = jnp.where(j <= i, first, second)
    packed_ref[HALF:bands, :] = full[HALF:bands, 0:HALF]
    if packed_ref.shape[0] > bands:
        packed_ref[bands:, :] = jnp.zeros((packed_ref.shape[0] - bands, HALF), f32)


def sum_kernel(count, pieces_ref, spread_ref):
    high = pieces_ref.shape[0] // count
    parts = [pieces_ref[n * high : (n + 1) * high, :] for n in range(count)]
    total = functools.reduce(jnp.add, parts)
    for n in range(count):
        spread_ref[n * high : (n + 1) * high, :] = total


def split3(x):
    high = x.astype(bf16)
    rest = x - high.astype(f32)
    mid = rest.astype(bf16)
    low = (rest - mid.astype(f32)).astype(bf16)
    return high, mid, low


def product(left, right, dims):
    def dot(a, b):
        return lax.dot_general(a, b, (dims, ((), ())), preferred_element_type=f32)

    n = left[0].shape[0]
    top = dot(jnp.concatenate(left, axis=0), right[0])
    middle = dot(jnp.concatenate(left[:2], axis=0), right[1])
    small = top[2 * n : 3 * n] + middle[n : 2 * n]
    if len(right) > 2:
        small = small + dot(left[0], right[2])
    return top[:n] + ((top[n : 2 * n] + middle[:n]) + small)


def unpack(packed, scale):
    i, j = iotas((HALF, HALF))
    merged = packed[0:HALF, :] * scale
    below = packed[HALF:BANDS, :] * scale
    below = jnp.concatenate([below, jnp.zeros((LANES - BANDS, HALF), f32)], axis=0)
    first = jnp.where(j <= i, merged, 0.0) + jnp.where(j < i, merged, 0.0).T
    moved = pltpu.roll(merged, HALF - 1, 1)
    inside = (i < TAIL) & (j < TAIL)
    second = jnp.where(inside & (j >= i), moved, 0.0) + jnp.where(inside & (j > i), moved, 0.0).T
    return jnp.concatenate(
        [
            jnp.concatenate([first, below.T], axis=1),
            jnp.concatenate([below, second], axis=1),
        ],
        axis=0,
    )


def orthonormal(grown, inner):
    row = lax.broadcasted_iota(jnp.int32, (RANK, HALF), 0)
    work = [
        jnp.concatenate([inner, jnp.zeros((RANK, HALF - RANK), f32)], axis=1),
        grown[:, :HALF],
        grown[:, HALF:],
    ]
    diagonal = jnp.ones((RANK, HALF), f32)
    for k in range(0, RANK, BLOCK):
        columns = [
            jnp.broadcast_to(work[0][:, k + c : k + c + 1], (RANK, HALF)) for c in range(BLOCK)
        ]
        tops = [[part[k + r : k + r + 1, :] for part in work] for r in range(BLOCK)]
        small = [
            [columns[c][k + r : k + r + 1, :] for c in range(r + 1)] for r in range(BLOCK)
        ]
        factors = []
        for j in range(BLOCK):
            pivot = small[j][j]
            inverse = pl.reciprocal(pivot, full_range=False)
            diagonal = jnp.where(row == k + j, pivot, diagonal)
            factor = jnp.where(row > k + j, columns[j] * inverse, 0.0)
            factors.append(factor)
            below = [small[i][j] for i in range(BLOCK) if i > j]
            for i in range(j + 1, BLOCK):
                ratio = small[i][j] * inverse
                for c in range(j + 1, i + 1):
                    small[i][c] = small[i][c] - ratio * below[c - j - 1]
                tops[i] = [x - ratio * y for x, y in zip(tops[i], tops[j])]
                columns[i] = columns[i] - factor * below[i - j - 1]
        for n in range(len(work)):
            if n > 0 or k + BLOCK < RANK:
                for j in range(BLOCK):
                    work[n] = work[n] - factors[j] * tops[j][n]
    scale = lax.rsqrt(diagonal)
    return jnp.concatenate([work[1] * scale, work[2] * scale], axis=1)


def subspace(gram, start, held):
    for n, part in enumerate(split3(gram)[:2]):
        held[n] = part

    def times_gram(pieces):
        return product(pieces, [held[0], held[1]], ((1,), (0,)))

    def iterate(_, grown):
        pieces = split3(grown)
        inner = product(pieces, pieces, ((1,), (1,)))
        return orthonormal(times_gram(pieces), inner)

    grown = lax.fori_loop(0, POWER_ITERS - 1, iterate, times_gram(split3(start)))
    pieces = split3(grown)
    return orthonormal(grown, product(pieces, pieces, ((1,), (1,))))


def halo_kernel(depth, left_ref, right_ref, top_ref, bottom_ref, up_ref, down_ref, side_ref, wide):
    rows, cols = side_ref.shape[0], top_ref.shape[1]
    wide[...] = jnp.zeros_like(wide)
    wide[:, 0:depth] = right_ref[...].astype(f32)
    wide[:, SIDE - depth :] = left_ref[...].astype(f32)
    side = wide[...].astype(bf16)
    side_ref[...] = side
    up_ref[:, 0:cols] = top_ref[...]
    up_ref[:, cols:] = side[:depth]
    down_ref[:, 0:cols] = bottom_ref[...]
    down_ref[:, cols:] = side[rows - depth :]


def subspace_kernel(inv_count, packed_ref, start_ref, basis_ref, held):
    basis_ref[...] = subspace(unpack(packed_ref[...], inv_count), start_ref[...], held)


def main_kernel(
    depth, n_rows, n_cols, basis_ref, mid_ref, above_ref, below_ref, side_ref,
    out_ref, proj_ref, fit, field_a, field_b, out_stage, proj_stage, out_sems, proj_sem
):
    rows, cols, bands = mid_ref.shape
    span = cols + SIDE
    proj_copy = pltpu.make_async_copy(proj_stage, proj_ref, proj_sem)

    def out_copy(n):
        part = pl.ds(n * OUT_ROWS, OUT_ROWS)
        return pltpu.make_async_copy(out_stage.at[part], out_ref.at[part], out_sems.at[n])

    high, mid, low = split3(basis_ref[...])
    tn = (((0,), (0,)), ((), ()))
    mixed = lax.dot_general(
        jnp.concatenate([high, high, high], axis=0),
        jnp.concatenate([high, mid, low], axis=0),
        tn,
        preferred_element_type=f32,
    )
    mixed = mixed * 4.0
    mixed_high = mixed.astype(bf16)
    mixed_low = (mixed - mixed_high.astype(f32)).astype(bf16)
    mixed_both = jnp.concatenate([mixed_high, mixed_low], axis=0)

    def fitted(flat):
        padded = jnp.concatenate([flat, jnp.zeros((flat.shape[0], LANES - bands), bf16)], axis=1)
        both = jnp.concatenate([padded, padded], axis=1)
        return jnp.dot(both, mixed_both, preferred_element_type=f32)

    def project():
        right = jnp.concatenate([high, high, high, mid, mid, low], axis=0)
        left = jnp.concatenate([high, mid, low, high, mid, high], axis=0)
        full = lax.dot_general(left, right, tn, preferred_element_type=f32)
        proj_stage[...] = full[:bands, :bands]
        proj_copy.start()

    def fit_rows(start, stop):
        n = stop - start
        if depth <= start < depth + rows:
            part = slice(start - depth, stop - depth)
            center = mid_ref[part].reshape(n * cols, bands)
            side = side_ref[part].astype(f32).reshape(n * SIDE, bands).astype(bf16)
            res = fitted(jnp.concatenate([center, side], axis=0))
            for h, lane in enumerate(lanes):
                fit[h, start:stop, 0:cols] = res[: n * cols, lane].reshape(n, cols, HALF)
                fit[h, start:stop, cols:span] = res[n * cols :, lane].reshape(n, SIDE, HALF)
        else:
            block = above_ref[...] if start < depth else below_ref[...]
            flat = block.astype(f32).reshape(n * span, bands).astype(bf16)
            res = fitted(flat)
            for h, lane in enumerate(lanes):
                fit[h, start:stop] = res[:, lane].reshape(n, span, HALF)

    row, col = lax.axis_index("narrow"), lax.axis_index("wide")
    at_top, at_bottom = row == 0, row == n_rows - 1
    at_left, at_right = col == 0, col == n_cols - 1
    per = span // SUB
    place = lax.broadcasted_iota(jnp.int32, (SUB, HALF), 0)
    keeps = {}
    for column, shut in ((cols - 1, at_right), (span - 1, at_left)):
        keep = jnp.where((place == column // per) & shut, 0.0, 1.0).astype(f32)
        keeps[column % per] = keeps[column % per] * keep if column % per in keeps else keep
    open_rows = {
        depth - 1: jnp.where(at_top, 0.0, 1.0),
        depth + rows - 1: jnp.where(at_bottom, 0.0, 1.0),
    }
    lanes = [slice(0, HALF), slice(HALF, LANES)]
    fields = [fit, field_a, field_b]

    def natural(ref, h, r):
        return [ref[h, r, pl.ds(w, SUB, stride=per), :] for w in range(per)]

    def spread(ref, h, r):
        return [ref[h, r, w * SUB : (w + 1) * SUB, :] for w in range(per)]

    def slopes(now, later, open_row=None):
        follow = now[1:] + [pltpu.roll(now[0], SUB - 1, 0)]
        downs, acrosses = [], []
        for w in range(per):
            down = later[w] - now[w]
            if open_row is not None:
                down = down * open_row
            across = follow[w] - now[w]
            if w in keeps:
                across = across * keeps[w]
            inverse = lax.rsqrt(down * down + (across * across + 4.0))
            downs.append(down * inverse)
            acrosses.append(across * inverse)
        return downs, acrosses

    def advance(base, before, down, across):
        behind = [pltpu.roll(across[-1], 1, 0)] + across[:-1]
        return [
            base[w] + ((down[w] - before[w]) + (across[w] - behind[w])) for w in range(per)
        ]

    def put(ref, h, r, value):
        for w in range(per):
            ref[h, r, w * SUB : (w + 1) * SUB, :] = value[w]

    tall = rows + 2 * depth
    groups = [(0, depth)]
    for n in FIT_ROWS:
        groups.append((groups[-1][1], groups[-1][1] + n))
    groups += [(depth + rows, tall)]
    ready = 0
    befores = [None] * len(lanes)
    for r in range(tall - 1):
        while ready < len(groups) and groups[ready][0] <= r + 1 + AHEAD:
            fit_rows(*groups[ready])
            ready += 1
            if ready == len(groups):
                project()
        for h in range(len(lanes)):
            now = natural(fit, h, r)
            down, across = slopes(now, natural(fit, h, r + 1), open_rows.get(r))
            if r > 0:
                put(field_a, h, r, advance(now, befores[h], down, across))
            befores[h] = down

    def step(s, first, trips, unroll):
        source, final = fields[s], s == TV_ITERS - 1

        @pl.when(at_top)
        def _():
            source[:, depth - 1] = source[:, depth]

        @pl.when(at_bottom)
        def _():
            source[:, depth + rows] = source[:, depth + rows - 1]

        def block_step(n, carry):
            carry = list(carry)
            for inner in range(unroll):
                r = first + n * unroll + inner
                for h, lane in enumerate(lanes):
                    now, before = carry[2 * h], carry[2 * h + 1]
                    later = spread(source, h, r + 1)
                    down, across = slopes(now, later)
                    base = [0.5 * (x + y) for x, y in zip(now, natural(fit, h, r))]
                    value = advance(base, before, down, across)
                    if final:
                        for w in range(per):
                            field_a[h, r, pl.ds(w, SUB, stride=per), :] = value[w]
                        result = (field_a[h, r, 0:cols, :] * 0.25).astype(bf16)
                        width = min(lane.stop, bands) - lane.start
                        out_stage[r - depth, :, lane.start : lane.start + width] = result[:, :width]
                    else:
                        put(fields[s + 1], h, r, value)
                    carry[2 * h], carry[2 * h + 1] = later, down
                if final and inner % OUT_ROWS == OUT_ROWS - 1:
                    out_copy(n * (unroll // OUT_ROWS) + inner // OUT_ROWS).start()
            return tuple(carry)

        carry = []
        for h in range(len(lanes)):
            before, now = spread(source, h, first - 1), spread(source, h, first)
            carry += [now, slopes(before, now)[0]]
        lax.fori_loop(0, trips, block_step, tuple(carry))

    step(1, 2, (rows + 2) // TV_ROWS[0], TV_ROWS[0])
    step(2, depth, rows // TV_ROWS[1], TV_ROWS[1])
    proj_copy.wait()
    for n in range(rows // OUT_ROWS):
        out_copy(n).wait()


def start_basis():
    bands = np.arange(BANDS, dtype=np.float32)[None, :]
    cols = np.arange(RANK, dtype=np.float32)[:, None]
    angle = np.float32(np.pi) * (bands + np.float32(0.5)) * cols / np.float32(BANDS)
    return np.pad(np.cos(angle).astype(np.float32), ((0, 0), (0, LANES - BANDS)))


def neighbours(block, axis, dim, width):
    count = lax.axis_size(axis)
    size = block.shape[dim]
    head = lax.slice_in_dim(block, 0, width, axis=dim)
    tail = lax.slice_in_dim(block, size - width, size, axis=dim)
    before = lax.ppermute(tail, axis, [(i, i + 1) for i in range(count - 1)])
    after = lax.ppermute(head, axis, [(i + 1, i) for i in range(count - 1)])
    return before, after


def exchange(pieces, axes):
    return lax.all_to_all(pieces, axes, split_axis=0, concat_axis=0)


def body(cube):
    n_rows = lax.axis_size("narrow")
    n_cols = lax.axis_size("wide")
    count = n_rows * n_cols
    rows, cols, bands = cube.shape
    depth = TV_ITERS
    axes = ("narrow", "wide")

    tall_packed = -(-bands // count) * count
    vmem = pl.BlockSpec(memory_space=pltpu.VMEM)
    packed = pl.pallas_call(
        gram_kernel,
        in_specs=[vmem],
        out_specs=vmem,
        out_shape=jax.ShapeDtypeStruct((tall_packed, HALF), f32),
        scratch_shapes=[pltpu.VMEM((LANES, LANES), f32)],
        compiler_params=pltpu.CompilerParams(vmem_limit_bytes=32 * 2**20),
    )(cube)
    packed, cube = lax.optimization_barrier((packed, cube))
    left, right = neighbours(cube, "wide", 1, depth)
    pieces_shape = (count, 1, tall_packed // count * HALF)
    part = exchange(packed.reshape(pieces_shape), axes).reshape(tall_packed, HALF)
    share = pl.pallas_call(
        functools.partial(sum_kernel, count),
        in_specs=[vmem],
        out_specs=vmem,
        out_shape=jax.ShapeDtypeStruct((tall_packed, HALF), f32),
        compiler_params=pltpu.CompilerParams(vmem_limit_bytes=16 * 2**20),
    )(part)
    gathered = exchange(share.reshape(pieces_shape), axes).reshape(tall_packed, HALF)

    tall, span = rows + 2 * depth, cols + SIDE
    up, down, side = pl.pallas_call(
        functools.partial(halo_kernel, depth),
        in_specs=[vmem] * 4,
        out_specs=[vmem] * 3,
        out_shape=[
            jax.ShapeDtypeStruct((depth, span, bands), bf16),
            jax.ShapeDtypeStruct((depth, span, bands), bf16),
            jax.ShapeDtypeStruct((rows, SIDE, bands), bf16),
        ],
        scratch_shapes=[pltpu.VMEM((rows, SIDE, bands), f32)],
        cost_estimate=pl.CostEstimate(flops=2**32, bytes_accessed=2**18, transcendentals=0),
        compiler_params=pltpu.CompilerParams(vmem_limit_bytes=16 * 2**20),
    )(left, right, cube[:depth], cube[rows - depth :])
    above = lax.ppermute(down, "narrow", [(i, i + 1) for i in range(n_rows - 1)])
    below = lax.ppermute(up, "narrow", [(i + 1, i) for i in range(n_rows - 1)])

    inv_count = 1.0 / (count * rows * cols)
    basis = pl.pallas_call(
        functools.partial(subspace_kernel, inv_count),
        in_specs=[vmem] * 2,
        out_specs=vmem,
        out_shape=jax.ShapeDtypeStruct((RANK, LANES), f32),
        scratch_shapes=[pltpu.VMEM((2, LANES, LANES), bf16)],
        cost_estimate=pl.CostEstimate(flops=2**32, bytes_accessed=2**18, transcendentals=0),
        compiler_params=pltpu.CompilerParams(vmem_limit_bytes=16 * 2**20),
    )(gathered, jnp.asarray(start_basis()))
    restored, projector = pl.pallas_call(
        functools.partial(main_kernel, depth, n_rows, n_cols),
        in_specs=[vmem] * 5,
        out_specs=[pl.BlockSpec(memory_space=pl.ANY)] * 2,
        out_shape=[
            jax.ShapeDtypeStruct((rows, cols, bands), bf16),
            jax.ShapeDtypeStruct((bands, bands), f32),
        ],
        scratch_shapes=[pltpu.VMEM((2, tall, span, HALF), f32)] * 3
        + [
            pltpu.VMEM((rows, cols, bands), bf16),
            pltpu.VMEM((bands, bands), f32),
            pltpu.SemaphoreType.DMA((rows // OUT_ROWS,)),
            pltpu.SemaphoreType.DMA,
        ],
        compiler_params=pltpu.CompilerParams(vmem_limit_bytes=48 * 2**20),
    )(basis, cube, above, below, side)
    return restored, projector


def solution(mesh):
    return jax.shard_map(
        body,
        mesh=mesh,
        in_specs=(P("narrow", "wide", None),),
        out_specs=(P("narrow", "wide", None), P()),
        check_vma=False,
    )
```
